32 devices in a mesh: ctx: 8 (over z, x), tp: 4 (over y, core).
Axes of the slice: x: 2, y: 2, z: 4, core: 2. Of those that a mesh axis runs over, the one named last changes fastest.
Arguments:
- tokens_in: bfloat16 [2048, 2048], P('ctx'), may hold values from -6 to 6
- block_order: int32 [2, 8], replicated, may hold values from 0 to 7, each once within a row
- routes: int32 [2048, 8], P('ctx'), may hold values from 0 to 31, all different within a row; in each aligned block of 256 rows (0 to 255, 256 to 511, ...) at most 128 rows name the same one
- norm1_gain: float32 [2048], replicated, may hold values from 0.5 to 1.5
- w_query: bfloat16 [2048, 4096], P(None, 'tp'), may hold values from -0.125 to 0.125
- key_weight: bfloat16 [2048, 512], P(None, 'tp'), may hold values from -0.125 to 0.125
- value_weight: bfloat16 [2048, 512], P(None, 'tp'), may hold values from -0.125 to 0.125
- query_gain: float32 [128], replicated, may hold values from 0.5 to 1.5
- key_gain: float32 [128], replicated, may hold values from 0.5 to 1.5
- w_out: bfloat16 [4096, 2048], P('tp'), may hold values from -1.5 to 1.5
- norm2_gain: float32 [2048], replicated, may hold values from 0.5 to 1.5
- w_router: bfloat16 [2048, 32], replicated, may hold values from -0.0625 to 0.0625
- w_gate: bfloat16 [32, 2048, 768], P('ctx', None, 'tp'), may hold values from -0.125 to 0.125
- w_up: bfloat16 [32, 2048, 768], P('ctx', None, 'tp'), may hold values from -0.125 to 0.125
- w_down: bfloat16 [32, 768, 2048], P('ctx', 'tp'), may hold values from -0.875 to 0.875
- cotangent: bfloat16 [2048, 2048], P('ctx'), may hold values from -6 to 6
Outputs:
- layer_out: bfloat16 [2048, 2048], P('ctx')
- grad_input: bfloat16 [2048, 2048], P('ctx')
- grad_norm1: float32 [2048], P('ctx')
- grad_query: float32 [2048, 4096], P('ctx', 'tp')
- grad_key: float32 [2048, 512], P('ctx', 'tp')
- grad_value: float32 [2048, 512], P('ctx', 'tp')
- grad_qgain: float32 [128], P('ctx')
- grad_kgain: float32 [128], P('ctx')
- grad_out: float32 [4096, 2048], P('tp', 'ctx')
- grad_norm2: float32 [2048], P('ctx')
- grad_router: float32 [2048, 32], P('ctx')
- grad_gate: float32 [32, 2048, 768], P('ctx', None, 'tp')
- grad_up: float32 [32, 2048, 768], P('ctx', None, 'tp')
- grad_down: float32 [32, 768, 2048], P('ctx', 'tp')
The draws below stay inside these ranges and needn't reach their ends.
Inputs may be any that keep to these rules, and one draw needn't show every extreme that they name: `block_order`: each row is a permutation: the ctx indices hold different block pairs of each sequence. `routes`: A token's 8 experts differ; among the rows of one ctx index no expert is named more than 128 times, a bound that some block reaches.
All inputs are finite; a program needn't handle non-finite values.
Results may differ from the reference program's by a relative error of at most 0.03.
Values may be sent and summed in bfloat16 or wider, within the bound.
A program may use at most 320 MiB of HBM per device.

```python
import math
import jax
import jax.numpy as jnp
import numpy as np
from jax import lax

MODEL_WIDTH = 2048
QUERY_HEADS = 32
KEY_VALUE_HEADS = 4
HEAD_WIDTH = 128
FFE = 768
TOPK = 8
EXPERTS = 32
SEQUENCE_COUNT = 2
BLOCK_TOKENS = 64
TOK_DEV = 256
TOKEN_TOTAL = 2048
SEQLEN = 1024
CAP = 128
N_CTX = 8
N_TP = 4


def shard_levels(stream_key, shape, shards, low, top_value):
    def one(position, shards_of):
        steps = jax.random.uniform(jax.random.fold_in(jax.random.fold_in(stream_key, 6), position), (shards_of,), jnp.float32, low / len(shards), top_value / len(shards))
        return jnp.repeat(jnp.exp(steps), shape[position] // shards_of).reshape((-1,) + (1,) * (len(shape) - position - 1))

    level = one(*shards[0])
    for cut in shards[1:]:
        level = level * one(*cut)
    return level


def routed_block(own_key, own, number, rows, amount, top, reach, skew):
    order = jax.random.permutation(own_key, amount)
    packed, common = portions_of(amount, rows * top, reach, skew, True), portions_of(amount, rows * top, reach, skew, False)
    places = jnp.arange(amount)

    def named(lengths, turn):
        used = int((lengths > 0).sum())
        fixed = max(1, used // 4)
        moved = fixed + (places - fixed + turn * (used - fixed)) % max(1, amount - fixed)
        return jnp.zeros((amount,), jnp.int32).at[order[jnp.where(places < fixed, places, moved)]].set(jnp.asarray(lengths, jnp.int32))

    lengths = jnp.where(number % 4 == 0, named(packed, number // 4), named(common, number - number // 4 - 1))
    mixed = jax.random.permutation(jax.random.fold_in(own, 3), amount)
    donor, sink = mixed[0:amount // 2 * 2:2], mixed[1:amount // 2 * 2:2]
    room = jnp.minimum(lengths[donor] - 1, reach - lengths[sink]) // 2
    room = jnp.where((donor == order[0]) | (sink == order[0]) | (lengths[sink] == 0), 0, jnp.maximum(room, 0))
    moved = jax.random.randint(jax.random.fold_in(own, 4), (amount // 2,), 0, 1 << 20) % (room + 1)
    lengths = lengths.at[donor].add(-moved).at[sink].add(moved)
    labels = jnp.searchsorted(jnp.cumsum(lengths), jnp.arange(rows * top), side="right").astype(jnp.int32)
    grid = labels.reshape(top, rows).T
    grid = grid[jax.random.permutation(jax.random.fold_in(own, 1), rows)]
    turn = jax.random.randint(jax.random.fold_in(own, 2), (rows, 1), 0, top)
    return jnp.take_along_axis(grid, (jnp.arange(top)[None, :] + turn) % top, axis=1)


def portions_of(amount, total, limit, skew, full):
    portions = [(1 << 20) // math.isqrt(rank ** skew) + 1 for rank in range(1, amount + 1)]
    largest = limit if full else min(limit, max(-(-total // amount), total * portions[0] // sum(portions)))
    least = 1 if total - largest >= amount - 1 else 0
    given, rest = [largest] + [least] * (amount - 1), total - largest - least * (amount - 1)
    while rest > 0:
        movable = [i for i in range(1, amount) if given[i] < largest] or [i for i in range(1, amount) if given[i] < limit]
        pool, remaining = sum([portions[i] for i in movable]), rest
        for i in movable:
            extra = min(limit - given[i], max(1, remaining * portions[i] // pool), rest)
            given[i] = given[i] + extra
            rest = rest - extra
    return np.array(given)


def gaussian(rng, shape, deviation, most, pieces=(), kind=jnp.bfloat16):
    values = jax.random.normal(rng, shape, jnp.float32) * deviation
    if len(pieces) > 0:
        values = shard_levels(rng, shape, pieces, -0.22, 0.18) * values
    return jnp.clip(values, min=-most, max=most).astype(kind)


def setup_inputs(seed: int = 0) -> dict:
    seeds = jax.random.split(jax.random.key(seed), 17)
    tokens_in = gaussian(seeds[0], (TOKEN_TOTAL, MODEL_WIDTH), 1.0, 6.0, ((0, 8),))
    block_order = jax.vmap(lambda own: jax.random.permutation(own, N_CTX))(jax.random.split(seeds[1], SEQUENCE_COUNT)).reshape((SEQUENCE_COUNT, N_CTX)).astype(jnp.int32)
    routes_keys = jax.random.split(jax.random.fold_in(seeds[2], 1), TOKEN_TOTAL // TOK_DEV)
    routes_turns = jax.random.permutation(jax.random.fold_in(seeds[2], 3), TOKEN_TOTAL // TOK_DEV)
    routes = jax.vmap(lambda own, number: routed_block(jax.random.fold_in(seeds[2], 2), own, number, TOK_DEV, EXPERTS, TOPK, CAP, 2))(routes_keys, routes_turns).reshape((TOKEN_TOTAL, TOPK))
    norm1_gain = jnp.clip(1.0 + 0.1 * jax.random.normal(seeds[3], (MODEL_WIDTH,), jnp.float32), 0.5, 1.5)
    w_query = gaussian(seeds[4], (MODEL_WIDTH, QUERY_HEADS * HEAD_WIDTH), MODEL_WIDTH ** -0.5, 0.125, ((1, 4),))
    key_weight = gaussian(seeds[5], (MODEL_WIDTH, KEY_VALUE_HEADS * HEAD_WIDTH), MODEL_WIDTH ** -0.5, 0.125, ((1, 4),))
    value_weight = gaussian(seeds[6], (MODEL_WIDTH, KEY_VALUE_HEADS * HEAD_WIDTH), MODEL_WIDTH ** -0.5, 0.125, ((1, 4),))
    query_gain = jnp.clip(1.0 + 0.1 * jax.random.normal(seeds[7], (HEAD_WIDTH,), jnp.float32), 0.5, 1.5)
    key_gain = jnp.clip(1.0 + 0.1 * jax.random.normal(seeds[8], (HEAD_WIDTH,), jnp.float32), 0.5, 1.5)
    w_out = gaussian(seeds[9], (QUERY_HEADS * HEAD_WIDTH, MODEL_WIDTH), (QUERY_HEADS * HEAD_WIDTH // (SEQLEN // 4)) ** -0.5, 1.5, ((0, 4),))
    norm2_gain = jnp.clip(1.0 + 0.1 * jax.random.normal(seeds[10], (MODEL_WIDTH,), jnp.float32), 0.5, 1.5)
    w_router = gaussian(seeds[11], (MODEL_WIDTH, EXPERTS), (4 * MODEL_WIDTH) ** -0.5, 0.0625)
    w_gate = gaussian(seeds[12], (EXPERTS, MODEL_WIDTH, FFE), MODEL_WIDTH ** -0.5, 0.125, ((0, 8), (2, 4)))
    w_up = gaussian(seeds[13], (EXPERTS, MODEL_WIDTH, FFE), MODEL_WIDTH ** -0.5, 0.125, ((0, 8), (2, 4)))
    w_down = gaussian(seeds[14], (EXPERTS, FFE, MODEL_WIDTH), (FFE // 16) ** -0.5, 0.875, ((0, 8), (1, 4)))
    cotangent = gaussian(seeds[15], (TOKEN_TOTAL, MODEL_WIDTH), 1.0, 6.0, ((0, 8),))
    return dict(tokens_in=tokens_in, block_order=block_order, routes=routes, norm1_gain=norm1_gain, w_query=w_query, key_weight=key_weight, value_weight=value_weight, query_gain=query_gain, key_gain=key_gain, w_out=w_out, norm2_gain=norm2_gain, w_router=w_router, w_gate=w_gate, w_up=w_up, w_down=w_down, cotangent=cotangent)


EPSILON = 1e-06
ROPE_BASE = 1000000.0
MASKED_SCORE = -1000000000.0

@jax.custom_vjp
def lower_precision(v):
    return lax.optimization_barrier(v.astype(jnp.bfloat16)).astype(jnp.float32)

@jax.custom_vjp
def low_back(v):
    return v

def low_keep(v):
    return (lower_precision(v), None)

def low_pass(kept, grad):
    return (grad,)

def back_keep(v):
    return (v, None)

def back_low(kept, grad):
    return (lower_precision(grad),)
lower_precision.defvjp(low_keep, low_pass)
low_back.defvjp(back_keep, back_low)

def matmul_high(left, right):
    return jnp.dot(left, right, precision=lax.Precision.HIGHEST, preferred_element_type=jnp.float32)

def rms_norm(values, gain_vec):
    factor = lax.rsqrt(lax.optimization_barrier(jnp.mean(values * values, axis=-1, keepdims=True)) + EPSILON)
    return values * factor * gain_vec

def soft_rows(scores):
    row_top = lax.optimization_barrier(jnp.max(scores, axis=-1, keepdims=True))
    exp_scores = jnp.exp(scores - row_top)
    return exp_scores / lax.optimization_barrier(jnp.sum(exp_scores, axis=-1, keepdims=True))

def silu_mix(gate_pre, up_pre):
    return gate_pre / (1.0 + jnp.exp(-gate_pre)) * up_pre

def rotate(values, rotary_angles):
    half_size = values.shape[-1] // 2
    first_half = values[..., :half_size]
    second_half = values[..., half_size:]
    cosine = jnp.cos(rotary_angles)
    sine_part = jnp.sin(rotary_angles)
    return jnp.concatenate([first_half * cosine - second_half * sine_part, second_half * cosine + first_half * sine_part], axis=-1)

def angles_of(token_positions, head_width):
    freq_steps = jnp.arange(head_width // 2).astype(jnp.float32) * (2.0 / head_width)
    frequency = jnp.exp(-math.log(ROPE_BASE) * freq_steps)
    return token_positions.astype(jnp.float32)[..., None] * frequency

def positions_of(block_order, dev_count, block_len):
    first_block = jnp.transpose(block_order)
    block_pair = jnp.stack([first_block, 2 * dev_count - 1 - first_block], axis=-1)
    spread = block_pair[..., None] * block_len + jnp.arange(block_len, dtype=jnp.int32)
    return spread.reshape(dev_count, block_order.shape[0], 2 * block_len)

def head_route_path(raw_heads, gain_vec, rotary_angles, head_count):
    shaped = raw_heads.reshape(raw_heads.shape[0], head_count, -1)
    return rotate(rms_norm(shaped, gain_vec), rotary_angles[:, None, :])

def reference(tokens_in, block_order, routes, norm1_gain, w_query, key_weight, value_weight, query_gain, key_gain, w_out, norm2_gain, w_router, w_gate, w_up, w_down, cotangent):
    query_group_width = QUERY_HEADS // KEY_VALUE_HEADS
    span_length = N_CTX * 2 * BLOCK_TOKENS
    part_width = FFE // N_TP
    score_scale = 1.0 / math.sqrt(HEAD_WIDTH)
    token_positions = positions_of(block_order, N_CTX, BLOCK_TOKENS)
    rotary_angles = angles_of(token_positions.reshape(-1), HEAD_WIDTH)
    sequence_position = jnp.repeat(jnp.transpose(token_positions, (1, 0, 2)).reshape(SEQUENCE_COUNT, span_length), KEY_VALUE_HEADS, axis=0)
    assign = routes.reshape(N_CTX, TOK_DEV * TOPK)
    route_hits = (assign[:, :, None] == jnp.arange(EXPERTS, dtype=jnp.int32)).astype(jnp.int32)
    slot_index = lax.optimization_barrier(jnp.sum((jnp.cumsum(route_hits, axis=1) - route_hits) * route_hits, axis=2))
    place_at = assign * (N_CTX * CAP) + jnp.arange(N_CTX, dtype=jnp.int32)[:, None] * CAP + slot_index
    slot_table = jnp.full((EXPERTS * N_CTX * CAP,), TOKEN_TOTAL * TOPK, jnp.int32)
    slot_table = slot_table.at[place_at.reshape(-1)].set(jnp.arange(TOKEN_TOTAL * TOPK, dtype=jnp.int32))
    slot_table = slot_table.reshape(EXPERTS, N_CTX * CAP)

    def attend(seq_item):
        query_rows, key_rows, value_rows, spot_pos = seq_item
        unscaled_scores = jnp.einsum('lgd,md->lgm', query_rows, key_rows, precision=lax.Precision.HIGHEST)
        scores = low_back(unscaled_scores) * score_scale
        allowed = spot_pos[:, None, None] >= spot_pos[None, None, :]
        scores = jnp.where(allowed, scores, MASKED_SCORE)
        prob_rows = lower_precision(soft_rows(scores))
        return jnp.einsum('lgm,md->lgd', prob_rows, value_rows, precision=lax.Precision.HIGHEST)

    def forward(inputs, gain_first, proj_query, proj_key, proj_value, gain_query, key_norm_gain, proj_out, gain_second, proj_router, proj_gate, proj_up, proj_down):
        first_in = lower_precision(rms_norm(inputs, gain_first))
        query_raw = low_back(matmul_high(first_in, proj_query))
        unrotated_key = low_back(matmul_high(first_in, proj_key))
        value_input_rows = low_back(lower_precision(matmul_high(first_in, proj_value)))
        query_input_rows = lower_precision(head_route_path(query_raw, gain_query, rotary_angles, QUERY_HEADS))
        key_input_rows = lower_precision(head_route_path(unrotated_key, key_norm_gain, rotary_angles, KEY_VALUE_HEADS))
        query_entries = query_input_rows.reshape(N_CTX, SEQUENCE_COUNT, 2 * BLOCK_TOKENS, KEY_VALUE_HEADS, query_group_width, HEAD_WIDTH).transpose(1, 3, 0, 2, 4, 5).reshape(SEQUENCE_COUNT * KEY_VALUE_HEADS, span_length, query_group_width, HEAD_WIDTH)
        key_entries = key_input_rows.reshape(N_CTX, SEQUENCE_COUNT, 2 * BLOCK_TOKENS, KEY_VALUE_HEADS, HEAD_WIDTH).transpose(1, 3, 0, 2, 4).reshape(SEQUENCE_COUNT * KEY_VALUE_HEADS, span_length, HEAD_WIDTH)
        value_entries = value_input_rows.reshape(N_CTX, SEQUENCE_COUNT, 2 * BLOCK_TOKENS, KEY_VALUE_HEADS, HEAD_WIDTH).transpose(1, 3, 0, 2, 4).reshape(SEQUENCE_COUNT * KEY_VALUE_HEADS, span_length, HEAD_WIDTH)
        attended_mix = lax.map(jax.checkpoint(attend), (query_entries, key_entries, value_entries, sequence_position))
        attended_mix = attended_mix.reshape(SEQUENCE_COUNT, KEY_VALUE_HEADS, N_CTX, 2 * BLOCK_TOKENS, query_group_width, HEAD_WIDTH).transpose(2, 0, 3, 1, 4, 5).reshape(TOKEN_TOTAL, QUERY_HEADS * HEAD_WIDTH)
        attended = low_back(lower_precision(attended_mix))
        residual = inputs + low_back(matmul_high(attended, proj_out))
        second_in = lower_precision(rms_norm(residual, gain_second))
        logits = low_back(matmul_high(second_in, proj_router))
        gate_weights = soft_rows(jnp.take_along_axis(logits, routes, axis=1))
        rows_pad = jnp.concatenate([second_in, jnp.zeros((1, MODEL_WIDTH), jnp.float32)], axis=0)
        gates_pad = jnp.concatenate([gate_weights.reshape(-1), jnp.zeros((1,), jnp.float32)])

        def expert(running, expert_item):
            slot_picks, gate_mat, up_mat, down_mat = expert_item
            taken_rows = slot_picks // TOPK
            entry_rows = rows_pad[taken_rows]
            summed = jnp.zeros((N_CTX * CAP, MODEL_WIDTH), jnp.float32)
            for piece_index in range(N_TP):
                part_cols = slice(piece_index * part_width, (piece_index + 1) * part_width)
                entry_low = low_back(entry_rows)
                gate_pre = low_back(matmul_high(entry_low, gate_mat[:, part_cols]))
                up_pre = low_back(matmul_high(entry_low, up_mat[:, part_cols]))
                hidden = lower_precision(silu_mix(gate_pre, up_pre))
                summed = summed + low_back(lower_precision(matmul_high(hidden, down_mat[part_cols, :])))
            return (running.at[taken_rows].add(gates_pad[slot_picks][:, None] * summed), None)
        running, _ = lax.scan(jax.checkpoint(expert), jnp.zeros((TOKEN_TOTAL + 1, MODEL_WIDTH), jnp.float32), (slot_table, proj_gate, proj_up, proj_down))
        return residual + running[:TOKEN_TOTAL]
    float_args = (tokens_in.astype(jnp.float32), norm1_gain.astype(jnp.float32), w_query.astype(jnp.float32), key_weight.astype(jnp.float32), value_weight.astype(jnp.float32), query_gain.astype(jnp.float32), key_gain.astype(jnp.float32), w_out.astype(jnp.float32), norm2_gain.astype(jnp.float32), w_router.astype(jnp.float32), w_gate.astype(jnp.float32), w_up.astype(jnp.float32), w_down.astype(jnp.float32))
    result, pullback = jax.vjp(forward, *float_args)
    gradients = pullback(cotangent.astype(jnp.float32))
    return (result.astype(jnp.bfloat16), gradients[0].astype(jnp.bfloat16), gradients[1], gradients[2], gradients[3], gradients[4], gradients[5], gradients[6], gradients[7], gradients[8], gradients[9], gradients[10], gradients[11], gradients[12])
```

```python
import math
import jax
import jax.numpy as jnp
from jax import lax
from jax.sharding import PartitionSpec as P
from jax.experimental import pallas as pl
from jax.experimental.pallas import tpu as pltpu
MESH=pl.DeviceIdType.MESH

def coords():
    ctx=lax.axis_index("ctx"); tp=lax.axis_index("tp")
    return ctx//2, ctx%2, tp//2, tp%2
def dev(z,x,y,c): return (z*2+x, y*2+c)
def pid(z,x,y,c): return (z*2+x)*4+y*2+c

def neighbours():
    z,x,y,c=coords()
    ax=x+(1-c)*(1-2*x); ay=y+c*(1-2*y)
    bx=x+c*(1-2*x); by=y+(1-c)*(1-2*y)
    return z,x,y,c,ax,ay,bx,by

def barrier_all():
    z,x,y,c=coords()
    b=pltpu.get_barrier_semaphore()
    def sig(d): pl.semaphore_signal(b,inc=1,device_id=d,device_id_type=MESH)
    sig(dev(z,1-x,y,c)); sig(dev(z,x,1-y,c)); sig(dev(z,x,y,1-c))
    @pl.when(z<3)
    def _(): sig(dev(z+1,x,y,c))
    @pl.when(z>0)
    def _(): sig(dev(z-1,x,y,c))
    pl.semaphore_wait(b,5-(3-z)//3-z//3)

def ag32_kernel(x_ref,out_ref,lsem,send,recv):
    rows=x_ref.shape[0]
    z,x,y,c,ax,ay,bx,by=neighbours()
    barrier_all()
    me=pid(z,x,y,c)
    def at(p): return out_ref.at[pl.ds(pl.multiple_of(p*rows,rows),rows)]
    def cp(p,d,k,own=False):
        return pltpu.make_async_remote_copy(src_ref=x_ref if own else at(p),dst_ref=at(p),send_sem=send.at[k,p],recv_sem=recv.at[p],device_id=d,device_id_type=MESH)
    up,down,A,B,C=dev(z+1,x,y,c),dev(z-1,x,y,c),dev(z,ax,ay,c),dev(z,bx,by,c),dev(z,x,y,1-c)
    def wait(p):
        cp(p,C,4).wait_recv()
    loc=pltpu.make_async_copy(x_ref,at(me),lsem); loc.start()
    @pl.when(z<3)
    def _(): cp(me,up,0,True).start()
    @pl.when(z>0)
    def _(): cp(me,down,1,True).start()
    cp(me,A,2,True).start(); cp(me,B,3,True).start(); cp(me,C,4,True).start()
    def zlow(d):
        @pl.when(z-d>=0)
        def _():
            p=pid(z-d,x,y,c); wait(p)
            @pl.when(z<3)
            def _(): cp(p,up,0).start()
            cp(p,A,2).start(); cp(p,B,3).start(); cp(p,C,4).start()
    def zhigh(d):
        @pl.when(z+d<=3)
        def _():
            p=pid(z+d,x,y,c); wait(p)
            @pl.when(z>0)
            def _(): cp(p,down,1).start()
            cp(p,A,2).start(); cp(p,B,3).start(); cp(p,C,4).start()
    def fa(zz):
        @pl.when((zz>=0)&(zz<=3))
        def _():
            p=pid(zz,ax,ay,c); wait(p)
            cp(p,B,3).start(); cp(p,C,4).start()
    def fb(zz,xx,yy):
        @pl.when((zz>=0)&(zz<=3))
        def _():
            p=pid(zz,xx,yy,c); wait(p); cp(p,C,4).start()
    zlow(1); zhigh(1); fa(z); zlow(2); zhigh(2); fa(z-1); fa(z+1); fb(z,bx,by); zlow(3); zhigh(3)
    fa(z-2); fa(z+2); fb(z-1,bx,by); fb(z+1,bx,by); fa(z-3); fa(z+3)
    dx,dy=1-x,1-y
    fb(z,dx,dy); fb(z-2,bx,by); fb(z+2,bx,by); fb(z-1,dx,dy); fb(z+1,dx,dy); fb(z-3,bx,by); fb(z+3,bx,by); fb(z-2,dx,dy); fb(z+2,dx,dy); fb(z-3,dx,dy); fb(z+3,dx,dy)
    for zz in range(4):
        for xx in range(2):
            for yy in range(2):
                wait(pid(zz,xx,yy,1-c))
    loc.wait()
    for zz in range(4):
        p=pid(zz,x,y,c)
        @pl.when((z<3)&(zz<=z))
        def _(): cp(p,up,0).wait_send()
        @pl.when((z>0)&(zz>=z))
        def _(): cp(p,down,1).wait_send()
        cp(p,A,2).wait_send(); cp(p,B,3).wait_send(); cp(p,C,4).wait_send()
        q=pid(zz,ax,ay,c)
        cp(q,B,3).wait_send(); cp(q,C,4).wait_send()
        cp(pid(zz,bx,by,c),C,4).wait_send(); cp(pid(zz,dx,dy,c),C,4).wait_send()

def ag32(piece,cid=0):
    rows,w=piece.shape
    return pl.pallas_call(ag32_kernel,out_shape=jax.ShapeDtypeStruct((rows*32,w),piece.dtype),
        in_specs=[pl.BlockSpec(memory_space=pl.ANY)],out_specs=pl.BlockSpec(memory_space=pl.ANY),
        scratch_shapes=[pltpu.SemaphoreType.DMA,pltpu.SemaphoreType.DMA((5,32)),pltpu.SemaphoreType.DMA((32,))],
        compiler_params=pltpu.CompilerParams(collective_id=cid,has_side_effects=True))(piece)

def zmask(z):
    return (3-z)//3, (z%3)%2, (z%3)//2, z//3
def zfar(z,k):
    m0,m1,m2,m3=zmask(z)
    t=((3,2,1,0),(3,0,2,1),(0,3,1,2),(0,1,2,3))
    return m0*t[0][k]+m1*t[1][k]+m2*t[2][k]+m3*t[3][k]

def zreduce(z,x,y,c,load,zup,zdn,stage,zsend,zrecv,out_store):
    def cp(buf,zz,d,k,r):
        return pltpu.make_async_remote_copy(src_ref=stage.at[zz],dst_ref=buf.at[zz],send_sem=zsend.at[zz],recv_sem=zrecv.at[r,zz],device_id=d,device_id_type=MESH)
    up,down=dev(z+1,x,y,c),dev(z-1,x,y,c)
    for k in range(3):
        zz=zfar(z,k)
        @pl.when(zz>z)
        def _():
            stage[zz]=load(zz).astype(stage.dtype)
            @pl.when(z>0)
            def _():
                cp(zup,zz,up,0,0).wait_recv()
                stage[zz]=(stage[zz].astype(jnp.float32)+zup[zz].astype(jnp.float32)).astype(stage.dtype)
            cp(zup,zz,up,0,0).start()
        @pl.when(zz<z)
        def _():
            stage[zz]=load(zz).astype(stage.dtype)
            @pl.when(z<3)
            def _():
                cp(zdn,zz,down,1,1).wait_recv()
                stage[zz]=(stage[zz].astype(jnp.float32)+zdn[zz].astype(jnp.float32)).astype(stage.dtype)
            cp(zdn,zz,down,1,1).start()
    out_store(load(z),True)
    @pl.when(z>0)
    def _():
        cp(zup,z,up,0,0).wait_recv()
        out_store(zup[z].astype(jnp.float32),False)
    @pl.when(z<3)
    def _():
        cp(zdn,z,down,1,1).wait_recv()
        out_store(zdn[z].astype(jnp.float32),False)
    for k in range(3):
        zz=zfar(z,k)
        cp(zup,zz,up,0,0).wait_send()

def rs32_kernel(in_ref,out_ref,acc,cbuf,bbuf,abuf,zup,zdn,stage,lsem,csend,crecv,bsend,brecv,asend,arecv,zsend,zrecv):
    rows=out_ref.shape[0]
    z,x,y,c,ax,ay,bx,by=neighbours()
    dx,dy=1-x,1-y
    barrier_all()
    f32=jnp.float32
    A,B,C=dev(z,ax,ay,c),dev(z,bx,by,c),dev(z,x,y,1-c)
    def q(zz,xx,yy): return zz*4+xx*2+yy
    def at(p): return in_ref.at[pl.ds(pl.multiple_of(p*rows,rows),rows)]
    def ccopy(zz,xx,yy,cc):
        return pltpu.make_async_remote_copy(src_ref=at(pid(zz,xx,yy,cc)),dst_ref=cbuf.at[q(zz,xx,yy)],send_sem=csend.at[q(zz,xx,yy)],recv_sem=crecv.at[q(zz,xx,yy)],device_id=C,device_id_type=MESH)
    def lcopy(zz,xx,yy):
        return pltpu.make_async_copy(at(pid(zz,xx,yy,c)),acc.at[q(zz,xx,yy)],lsem.at[q(zz,xx,yy)])
    sides=[(dx,dy),(bx,by),(ax,ay),(x,y)]
    for (xx,yy) in sides:
        for k in range(4):
            zz=zfar(z,k)
            lcopy(zz,xx,yy).start()
    for (xx,yy) in [(dx,dy),(ax,ay),(bx,by),(x,y)]:
        for k in range(4):
            zz=zfar(z,k)
            ccopy(zz,xx,yy,1-c).start()
    def have_c(zz,xx,yy):
        lcopy(zz,xx,yy).wait(); ccopy(zz,xx,yy,1-c).wait_recv()
        i=q(zz,xx,yy)
        return acc[i].astype(f32)+cbuf[i].astype(f32)
    def bcopy(zz,far):
        xx,yy=(dx,dy) if far else (bx,by)
        i=zz+4*far
        return pltpu.make_async_remote_copy(src_ref=acc.at[q(zz,xx,yy)],dst_ref=bbuf.at[i],send_sem=bsend.at[i],recv_sem=brecv.at[i],device_id=B,device_id_type=MESH)
    for far in (1,0):
        xx,yy=(dx,dy) if far else (bx,by)
        for k in range(4):
            zz=zfar(z,k)
            acc[q(zz,xx,yy)]=have_c(zz,xx,yy).astype(acc.dtype)
            bcopy(zz,far).start()
    def acopy(zz):
        return pltpu.make_async_remote_copy(src_ref=acc.at[q(zz,ax,ay)],dst_ref=abuf.at[zz],send_sem=asend.at[zz],recv_sem=arecv.at[zz],device_id=A,device_id_type=MESH)
    for k in range(4):
        zz=zfar(z,k)
        v=have_c(zz,ax,ay)
        bcopy(zz,1).wait_recv()
        acc[q(zz,ax,ay)]=(v+bbuf[zz+4].astype(f32)).astype(acc.dtype)
        acopy(zz).start()
    def load(zz):
        v=have_c(zz,x,y)
        bcopy(zz,0).wait_recv(); acopy(zz).wait_recv()
        return v+bbuf[zz].astype(f32)+abuf[zz].astype(f32)
    def store(v,first):
        out_ref[...]=v if first else out_ref[...]+v
    zreduce(z,x,y,c,load,zup,zdn,stage,zsend,zrecv,store)
    for zz in range(4):
        for (xx,yy) in sides: ccopy(zz,xx,yy,1-c).wait_send()
        bcopy(zz,1).wait_send(); bcopy(zz,0).wait_send(); acopy(zz).wait_send()

def rs32(part,cid=1):
    n,w=part.shape; rows=n//32
    S=pltpu.SemaphoreType.DMA
    def V(k): return pltpu.VMEM((k,rows,w),part.dtype)
    return pl.pallas_call(rs32_kernel,out_shape=jax.ShapeDtypeStruct((rows,w),jnp.float32),
        in_specs=[pl.BlockSpec(memory_space=pl.ANY)],out_specs=pl.BlockSpec(memory_space=pltpu.VMEM),
        scratch_shapes=[V(16),V(16),V(8),V(4),V(4),V(4),V(4),S((16,)),S((16,)),S((16,)),S((8,)),S((8,)),S((4,)),S((4,)),S((4,)),S((2,4))],
        compiler_params=pltpu.CompilerParams(collective_id=cid,has_side_effects=True,vmem_limit_bytes=48*2**20))(part)

def barrier_plane():
    z,x,y,c=coords()
    b=pltpu.get_barrier_semaphore()
    def sig(d): pl.semaphore_signal(b,inc=1,device_id=d,device_id_type=MESH)
    sig(dev(z,1-x,y,c))
    @pl.when(z<3)
    def _(): sig(dev(z+1,x,y,c))
    @pl.when(z>0)
    def _(): sig(dev(z-1,x,y,c))
    pl.semaphore_wait(b,3-(3-z)//3-z//3)

def barrier_tp():
    z,x,y,c=coords()
    b=pltpu.get_barrier_semaphore()
    for d in (dev(z,x,1-y,c),dev(z,x,y,1-c)):
        pl.semaphore_signal(b,inc=1,device_id=d,device_id_type=MESH)
    pl.semaphore_wait(b,2)

def agctx_kernel(x_ref,out_ref,lsem,send,recv):
    rows=x_ref.shape[0]
    z,x,y,c=coords()
    barrier_plane()
    def at(p): return out_ref.at[pl.ds(pl.multiple_of(p*rows,rows),rows)]
    def cp(p,d,k,own=False):
        return pltpu.make_async_remote_copy(src_ref=x_ref if own else at(p),dst_ref=at(p),send_sem=send.at[k,p],recv_sem=recv.at[p],device_id=d,device_id_type=MESH)
    up,down,X=dev(z+1,x,y,c),dev(z-1,x,y,c),dev(z,1-x,y,c)
    me=z*2+x
    loc=pltpu.make_async_copy(x_ref,at(me),lsem); loc.start()
    @pl.when(z<3)
    def _(): cp(me,up,0,True).start()
    @pl.when(z>0)
    def _(): cp(me,down,1,True).start()
    cp(me,X,2,True).start()
    for d in (1,2,3):
        @pl.when(z-d>=0)
        def _():
            p=(z-d)*2+x; cp(p,X,2).wait_recv()
            @pl.when(z<3)
            def _(): cp(p,up,0).start()
            cp(p,X,2).start()
        @pl.when(z+d<=3)
        def _():
            p=(z+d)*2+x; cp(p,X,2).wait_recv()
            @pl.when(z>0)
            def _(): cp(p,down,1).start()
            cp(p,X,2).start()
    loc.wait()
    for zz in range(4):
        cp(zz*2+1-x,X,2).wait_recv()
        p=zz*2+x
        @pl.when((z<3)&(zz<=z))
        def _(): cp(p,up,0).wait_send()
        @pl.when((z>0)&(zz>=z))
        def _(): cp(p,down,1).wait_send()
        cp(p,X,2).wait_send()

def agctx(piece,cid=2):
    rows,w=piece.shape
    S=pltpu.SemaphoreType.DMA
    return pl.pallas_call(agctx_kernel,out_shape=jax.ShapeDtypeStruct((rows*8,w),piece.dtype),
        in_specs=[pl.BlockSpec(memory_space=pl.ANY)],out_specs=pl.BlockSpec(memory_space=pl.ANY),
        scratch_shapes=[S,S((3,8)),S((8,))],
        compiler_params=pltpu.CompilerParams(collective_id=cid,has_side_effects=True))(piece)

def rsctx_kernel(in_ref,out_ref,xbuf,zup,zdn,stage,xsend,xrecv,zsend,zrecv):
    rows=out_ref.shape[0]
    z,x,y,c=coords()
    barrier_plane()
    f32=jnp.float32
    X=dev(z,1-x,y,c)
    def at(p): return in_ref.at[pl.ds(pl.multiple_of(p*rows,rows),rows)]
    def xcopy(zz):
        return pltpu.make_async_remote_copy(src_ref=at(zz*2+1-x),dst_ref=xbuf.at[zz],send_sem=xsend.at[zz],recv_sem=xrecv.at[zz],device_id=X,device_id_type=MESH)
    for k in range(4): xcopy(zfar(z,k)).start()
    def load(zz):
        xcopy(zz).wait_recv()
        return at(zz*2+x)[...].astype(f32)+xbuf[zz].astype(f32)
    def store(v,first):
        out_ref[...]=v if first else out_ref[...]+v
    zreduce(z,x,y,c,load,zup,zdn,stage,zsend,zrecv,store)
    for zz in range(4): xcopy(zz).wait_send()

def rsctx(part,cid=3):
    n,w=part.shape; rows=n//8
    S=pltpu.SemaphoreType.DMA
    def V(k): return pltpu.VMEM((k,rows,w),part.dtype)
    return pl.pallas_call(rsctx_kernel,out_shape=jax.ShapeDtypeStruct((rows,w),jnp.float32),
        in_specs=[pl.BlockSpec(memory_space=pltpu.VMEM)],out_specs=pl.BlockSpec(memory_space=pltpu.VMEM),
        scratch_shapes=[V(4),V(4),V(4),V(4),S((4,)),S((4,)),S((4,)),S((2,4))],
        compiler_params=pltpu.CompilerParams(collective_id=cid,has_side_effects=True,vmem_limit_bytes=32*2**20))(part)

def rstp_kernel(in_ref,out_ref,cbuf,ybuf,stage,csend,crecv,ysend,yrecv):
    rows=out_ref.shape[0]
    z,x,y,c=coords()
    barrier_tp()
    f32=jnp.float32
    def at(yy,cc): return in_ref.at[pl.ds(pl.multiple_of((yy*2+cc)*rows,rows),rows)]
    def ccopy(yy):
        return pltpu.make_async_remote_copy(src_ref=at(yy,1-c),dst_ref=cbuf.at[yy],send_sem=csend.at[yy],recv_sem=crecv.at[yy],device_id=dev(z,x,y,1-c),device_id_type=MESH)
    ccopy(1-y).start(); ccopy(y).start()
    ccopy(1-y).wait_recv()
    stage[...]=(at(1-y,c)[...].astype(f32)+cbuf[1-y].astype(f32)).astype(stage.dtype)
    yc=pltpu.make_async_remote_copy(src_ref=stage,dst_ref=ybuf,send_sem=ysend,recv_sem=yrecv,device_id=dev(z,x,1-y,c),device_id_type=MESH)
    yc.start()
    ccopy(y).wait_recv()
    out_ref[...]=at(y,c)[...].astype(f32)+cbuf[y].astype(f32)
    yc.wait_recv()
    out_ref[...]+=ybuf[...].astype(f32)
    yc.wait_send(); ccopy(0).wait_send(); ccopy(1).wait_send()

def rstp(part,cid=4):
    n,w=part.shape; rows=n//4
    S=pltpu.SemaphoreType.DMA
    return pl.pallas_call(rstp_kernel,out_shape=jax.ShapeDtypeStruct((rows,w),jnp.float32),
        in_specs=[pl.BlockSpec(memory_space=pltpu.VMEM)],out_specs=pl.BlockSpec(memory_space=pltpu.VMEM),
        scratch_shapes=[pltpu.VMEM((2,rows,w),part.dtype),pltpu.VMEM((rows,w),part.dtype),pltpu.VMEM((rows,w),part.dtype),S((2,)),S((2,)),S,S],
        compiler_params=pltpu.CompilerParams(collective_id=cid,has_side_effects=True,vmem_limit_bytes=32*2**20))(part)

def agtp_kernel(x_ref,out_ref,lsem,send,recv):
    rows=x_ref.shape[0]
    z,x,y,c=coords()
    barrier_tp()
    def at(yy,cc): return out_ref.at[pl.ds(pl.multiple_of((yy*2+cc)*rows,rows),rows)]
    def cp(src,yy,cc,d,k):
        return pltpu.make_async_remote_copy(src_ref=src,dst_ref=at(yy,cc),send_sem=send.at[k],recv_sem=recv.at[yy*2+cc],device_id=d,device_id_type=MESH)
    Y,C=dev(z,x,1-y,c),dev(z,x,y,1-c)
    loc=pltpu.make_async_copy(x_ref,at(y,c),lsem); loc.start()
    cp(x_ref,y,c,Y,0).start(); cp(x_ref,y,c,C,1).start()
    cp(x_ref,1-y,c,Y,0).wait_recv()
    cp(at(1-y,c),1-y,c,C,2).start()
    cp(x_ref,y,1-c,C,1).wait_recv(); cp(x_ref,1-y,1-c,C,2).wait_recv()
    loc.wait()
    cp(x_ref,y,c,Y,0).wait_send(); cp(x_ref,y,c,C,1).wait_send(); cp(at(1-y,c),1-y,c,C,2).wait_send()

def agtp(piece,cid=5):
    rows,w=piece.shape
    S=pltpu.SemaphoreType.DMA
    return pl.pallas_call(agtp_kernel,out_shape=jax.ShapeDtypeStruct((rows*4,w),piece.dtype),
        in_specs=[pl.BlockSpec(memory_space=pl.ANY)],out_specs=pl.BlockSpec(memory_space=pl.ANY),
        scratch_shapes=[S,S((3,)),S((4,))],
        compiler_params=pltpu.CompilerParams(collective_id=cid,has_side_effects=True))(piece)


EPSILON = 1e-06
ROPE_BASE = 1000000.0
MASKED_SCORE = -1000000000.0
BF = jnp.bfloat16
F32 = jnp.float32


def dotf(a, b, dims):
    return lax.dot_general(a, b, (dims, ((), ())), preferred_element_type=F32)


class Links:
    def __init__(self, own):
        self.own = own

    def ag_all(self, piece, cid):
        if self.own:
            return ag32(piece, cid)
        return lax.all_gather(piece, ("ctx", "tp"), axis=0, tiled=True)

    def rs_all(self, part, cid):
        if self.own:
            return rs32(part, cid)
        return lax.psum_scatter(part, ("ctx", "tp"), scatter_dimension=0, tiled=True).astype(F32)

    def ag_ctx(self, piece, cid):
        if self.own:
            return agctx(piece, cid)
        return lax.all_gather(piece, "ctx", axis=0, tiled=True)

    def rs_ctx(self, part, cid):
        if self.own:
            return rsctx(part, cid)
        return lax.psum_scatter(part, "ctx", scatter_dimension=0, tiled=True).astype(F32)

    def rs_tp(self, part, cid):
        if self.own:
            return rstp(part, cid)
        return lax.psum_scatter(part, "tp", scatter_dimension=0, tiled=True).astype(F32)

    def ag_tp(self, piece, cid):
        if self.own:
            return agtp(piece, cid)
        return lax.all_gather(piece, "tp", axis=0, tiled=True)


def rms_norm(values, gain_vec):
    factor = lax.rsqrt(jnp.mean(values * values, axis=-1, keepdims=True) + EPSILON)
    return values * factor * gain_vec


def rotate(values, rotary_angles):
    half_size = values.shape[-1] // 2
    first_half = values[..., :half_size]
    second_half = values[..., half_size:]
    cosine = jnp.cos(rotary_angles)
    sine_part = jnp.sin(rotary_angles)
    return jnp.concatenate(
        [
            first_half * cosine - second_half * sine_part,
            second_half * cosine + first_half * sine_part,
        ],
        axis=-1,
    )


def angles_of(token_positions, head_width):
    freq_steps = jnp.arange(head_width // 2).astype(F32) * (2.0 / head_width)
    frequency = jnp.exp(-math.log(ROPE_BASE) * freq_steps)
    return token_positions.astype(F32)[..., None] * frequency


def positions_of(block_order, dev_count, block_len):
    first_block = jnp.transpose(block_order)
    block_pair = jnp.stack([first_block, 2 * dev_count - 1 - first_block], axis=-1)
    spread = block_pair[..., None] * block_len + jnp.arange(block_len, dtype=jnp.int32)
    return spread.reshape(dev_count, block_order.shape[0], 2 * block_len)


def head_route_path(raw_heads, gain_vec, rotary_angles, head_count):
    shaped = raw_heads.reshape(raw_heads.shape[0], head_count, -1)
    return rotate(rms_norm(shaped, gain_vec), rotary_angles[:, None, :])


def attend_forward(seq_item):
    query_matrix, every_key_row, every_value_row, query_pos, key_pos = seq_item
    score_scale = 1.0 / math.sqrt(query_matrix.shape[-1])
    unscaled_scores = jnp.einsum(
        "upnj,apj->upna", query_matrix, every_key_row, preferred_element_type=F32
    )
    allowed = query_pos[:, None, None, None] >= key_pos[None, None, None, :]
    scores = jnp.where(allowed, unscaled_scores * score_scale, MASKED_SCORE)
    row_top = jnp.max(scores, axis=-1, keepdims=True)
    exp_scores = jnp.exp(scores - row_top)
    totals = jnp.sum(exp_scores, axis=-1, keepdims=True)
    lower_attention_probs = (exp_scores / totals).astype(BF)
    attended_mix = jnp.einsum(
        "jzfq,qzx->jzfx", lower_attention_probs, every_value_row, preferred_element_type=F32
    )
    return (attended_mix, (row_top + jnp.log(totals))[..., 0])


def attend_backward(seq_item):
    (
        query_matrix,
        every_key_row,
        every_value_row,
        query_pos,
        key_pos,
        grad_attended_mix,
        log_total,
    ) = seq_item
    score_scale = 1.0 / math.sqrt(query_matrix.shape[-1])
    unscaled_scores = jnp.einsum(
        "upnj,apj->upna", query_matrix, every_key_row, preferred_element_type=F32
    )
    allowed = query_pos[:, None, None, None] >= key_pos[None, None, None, :]
    scores = jnp.where(allowed, unscaled_scores * score_scale, MASKED_SCORE)
    attention_probs = jnp.exp(scores - log_total[..., None])
    grad_probs = jnp.einsum(
        "upnj,apj->upna", grad_attended_mix, every_value_row, preferred_element_type=F32
    )
    row_inner = jnp.sum(attention_probs * grad_probs, axis=-1, keepdims=True)
    grad_score_dots = (attention_probs * (grad_probs - row_inner) * score_scale).astype(BF)
    grad_queries = jnp.einsum(
        "jzfq,qzx->jzfx", grad_score_dots, every_key_row, preferred_element_type=F32
    )
    grad_key_rows = jnp.einsum(
        "axfv,axfz->vxz", grad_score_dots, query_matrix, preferred_element_type=F32
    )
    grad_values = jnp.einsum(
        "axfv,axfz->vxz", attention_probs.astype(BF), grad_attended_mix, preferred_element_type=F32
    )
    return (grad_queries, grad_key_rows, grad_values)


def gates_of(logits, routes):
    experts = logits.shape[1]
    named = jnp.any(routes[:, :, None] == jnp.arange(experts, dtype=jnp.int32), axis=1)
    masked = jnp.where(named, logits, -jnp.inf)
    top = jnp.max(masked, axis=1, keepdims=True)
    weights = jnp.where(named, jnp.exp(masked - top), 0.0)
    return weights / jnp.sum(weights, axis=1, keepdims=True)


def shards(
    tokens_in,
    block_order,
    routes,
    norm1_gain,
    w_query,
    key_weight,
    value_weight,
    query_gain,
    key_gain,
    w_out,
    norm2_gain,
    w_router,
    w_gate,
    w_up,
    w_down,
    cotangent,
):
    tok_count, model_width = tokens_in.shape
    head_size = query_gain.shape[0]
    local_heads = w_query.shape[1] // head_size
    local_kv = key_weight.shape[1] // head_size
    query_group_width = local_heads // local_kv
    seq_count = block_order.shape[0]
    devices, tp_size = lax.axis_size("ctx"), lax.axis_size("tp")
    links = Links(devices == 8 and tp_size == 4)
    me, tp_me = lax.axis_index("ctx"), lax.axis_index("tp")
    rows = tok_count // tp_size
    block_len = tok_count // (2 * seq_count)
    experts = w_router.shape[1]
    own_experts, _, units = w_gate.shape
    hid = own_experts * units
    all_tok = devices * tok_count

    def own_rows(v):
        return lax.dynamic_slice_in_dim(v, tp_me * rows, rows, axis=0)

    cot_own = own_rows(cotangent)
    cot_all = links.ag_all(cot_own, 0)
    routes_all = lax.all_gather(routes, "ctx", axis=0, tiled=True)

    token_positions = positions_of(block_order, devices, block_len)
    query_pos = lax.dynamic_index_in_dim(token_positions, me, 0, keepdims=False)
    key_pos = jnp.transpose(token_positions, (1, 0, 2)).reshape(seq_count, devices * 2 * block_len)
    rotary_angles = angles_of(query_pos.reshape(-1), head_size)
    inputs = tokens_in.astype(F32)
    first_in = rms_norm(inputs, norm1_gain).astype(BF)
    query_raw = jnp.dot(first_in, w_query, preferred_element_type=F32)
    unrotated_key = jnp.dot(first_in, key_weight, preferred_element_type=F32)
    value_rows = jnp.dot(first_in, value_weight, preferred_element_type=F32).astype(BF)

    def rope_heads(raw_query, raw_key, gain_query, key_norm_gain):
        return (
            head_route_path(raw_query, gain_query, rotary_angles, local_heads),
            head_route_path(raw_key, key_norm_gain, rotary_angles, local_kv),
        )

    (query_rot, key_rot), rope_back = jax.vjp(
        rope_heads, query_raw, unrotated_key, query_gain, key_gain
    )
    query_rows = query_rot.astype(BF).reshape(
        seq_count, 2 * block_len, local_kv, query_group_width, head_size
    )
    kv_width = local_kv * head_size
    kv_own = jnp.concatenate([key_rot.astype(BF).reshape(tok_count, kv_width), value_rows], axis=1)
    kv_all = links.ag_ctx(kv_own, 1)
    kv_seq = kv_all.reshape(devices, seq_count, 2 * block_len, 2, local_kv, head_size)
    kv_seq = kv_seq.transpose(3, 1, 0, 2, 4, 5).reshape(
        2, seq_count, devices * 2 * block_len, local_kv, head_size
    )
    key_full, value_full = kv_seq[0], kv_seq[1]
    attended_mix, log_total = lax.map(
        attend_forward, (query_rows, key_full, value_full, query_pos, key_pos)
    )
    attended = attended_mix.reshape(tok_count, local_heads * head_size).astype(BF)
    attn_part = jnp.dot(attended, w_out, preferred_element_type=F32).astype(BF)
    residual = own_rows(inputs) + links.rs_tp(attn_part, 2)
    second_normed, second_back = jax.vjp(rms_norm, residual, norm2_gain)
    second_in = second_normed.astype(BF)
    second_all = links.ag_all(second_in, 3)

    gates_all = gates_of(jnp.dot(second_all, w_router, preferred_element_type=F32), routes_all)
    gates_mine = lax.dynamic_slice_in_dim(gates_all, me * own_experts, own_experts, axis=1)
    gates_own = lax.dynamic_slice_in_dim(
        gates_all, (me * tp_size + tp_me) * rows, rows, axis=0
    )
    spread = jnp.repeat(gates_mine, units, axis=1)
    gate_mat = w_gate.transpose(1, 0, 2).reshape(model_width, hid)
    up_mat = w_up.transpose(1, 0, 2).reshape(model_width, hid)
    down_mat = w_down.reshape(hid, model_width)
    def expert_block(block):
        rows_in, cots, weights, own = block
        gate_pre = jnp.dot(rows_in, gate_mat, preferred_element_type=F32)
        up_pre = jnp.dot(rows_in, up_mat, preferred_element_type=F32)
        sig = 1.0 / (1.0 + jnp.exp(-gate_pre))
        silu = gate_pre * sig
        hidden = silu * up_pre
        hidden_low = (hidden * weights).astype(BF)
        out_part = jnp.dot(hidden_low, down_mat, preferred_element_type=F32).astype(BF)
        back = dotf(cots, down_mat, ((1,), (1,)))
        gate_grad = jnp.sum((hidden * back).reshape(-1, own_experts, units), axis=2)
        grad_hidden = back * weights
        gate_low = (grad_hidden * up_pre * sig * (1.0 + gate_pre * (1.0 - sig))).astype(BF)
        up_low = (grad_hidden * silu).astype(BF)
        entry = dotf(gate_low, gate_mat, ((1,), (1,))) + dotf(up_low, up_mat, ((1,), (1,)))
        gate_wide = lax.dynamic_update_slice(
            jnp.zeros((rows_in.shape[0], extra), F32), gate_grad, (0, me * own_experts)
        )
        entry = jnp.concatenate([entry.astype(BF), gate_wide.astype(BF)], axis=1)
        sums = (
            dotf(rows_in, gate_low, ((0,), (0,))),
            dotf(rows_in, up_low, ((0,), (0,))),
            dotf(hidden_low, cots, ((0,), (0,))),
        )
        return out_part, entry, sums

    extra = -(-experts // 128) * 128
    steps = max(1, all_tok // 2048)
    if steps == 1:
        out_part, entry, sums = expert_block((second_all, cot_all, spread, gates_mine))
    else:

        def step(total, block):
            out_part, entry, sums = expert_block(block)
            return tuple(a + b for a, b in zip(total, sums)), (out_part, entry)

        def cut(v):
            return v.reshape(steps, -1, v.shape[1])

        zero = jnp.zeros((model_width, hid), F32)
        sums, (out_part, entry) = lax.scan(
            step, (zero, zero, zero.T), (cut(second_all), cut(cot_all), cut(spread), cut(gates_mine))
        )
        out_part = out_part.reshape(all_tok, model_width)
        entry = entry.reshape(all_tok, model_width + extra)
    out_own = links.rs_all(out_part, 4)
    layer_out = links.ag_tp((residual + out_own).astype(BF), 5)
    grad_gate = sums[0].reshape(model_width, own_experts, units).transpose(1, 0, 2)
    grad_up = sums[1].reshape(model_width, own_experts, units).transpose(1, 0, 2)
    grad_down = sums[2].reshape(own_experts, units, model_width)
    entry_own = links.rs_all(entry, 6)
    gate_total = entry_own[:, model_width : model_width + experts]
    grad_logits = (
        gates_own * (gate_total - jnp.sum(gates_own * gate_total, axis=1, keepdims=True))
    ).astype(BF)
    logits_all = lax.all_gather(grad_logits, ("ctx", "tp"), axis=0, tiled=True)
    width_part = model_width // devices
    second_cols = lax.dynamic_slice_in_dim(second_all, me * width_part, width_part, axis=1)
    grad_router = dotf(second_cols, logits_all, ((0,), (0,)))
    grad_second = entry_own[:, :model_width] + dotf(grad_logits, w_router, ((1,), (1,)))
    grad_resid_norm, grad_norm2 = second_back(grad_second)
    grad_residual = cot_own.astype(F32) + grad_resid_norm
    grad_attn_low = links.ag_tp(grad_residual.astype(BF), 7)
    grad_out = dotf(attended, grad_attn_low, ((0,), (0,)))
    grad_mixed = dotf(grad_attn_low, w_out, ((1,), (1,))).astype(BF)
    grad_mixed = grad_mixed.reshape(
        seq_count, 2 * block_len, local_kv, query_group_width, head_size
    )
    grad_query_seq, grad_key_seq, grad_value_seq = lax.map(
        attend_backward,
        (query_rows, key_full, value_full, query_pos, key_pos, grad_mixed, log_total),
    )
    grad_kv = jnp.stack([grad_key_seq, grad_value_seq]).astype(BF)
    grad_kv = grad_kv.reshape(2, seq_count, devices, 2 * block_len, kv_width)
    grad_kv = grad_kv.transpose(2, 1, 3, 0, 4).reshape(all_tok, 2 * kv_width)
    grad_kv_own = links.rs_ctx(grad_kv, 8)
    grad_query_rot = grad_query_seq.reshape(tok_count, local_heads, head_size)
    grad_key_rot = grad_kv_own[:, :kv_width].reshape(tok_count, local_kv, head_size)
    grad_query_raw, grad_key_raw, grad_qgain, grad_kgain = rope_back(
        (grad_query_rot, grad_key_rot)
    )
    query_low = grad_query_raw.astype(BF)
    key_low = grad_key_raw.astype(BF)
    value_low = grad_kv_own[:, kv_width:].astype(BF)
    first_part = dotf(query_low, w_query, ((1,), (1,)))
    first_part = first_part + dotf(key_low, key_weight, ((1,), (1,)))
    first_part = first_part + dotf(value_low, value_weight, ((1,), (1,)))
    grad_first = links.rs_tp(first_part.astype(BF), 9)
    _, first_back = jax.vjp(rms_norm, own_rows(inputs), norm1_gain)
    grad_input_norm, grad_norm1 = first_back(grad_first)
    grad_input = links.ag_tp((grad_residual + grad_input_norm).astype(BF), 10)

    def over_ctx(v, dim):
        return lax.psum_scatter(v.astype(BF), "ctx", scatter_dimension=dim, tiled=True).astype(F32)

    low_all = jnp.concatenate([query_low, key_low, value_low], axis=1)
    weight_grads = over_ctx(dotf(first_in, low_all, ((0,), (0,))), 0)
    wide = query_low.shape[1]
    grad_query = weight_grads[:, :wide]
    grad_key = weight_grads[:, wide : wide + kv_width]
    grad_value = weight_grads[:, wide + kv_width :]
    grad_out = over_ctx(grad_out, 1)
    vectors = lax.psum(
        jnp.concatenate([grad_norm1, grad_norm2, grad_qgain, grad_kgain]), ("ctx", "tp")
    )

    def piece_of(start, size):
        part = size // devices
        return lax.dynamic_slice_in_dim(vectors, start + me * part, part, axis=0)

    return (
        layer_out,
        grad_input,
        piece_of(0, model_width),
        grad_query,
        grad_key,
        grad_value,
        piece_of(2 * model_width, head_size),
        piece_of(2 * model_width + head_size, head_size),
        grad_out,
        piece_of(model_width, model_width),
        grad_router,
        grad_gate,
        grad_up,
        grad_down,
    )


def solution(mesh):
    in_specs = (
        P("ctx", None),
        P(),
        P("ctx", None),
        P(),
        P(None, "tp"),
        P(None, "tp"),
        P(None, "tp"),
        P(),
        P(),
        P("tp", None),
        P(),
        P(),
        P("ctx", None, "tp"),
        P("ctx", None, "tp"),
        P("ctx", "tp", None),
        P("ctx", None),
    )
    out_specs = (
        P("ctx", None),
        P("ctx", None),
        P("ctx"),
        P("ctx", "tp"),
        P("ctx", "tp"),
        P("ctx", "tp"),
        P("ctx"),
        P("ctx"),
        P("tp", "ctx"),
        P("ctx"),
        P("ctx", None),
        P("ctx", None, "tp"),
        P("ctx", None, "tp"),
        P("ctx", "tp", None),
    )
    return jax.shard_map(shards, mesh=mesh, in_specs=in_specs, out_specs=out_specs, check_vma=False)
```

```python
import math
import jax
import jax.numpy as jnp
from jax import lax
from jax.sharding import PartitionSpec as P
from jax.experimental import pallas as pl
from jax.experimental.pallas import tpu as pltpu
MESH=pl.DeviceIdType.MESH

def coords():
    ctx=lax.axis_index("ctx"); tp=lax.axis_index("tp")
    return ctx//2, ctx%2, tp//2, tp%2
def dev(z,x,y,c): return (z*2+x, y*2+c)
def pid(z,x,y,c): return (z*2+x)*4+y*2+c

def neighbours():
    z,x,y,c=coords()
    ax=x+(1-c)*(1-2*x); ay=y+c*(1-2*y)
    bx=x+c*(1-2*x); by=y+(1-c)*(1-2*y)
    return z,x,y,c,ax,ay,bx,by

def barrier_all():
    z,x,y,c=coords()
    b=pltpu.get_barrier_semaphore()
    def sig(d): pl.semaphore_signal(b,inc=1,device_id=d,device_id_type=MESH)
    sig(dev(z,1-x,y,c)); sig(dev(z,x,1-y,c)); sig(dev(z,x,y,1-c))
    @pl.when(z<3)
    def _(): sig(dev(z+1,x,y,c))
    @pl.when(z>0)
    def _(): sig(dev(z-1,x,y,c))
    pl.semaphore_wait(b,5-(3-z)//3-z//3)

def ag32_kernel(x_ref,out_ref,lsem,send,recv):
    rows=x_ref.shape[0]
    z,x,y,c,ax,ay,bx,by=neighbours()
    barrier_all()
    me=pid(z,x,y,c)
    def at(p): return out_ref.at[pl.ds(pl.multiple_of(p*rows,rows),rows)]
    def cp(p,d,k,own=False):
        return pltpu.make_async_remote_copy(src_ref=x_ref if own else at(p),dst_ref=at(p),send_sem=send.at[k,p],recv_sem=recv.at[p],device_id=d,device_id_type=MESH)
    up,down,A,B,C=dev(z+1,x,y,c),dev(z-1,x,y,c),dev(z,ax,ay,c),dev(z,bx,by,c),dev(z,x,y,1-c)
    def wait(p):
        cp(p,C,4).wait_recv()
    loc=pltpu.make_async_copy(x_ref,at(me),lsem); loc.start()
    @pl.when(z<3)
    def _(): cp(me,up,0,True).start()
    @pl.when(z>0)
    def _(): cp(me,down,1,True).start()
    cp(me,A,2,True).start(); cp(me,B,3,True).start(); cp(me,C,4,True).start()
    def zlow(d):
        @pl.when(z-d>=0)
        def _():
            p=pid(z-d,x,y,c); wait(p)
            @pl.when(z<3)
            def _(): cp(p,up,0).start()
            cp(p,A,2).start(); cp(p,B,3).start(); cp(p,C,4).start()
    def zhigh(d):
        @pl.when(z+d<=3)
        def _():
            p=pid(z+d,x,y,c); wait(p)
            @pl.when(z>0)
            def _(): cp(p,down,1).start()
            cp(p,A,2).start(); cp(p,B,3).start(); cp(p,C,4).start()
    def fa(zz):
        @pl.when((zz>=0)&(zz<=3))
        def _():
            p=pid(zz,ax,ay,c); wait(p)
            cp(p,B,3).start(); cp(p,C,4).start()
    def fb(zz,xx,yy):
        @pl.when((zz>=0)&(zz<=3))
        def _():
            p=pid(zz,xx,yy,c); wait(p); cp(p,C,4).start()
    zlow(1); zhigh(1); fa(z); zlow(2); zhigh(2); fa(z-1); fa(z+1); fb(z,bx,by); zlow(3); zhigh(3)
    fa(z-2); fa(z+2); fb(z-1,bx,by); fb(z+1,bx,by); fa(z-3); fa(z+3)
    dx,dy=1-x,1-y
    fb(z,dx,dy); fb(z-2,bx,by); fb(z+2,bx,by); fb(z-1,dx,dy); fb(z+1,dx,dy); fb(z-3,bx,by); fb(z+3,bx,by); fb(z-2,dx,dy); fb(z+2,dx,dy); fb(z-3,dx,dy); fb(z+3,dx,dy)
    for zz in range(4):
        for xx in range(2):
            for yy in range(2):
                wait(pid(zz,xx,yy,1-c))
    loc.wait()
    for zz in range(4):
        p=pid(zz,x,y,c)
        @pl.when((z<3)&(zz<=z))
        def _(): cp(p,up,0).wait_send()
        @pl.when((z>0)&(zz>=z))
        def _(): cp(p,down,1).wait_send()
        cp(p,A,2).wait_send(); cp(p,B,3).wait_send(); cp(p,C,4).wait_send()
        q=pid(zz,ax,ay,c)
        cp(q,B,3).wait_send(); cp(q,C,4).wait_send()
        cp(pid(zz,bx,by,c),C,4).wait_send(); cp(pid(zz,dx,dy,c),C,4).wait_send()

def ag32(piece,cid=0):
    rows,w=piece.shape
    return pl.pallas_call(ag32_kernel,out_shape=jax.ShapeDtypeStruct((rows*32,w),piece.dtype),
        in_specs=[pl.BlockSpec(memory_space=pl.ANY)],out_specs=pl.BlockSpec(memory_space=pl.ANY),
        scratch_shapes=[pltpu.SemaphoreType.DMA,pltpu.SemaphoreType.DMA((5,32)),pltpu.SemaphoreType.DMA((32,))],
        compiler_params=pltpu.CompilerParams(collective_id=cid,has_side_effects=True))(piece)

def zmask(z):
    return (3-z)//3, (z%3)%2, (z%3)//2, z//3
def zfar(z,k):
    m0,m1,m2,m3=zmask(z)
    t=((3,2,1,0),(3,0,2,1),(0,3,1,2),(0,1,2,3))
    return m0*t[0][k]+m1*t[1][k]+m2*t[2][k]+m3*t[3][k]

def zreduce(z,x,y,c,load,zup,zdn,stage,zsend,zrecv,out_store):
    def cp(buf,zz,d,k,r):
        return pltpu.make_async_remote_copy(src_ref=stage.at[zz],dst_ref=buf.at[zz],send_sem=zsend.at[zz],recv_sem=zrecv.at[r,zz],device_id=d,device_id_type=MESH)
    up,down=dev(z+1,x,y,c),dev(z-1,x,y,c)
    for k in range(3):
        zz=zfar(z,k)
        @pl.when(zz>z)
        def _():
            stage[zz]=load(zz).astype(stage.dtype)
            @pl.when(z>0)
            def _():
                cp(zup,zz,up,0,0).wait_recv()
                stage[zz]=(stage[zz].astype(jnp.float32)+zup[zz].astype(jnp.float32)).astype(stage.dtype)
            cp(zup,zz,up,0,0).start()
        @pl.when(zz<z)
        def _():
            stage[zz]=load(zz).astype(stage.dtype)
            @pl.when(z<3)
            def _():
                cp(zdn,zz,down,1,1).wait_recv()
                stage[zz]=(stage[zz].astype(jnp.float32)+zdn[zz].astype(jnp.float32)).astype(stage.dtype)
            cp(zdn,zz,down,1,1).start()
    out_store(load(z),True)
    @pl.when(z>0)
    def _():
        cp(zup,z,up,0,0).wait_recv()
        out_store(zup[z].astype(jnp.float32),False)
    @pl.when(z<3)
    def _():
        cp(zdn,z,down,1,1).wait_recv()
        out_store(zdn[z].astype(jnp.float32),False)
    for k in range(3):
        zz=zfar(z,k)
        cp(zup,zz,up,0,0).wait_send()


def far_z(z, k):
    half = z // 2
    near = z + half * (3 - 2 * z)
    place = 3 - k + (k // 2) * (2 * (k % 2) - 1) * near
    return place + half * (3 - 2 * place)


def reduce_all_kernel(
    part_ref,
    out_ref,
    acc, cbuf, bbuf, abuf, zbuf,
    lsem, csend, crecv, bsend, brecv, asend, arecv, zsend, zrecv,
):
    f32 = jnp.float32
    rows = out_ref.shape[0]
    z, x, y, c, ax, ay, bx, by = neighbours()
    dx, dy = 1 - x, 1 - y
    A, B, C = dev(z, ax, ay, c), dev(z, bx, by, c), dev(z, x, y, 1 - c)
    up, down = dev(z + 1, x, y, c), dev(z - 1, x, y, c)

    def q(zz, xx, yy):
        return zz * 4 + xx * 2 + yy

    def at(p):
        return part_ref.at[pl.ds(pl.multiple_of(p * rows, rows), rows)]

    def ccopy(zz, xx, yy):
        i = q(zz, xx, yy)
        return pltpu.make_async_remote_copy(
            src_ref=at(pid(zz, xx, yy, 1 - c)), dst_ref=cbuf.at[i], send_sem=csend.at[i],
            recv_sem=crecv.at[i], device_id=C, device_id_type=MESH)

    def lcopy(zz, xx, yy):
        i = q(zz, xx, yy)
        return pltpu.make_async_copy(at(pid(zz, xx, yy, c)), acc.at[i], lsem.at[i])

    def bcopy(zz, far):
        i = zz + 4 * far
        place = q(zz, dx, dy) if far else q(zz, bx, by)
        return pltpu.make_async_remote_copy(
            src_ref=acc.at[place], dst_ref=bbuf.at[i], send_sem=bsend.at[i],
            recv_sem=brecv.at[i], device_id=B, device_id_type=MESH)

    def acopy(zz):
        return pltpu.make_async_remote_copy(
            src_ref=acc.at[q(zz, ax, ay)], dst_ref=abuf.at[zz], send_sem=asend.at[zz],
            recv_sem=arecv.at[zz], device_id=A, device_id_type=MESH)

    def zcopy(zz, to, slot):
        return pltpu.make_async_remote_copy(
            src_ref=acc.at[q(zz, x, y)], dst_ref=zbuf.at[slot], send_sem=zsend.at[zz],
            recv_sem=zrecv.at[slot], device_id=to, device_id_type=MESH)

    def stage_c(k):
        zz = far_z(z, k)
        for xx, yy in ((dx, dy), (bx, by), (ax, ay), (x, y)):
            lcopy(zz, xx, yy).start()
        for xx, yy in ((dx, dy), (ax, ay), (bx, by), (x, y)):
            ccopy(zz, xx, yy).start()

    def plus_c(zz, xx, yy):
        lcopy(zz, xx, yy).wait()
        ccopy(zz, xx, yy).wait_recv()
        i = q(zz, xx, yy)
        return acc[i].astype(f32) + cbuf[i].astype(f32)

    def stage_b(k):
        zz = far_z(z, k)
        acc[q(zz, dx, dy)] = plus_c(zz, dx, dy).astype(acc.dtype)
        bcopy(zz, 1).start()
        acc[q(zz, bx, by)] = plus_c(zz, bx, by).astype(acc.dtype)
        bcopy(zz, 0).start()

    def stage_a(k):
        zz = far_z(z, k)
        value = plus_c(zz, ax, ay)
        bcopy(zz, 1).wait_recv()
        acc[q(zz, ax, ay)] = (value + bbuf[zz + 4].astype(f32)).astype(acc.dtype)
        acopy(zz).start()

    def stage_z(k):
        zz = far_z(z, k)
        place = q(zz, x, y)
        value = plus_c(zz, x, y)
        bcopy(zz, 0).wait_recv()
        acopy(zz).wait_recv()
        value = value + bbuf[zz].astype(f32) + abuf[zz].astype(f32)

        @pl.when(zz != z)
        def _():
            acc[place] = value.astype(acc.dtype)

            @pl.when((zz > z) & (z > 0))
            def _():
                zcopy(zz, up, zz).wait_recv()
                acc[place] = (acc[place].astype(f32) + zbuf[zz].astype(f32)).astype(acc.dtype)

            @pl.when((zz < z) & (z < 3))
            def _():
                zcopy(zz, down, zz).wait_recv()
                acc[place] = (acc[place].astype(f32) + zbuf[zz].astype(f32)).astype(acc.dtype)

            @pl.when(zz > z)
            def _():
                zcopy(zz, up, zz).start()

            @pl.when((zz < z) & (zz != z - 1))
            def _():
                zcopy(zz, down, zz).start()

            @pl.when(zz == z - 1)
            def _():
                zcopy(zz, down, 4).start()

        @pl.when(zz == z)
        def _():
            out_ref[...] = value

            @pl.when(z > 0)
            def _():
                zcopy(z, up, z).wait_recv()
                out_ref[...] += zbuf[z].astype(f32)

            @pl.when(z < 3)
            def _():
                zcopy(z, down, 4).wait_recv()
                out_ref[...] += zbuf[4].astype(f32)

    barrier_all()

    def first(k, carry):
        stage_c(k)
        return carry

    lax.fori_loop(0, 4, first, 0)
    stage_b(0)

    def step(t, carry):
        @pl.when(t < 3)
        def _():
            stage_b(t + 1)

        @pl.when(t < 4)
        def _():
            stage_a(t)

        @pl.when(t > 0)
        def _():
            stage_z(t - 1)

        return carry

    lax.fori_loop(0, 5, step, 0)
    def last(zz, carry):
        for xx, yy in ((dx, dy), (bx, by), (ax, ay), (x, y)):
            ccopy(zz, xx, yy).wait_send()
        bcopy(zz, 1).wait_send()
        bcopy(zz, 0).wait_send()
        acopy(zz).wait_send()

        @pl.when(zz != z)
        def _():
            zcopy(zz, up, zz).wait_send()

        return carry

    lax.fori_loop(0, 4, last, 0)


def reduce_all(part, cid):
    n, w = part.shape
    rows = n // 32
    dma = pltpu.SemaphoreType.DMA

    def pieces(k):
        return pltpu.VMEM((k, rows, w), part.dtype)

    return pl.pallas_call(
        reduce_all_kernel,
        in_specs=[pl.BlockSpec(memory_space=pl.ANY)],
        out_specs=pl.BlockSpec(memory_space=pltpu.VMEM),
        out_shape=jax.ShapeDtypeStruct((rows, w), jnp.float32),
        scratch_shapes=[
            pieces(16), pieces(16), pieces(8), pieces(4), pieces(5),
            dma((16,)), dma((16,)), dma((16,)), dma((8,)), dma((8,)), dma((4,)), dma((4,)),
            dma((4,)), dma((5,)),
        ],
        compiler_params=pltpu.CompilerParams(
            collective_id=cid, has_side_effects=True, vmem_limit_bytes=48 * 2**20
        ),
        name="reduce_all",
    )(part)


def barrier_plane():
    z,x,y,c=coords()
    b=pltpu.get_barrier_semaphore()
    def sig(d): pl.semaphore_signal(b,inc=1,device_id=d,device_id_type=MESH)
    sig(dev(z,1-x,y,c))
    @pl.when(z<3)
    def _(): sig(dev(z+1,x,y,c))
    @pl.when(z>0)
    def _(): sig(dev(z-1,x,y,c))
    pl.semaphore_wait(b,3-(3-z)//3-z//3)

def barrier_tp():
    z,x,y,c=coords()
    b=pltpu.get_barrier_semaphore()
    for d in (dev(z,x,1-y,c),dev(z,x,y,1-c)):
        pl.semaphore_signal(b,inc=1,device_id=d,device_id_type=MESH)
    pl.semaphore_wait(b,2)

def agctx_kernel(x_ref,out_ref,lsem,send,recv):
    rows=x_ref.shape[0]
    z,x,y,c=coords()
    barrier_plane()
    def at(p): return out_ref.at[pl.ds(pl.multiple_of(p*rows,rows),rows)]
    def cp(p,d,k,own=False):
        return pltpu.make_async_remote_copy(src_ref=x_ref if own else at(p),dst_ref=at(p),send_sem=send.at[k,p],recv_sem=recv.at[p],device_id=d,device_id_type=MESH)
    up,down,X=dev(z+1,x,y,c),dev(z-1,x,y,c),dev(z,1-x,y,c)
    me=z*2+x
    loc=pltpu.make_async_copy(x_ref,at(me),lsem); loc.start()
    @pl.when(z<3)
    def _(): cp(me,up,0,True).start()
    @pl.when(z>0)
    def _(): cp(me,down,1,True).start()
    cp(me,X,2,True).start()
    for d in (1,2,3):
        @pl.when(z-d>=0)
        def _():
            p=(z-d)*2+x; cp(p,X,2).wait_recv()
            @pl.when(z<3)
            def _(): cp(p,up,0).start()
            cp(p,X,2).start()
        @pl.when(z+d<=3)
        def _():
            p=(z+d)*2+x; cp(p,X,2).wait_recv()
            @pl.when(z>0)
            def _(): cp(p,down,1).start()
            cp(p,X,2).start()
    loc.wait()
    for zz in range(4):
        cp(zz*2+1-x,X,2).wait_recv()
        p=zz*2+x
        @pl.when((z<3)&(zz<=z))
        def _(): cp(p,up,0).wait_send()
        @pl.when((z>0)&(zz>=z))
        def _(): cp(p,down,1).wait_send()
        cp(p,X,2).wait_send()

def agctx(piece,cid=2):
    rows,w=piece.shape
    S=pltpu.SemaphoreType.DMA
    return pl.pallas_call(agctx_kernel,out_shape=jax.ShapeDtypeStruct((rows*8,w),piece.dtype),
        in_specs=[pl.BlockSpec(memory_space=pl.ANY)],out_specs=pl.BlockSpec(memory_space=pl.ANY),
        scratch_shapes=[S,S((3,8)),S((8,))],
        compiler_params=pltpu.CompilerParams(collective_id=cid,has_side_effects=True))(piece)

def rsctx_kernel(in_ref,out_ref,xbuf,zup,zdn,stage,xsend,xrecv,zsend,zrecv):
    rows=out_ref.shape[0]
    z,x,y,c=coords()
    barrier_plane()
    f32=jnp.float32
    X=dev(z,1-x,y,c)
    def at(p): return in_ref.at[pl.ds(pl.multiple_of(p*rows,rows),rows)]
    def xcopy(zz):
        return pltpu.make_async_remote_copy(src_ref=at(zz*2+1-x),dst_ref=xbuf.at[zz],send_sem=xsend.at[zz],recv_sem=xrecv.at[zz],device_id=X,device_id_type=MESH)
    for k in range(4): xcopy(zfar(z,k)).start()
    def load(zz):
        xcopy(zz).wait_recv()
        return at(zz*2+x)[...].astype(f32)+xbuf[zz].astype(f32)
    def store(v,first):
        out_ref[...]=v if first else out_ref[...]+v
    zreduce(z,x,y,c,load,zup,zdn,stage,zsend,zrecv,store)
    for zz in range(4): xcopy(zz).wait_send()

def rsctx(part,cid=3):
    n,w=part.shape; rows=n//8
    S=pltpu.SemaphoreType.DMA
    def V(k): return pltpu.VMEM((k,rows,w),part.dtype)
    return pl.pallas_call(rsctx_kernel,out_shape=jax.ShapeDtypeStruct((rows,w),jnp.float32),
        in_specs=[pl.BlockSpec(memory_space=pltpu.VMEM)],out_specs=pl.BlockSpec(memory_space=pltpu.VMEM),
        scratch_shapes=[V(4),V(4),V(4),V(4),S((4,)),S((4,)),S((4,)),S((2,4))],
        compiler_params=pltpu.CompilerParams(collective_id=cid,has_side_effects=True,vmem_limit_bytes=32*2**20))(part)

def rstp_kernel(in_ref,out_ref,cbuf,ybuf,stage,csend,crecv,ysend,yrecv):
    rows=out_ref.shape[0]
    z,x,y,c=coords()
    barrier_tp()
    f32=jnp.float32
    def at(yy,cc): return in_ref.at[pl.ds(pl.multiple_of((yy*2+cc)*rows,rows),rows)]
    def ccopy(yy):
        return pltpu.make_async_remote_copy(src_ref=at(yy,1-c),dst_ref=cbuf.at[yy],send_sem=csend.at[yy],recv_sem=crecv.at[yy],device_id=dev(z,x,y,1-c),device_id_type=MESH)
    ccopy(1-y).start(); ccopy(y).start()
    ccopy(1-y).wait_recv()
    stage[...]=(at(1-y,c)[...].astype(f32)+cbuf[1-y].astype(f32)).astype(stage.dtype)
    yc=pltpu.make_async_remote_copy(src_ref=stage,dst_ref=ybuf,send_sem=ysend,recv_sem=yrecv,device_id=dev(z,x,1-y,c),device_id_type=MESH)
    yc.start()
    ccopy(y).wait_recv()
    out_ref[...]=at(y,c)[...].astype(f32)+cbuf[y].astype(f32)
    yc.wait_recv()
    out_ref[...]+=ybuf[...].astype(f32)
    yc.wait_send(); ccopy(0).wait_send(); ccopy(1).wait_send()

def rstp(part,cid=4):
    n,w=part.shape; rows=n//4
    S=pltpu.SemaphoreType.DMA
    return pl.pallas_call(rstp_kernel,out_shape=jax.ShapeDtypeStruct((rows,w),jnp.float32),
        in_specs=[pl.BlockSpec(memory_space=pltpu.VMEM)],out_specs=pl.BlockSpec(memory_space=pltpu.VMEM),
        scratch_shapes=[pltpu.VMEM((2,rows,w),part.dtype),pltpu.VMEM((rows,w),part.dtype),pltpu.VMEM((rows,w),part.dtype),S((2,)),S((2,)),S,S],
        compiler_params=pltpu.CompilerParams(collective_id=cid,has_side_effects=True,vmem_limit_bytes=32*2**20))(part)

def agtp_kernel(x_ref,out_ref,lsem,send,recv):
    rows=x_ref.shape[0]
    z,x,y,c=coords()
    barrier_tp()
    def at(yy,cc): return out_ref.at[pl.ds(pl.multiple_of((yy*2+cc)*rows,rows),rows)]
    def cp(src,yy,cc,d,k):
        return pltpu.make_async_remote_copy(src_ref=src,dst_ref=at(yy,cc),send_sem=send.at[k],recv_sem=recv.at[yy*2+cc],device_id=d,device_id_type=MESH)
    Y,C=dev(z,x,1-y,c),dev(z,x,y,1-c)
    loc=pltpu.make_async_copy(x_ref,at(y,c),lsem); loc.start()
    cp(x_ref,y,c,Y,0).start(); cp(x_ref,y,c,C,1).start()
    cp(x_ref,1-y,c,Y,0).wait_recv()
    cp(at(1-y,c),1-y,c,C,2).start()
    cp(x_ref,y,1-c,C,1).wait_recv(); cp(x_ref,1-y,1-c,C,2).wait_recv()
    loc.wait()
    cp(x_ref,y,c,Y,0).wait_send(); cp(x_ref,y,c,C,1).wait_send(); cp(at(1-y,c),1-y,c,C,2).wait_send()

def agtp(piece,cid=5):
    rows,w=piece.shape
    S=pltpu.SemaphoreType.DMA
    return pl.pallas_call(agtp_kernel,out_shape=jax.ShapeDtypeStruct((rows*4,w),piece.dtype),
        in_specs=[pl.BlockSpec(memory_space=pl.ANY)],out_specs=pl.BlockSpec(memory_space=pl.ANY),
        scratch_shapes=[S,S((3,)),S((4,))],
        compiler_params=pltpu.CompilerParams(collective_id=cid,has_side_effects=True))(piece)


def finish_kernel(a_ref,b_ref,v_ref,ao_ref,bo_ref,vo_ref,vbuf,part,tbuf,lsem,send,recv,vsend,vrecv,tsend,trecv):
    rows=a_ref.shape[0]; vr=vo_ref.shape[0]
    z,x,y,c=coords()
    ctx=lax.axis_index("ctx"); tp=lax.axis_index("tp")
    b=pltpu.get_barrier_semaphore()
    Y,C,D=dev(z,x,1-y,c),dev(z,x,y,1-c),dev(z,x,1-y,1-c)
    peers=[((ctx+i)%8,tp) for i in range(1,8)]+[Y,C,D]
    for d in peers: pl.semaphore_signal(b,inc=1,device_id=d,device_id_type=MESH)
    pl.semaphore_wait(b,10)
    def vcopy(i):
        to=(ctx+i)%8
        return pltpu.make_async_remote_copy(src_ref=v_ref.at[pl.ds(pl.multiple_of(to*vr,vr),vr)],dst_ref=vbuf.at[i],send_sem=vsend.at[i],recv_sem=vrecv.at[i],device_id=(to,tp),device_id_type=MESH)
    for i in range(1,8): vcopy(i).start()
    def at(o,yy,cc): return o.at[pl.ds(pl.multiple_of((yy*2+cc)*rows,rows),rows)]
    pairs=[(a_ref,ao_ref),(b_ref,bo_ref)]
    def cp(n,src,yy,cc,d,k):
        return pltpu.make_async_remote_copy(src_ref=src,dst_ref=at(pairs[n][1],yy,cc),send_sem=send.at[n,k],recv_sem=recv.at[n,yy*2+cc],device_id=d,device_id_type=MESH)
    locs=[]
    for n,(s,o) in enumerate(pairs):
        l=pltpu.make_async_copy(s,at(o,y,c),lsem.at[n]); l.start(); locs.append(l)
        cp(n,s,y,c,Y,0).start(); cp(n,s,y,c,C,1).start()
    total=v_ref[pl.ds(pl.multiple_of(ctx*vr,vr),vr)]
    for i in range(1,8):
        vcopy(i).wait_recv()
        total=total+vbuf[i]
    part[...]=total
    def tcopy(k,d):
        return pltpu.make_async_remote_copy(src_ref=part,dst_ref=tbuf.at[k],send_sem=tsend.at[k],recv_sem=trecv.at[k],device_id=d,device_id_type=MESH)
    ts=[tcopy(k,d) for k,d in enumerate((Y,C,D))]
    for t in ts: t.start()
    for n,(s,o) in enumerate(pairs):
        cp(n,s,1-y,c,Y,0).wait_recv()
        cp(n,at(o,1-y,c),1-y,c,C,2).start()
    for t in ts: t.wait_recv()
    vo_ref[...]=(part[...]+tbuf[0])+(tbuf[1]+tbuf[2])
    for n,(s,o) in enumerate(pairs):
        cp(n,s,y,1-c,C,1).wait_recv(); cp(n,s,1-y,1-c,C,2).wait_recv()
        locs[n].wait()
        cp(n,s,y,c,Y,0).wait_send(); cp(n,s,y,c,C,1).wait_send(); cp(n,at(o,1-y,c),1-y,c,C,2).wait_send()
    for t in ts: t.wait_send()
    for i in range(1,8): vcopy(i).wait_send()

def finish(a,b,v,cid):
    rows,w=a.shape; vr=v.shape[0]//8
    S=pltpu.SemaphoreType.DMA
    any_=pl.BlockSpec(memory_space=pl.ANY); vm=pl.BlockSpec(memory_space=pltpu.VMEM)
    return pl.pallas_call(finish_kernel,out_shape=[jax.ShapeDtypeStruct((rows*4,w),a.dtype),jax.ShapeDtypeStruct((rows*4,w),a.dtype),jax.ShapeDtypeStruct((vr,128),jnp.float32)],
        in_specs=[any_,any_,vm],out_specs=[any_,any_,vm],
        scratch_shapes=[pltpu.VMEM((8,vr,128),jnp.float32),pltpu.VMEM((vr,128),jnp.float32),pltpu.VMEM((3,vr,128),jnp.float32),S((2,)),S((2,3)),S((2,4)),S((8,)),S((8,)),S((3,)),S((3,))],
        compiler_params=pltpu.CompilerParams(collective_id=cid,has_side_effects=True))(a,b,v)


EPSILON = 1e-06
ROPE_BASE = 1000000.0
MASKED_SCORE = -1000000000.0
BF = jnp.bfloat16
F32 = jnp.float32


def dotf(a, b, dims):
    return lax.dot_general(a, b, (dims, ((), ())), preferred_element_type=F32)


def nt(a, b):
    return lax.dot_general(a, b, (((1,), (1,)), ((), ())), preferred_element_type=jnp.float32)


def nn(a, b):
    return lax.dot_general(a, b, (((1,), (0,)), ((), ())), preferred_element_type=jnp.float32)


def tn(a, b):
    return lax.dot_general(a, b, (((0,), (0,)), ((), ())), preferred_element_type=jnp.float32)


def expert_kernel(x_ref, cot_ref, wg_ref, wu_ref, wd_ref, s_ref, t_ref, part_ref, gl_ref, ul_ref, hs_ref):
    bf = jnp.bfloat16
    width = cot_ref.shape[1]
    x = x_ref[:, :width]
    spread = nn(x_ref[:, width:], s_ref[...])
    gate = nt(x, wg_ref[...])
    up = nt(x, wu_ref[...])
    back = nt(cot_ref[...], wd_ref[...])
    sig = 1.0 / (1.0 + jnp.exp(-gate))
    silu = gate * sig
    hidden = silu * up
    hs = (hidden * spread).astype(bf)
    hs_ref[...] = hs.T
    part_ref[:, :width] = nn(hs, wd_ref[...]).astype(bf)
    prod = hidden * back
    high = prod.astype(bf)
    low = (prod - high.astype(jnp.float32)).astype(bf)
    part_ref[:, 2 * width :] = (nn(high, t_ref[...]) + nn(low, t_ref[...])).astype(bf)
    grad = back * spread
    gl = (grad * up * sig * (1.0 + gate * (1.0 - sig))).astype(bf)
    ul = (grad * silu).astype(bf)
    gl_ref[...] = gl.T
    ul_ref[...] = ul.T
    part_ref[:, width : 2 * width] = (nn(gl, wg_ref[...]) + nn(ul, wu_ref[...])).astype(bf)


def expert_blocks(x_all, cot_all, gate_mat, up_mat, down_mat, spread_mat, pick_mat, block=256):
    n, width = cot_all.shape
    wide = x_all.shape[1]
    hid = gate_mat.shape[0]
    bf = jnp.bfloat16

    def rows(w):
        return pl.BlockSpec((block, w), lambda i: (i, 0))

    def whole(v):
        return pl.BlockSpec(v.shape, lambda i: (0, 0), pipeline_mode=pl.Buffered(1))

    return pl.pallas_call(
        expert_kernel,
        grid=(n // block,),
        in_specs=[rows(wide), rows(width)]
        + [whole(v) for v in (gate_mat, up_mat, down_mat, spread_mat, pick_mat)],
        out_specs=[rows(width + wide)] + [pl.BlockSpec((hid, block), lambda i: (0, i))] * 3,
        out_shape=[jax.ShapeDtypeStruct((n, width + wide), bf)]
        + [jax.ShapeDtypeStruct((hid, n), bf)] * 3,
        compiler_params=pltpu.CompilerParams(
            dimension_semantics=("arbitrary",), vmem_limit_bytes=56 * 2**20
        ),
        cost_estimate=pl.CostEstimate(
            flops=12 * n * width * hid, bytes_accessed=10 * n * width, transcendentals=n * hid
        ),
        name="experts",
    )(x_all, cot_all, gate_mat, up_mat, down_mat, spread_mat, pick_mat)


def expert_grad_kernel(x_ref, cot_ref, gl_ref, ul_ref, hs_ref, gg_ref, gu_ref, gd_ref):
    first = pl.program_id(1) == 0

    def put(ref, low, full):
        value = nn(low[...], full[...])

        @pl.when(first)
        def _():
            ref[...] = value

        @pl.when(jnp.logical_not(first))
        def _():
            ref[...] += value

    put(gg_ref, gl_ref, x_ref)
    put(gu_ref, ul_ref, x_ref)
    put(gd_ref, hs_ref, cot_ref)


def expert_grads(x_all, cot_all, gl, ul, hs, block=256):
    n, width = cot_all.shape
    hid = gl.shape[0]
    span = min(n, 2048)
    cols = pl.BlockSpec((span, block), lambda i, j: (j, i))
    rows = pl.BlockSpec((hid, span), lambda i, j: (0, j))
    out = pl.BlockSpec((hid, block), lambda i, j: (0, i))
    return pl.pallas_call(
        expert_grad_kernel,
        grid=(width // block, n // span),
        in_specs=[cols, cols, rows, rows, rows],
        out_specs=[out] * 3,
        out_shape=[jax.ShapeDtypeStruct((hid, width), jnp.float32)] * 3,
        compiler_params=pltpu.CompilerParams(
            dimension_semantics=("arbitrary", "arbitrary"), vmem_limit_bytes=56 * 2**20
        ),
        cost_estimate=pl.CostEstimate(
            flops=6 * n * width * hid, bytes_accessed=10 * n * width, transcendentals=0
        ),
        name="expert_grads",
    )(x_all, cot_all, gl, ul, hs)


class Links:
    def __init__(self, own):
        self.own = own

    def ag_all(self, piece, cid):
        if self.own:
            return ag32(piece, cid)
        return lax.all_gather(piece, ("ctx", "tp"), axis=0, tiled=True)

    def rs_all(self, part, cid):
        if self.own:
            return reduce_all(part, cid)
        return lax.psum_scatter(part, ("ctx", "tp"), scatter_dimension=0, tiled=True).astype(F32)

    def ag_ctx(self, piece, cid):
        if self.own:
            return agctx(piece, cid)
        return lax.all_gather(piece, "ctx", axis=0, tiled=True)

    def rs_ctx(self, part, cid):
        if self.own:
            return rsctx(part, cid)
        return lax.psum_scatter(part, "ctx", scatter_dimension=0, tiled=True).astype(F32)

    def rs_tp(self, part, cid):
        if self.own:
            return rstp(part, cid)
        return lax.psum_scatter(part, "tp", scatter_dimension=0, tiled=True).astype(F32)

    def ag_tp(self, piece, cid):
        if self.own:
            return agtp(piece, cid)
        return lax.all_gather(piece, "tp", axis=0, tiled=True)


    def finish(self, a, b, vectors, cid):
        if self.own:
            return finish(a, b, vectors, cid)
        total = lax.psum_scatter(vectors, "ctx", scatter_dimension=0, tiled=True)
        gathered = (lax.all_gather(v, "tp", axis=0, tiled=True) for v in (a, b))
        return (*gathered, lax.psum(total, "tp"))


def rms_norm(values, gain_vec):
    factor = lax.rsqrt(jnp.mean(values * values, axis=-1, keepdims=True) + EPSILON)
    return values * factor * gain_vec


def rotate(values, rotary_angles):
    half_size = values.shape[-1] // 2
    first_half = values[..., :half_size]
    second_half = values[..., half_size:]
    cosine = jnp.cos(rotary_angles)
    sine_part = jnp.sin(rotary_angles)
    return jnp.concatenate(
        [
            first_half * cosine - second_half * sine_part,
            second_half * cosine + first_half * sine_part,
        ],
        axis=-1,
    )


def angles_of(token_positions, head_width):
    freq_steps = jnp.arange(head_width // 2).astype(F32) * (2.0 / head_width)
    frequency = jnp.exp(-math.log(ROPE_BASE) * freq_steps)
    return token_positions.astype(F32)[..., None] * frequency


def positions_of(block_order, dev_count, block_len):
    first_block = jnp.transpose(block_order)
    block_pair = jnp.stack([first_block, 2 * dev_count - 1 - first_block], axis=-1)
    spread = block_pair[..., None] * block_len + jnp.arange(block_len, dtype=jnp.int32)
    return spread.reshape(dev_count, block_order.shape[0], 2 * block_len)


def head_route_path(raw_heads, gain_vec, rotary_angles, head_count):
    shaped = raw_heads.reshape(raw_heads.shape[0], head_count, -1)
    return rotate(rms_norm(shaped, gain_vec), rotary_angles[:, None, :])


def attend_forward(seq_item):
    query_matrix, every_key_row, every_value_row, query_pos, key_pos = seq_item
    score_scale = 1.0 / math.sqrt(query_matrix.shape[-1])
    unscaled_scores = jnp.einsum(
        "upnj,apj->upna", query_matrix, every_key_row, preferred_element_type=F32
    )
    allowed = query_pos[:, None, None, None] >= key_pos[None, None, None, :]
    scores = jnp.where(allowed, unscaled_scores * score_scale, MASKED_SCORE)
    row_top = jnp.max(scores, axis=-1, keepdims=True)
    exp_scores = jnp.exp(scores - row_top)
    totals = jnp.sum(exp_scores, axis=-1, keepdims=True)
    lower_attention_probs = (exp_scores / totals).astype(BF)
    attended_mix = jnp.einsum(
        "jzfq,qzx->jzfx", lower_attention_probs, every_value_row, preferred_element_type=F32
    )
    return (attended_mix, (row_top + jnp.log(totals))[..., 0])


def attend_backward(seq_item):
    (
        query_matrix,
        every_key_row,
        every_value_row,
        query_pos,
        key_pos,
        grad_attended_mix,
        log_total,
    ) = seq_item
    score_scale = 1.0 / math.sqrt(query_matrix.shape[-1])
    unscaled_scores = jnp.einsum(
        "upnj,apj->upna", query_matrix, every_key_row, preferred_element_type=F32
    )
    allowed = query_pos[:, None, None, None] >= key_pos[None, None, None, :]
    scores = jnp.where(allowed, unscaled_scores * score_scale, MASKED_SCORE)
    attention_probs = jnp.exp(scores - log_total[..., None])
    grad_probs = jnp.einsum(
        "upnj,apj->upna", grad_attended_mix, every_value_row, preferred_element_type=F32
    )
    row_inner = jnp.sum(attention_probs * grad_probs, axis=-1, keepdims=True)
    grad_score_dots = (attention_probs * (grad_probs - row_inner) * score_scale).astype(BF)
    grad_queries = jnp.einsum(
        "jzfq,qzx->jzfx", grad_score_dots, every_key_row, preferred_element_type=F32
    )
    grad_key_rows = jnp.einsum(
        "axfv,axfz->vxz", grad_score_dots, query_matrix, preferred_element_type=F32
    )
    grad_values = jnp.einsum(
        "axfv,axfz->vxz", attention_probs.astype(BF), grad_attended_mix, preferred_element_type=F32
    )
    return (grad_queries, grad_key_rows, grad_values)


def gates_of(logits, routes):
    experts = logits.shape[1]
    named = jnp.any(routes[:, :, None] == jnp.arange(experts, dtype=jnp.int32), axis=1)
    masked = jnp.where(named, logits, -jnp.inf)
    top = jnp.max(masked, axis=1, keepdims=True)
    weights = jnp.where(named, jnp.exp(masked - top), 0.0)
    return weights / jnp.sum(weights, axis=1, keepdims=True)


def shards(
    tokens_in,
    block_order,
    routes,
    norm1_gain,
    w_query,
    key_weight,
    value_weight,
    query_gain,
    key_gain,
    w_out,
    norm2_gain,
    w_router,
    w_gate,
    w_up,
    w_down,
    cotangent,
):
    tok_count, model_width = tokens_in.shape
    head_size = query_gain.shape[0]
    local_heads = w_query.shape[1] // head_size
    local_kv = key_weight.shape[1] // head_size
    query_group_width = local_heads // local_kv
    seq_count = block_order.shape[0]
    devices, tp_size = lax.axis_size("ctx"), lax.axis_size("tp")
    links = Links(devices == 8 and tp_size == 4)
    me, tp_me = lax.axis_index("ctx"), lax.axis_index("tp")
    rows = tok_count // tp_size
    block_len = tok_count // (2 * seq_count)
    experts = w_router.shape[1]
    own_experts, _, units = w_gate.shape
    hid = own_experts * units
    all_tok = devices * tok_count

    def own_rows(v):
        return lax.dynamic_slice_in_dim(v, tp_me * rows, rows, axis=0)

    cot_own = own_rows(cotangent)
    cot_all = lax.all_gather(cot_own, ("ctx", "tp"), axis=0, tiled=True)

    token_positions = positions_of(block_order, devices, block_len)
    query_pos = lax.dynamic_index_in_dim(token_positions, me, 0, keepdims=False)
    key_pos = jnp.transpose(token_positions, (1, 0, 2)).reshape(seq_count, devices * 2 * block_len)
    rotary_angles = angles_of(query_pos.reshape(-1), head_size)
    inputs = tokens_in.astype(F32)
    first_in = rms_norm(inputs, norm1_gain).astype(BF)
    query_raw = jnp.dot(first_in, w_query, preferred_element_type=F32)
    unrotated_key = jnp.dot(first_in, key_weight, preferred_element_type=F32)
    value_rows = jnp.dot(first_in, value_weight, preferred_element_type=F32).astype(BF)

    def rope_heads(raw_query, raw_key, gain_query, key_norm_gain):
        return (
            head_route_path(raw_query, gain_query, rotary_angles, local_heads),
            head_route_path(raw_key, key_norm_gain, rotary_angles, local_kv),
        )

    (query_rot, key_rot), rope_back = jax.vjp(
        rope_heads, query_raw, unrotated_key, query_gain, key_gain
    )
    query_rows = query_rot.astype(BF).reshape(
        seq_count, 2 * block_len, local_kv, query_group_width, head_size
    )
    kv_width = local_kv * head_size
    kv_own = jnp.concatenate([key_rot.astype(BF).reshape(tok_count, kv_width), value_rows], axis=1)
    kv_all = links.ag_ctx(kv_own, 1)
    kv_seq = kv_all.reshape(devices, seq_count, 2 * block_len, 2, local_kv, head_size)
    kv_seq = kv_seq.transpose(3, 1, 0, 2, 4, 5).reshape(
        2, seq_count, devices * 2 * block_len, local_kv, head_size
    )
    key_full, value_full = kv_seq[0], kv_seq[1]
    attended_mix, log_total = lax.map(
        attend_forward, (query_rows, key_full, value_full, query_pos, key_pos)
    )
    attended = attended_mix.reshape(tok_count, local_heads * head_size).astype(BF)
    attn_part = jnp.dot(attended, w_out, preferred_element_type=F32).astype(BF)
    residual = own_rows(inputs) + links.rs_tp(attn_part, 2)
    second_normed, second_back = jax.vjp(rms_norm, residual, norm2_gain)
    second_in = second_normed.astype(BF)
    extra = -(-2 * experts // 128) * 128
    gates = gates_of(jnp.dot(second_in, w_router, preferred_element_type=F32), own_rows(routes))
    gates_high = gates.astype(BF)
    gates_low = (gates - gates_high.astype(F32)).astype(BF)
    pad = jnp.zeros((rows, extra - 2 * experts), BF)
    second_all = links.ag_all(
        jnp.concatenate([second_in, gates_high, gates_low, pad], axis=1), 3
    )
    column = jnp.arange(extra, dtype=jnp.int32)[:, None]
    named = me * own_experts + jnp.arange(hid, dtype=jnp.int32)[None, :] // units
    pick = (column == named).astype(BF)
    spread = pick + (column == named + experts).astype(BF)
    gate_mat = w_gate.transpose(0, 2, 1).reshape(hid, model_width)
    up_mat = w_up.transpose(0, 2, 1).reshape(hid, model_width)
    down_mat = w_down.reshape(hid, model_width)
    part, gate_low, up_low, hidden_low = expert_blocks(
        second_all, cot_all, gate_mat, up_mat, down_mat, spread, pick.T
    )
    sums_own = links.rs_all(part, 6)
    out_own = sums_own[:, :model_width]
    entry_own = sums_own[:, model_width:]
    gate_total = entry_own[:, model_width : model_width + experts]
    grad_logits = (
        gates * (gate_total - jnp.sum(gates * gate_total, axis=1, keepdims=True))
    ).astype(BF)
    grad_second = entry_own[:, :model_width] + dotf(grad_logits, w_router, ((1,), (1,)))
    grad_resid_norm, grad_norm2 = second_back(grad_second)
    grad_residual = cot_own.astype(F32) + grad_resid_norm
    pad = jnp.zeros((rows, -experts % 128), BF)
    back_all = links.ag_tp(
        jnp.concatenate([grad_residual.astype(BF), grad_logits, pad], axis=1), 7
    )
    grad_attn_low = back_all[:, :model_width]
    second_own = lax.dynamic_slice(second_all, (me * tok_count, 0), (tok_count, model_width))
    router_part = dotf(second_own, back_all[:, model_width:], ((0,), (0,)))
    grad_out = dotf(attended, grad_attn_low, ((0,), (0,)))
    grad_mixed = dotf(grad_attn_low, w_out, ((1,), (1,))).astype(BF)
    grad_mixed = grad_mixed.reshape(
        seq_count, 2 * block_len, local_kv, query_group_width, head_size
    )
    grad_query_seq, grad_key_seq, grad_value_seq = lax.map(
        attend_backward,
        (query_rows, key_full, value_full, query_pos, key_pos, grad_mixed, log_total),
    )
    grad_kv = jnp.stack([grad_key_seq, grad_value_seq]).astype(BF)
    grad_kv = grad_kv.reshape(2, seq_count, devices, 2 * block_len, kv_width)
    grad_kv = grad_kv.transpose(2, 1, 3, 0, 4).reshape(all_tok, 2 * kv_width)
    grad_kv_own = links.rs_ctx(grad_kv, 8)
    grad_query_rot = grad_query_seq.reshape(tok_count, local_heads, head_size)
    grad_key_rot = grad_kv_own[:, :kv_width].reshape(tok_count, local_kv, head_size)
    grad_query_raw, grad_key_raw, grad_qgain, grad_kgain = rope_back(
        (grad_query_rot, grad_key_rot)
    )
    query_low = grad_query_raw.astype(BF)
    key_low = grad_key_raw.astype(BF)
    value_low = grad_kv_own[:, kv_width:].astype(BF)
    first_part = dotf(query_low, w_query, ((1,), (1,)))
    first_part = first_part + dotf(key_low, key_weight, ((1,), (1,)))
    first_part = first_part + dotf(value_low, value_weight, ((1,), (1,)))
    grad_first = links.rs_tp(first_part.astype(BF), 9)
    grad_first, gate_low = lax.optimization_barrier((grad_first, gate_low))
    grads = expert_grads(second_all, cot_all, gate_low, up_low, hidden_low)
    grad_gate, grad_up = (
        v.reshape(own_experts, units, model_width).transpose(0, 2, 1) for v in grads[:2]
    )
    grad_down = grads[2].reshape(own_experts, units, model_width)
    _, first_back = jax.vjp(rms_norm, own_rows(inputs), norm1_gain)
    grad_input_norm, grad_norm1 = first_back(grad_first)
    def over_ctx(v, dim):
        return lax.psum_scatter(v.astype(BF), "ctx", scatter_dimension=dim, tiled=True).astype(F32)

    grad_query = over_ctx(dotf(first_in, query_low, ((0,), (0,))), 0)
    kv_part = dotf(first_in, jnp.concatenate([key_low, value_low], axis=1), ((0,), (0,)))
    small = links.rs_ctx(jnp.concatenate([kv_part, router_part], axis=1).astype(BF), 11)
    grad_key = small[:, :kv_width]
    grad_value = small[:, kv_width : 2 * kv_width]
    grad_router = small[:, 2 * kv_width : 2 * kv_width + experts]
    grad_out = over_ctx(grad_out, 1)
    vectors = [
        v.reshape(devices, -1) for v in (grad_norm1, grad_norm2, grad_qgain, grad_kgain)
    ]
    sizes = [v.shape[1] for v in vectors]
    pad = jnp.zeros((devices, -sum(sizes) % 1024), F32)
    packed = jnp.concatenate([*vectors, pad], axis=1).reshape(-1, 128)
    grad_input, layer_out, total = links.finish(
        (grad_residual + grad_input_norm).astype(BF), (residual + out_own).astype(BF), packed, 10
    )
    total = total.reshape(-1)

    def piece_of(n):
        start = sum(sizes[:n])
        return total[start : start + sizes[n]]

    return (
        layer_out,
        grad_input,
        piece_of(0),
        grad_query,
        grad_key,
        grad_value,
        piece_of(2),
        piece_of(3),
        grad_out,
        piece_of(1),
        grad_router,
        grad_gate,
        grad_up,
        grad_down,
    )


def solution(mesh):
    in_specs = (
        P("ctx", None),
        P(),
        P("ctx", None),
        P(),
        P(None, "tp"),
        P(None, "tp"),
        P(None, "tp"),
        P(),
        P(),
        P("tp", None),
        P(),
        P(),
        P("ctx", None, "tp"),
        P("ctx", None, "tp"),
        P("ctx", "tp", None),
        P("ctx", None),
    )
    out_specs = (
        P("ctx", None),
        P("ctx", None),
        P("ctx"),
        P("ctx", "tp"),
        P("ctx", "tp"),
        P("ctx", "tp"),
        P("ctx"),
        P("ctx"),
        P("tp", "ctx"),
        P("ctx"),
        P("ctx", None),
        P("ctx", None, "tp"),
        P("ctx", None, "tp"),
        P("ctx", "tp", None),
    )
    return jax.shard_map(shards, mesh=mesh, in_specs=in_specs, out_specs=out_specs, check_vma=False)
```

```python
import math
import jax
import jax.numpy as jnp
from jax import lax
from jax.sharding import PartitionSpec as P
from jax.experimental import pallas as pl
from jax.experimental.pallas import tpu as pltpu
MESH=pl.DeviceIdType.MESH

def coords():
    ctx=lax.axis_index("ctx"); tp=lax.axis_index("tp")
    return ctx//2, ctx%2, tp//2, tp%2
def dev(z,x,y,c): return (z*2+x, y*2+c)
def pid(z,x,y,c): return (z*2+x)*4+y*2+c

def neighbours():
    z,x,y,c=coords()
    ax=x+(1-c)*(1-2*x); ay=y+c*(1-2*y)
    bx=x+c*(1-2*x); by=y+(1-c)*(1-2*y)
    return z,x,y,c,ax,ay,bx,by

def barrier_all():
    z,x,y,c=coords()
    b=pltpu.get_barrier_semaphore()
    def sig(d): pl.semaphore_signal(b,inc=1,device_id=d,device_id_type=MESH)
    sig(dev(z,1-x,y,c)); sig(dev(z,x,1-y,c)); sig(dev(z,x,y,1-c))
    @pl.when(z<3)
    def _(): sig(dev(z+1,x,y,c))
    @pl.when(z>0)
    def _(): sig(dev(z-1,x,y,c))
    pl.semaphore_wait(b,5-(3-z)//3-z//3)

def ag32_kernel(x_ref,out_ref,lsem,send,recv):
    rows=x_ref.shape[0]
    z,x,y,c,ax,ay,bx,by=neighbours()
    barrier_all()
    me=pid(z,x,y,c)
    def at(p): return out_ref.at[pl.ds(pl.multiple_of(p*rows,rows),rows)]
    def cp(p,d,k,own=False):
        return pltpu.make_async_remote_copy(src_ref=x_ref if own else at(p),dst_ref=at(p),send_sem=send.at[k,p],recv_sem=recv.at[p],device_id=d,device_id_type=MESH)
    up,down,A,B,C=dev(z+1,x,y,c),dev(z-1,x,y,c),dev(z,ax,ay,c),dev(z,bx,by,c),dev(z,x,y,1-c)
    def wait(p):
        cp(p,C,4).wait_recv()
    loc=pltpu.make_async_copy(x_ref,at(me),lsem); loc.start()
    @pl.when(z<3)
    def _(): cp(me,up,0,True).start()
    @pl.when(z>0)
    def _(): cp(me,down,1,True).start()
    cp(me,A,2,True).start(); cp(me,B,3,True).start(); cp(me,C,4,True).start()
    def zlow(d):
        @pl.when(z-d>=0)
        def _():
            p=pid(z-d,x,y,c); wait(p)
            @pl.when(z<3)
            def _(): cp(p,up,0).start()
            cp(p,A,2).start(); cp(p,B,3).start(); cp(p,C,4).start()
    def zhigh(d):
        @pl.when(z+d<=3)
        def _():
            p=pid(z+d,x,y,c); wait(p)
            @pl.when(z>0)
            def _(): cp(p,down,1).start()
            cp(p,A,2).start(); cp(p,B,3).start(); cp(p,C,4).start()
    def fa(zz):
        @pl.when((zz>=0)&(zz<=3))
        def _():
            p=pid(zz,ax,ay,c); wait(p)
            cp(p,B,3).start(); cp(p,C,4).start()
    def fb(zz,xx,yy):
        @pl.when((zz>=0)&(zz<=3))
        def _():
            p=pid(zz,xx,yy,c); wait(p); cp(p,C,4).start()
    zlow(1); zhigh(1); fa(z); zlow(2); zhigh(2); fa(z-1); fa(z+1); fb(z,bx,by); zlow(3); zhigh(3)
    fa(z-2); fa(z+2); fb(z-1,bx,by); fb(z+1,bx,by); fa(z-3); fa(z+3)
    dx,dy=1-x,1-y
    fb(z,dx,dy); fb(z-2,bx,by); fb(z+2,bx,by); fb(z-1,dx,dy); fb(z+1,dx,dy); fb(z-3,bx,by); fb(z+3,bx,by); fb(z-2,dx,dy); fb(z+2,dx,dy); fb(z-3,dx,dy); fb(z+3,dx,dy)
    for zz in range(4):
        for xx in range(2):
            for yy in range(2):
                wait(pid(zz,xx,yy,1-c))
    loc.wait()
    for zz in range(4):
        p=pid(zz,x,y,c)
        @pl.when((z<3)&(zz<=z))
        def _(): cp(p,up,0).wait_send()
        @pl.when((z>0)&(zz>=z))
        def _(): cp(p,down,1).wait_send()
        cp(p,A,2).wait_send(); cp(p,B,3).wait_send(); cp(p,C,4).wait_send()
        q=pid(zz,ax,ay,c)
        cp(q,B,3).wait_send(); cp(q,C,4).wait_send()
        cp(pid(zz,bx,by,c),C,4).wait_send(); cp(pid(zz,dx,dy,c),C,4).wait_send()

def ag32(piece,cid=0):
    rows,w=piece.shape
    return pl.pallas_call(ag32_kernel,out_shape=jax.ShapeDtypeStruct((rows*32,w),piece.dtype),
        in_specs=[pl.BlockSpec(memory_space=pl.ANY)],out_specs=pl.BlockSpec(memory_space=pl.ANY),
        scratch_shapes=[pltpu.SemaphoreType.DMA,pltpu.SemaphoreType.DMA((5,32)),pltpu.SemaphoreType.DMA((32,))],
        compiler_params=pltpu.CompilerParams(collective_id=cid,has_side_effects=True))(piece)

def far_z(z, k):
    half = z // 2
    near = z + half * (3 - 2 * z)
    place = 3 - k + (k // 2) * (2 * (k % 2) - 1) * near
    return place + half * (3 - 2 * place)


def reduce_all_kernel(
    part_ref,
    out_ref,
    acc, cbuf, bbuf, abuf, zbuf,
    lsem, csend, crecv, bsend, brecv, asend, arecv, zsend, zrecv,
):
    f32 = jnp.float32
    rows = out_ref.shape[0]
    z, x, y, c, ax, ay, bx, by = neighbours()
    dx, dy = 1 - x, 1 - y
    A, B, C = dev(z, ax, ay, c), dev(z, bx, by, c), dev(z, x, y, 1 - c)
    up, down = dev(z + 1, x, y, c), dev(z - 1, x, y, c)

    def q(zz, xx, yy):
        return zz * 4 + xx * 2 + yy

    def at(p):
        return part_ref.at[pl.ds(pl.multiple_of(p * rows, rows), rows)]

    def ccopy(zz, xx, yy):
        i = q(zz, xx, yy)
        return pltpu.make_async_remote_copy(
            src_ref=at(pid(zz, xx, yy, 1 - c)), dst_ref=cbuf.at[i], send_sem=csend.at[i],
            recv_sem=crecv.at[i], device_id=C, device_id_type=MESH)

    def lcopy(zz, xx, yy):
        i = q(zz, xx, yy)
        return pltpu.make_async_copy(at(pid(zz, xx, yy, c)), acc.at[i], lsem.at[i])

    def bcopy(zz, far):
        i = zz + 4 * far
        place = q(zz, dx, dy) if far else q(zz, bx, by)
        return pltpu.make_async_remote_copy(
            src_ref=acc.at[place], dst_ref=bbuf.at[i], send_sem=bsend.at[i],
            recv_sem=brecv.at[i], device_id=B, device_id_type=MESH)

    def acopy(zz):
        return pltpu.make_async_remote_copy(
            src_ref=acc.at[q(zz, ax, ay)], dst_ref=abuf.at[zz], send_sem=asend.at[zz],
            recv_sem=arecv.at[zz], device_id=A, device_id_type=MESH)

    def zcopy(zz, to, slot):
        return pltpu.make_async_remote_copy(
            src_ref=acc.at[q(zz, x, y)], dst_ref=zbuf.at[slot], send_sem=zsend.at[zz],
            recv_sem=zrecv.at[slot], device_id=to, device_id_type=MESH)

    def stage_c(k):
        zz = far_z(z, k)
        for xx, yy in ((dx, dy), (bx, by), (ax, ay), (x, y)):
            lcopy(zz, xx, yy).start()
        for xx, yy in ((dx, dy), (ax, ay), (bx, by), (x, y)):
            ccopy(zz, xx, yy).start()

    def plus_c(zz, xx, yy):
        lcopy(zz, xx, yy).wait()
        ccopy(zz, xx, yy).wait_recv()
        i = q(zz, xx, yy)
        return acc[i].astype(f32) + cbuf[i].astype(f32)

    def stage_b(k):
        zz = far_z(z, k)
        acc[q(zz, dx, dy)] = plus_c(zz, dx, dy).astype(acc.dtype)
        bcopy(zz, 1).start()
        acc[q(zz, bx, by)] = plus_c(zz, bx, by).astype(acc.dtype)
        bcopy(zz, 0).start()

    def stage_a(k):
        zz = far_z(z, k)
        value = plus_c(zz, ax, ay)
        bcopy(zz, 1).wait_recv()
        acc[q(zz, ax, ay)] = (value + bbuf[zz + 4].astype(f32)).astype(acc.dtype)
        acopy(zz).start()

    def stage_z(k):
        zz = far_z(z, k)
        place = q(zz, x, y)
        value = plus_c(zz, x, y)
        bcopy(zz, 0).wait_recv()
        acopy(zz).wait_recv()
        value = value + bbuf[zz].astype(f32) + abuf[zz].astype(f32)

        @pl.when(zz != z)
        def _():
            acc[place] = value.astype(acc.dtype)

            @pl.when((zz > z) & (z > 0))
            def _():
                zcopy(zz, up, zz).wait_recv()
                acc[place] = (acc[place].astype(f32) + zbuf[zz].astype(f32)).astype(acc.dtype)

            @pl.when((zz < z) & (z < 3))
            def _():
                zcopy(zz, down, zz).wait_recv()
                acc[place] = (acc[place].astype(f32) + zbuf[zz].astype(f32)).astype(acc.dtype)

            @pl.when(zz > z)
            def _():
                zcopy(zz, up, zz).start()

            @pl.when((zz < z) & (zz != z - 1))
            def _():
                zcopy(zz, down, zz).start()

            @pl.when(zz == z - 1)
            def _():
                zcopy(zz, down, 4).start()

        @pl.when(zz == z)
        def _():
            out_ref[...] = value

            @pl.when(z > 0)
            def _():
                zcopy(z, up, z).wait_recv()
                out_ref[...] += zbuf[z].astype(f32)

            @pl.when(z < 3)
            def _():
                zcopy(z, down, 4).wait_recv()
                out_ref[...] += zbuf[4].astype(f32)

    barrier_all()

    def first(k, carry):
        stage_c(k)
        return carry

    lax.fori_loop(0, 4, first, 0)
    stage_b(0)

    def step(t, carry):
        @pl.when(t < 3)
        def _():
            stage_b(t + 1)

        @pl.when(t < 4)
        def _():
            stage_a(t)

        @pl.when(t > 0)
        def _():
            stage_z(t - 1)

        return carry

    lax.fori_loop(0, 5, step, 0)
    def last(zz, carry):
        for xx, yy in ((dx, dy), (bx, by), (ax, ay), (x, y)):
            ccopy(zz, xx, yy).wait_send()
        bcopy(zz, 1).wait_send()
        bcopy(zz, 0).wait_send()
        acopy(zz).wait_send()

        @pl.when(zz != z)
        def _():
            zcopy(zz, up, zz).wait_send()

        return carry

    lax.fori_loop(0, 4, last, 0)


def reduce_all(part, cid):
    n, w = part.shape
    rows = n // 32
    dma = pltpu.SemaphoreType.DMA

    def pieces(k):
        return pltpu.VMEM((k, rows, w), part.dtype)

    return pl.pallas_call(
        reduce_all_kernel,
        in_specs=[pl.BlockSpec(memory_space=pl.ANY)],
        out_specs=pl.BlockSpec(memory_space=pltpu.VMEM),
        out_shape=jax.ShapeDtypeStruct((rows, w), jnp.float32),
        scratch_shapes=[
            pieces(16), pieces(16), pieces(8), pieces(4), pieces(5),
            dma((16,)), dma((16,)), dma((16,)), dma((8,)), dma((8,)), dma((4,)), dma((4,)),
            dma((4,)), dma((5,)),
        ],
        compiler_params=pltpu.CompilerParams(
            collective_id=cid, has_side_effects=True, vmem_limit_bytes=48 * 2**20
        ),
        name="reduce_all",
    )(part)


def barrier_wide():
    z, x, y, c = coords()
    ctx, tp = lax.axis_index("ctx"), lax.axis_index("tp")
    bar = pltpu.get_barrier_semaphore()
    for i in range(1, 8):
        pl.semaphore_signal(bar, inc=1, device_id=((ctx + i) % 8, tp), device_id_type=MESH)
    for to in (dev(z, x, 1 - y, c), dev(z, x, y, 1 - c), dev(z, x, 1 - y, 1 - c)):
        pl.semaphore_signal(bar, inc=1, device_id=to, device_id_type=MESH)
    pl.semaphore_wait(bar, 10)


class Columns:
    def __init__(self, src, buf, send, recv, tsend, trecv):
        self.src, self.buf, self.send, self.recv = src, buf, send, recv
        self.tsend, self.trecv = tsend, trecv
        self.ctx, self.tp = lax.axis_index("ctx"), lax.axis_index("tp")
        z, x, y, c = coords()
        self.Y, self.C = dev(z, x, 1 - y, c), dev(z, x, y, 1 - c)
        self.mine, self.by_y, self.by_c, self.by_d = y * 2 + c, (1 - y) * 2 + c, y * 2 + 1 - c, (1 - y) * 2 + 1 - c

    def push(self, i):
        to = (self.ctx + i) % 8
        return pltpu.make_async_remote_copy(
            src_ref=self.src.at[to], dst_ref=self.buf.at[self.ctx, self.tp],
            send_sem=self.send.at[i], recv_sem=self.recv.at[i], device_id=(to, self.tp),
            device_id_type=MESH)

    def over(self, part, to, k):
        return pltpu.make_async_remote_copy(
            src_ref=self.buf.at[:, part], dst_ref=self.buf.at[:, part], send_sem=self.tsend.at[k],
            recv_sem=self.trecv.at[part], device_id=to, device_id_type=MESH)

    def start(self):
        for i in range(1, 8):
            self.push(i).start()
        self.buf[self.ctx, self.tp] = self.src[self.ctx]

    def exchange(self):
        for i in range(1, 8):
            self.push(i).wait_recv()
        self.over(self.mine, self.Y, 0).start()
        self.over(self.mine, self.C, 1).start()

    def forward(self):
        self.over(self.by_y, self.Y, 0).wait_recv()
        self.over(self.by_y, self.C, 2).start()

    def finish(self):
        self.over(self.by_c, self.C, 1).wait_recv()
        self.over(self.by_d, self.C, 2).wait_recv()
        for i in range(1, 8):
            self.push(i).wait_send()
        self.over(self.mine, self.Y, 0).wait_send()
        self.over(self.mine, self.C, 1).wait_send()
        self.over(self.by_y, self.C, 2).wait_send()


class Spread:
    def __init__(self, place, send, recv, first=None):
        self.place, self.send, self.recv, self.first = place, send, recv, first
        z, x, y, c = coords()
        self.z, self.x = z, x
        self.X = dev(z, 1 - x, y, c)
        self.up, self.down = dev(z + 1, x, y, c), dev(z - 1, x, y, c)
        self.me = z * 2 + x

    def copy(self, p, to, k, own=False):
        src = self.first if own and self.first is not None else self.place(p)
        return pltpu.make_async_remote_copy(
            src_ref=src, dst_ref=self.place(p), send_sem=self.send.at[k, p],
            recv_sem=self.recv.at[p], device_id=to, device_id_type=MESH)

    def start_x(self):
        self.copy(self.me, self.X, 2, True).start()

    def start_z(self):
        @pl.when(self.z < 3)
        def _():
            self.copy(self.me, self.up, 0, True).start()

        @pl.when(self.z > 0)
        def _():
            self.copy(self.me, self.down, 1, True).start()

    def pass_on(self, d):
        z, x = self.z, self.x

        @pl.when(z - d >= 0)
        def _():
            p = (z - d) * 2 + x
            self.copy(p, self.X, 2).wait_recv()

            @pl.when(z < 3)
            def _():
                self.copy(p, self.up, 0).start()

            self.copy(p, self.X, 2).start()

        @pl.when(z + d <= 3)
        def _():
            p = (z + d) * 2 + x
            self.copy(p, self.X, 2).wait_recv()

            @pl.when(z > 0)
            def _():
                self.copy(p, self.down, 1).start()

            self.copy(p, self.X, 2).start()

    def arrive(self):
        for zz in range(4):
            self.copy(zz * 2 + 1 - self.x, self.X, 2).wait_recv()

    def finish(self):
        z, x = self.z, self.x
        for zz in range(4):
            p = zz * 2 + x

            @pl.when((z < 3) & (zz <= z))
            def _():
                self.copy(p, self.up, 0).wait_send()

            @pl.when((z > 0) & (zz >= z))
            def _():
                self.copy(p, self.down, 1).wait_send()

            self.copy(p, self.X, 2).wait_send()


def row_norm(v):
    return lax.rsqrt(jnp.mean(v * v, axis=1, keepdims=True) + 1e-06)


def turn(v, cos, sin):
    return v * cos + pltpu.roll(v, v.shape[1] // 2, 1) * sin


def turn_back(v, cos, sin):
    return v * cos - pltpu.roll(v, v.shape[1] // 2, 1) * sin


def front_kernel(
    x_ref, g1_ref, wq_ref, wk_ref, wv_ref, qg_ref, kg_ref, cos_ref, sin_ref, qpos_ref, kpos_ref,
    wo_ref, g2_ref, wr_ref, routes_ref,
    first_ref, qraw_ref, kraw_ref, qrot_ref, kv_ref, att_ref, log_ref, res_ref, gates_ref, piece_ref, cols_ref,
    wq, wo, part, cbuf, ybuf, stage, csrc,
    wsem, ksend, krecv, csend, crecv, ysend, yrecv, psend, precv, tsend, trecv,
):
    f32, bf = jnp.float32, jnp.bfloat16
    z, x, y, c = coords()
    rows = res_ref.shape[0]
    experts = wr_ref.shape[0] // 4
    head = qg_ref.shape[1]
    heads = wq_ref.shape[1] // head
    half = x_ref.shape[0] // 2
    wqc = pltpu.make_async_copy(wq_ref, wq, wsem.at[0])
    woc = pltpu.make_async_copy(wo_ref, wo, wsem.at[1])
    wqc.start()
    woc.start()
    Y, C = dev(z, x, 1 - y, c), dev(z, x, y, 1 - c)
    barrier_wide()

    value = x_ref[...].astype(f32)
    first = (value * row_norm(value) * g1_ref[...]).astype(bf)
    first_ref[...] = first
    cos, sin = cos_ref[...], sin_ref[...]
    kraw = nn(first, wk_ref[...])
    kraw_ref[...] = kraw
    krot = turn(kraw * row_norm(kraw) * kg_ref[...], cos, sin).astype(bf)
    vrow = nn(first, wv_ref[...]).astype(bf)
    me = z * 2 + x
    for s in range(2):
        kv_ref[s, me] = krot[s * half : (s + 1) * half]
        kv_ref[2 + s, me] = vrow[s * half : (s + 1) * half]

    keys_out = Spread(lambda p: kv_ref.at[:, p], ksend, krecv)
    keys_out.start_z()
    keys_out.start_x()

    wqc.wait()
    qraw_ref[...] = nn(first, wq[...])
    keys_out.pass_on(1)

    def rope_head(h, carry):
        lanes = pl.ds(pl.multiple_of(h * head, head), head)
        raw = qraw_ref[:, lanes]
        rot = turn(raw * row_norm(raw) * qg_ref[...], cos_ref[...], sin_ref[...]).astype(bf)
        qrot_ref[h] = rot[:half]
        qrot_ref[heads + h] = rot[half:]
        return carry

    lax.fori_loop(0, heads // 2, rope_head, 0)
    keys_out.pass_on(2)
    lax.fori_loop(heads // 2, heads, rope_head, 0)
    keys_out.pass_on(3)
    keys_out.arrive()
    width = first.shape[1]
    per = width // 8
    own = pl.ds(pl.multiple_of((y * 2 + c) * rows, rows), rows)
    for i in range(8):
        csrc[i] = first_ref[own, i * per : (i + 1) * per]
    blocks = Columns(csrc, cols_ref, psend, precv, tsend, trecv)
    blocks.start()

    scale = 1.0 / math.sqrt(head)

    def attend(i, carry):
        s = i // heads
        h = i % heads
        span = pl.ds(pl.multiple_of(s * half, half), half)
        keys = kv_ref[s].reshape(8 * half, head)
        vals = kv_ref[2 + s].reshape(8 * half, head)
        scores = nt(qrot_ref[i], keys) * scale
        allowed = qpos_ref[span, :1] >= kpos_ref[pl.ds(s, 1), :]
        scores = jnp.where(allowed, scores, -1e9)
        top = jnp.max(scores, axis=1, keepdims=True)
        weights = jnp.exp(scores - top)
        total = jnp.sum(weights, axis=1, keepdims=True)
        probs = (weights / total).astype(bf)
        att_ref[span, pl.ds(pl.multiple_of(h * head, head), head)] = nn(probs, vals).astype(bf)
        log_ref[i] = jnp.broadcast_to(top + jnp.log(total), (half, head))
        return carry

    lax.fori_loop(0, heads, attend, 0)
    blocks.exchange()
    lax.fori_loop(heads, 2 * heads, attend, 0)
    blocks.forward()
    woc.wait()

    def at(yy, cc):
        return part.at[pl.ds(pl.multiple_of((yy * 2 + cc) * rows, rows), rows)]

    def project(yy):
        span = pl.ds(pl.multiple_of(yy * 2 * rows, 2 * rows), 2 * rows)
        part[span] = nn(att_ref[span], wo[...]).astype(bf)

    def ccopy(yy):
        return pltpu.make_async_remote_copy(
            src_ref=at(yy, 1 - c), dst_ref=cbuf.at[yy], send_sem=csend.at[yy],
            recv_sem=crecv.at[yy], device_id=C, device_id_type=MESH)

    project(1 - y)
    ccopy(1 - y).start()
    project(y)
    ccopy(y).start()
    ccopy(1 - y).wait_recv()
    stage[...] = (at(1 - y, c)[...].astype(f32) + cbuf[1 - y].astype(f32)).astype(bf)
    yc = pltpu.make_async_remote_copy(
        src_ref=stage, dst_ref=ybuf, send_sem=ysend, recv_sem=yrecv, device_id=Y, device_id_type=MESH)
    yc.start()
    ccopy(y).wait_recv()
    res = x_ref[own].astype(f32) + (at(y, c)[...].astype(f32) + cbuf[y].astype(f32))
    lane = lax.broadcasted_iota(jnp.int32, (rows, 4 * experts), 1)
    named = jnp.zeros((rows, 4 * experts), jnp.bool_)
    routes = routes_ref[...]
    for k in range(routes.shape[1]):
        named = named | (lane % experts == routes[:, k : k + 1])
    yc.wait_recv()
    res = res + ybuf[...].astype(f32)
    res_ref[...] = res
    second = (res * row_norm(res) * g2_ref[...]).astype(bf)
    piece_ref[:, :width] = second
    logits = nt(second, wr_ref[...])
    masked = jnp.where(named & (lane < 2 * experts), logits, -1e30)
    top = jnp.max(masked, axis=1, keepdims=True)
    weights = jnp.where(named & (lane < 2 * experts), jnp.exp(masked - top), 0.0)
    total = jnp.sum(jnp.where(lane < experts, weights, 0.0), axis=1, keepdims=True)
    gates = weights / total
    high = gates.astype(bf)
    low = (gates - high.astype(f32)).astype(bf)
    gates_ref[...] = jnp.where(lane < experts, gates, 0.0)
    piece_ref[:, width:] = jnp.where(lane < experts, high, low)

    yc.wait_send()
    ccopy(0).wait_send()
    ccopy(1).wait_send()
    blocks.finish()
    keys_out.finish()


def front(x, g1, wq, wk, wv, qg, kg, cos, sin, qpos, kpos, wo, g2, wr, routes, cid):
    tok, width = x.shape
    head = qg.shape[1]
    cols = wq.shape[1]
    heads = cols // head
    rows, half = tok // 4, tok // 2
    f32, bf = jnp.float32, jnp.bfloat16
    dma = pltpu.SemaphoreType.DMA
    vm, anywhere = pl.BlockSpec(memory_space=pltpu.VMEM), pl.BlockSpec(memory_space=pl.ANY)

    def out(shape, kind):
        return jax.ShapeDtypeStruct(shape, kind)

    return pl.pallas_call(
        front_kernel,
        in_specs=[vm, vm, anywhere] + [vm] * 8 + [anywhere] + [vm] * 3,
        out_specs=[vm] * 11,
        out_shape=[
            out((tok, width), bf), out((tok, cols), f32), out((tok, head), f32),
            out((2 * heads, half, head), bf), out((4, 8, half, head), bf), out((tok, cols), bf),
            out((2 * heads, half, head), f32), out((rows, width), f32), out((rows, 128), f32),
            out((rows, width + 128), bf), out((8, 4, rows, width // 8), bf),
        ],
        scratch_shapes=[
            pltpu.VMEM((width, cols), bf), pltpu.VMEM((cols, width), bf), pltpu.VMEM((tok, width), bf),
            pltpu.VMEM((2, rows, width), bf), pltpu.VMEM((rows, width), bf), pltpu.VMEM((rows, width), bf),
            pltpu.VMEM((8, rows, width // 8), bf),
            dma((2,)), dma((3, 8)), dma((8,)), dma((2,)), dma((2,)), dma, dma,
            dma((8,)), dma((8,)), dma((3,)), dma((4,)),
        ],
        compiler_params=pltpu.CompilerParams(
            collective_id=cid, has_side_effects=True, vmem_limit_bytes=52 * 2**20
        ),
        name="front",
    )(x, g1, wq, wk, wv, qg, kg, cos, sin, qpos, kpos, wo, g2, wr, routes)


def middle_kernel(
    sums_ref, res_ref, gates_ref, cot_ref, g2_ref, wr_ref, wo_ref, qrot_ref, kv_ref, log_ref,
    qraw_ref, qg_ref, cos_ref, sin_ref, qpos_ref, kpos_ref,
    layer_ref, gres_ref, gn2_ref, cols_ref, qlow_ref, dkv_ref, qgain_ref,
    wo, back, mixed, dk, dv, csrc, wsem, send, recv, psend, precv, tsend, trecv,
):
    f32, bf = jnp.float32, jnp.bfloat16
    z, x, y, c = coords()
    rows, width = res_ref.shape
    experts = wr_ref.shape[0] // 4
    head = qg_ref.shape[1]
    heads = qraw_ref.shape[1] // head
    half = qraw_ref.shape[0] // 2
    woc = pltpu.make_async_copy(wo_ref, wo, wsem)
    woc.start()
    barrier_wide()
    Y, C = dev(z, x, 1 - y, c), dev(z, x, y, 1 - c)

    def at(yy, cc):
        return back.at[pl.ds(pl.multiple_of((yy * 2 + cc) * rows, rows), rows)]

    res = res_ref[...]
    layer_ref[...] = (res + sums_ref[:, :width]).astype(bf)
    gates = gates_ref[...]
    pair = sums_ref[:, 2 * width :]
    glog = (gates * (pair - jnp.sum(gates * pair, axis=1, keepdims=True))).astype(bf)
    gsec = sums_ref[:, width : 2 * width] + nn(glog, wr_ref[...])
    rs = row_norm(res)
    unit = res * rs
    gn2_ref[...] = jnp.sum(gsec * unit, axis=0, keepdims=True)
    cg = gsec * g2_ref[...]
    gres = cot_ref[...].astype(f32) + rs * (cg - unit * jnp.mean(cg * unit, axis=1, keepdims=True))
    gres_ref[...] = gres
    mine = pl.ds(pl.multiple_of((y * 2 + c) * rows, rows), rows)
    glow = gres.astype(bf)
    back[mine] = glow

    def cp(yy, cc, to, k):
        return pltpu.make_async_remote_copy(
            src_ref=at(yy, cc), dst_ref=at(yy, cc), send_sem=send.at[k],
            recv_sem=recv.at[yy * 2 + cc], device_id=to, device_id_type=MESH)

    cp(y, c, Y, 0).start()
    cp(y, c, C, 1).start()
    per = width // 8
    for i in range(8):
        csrc[i, :, :per] = glow[:, i * per : (i + 1) * per]
        csrc[i, :, per:] = glog
    blocks = Columns(csrc, cols_ref, psend, precv, tsend, trecv)
    blocks.start()
    dk[...] = jnp.zeros_like(dk)
    dv[...] = jnp.zeros_like(dv)
    qgain_ref[...] = jnp.zeros_like(qgain_ref)
    woc.wait()

    def mix(yy):
        span = pl.ds(pl.multiple_of(yy * 2 * rows, 2 * rows), 2 * rows)
        mixed[span] = nt(back[span], wo[...]).astype(bf)

    cp(y, 1 - c, C, 1).wait_recv()
    mix(y)
    cp(1 - y, c, Y, 0).wait_recv()
    cp(1 - y, c, C, 2).start()
    cp(1 - y, 1 - c, C, 2).wait_recv()
    mix(1 - y)
    scale = 1.0 / math.sqrt(head)

    def attend(i, carry):
        s = i // heads
        h = i % heads
        span = pl.ds(pl.multiple_of(s * half, half), half)
        lanes = pl.ds(pl.multiple_of(h * head, head), head)
        keys = kv_ref[s].reshape(8 * half, head)
        vals = kv_ref[2 + s].reshape(8 * half, head)
        query = qrot_ref[i]
        grad = mixed[span, lanes]
        scores = nt(query, keys) * scale
        allowed = qpos_ref[span, :1] >= kpos_ref[pl.ds(s, 1), :]
        probs = jnp.where(allowed, jnp.exp(scores - log_ref[i][:, :1]), 0.0)
        gprobs = nt(grad, vals)
        inner = jnp.sum(probs * gprobs, axis=1, keepdims=True)
        dots = (probs * (gprobs - inner) * scale).astype(bf)
        dk[s] += tn(dots, query)
        dv[s] += tn(probs.astype(bf), grad)
        drot = nn(dots, keys)
        raw = qraw_ref[span, lanes]
        dn = turn_back(drot, cos_ref[span], sin_ref[span])
        rs = row_norm(raw)
        unit = raw * rs
        qgain_ref[...] += jnp.sum((dn * unit).reshape(half // 8, 8, head), axis=0)
        cg = dn * qg_ref[...]
        qlow_ref[span, lanes] = (rs * (cg - unit * jnp.mean(cg * unit, axis=1, keepdims=True))).astype(bf)
        return carry

    lax.fori_loop(0, heads, attend, 0)
    blocks.exchange()
    lax.fori_loop(heads, 3 * heads // 2, attend, 0)
    blocks.forward()
    lax.fori_loop(3 * heads // 2, 2 * heads, attend, 0)
    for s in range(2):
        dkv_ref[s] = dk[s].astype(bf).reshape(8, half, head)
        dkv_ref[2 + s] = dv[s].astype(bf).reshape(8, half, head)
    cp(y, c, Y, 0).wait_send()
    cp(y, c, C, 1).wait_send()
    cp(1 - y, c, C, 2).wait_send()
    blocks.finish()


def middle(sums, res, gates, cot, g2, wr, wo, qrot, kv, logs, qraw, qg, cos, sin, qpos, kpos, cid):
    rows, width = res.shape
    tok, cols = qraw.shape
    head = qg.shape[1]
    half = tok // 2
    f32, bf = jnp.float32, jnp.bfloat16
    dma = pltpu.SemaphoreType.DMA
    vm, anywhere = pl.BlockSpec(memory_space=pltpu.VMEM), pl.BlockSpec(memory_space=pl.ANY)

    def out(shape, kind):
        return jax.ShapeDtypeStruct(shape, kind)

    return pl.pallas_call(
        middle_kernel,
        in_specs=[vm] * 6 + [anywhere] + [vm] * 9,
        out_specs=[vm] * 7,
        out_shape=[
            out((rows, width), bf), out((rows, width), f32), out((1, width), f32),
            out((8, 4, rows, width // 8 + 128), bf), out((tok, cols), bf), out((4, 8, half, head), bf),
            out((8, head), f32),
        ],
        scratch_shapes=[
            pltpu.VMEM((cols, width), bf), pltpu.VMEM((tok, width), bf), pltpu.VMEM((tok, cols), bf),
            pltpu.VMEM((2, 8 * half, head), f32), pltpu.VMEM((2, 8 * half, head), f32),
            pltpu.VMEM((8, rows, width // 8 + 128), bf),
            dma, dma((3,)), dma((4,)), dma((8,)), dma((8,)), dma((3,)), dma((4,)),
        ],
        compiler_params=pltpu.CompilerParams(
            collective_id=cid, has_side_effects=True, vmem_limit_bytes=52 * 2**20
        ),
        name="middle",
    )(sums, res, gates, cot, g2, wr, wo, qrot, kv, logs, qraw, qg, cos, sin, qpos, kpos)


def tail_kernel(
    dkv_ref, qlow_ref, kraw_ref, kg_ref, cos_ref, sin_ref, wq_ref, wk_ref, wv_ref, x_ref, g1_ref,
    gres_ref, layer_ref, vec_ref,
    gin_ref, lout_ref, kvall_ref, qall_ref, vo_ref,
    wq, xbuf, zbuf, zst, part, cbuf, ybuf, stage, vbuf, vpart, tbuf, gin, kvlow,
    wsem, xsend, xrecv, zsend, zrecv, csend, crecv, ysend, yrecv, send, recv, vsend, vrecv, tsend, trecv,
    lsem, qsend, qrecv, ksend, krecv,
):
    f32, bf = jnp.float32, jnp.bfloat16
    z, x, y, c = coords()
    ctx, tp = lax.axis_index("ctx"), lax.axis_index("tp")
    rows, width = gres_ref.shape
    half, head = dkv_ref.shape[2:]
    wqc = pltpu.make_async_copy(wq_ref, wq, wsem.at[0])
    wqc.start()
    X, Y, C, D = dev(z, 1 - x, y, c), dev(z, x, 1 - y, c), dev(z, x, y, 1 - c), dev(z, x, 1 - y, 1 - c)
    up, down = dev(z + 1, x, y, c), dev(z - 1, x, y, c)
    barrier_wide()

    def xcopy(zz):
        return pltpu.make_async_remote_copy(
            src_ref=dkv_ref.at[:, zz * 2 + 1 - x], dst_ref=xbuf.at[zz], send_sem=xsend.at[zz],
            recv_sem=xrecv.at[zz], device_id=X, device_id_type=MESH)

    def zcopy(zz, to, slot):
        return pltpu.make_async_remote_copy(
            src_ref=zst.at[zz], dst_ref=zbuf.at[slot], send_sem=zsend.at[zz],
            recv_sem=zrecv.at[slot], device_id=to, device_id_type=MESH)

    tok = qlow_ref.shape[0]
    queries = Spread(
        lambda p: qall_ref.at[pl.ds(pl.multiple_of(p * tok, tok), tok)], qsend, qrecv, qlow_ref)
    keys = Spread(
        lambda p: kvall_ref.at[pl.ds(pl.multiple_of(p * tok, tok), tok)], ksend, krecv, kvlow)
    mine = [
        pltpu.make_async_copy(s.first, s.place(s.me), lsem.at[n]) for n, s in enumerate((queries, keys))
    ]
    for k in range(4):
        xcopy(far_z(z, k)).start()
    queries.start_x()
    mine[0].start()

    def sum_z(k):
        zz = far_z(z, k)
        xcopy(zz).wait_recv()
        total = dkv_ref[:, zz * 2 + x].astype(f32) + xbuf[zz].astype(f32)
        zst[zz] = total.astype(bf)

        @pl.when((zz > z) & (z > 0))
        def _():
            zcopy(zz, up, zz).wait_recv()
            zst[zz] = (zst[zz].astype(f32) + zbuf[zz].astype(f32)).astype(bf)

        @pl.when((zz < z) & (z < 3))
        def _():
            zcopy(zz, down, zz).wait_recv()
            zst[zz] = (zst[zz].astype(f32) + zbuf[zz].astype(f32)).astype(bf)

        @pl.when(zz > z)
        def _():
            zcopy(zz, up, zz).start()

        @pl.when((zz < z) & (zz != z - 1))
        def _():
            zcopy(zz, down, zz).start()

        @pl.when(zz == z - 1)
        def _():
            zcopy(zz, down, 4).start()

    def at(yy, cc):
        return part.at[pl.ds(pl.multiple_of((yy * 2 + cc) * rows, rows), rows)]

    def two(yy):
        return pl.ds(pl.multiple_of(yy * 2 * rows, 2 * rows), 2 * rows)

    sum_z(0)
    wqc.wait()
    first_a = nt(qlow_ref[two(1 - y)], wq[...])
    sum_z(1)
    first_b = nt(qlow_ref[two(y)], wq[...])
    sum_z(2)
    queries.start_z()
    xcopy(z).wait_recv()
    dkv = dkv_ref[:, ctx].astype(f32) + xbuf[z].astype(f32)

    @pl.when(z > 0)
    def _():
        zcopy(z, up, z).wait_recv()

    @pl.when(z == 0)
    def _():
        zbuf[0] = jnp.zeros_like(zbuf[0])

    @pl.when(z < 3)
    def _():
        zcopy(z, down, 4).wait_recv()

    @pl.when(z == 3)
    def _():
        zbuf[4] = jnp.zeros_like(zbuf[4])

    dkv = dkv + zbuf[z].astype(f32) + zbuf[4].astype(f32)
    dkey = jnp.concatenate([dkv[0], dkv[1]], axis=0)
    vlow = jnp.concatenate([dkv[2], dkv[3]], axis=0).astype(bf)
    raw = kraw_ref[...]
    dn = turn_back(dkey, cos_ref[...], sin_ref[...])
    rs = row_norm(raw)
    unit = raw * rs
    kgain = jnp.sum(dn * unit, axis=0, keepdims=True)
    cg = dn * kg_ref[...]
    klow = (rs * (cg - unit * jnp.mean(cg * unit, axis=1, keepdims=True))).astype(bf)
    kvlow[:, :head] = klow
    kvlow[:, head:] = vlow
    keys.start_z()
    keys.start_x()
    mine[1].start()

    def ccopy(yy):
        return pltpu.make_async_remote_copy(
            src_ref=at(yy, 1 - c), dst_ref=cbuf.at[yy], send_sem=csend.at[yy],
            recv_sem=crecv.at[yy], device_id=C, device_id_type=MESH)

    def project(yy, first):
        keys, vals = kvlow[two(yy), :head], kvlow[two(yy), head:]
        part[two(yy)] = (first + nt(keys, wk_ref[...]) + nt(vals, wv_ref[...])).astype(bf)
        ccopy(yy).start()

    project(1 - y, first_a)
    project(y, first_b)
    ccopy(1 - y).wait_recv()
    stage[...] = (at(1 - y, c)[...].astype(f32) + cbuf[1 - y].astype(f32)).astype(bf)
    yc = pltpu.make_async_remote_copy(
        src_ref=stage, dst_ref=ybuf, send_sem=ysend, recv_sem=yrecv, device_id=Y, device_id_type=MESH)
    yc.start()
    queries.pass_on(1)
    ccopy(y).wait_recv()
    gfirst = at(y, c)[...].astype(f32) + cbuf[y].astype(f32)
    own = pl.ds(pl.multiple_of((y * 2 + c) * rows, rows), rows)
    value = x_ref[own].astype(f32)
    rs = row_norm(value)
    unit = value * rs
    yc.wait_recv()
    gfirst = gfirst + ybuf[...].astype(f32)
    gn1 = jnp.sum(gfirst * unit, axis=0, keepdims=True)
    cg = gfirst * g1_ref[...]
    gin[...] = (gres_ref[...] + rs * (cg - unit * jnp.mean(cg * unit, axis=1, keepdims=True))).astype(bf)

    keys.pass_on(1)
    pairs = [(gin, gin_ref), (layer_ref, lout_ref)]

    def place(ref, yy, cc):
        return ref.at[pl.ds(pl.multiple_of((yy * 2 + cc) * rows, rows), rows)]

    def cp(n, src, yy, cc, to, k):
        return pltpu.make_async_remote_copy(
            src_ref=src, dst_ref=place(pairs[n][1], yy, cc), send_sem=send.at[n, k],
            recv_sem=recv.at[n, yy * 2 + cc], device_id=to, device_id_type=MESH)

    for n, (src, dst) in enumerate(pairs):
        cp(n, src, y, c, Y, 0).start()
        cp(n, src, y, c, C, 1).start()
        dst[own] = src[...]
    per = width // 8
    for i in range(8):
        for j in range(per // 128):
            lo = i * per + j * 128
            vpart[i, j : j + 1] = gn1[:, lo : lo + 128]
        vpart[i, per // 128 : 8] = vec_ref[i, per // 128 : 8]
        vpart[i, 7:8] = jnp.broadcast_to(kgain, (1, head))

    def vcopy(i):
        to = (ctx + i) % 8
        return pltpu.make_async_remote_copy(
            src_ref=vpart.at[to], dst_ref=vbuf.at[i], send_sem=vsend.at[i], recv_sem=vrecv.at[i],
            device_id=(to, tp), device_id_type=MESH)

    for i in range(1, 8):
        vcopy(i).start()
    queries.pass_on(2)
    keys.pass_on(2)
    total = vpart[ctx]
    for i in range(1, 8):
        vcopy(i).wait_recv()
        total = total + vbuf[i]
    tbuf[3] = total

    def tcopy(k, to):
        return pltpu.make_async_remote_copy(
            src_ref=tbuf.at[3], dst_ref=tbuf.at[k], send_sem=tsend.at[k], recv_sem=trecv.at[k],
            device_id=to, device_id_type=MESH)

    sums = [tcopy(k, to) for k, to in enumerate((Y, C, D))]
    for t in sums:
        t.start()
    for n, (src, dst) in enumerate(pairs):
        cp(n, src, 1 - y, c, Y, 0).wait_recv()
        cp(n, place(dst, 1 - y, c), 1 - y, c, C, 2).start()
    keys.pass_on(3)
    queries.pass_on(3)
    for t in sums:
        t.wait_recv()
    vo_ref[...] = (tbuf[3] + tbuf[0]) + (tbuf[1] + tbuf[2])
    for n, (src, dst) in enumerate(pairs):
        cp(n, src, y, 1 - c, C, 1).wait_recv()
        cp(n, src, 1 - y, 1 - c, C, 2).wait_recv()
        cp(n, src, y, c, Y, 0).wait_send()
        cp(n, src, y, c, C, 1).wait_send()
        cp(n, place(dst, 1 - y, c), 1 - y, c, C, 2).wait_send()
    for t in sums:
        t.wait_send()
    for i in range(1, 8):
        vcopy(i).wait_send()
    for s in (keys, queries):
        s.arrive()
        s.finish()
    for cp_own in mine:
        cp_own.wait()
    yc.wait_send()
    ccopy(0).wait_send()
    ccopy(1).wait_send()
    for zz in range(4):
        xcopy(zz).wait_send()

        @pl.when(zz != z)
        def _():
            zcopy(zz, up, zz).wait_send()


def tail(dkv, qlow, kraw, kg, cos, sin, wq, wk, wv, x, g1, gres, layer, vec, cid):
    tok, width = x.shape
    rows = gres.shape[0]
    half, head = dkv.shape[2:]
    f32, bf = jnp.float32, jnp.bfloat16
    dma = pltpu.SemaphoreType.DMA
    vm, anywhere = pl.BlockSpec(memory_space=pltpu.VMEM), pl.BlockSpec(memory_space=pl.ANY)

    def out(shape, kind):
        return jax.ShapeDtypeStruct(shape, kind)

    def mem(*shape, kind=bf):
        return pltpu.VMEM(shape, kind)

    return pl.pallas_call(
        tail_kernel,
        in_specs=[vm] * 6 + [anywhere] + [vm] * 7,
        out_specs=[vm] * 2 + [anywhere] * 2 + [vm],
        out_shape=[
            out((tok, width), bf), out((tok, width), bf), out((8 * tok, 2 * head), bf),
            out((8 * tok, qlow.shape[1]), bf), out((8, 128), f32),
        ],
        scratch_shapes=[
            mem(*wq.shape), mem(4, 4, half, head), mem(5, 4, half, head), mem(4, 4, half, head),
            mem(tok, width), mem(2, rows, width), mem(rows, width), mem(rows, width),
            mem(8, 8, 128, kind=f32), mem(8, 8, 128, kind=f32), mem(4, 8, 128, kind=f32), mem(rows, width),
            mem(tok, 2 * head),
            dma((1,)), dma((4,)), dma((4,)), dma((4,)), dma((5,)), dma((2,)), dma((2,)), dma, dma,
            dma((2, 3)), dma((2, 4)), dma((8,)), dma((8,)), dma((3,)), dma((3,)),
            dma((2,)), dma((3, 8)), dma((8,)), dma((3, 8)), dma((8,)),
        ],
        compiler_params=pltpu.CompilerParams(
            collective_id=cid, has_side_effects=True, vmem_limit_bytes=52 * 2**20
        ),
        name="tail",
    )(dkv, qlow, kraw, kg, cos, sin, wq, wk, wv, x, g1, gres, layer, vec)


EPSILON = 1e-06
ROPE_BASE = 1000000.0
MASKED_SCORE = -1000000000.0
BF = jnp.bfloat16
F32 = jnp.float32


def dotf(a, b, dims):
    return lax.dot_general(a, b, (dims, ((), ())), preferred_element_type=F32)


def nt(a, b):
    return lax.dot_general(a, b, (((1,), (1,)), ((), ())), preferred_element_type=jnp.float32)


def nn(a, b):
    return lax.dot_general(a, b, (((1,), (0,)), ((), ())), preferred_element_type=jnp.float32)


def tn(a, b):
    return lax.dot_general(a, b, (((0,), (0,)), ((), ())), preferred_element_type=jnp.float32)


def expert_kernel(x_ref, cot_ref, wg_ref, wu_ref, wd_ref, s_ref, t_ref, part_ref, gl_ref, ul_ref, hs_ref):
    bf = jnp.bfloat16
    width = cot_ref.shape[1]
    x = x_ref[:, :width]
    spread = nn(x_ref[:, width:], s_ref[...])
    gate = nt(x, wg_ref[...])
    up = nt(x, wu_ref[...])
    back = nt(cot_ref[...], wd_ref[...])
    sig = 1.0 / (1.0 + jnp.exp(-gate))
    silu = gate * sig
    hidden = silu * up
    hs = (hidden * spread).astype(bf)
    hs_ref[...] = hs.T
    part_ref[:, :width] = nn(hs, wd_ref[...]).astype(bf)
    prod = hidden * back
    high = prod.astype(bf)
    low = (prod - high.astype(jnp.float32)).astype(bf)
    part_ref[:, 2 * width :] = (nn(high, t_ref[...]) + nn(low, t_ref[...])).astype(bf)
    grad = back * spread
    gl = (grad * up * sig * (1.0 + gate * (1.0 - sig))).astype(bf)
    ul = (grad * silu).astype(bf)
    gl_ref[...] = gl.T
    ul_ref[...] = ul.T
    part_ref[:, width : 2 * width] = (nn(gl, wg_ref[...]) + nn(ul, wu_ref[...])).astype(bf)


def expert_blocks(x_all, cot_all, gate_mat, up_mat, down_mat, spread_mat, pick_mat, block=256):
    n, width = cot_all.shape
    wide = x_all.shape[1]
    hid = gate_mat.shape[0]
    bf = jnp.bfloat16

    def rows(w):
        return pl.BlockSpec((block, w), lambda i: (i, 0))

    def whole(v):
        return pl.BlockSpec(v.shape, lambda i: (0, 0), pipeline_mode=pl.Buffered(1))

    return pl.pallas_call(
        expert_kernel,
        grid=(n // block,),
        in_specs=[rows(wide), rows(width)]
        + [whole(v) for v in (gate_mat, up_mat, down_mat, spread_mat, pick_mat)],
        out_specs=[rows(width + wide)] + [pl.BlockSpec((hid, block), lambda i: (0, i))] * 3,
        out_shape=[jax.ShapeDtypeStruct((n, width + wide), bf)]
        + [jax.ShapeDtypeStruct((hid, n), bf)] * 3,
        compiler_params=pltpu.CompilerParams(
            dimension_semantics=("arbitrary",), vmem_limit_bytes=56 * 2**20
        ),
        cost_estimate=pl.CostEstimate(
            flops=12 * n * width * hid, bytes_accessed=10 * n * width, transcendentals=n * hid
        ),
        name="experts",
    )(x_all, cot_all, gate_mat, up_mat, down_mat, spread_mat, pick_mat)


def expert_grad_kernel(x_ref, cot_ref, gl_ref, ul_ref, hs_ref, gg_ref, gu_ref, gd_ref):
    first = pl.program_id(1) == 0

    def put(ref, low, full):
        value = nn(low[...], full[...])

        @pl.when(first)
        def _():
            ref[...] = value

        @pl.when(jnp.logical_not(first))
        def _():
            ref[...] += value

    put(gg_ref, gl_ref, x_ref)
    put(gu_ref, ul_ref, x_ref)
    put(gd_ref, hs_ref, cot_ref)


def expert_grads(x_all, cot_all, gl, ul, hs, block=256):
    n, width = cot_all.shape
    hid = gl.shape[0]
    span = min(n, 2048)
    cols = pl.BlockSpec((span, block), lambda i, j: (j, i))
    rows = pl.BlockSpec((hid, span), lambda i, j: (0, j))
    out = pl.BlockSpec((hid, block), lambda i, j: (0, i))
    return pl.pallas_call(
        expert_grad_kernel,
        grid=(width // block, n // span),
        in_specs=[cols, cols, rows, rows, rows],
        out_specs=[out] * 3,
        out_shape=[jax.ShapeDtypeStruct((hid, width), jnp.float32)] * 3,
        compiler_params=pltpu.CompilerParams(
            dimension_semantics=("arbitrary", "arbitrary"), vmem_limit_bytes=56 * 2**20
        ),
        cost_estimate=pl.CostEstimate(
            flops=6 * n * width * hid, bytes_accessed=10 * n * width, transcendentals=0
        ),
        name="expert_grads",
    )(x_all, cot_all, gl, ul, hs)


class Links:
    def ag_all(self, piece):
        return lax.all_gather(piece, ("ctx", "tp"), axis=0, tiled=True)

    def rs_all(self, part):
        return lax.psum_scatter(part, ("ctx", "tp"), scatter_dimension=0, tiled=True).astype(F32)

    def ag_ctx(self, piece):
        return lax.all_gather(piece, "ctx", axis=0, tiled=True)

    def rs_ctx(self, part):
        return lax.psum_scatter(part, "ctx", scatter_dimension=0, tiled=True).astype(F32)

    def rs_tp(self, part):
        return lax.psum_scatter(part, "tp", scatter_dimension=0, tiled=True).astype(F32)

    def ag_tp(self, piece):
        return lax.all_gather(piece, "tp", axis=0, tiled=True)

    def finish(self, a, b, vectors):
        total = lax.psum_scatter(vectors, "ctx", scatter_dimension=0, tiled=True)
        gathered = (lax.all_gather(v, "tp", axis=0, tiled=True) for v in (a, b))
        return (*gathered, lax.psum(total, "tp"))


def rms_norm(values, gain_vec):
    factor = lax.rsqrt(jnp.mean(values * values, axis=-1, keepdims=True) + EPSILON)
    return values * factor * gain_vec


def rotate(values, rotary_angles):
    half_size = values.shape[-1] // 2
    first_half = values[..., :half_size]
    second_half = values[..., half_size:]
    cosine = jnp.cos(rotary_angles)
    sine_part = jnp.sin(rotary_angles)
    return jnp.concatenate(
        [
            first_half * cosine - second_half * sine_part,
            second_half * cosine + first_half * sine_part,
        ],
        axis=-1,
    )


def angles_of(token_positions, head_width):
    freq_steps = jnp.arange(head_width // 2).astype(F32) * (2.0 / head_width)
    frequency = jnp.exp(-math.log(ROPE_BASE) * freq_steps)
    return token_positions.astype(F32)[..., None] * frequency


def positions_of(block_order, dev_count, block_len):
    first_block = jnp.transpose(block_order)
    block_pair = jnp.stack([first_block, 2 * dev_count - 1 - first_block], axis=-1)
    spread = block_pair[..., None] * block_len + jnp.arange(block_len, dtype=jnp.int32)
    return spread.reshape(dev_count, block_order.shape[0], 2 * block_len)


def head_route_path(raw_heads, gain_vec, rotary_angles, head_count):
    shaped = raw_heads.reshape(raw_heads.shape[0], head_count, -1)
    return rotate(rms_norm(shaped, gain_vec), rotary_angles[:, None, :])


def attend_forward(seq_item):
    query_matrix, every_key_row, every_value_row, query_pos, key_pos = seq_item
    score_scale = 1.0 / math.sqrt(query_matrix.shape[-1])
    unscaled_scores = jnp.einsum(
        "upnj,apj->upna", query_matrix, every_key_row, preferred_element_type=F32
    )
    allowed = query_pos[:, None, None, None] >= key_pos[None, None, None, :]
    scores = jnp.where(allowed, unscaled_scores * score_scale, MASKED_SCORE)
    row_top = jnp.max(scores, axis=-1, keepdims=True)
    exp_scores = jnp.exp(scores - row_top)
    totals = jnp.sum(exp_scores, axis=-1, keepdims=True)
    lower_attention_probs = (exp_scores / totals).astype(BF)
    attended_mix = jnp.einsum(
        "jzfq,qzx->jzfx", lower_attention_probs, every_value_row, preferred_element_type=F32
    )
    return (attended_mix, (row_top + jnp.log(totals))[..., 0])


def attend_backward(seq_item):
    (
        query_matrix,
        every_key_row,
        every_value_row,
        query_pos,
        key_pos,
        grad_attended_mix,
        log_total,
    ) = seq_item
    score_scale = 1.0 / math.sqrt(query_matrix.shape[-1])
    unscaled_scores = jnp.einsum(
        "upnj,apj->upna", query_matrix, every_key_row, preferred_element_type=F32
    )
    allowed = query_pos[:, None, None, None] >= key_pos[None, None, None, :]
    scores = jnp.where(allowed, unscaled_scores * score_scale, MASKED_SCORE)
    attention_probs = jnp.exp(scores - log_total[..., None])
    grad_probs = jnp.einsum(
        "upnj,apj->upna", grad_attended_mix, every_value_row, preferred_element_type=F32
    )
    row_inner = jnp.sum(attention_probs * grad_probs, axis=-1, keepdims=True)
    grad_score_dots = (attention_probs * (grad_probs - row_inner) * score_scale).astype(BF)
    grad_queries = jnp.einsum(
        "jzfq,qzx->jzfx", grad_score_dots, every_key_row, preferred_element_type=F32
    )
    grad_key_rows = jnp.einsum(
        "axfv,axfz->vxz", grad_score_dots, query_matrix, preferred_element_type=F32
    )
    grad_values = jnp.einsum(
        "axfv,axfz->vxz", attention_probs.astype(BF), grad_attended_mix, preferred_element_type=F32
    )
    return (grad_queries, grad_key_rows, grad_values)


def gates_of(logits, routes):
    experts = logits.shape[1]
    named = jnp.any(routes[:, :, None] == jnp.arange(experts, dtype=jnp.int32), axis=1)
    masked = jnp.where(named, logits, -jnp.inf)
    top = jnp.max(masked, axis=1, keepdims=True)
    weights = jnp.where(named, jnp.exp(masked - top), 0.0)
    return weights / jnp.sum(weights, axis=1, keepdims=True)


def plain_shards(
    tokens_in,
    block_order,
    routes,
    norm1_gain,
    w_query,
    key_weight,
    value_weight,
    query_gain,
    key_gain,
    w_out,
    norm2_gain,
    w_router,
    w_gate,
    w_up,
    w_down,
    cotangent,
):
    tok_count, model_width = tokens_in.shape
    head_size = query_gain.shape[0]
    local_heads = w_query.shape[1] // head_size
    local_kv = key_weight.shape[1] // head_size
    query_group_width = local_heads // local_kv
    seq_count = block_order.shape[0]
    devices, tp_size = lax.axis_size("ctx"), lax.axis_size("tp")
    links = Links()
    me, tp_me = lax.axis_index("ctx"), lax.axis_index("tp")
    rows = tok_count // tp_size
    block_len = tok_count // (2 * seq_count)
    experts = w_router.shape[1]
    own_experts, _, units = w_gate.shape
    hid = own_experts * units
    all_tok = devices * tok_count

    def own_rows(v):
        return lax.dynamic_slice_in_dim(v, tp_me * rows, rows, axis=0)

    cot_own = own_rows(cotangent)
    cot_all = lax.all_gather(cot_own, ("ctx", "tp"), axis=0, tiled=True)

    token_positions = positions_of(block_order, devices, block_len)
    query_pos = lax.dynamic_index_in_dim(token_positions, me, 0, keepdims=False)
    key_pos = jnp.transpose(token_positions, (1, 0, 2)).reshape(seq_count, devices * 2 * block_len)
    rotary_angles = angles_of(query_pos.reshape(-1), head_size)
    inputs = tokens_in.astype(F32)
    first_in = rms_norm(inputs, norm1_gain).astype(BF)
    query_raw = jnp.dot(first_in, w_query, preferred_element_type=F32)
    unrotated_key = jnp.dot(first_in, key_weight, preferred_element_type=F32)
    value_rows = jnp.dot(first_in, value_weight, preferred_element_type=F32).astype(BF)

    def rope_heads(raw_query, raw_key, gain_query, key_norm_gain):
        return (
            head_route_path(raw_query, gain_query, rotary_angles, local_heads),
            head_route_path(raw_key, key_norm_gain, rotary_angles, local_kv),
        )

    (query_rot, key_rot), rope_back = jax.vjp(
        rope_heads, query_raw, unrotated_key, query_gain, key_gain
    )
    query_rows = query_rot.astype(BF).reshape(
        seq_count, 2 * block_len, local_kv, query_group_width, head_size
    )
    kv_width = local_kv * head_size
    kv_own = jnp.concatenate([key_rot.astype(BF).reshape(tok_count, kv_width), value_rows], axis=1)
    kv_all = links.ag_ctx(kv_own)
    kv_seq = kv_all.reshape(devices, seq_count, 2 * block_len, 2, local_kv, head_size)
    kv_seq = kv_seq.transpose(3, 1, 0, 2, 4, 5).reshape(
        2, seq_count, devices * 2 * block_len, local_kv, head_size
    )
    key_full, value_full = kv_seq[0], kv_seq[1]
    attended_mix, log_total = lax.map(
        attend_forward, (query_rows, key_full, value_full, query_pos, key_pos)
    )
    attended = attended_mix.reshape(tok_count, local_heads * head_size).astype(BF)
    attn_part = jnp.dot(attended, w_out, preferred_element_type=F32).astype(BF)
    residual = own_rows(inputs) + links.rs_tp(attn_part)
    second_normed, second_back = jax.vjp(rms_norm, residual, norm2_gain)
    second_in = second_normed.astype(BF)
    extra = -(-2 * experts // 128) * 128
    gates = gates_of(jnp.dot(second_in, w_router, preferred_element_type=F32), own_rows(routes))
    gates_high = gates.astype(BF)
    gates_low = (gates - gates_high.astype(F32)).astype(BF)
    pad = jnp.zeros((rows, extra - 2 * experts), BF)
    second_all = links.ag_all(
        jnp.concatenate([second_in, gates_high, gates_low, pad], axis=1)
    )
    column = jnp.arange(extra, dtype=jnp.int32)[:, None]
    named = me * own_experts + jnp.arange(hid, dtype=jnp.int32)[None, :] // units
    pick = (column == named).astype(BF)
    spread = pick + (column == named + experts).astype(BF)
    gate_mat = w_gate.transpose(0, 2, 1).reshape(hid, model_width)
    up_mat = w_up.transpose(0, 2, 1).reshape(hid, model_width)
    down_mat = w_down.reshape(hid, model_width)
    part, gate_low, up_low, hidden_low = expert_blocks(
        second_all, cot_all, gate_mat, up_mat, down_mat, spread, pick.T
    )
    sums_own = links.rs_all(part)
    out_own = sums_own[:, :model_width]
    entry_own = sums_own[:, model_width:]
    gate_total = entry_own[:, model_width : model_width + experts]
    grad_logits = (
        gates * (gate_total - jnp.sum(gates * gate_total, axis=1, keepdims=True))
    ).astype(BF)
    grad_second = entry_own[:, :model_width] + dotf(grad_logits, w_router, ((1,), (1,)))
    grad_resid_norm, grad_norm2 = second_back(grad_second)
    grad_residual = cot_own.astype(F32) + grad_resid_norm
    pad = jnp.zeros((rows, -experts % 128), BF)
    back_all = links.ag_tp(
        jnp.concatenate([grad_residual.astype(BF), grad_logits, pad], axis=1)
    )
    grad_attn_low = back_all[:, :model_width]
    second_own = lax.dynamic_slice(second_all, (me * tok_count, 0), (tok_count, model_width))
    router_part = dotf(second_own, back_all[:, model_width:], ((0,), (0,)))
    grad_out = dotf(attended, grad_attn_low, ((0,), (0,)))
    grad_mixed = dotf(grad_attn_low, w_out, ((1,), (1,))).astype(BF)
    grad_mixed = grad_mixed.reshape(
        seq_count, 2 * block_len, local_kv, query_group_width, head_size
    )
    grad_query_seq, grad_key_seq, grad_value_seq = lax.map(
        attend_backward,
        (query_rows, key_full, value_full, query_pos, key_pos, grad_mixed, log_total),
    )
    grad_kv = jnp.stack([grad_key_seq, grad_value_seq]).astype(BF)
    grad_kv = grad_kv.reshape(2, seq_count, devices, 2 * block_len, kv_width)
    grad_kv = grad_kv.transpose(2, 1, 3, 0, 4).reshape(all_tok, 2 * kv_width)
    grad_kv_own = links.rs_ctx(grad_kv)
    grad_query_rot = grad_query_seq.reshape(tok_count, local_heads, head_size)
    grad_key_rot = grad_kv_own[:, :kv_width].reshape(tok_count, local_kv, head_size)
    grad_query_raw, grad_key_raw, grad_qgain, grad_kgain = rope_back(
        (grad_query_rot, grad_key_rot)
    )
    query_low = grad_query_raw.astype(BF)
    key_low = grad_key_raw.astype(BF)
    value_low = grad_kv_own[:, kv_width:].astype(BF)
    first_part = dotf(query_low, w_query, ((1,), (1,)))
    first_part = first_part + dotf(key_low, key_weight, ((1,), (1,)))
    first_part = first_part + dotf(value_low, value_weight, ((1,), (1,)))
    grad_first = links.rs_tp(first_part.astype(BF))
    grad_first, gate_low = lax.optimization_barrier((grad_first, gate_low))
    grads = expert_grads(second_all, cot_all, gate_low, up_low, hidden_low)
    grad_gate, grad_up = (
        v.reshape(own_experts, units, model_width).transpose(0, 2, 1) for v in grads[:2]
    )
    grad_down = grads[2].reshape(own_experts, units, model_width)
    _, first_back = jax.vjp(rms_norm, own_rows(inputs), norm1_gain)
    grad_input_norm, grad_norm1 = first_back(grad_first)
    def over_ctx(v, dim):
        return lax.psum_scatter(v.astype(BF), "ctx", scatter_dimension=dim, tiled=True).astype(F32)

    grad_query = over_ctx(dotf(first_in, query_low, ((0,), (0,))), 0)
    kv_part = dotf(first_in, jnp.concatenate([key_low, value_low], axis=1), ((0,), (0,)))
    small = links.rs_ctx(jnp.concatenate([kv_part, router_part], axis=1).astype(BF))
    grad_key = small[:, :kv_width]
    grad_value = small[:, kv_width : 2 * kv_width]
    grad_router = small[:, 2 * kv_width : 2 * kv_width + experts]
    grad_out = over_ctx(grad_out, 1)
    vectors = [
        v.reshape(devices, -1) for v in (grad_norm1, grad_norm2, grad_qgain, grad_kgain)
    ]
    sizes = [v.shape[1] for v in vectors]
    pad = jnp.zeros((devices, -sum(sizes) % 1024), F32)
    packed = jnp.concatenate([*vectors, pad], axis=1).reshape(-1, 128)
    grad_input, layer_out, total = links.finish(
        (grad_residual + grad_input_norm).astype(BF), (residual + out_own).astype(BF), packed
    )
    total = total.reshape(-1)

    def piece_of(n):
        start = sum(sizes[:n])
        return total[start : start + sizes[n]]

    return (
        layer_out,
        grad_input,
        piece_of(0),
        grad_query,
        grad_key,
        grad_value,
        piece_of(2),
        piece_of(3),
        grad_out,
        piece_of(1),
        grad_router,
        grad_gate,
        grad_up,
        grad_down,
    )


def fast_shards(
    tokens_in,
    block_order,
    routes,
    norm1_gain,
    w_query,
    key_weight,
    value_weight,
    query_gain,
    key_gain,
    w_out,
    norm2_gain,
    w_router,
    w_gate,
    w_up,
    w_down,
    cotangent,
):
    tok_count, model_width = tokens_in.shape
    head_size = query_gain.shape[0]
    seq_count = block_order.shape[0]
    devices, tp_size = lax.axis_size("ctx"), lax.axis_size("tp")
    me, tp_me = lax.axis_index("ctx"), lax.axis_index("tp")
    rows = tok_count // tp_size
    block_len = tok_count // (2 * seq_count)
    experts = w_router.shape[1]
    own_experts, _, units = w_gate.shape
    hid = own_experts * units

    def own_rows(v):
        return lax.dynamic_slice_in_dim(v, tp_me * rows, rows, axis=0)

    def row(v):
        return v.reshape(1, -1)

    cot_own = own_rows(cotangent)
    cot_all = lax.all_gather(cot_own, ("ctx", "tp"), axis=0, tiled=True)

    token_positions = positions_of(block_order, devices, block_len)
    query_pos = lax.dynamic_index_in_dim(token_positions, me, 0, keepdims=False).reshape(-1)
    key_pos = jnp.transpose(token_positions, (1, 0, 2)).reshape(seq_count, -1).astype(F32)
    angles = angles_of(query_pos, head_size)
    cos = jnp.concatenate([jnp.cos(angles)] * 2, axis=1)
    sin = jnp.concatenate([-jnp.sin(angles), jnp.sin(angles)], axis=1)
    query_pos = jnp.broadcast_to(query_pos.astype(F32)[:, None], (tok_count, head_size))
    router_rows = w_router.T
    router_rows = jnp.concatenate([router_rows, router_rows, jnp.zeros((2 * experts, model_width), BF)])
    _, query_raw, key_raw, query_rot, kv_all, attended, logs, residual, gates, piece, first_cols = front(
        tokens_in, row(norm1_gain), w_query, key_weight, value_weight, row(query_gain),
        row(key_gain), cos, sin, query_pos, key_pos, w_out, row(norm2_gain), router_rows,
        own_rows(routes), 1,
    )
    second_all = ag32(piece, 3)
    attended_all = lax.all_gather(attended, "ctx", axis=0, tiled=True)
    all_tok = devices * tok_count
    first_cols = first_cols.reshape(all_tok, -1)

    extra = 4 * experts
    column = jnp.arange(extra, dtype=jnp.int32)[:, None]
    named = me * own_experts + jnp.arange(hid, dtype=jnp.int32)[None, :] // units
    pick = (column == named).astype(BF)
    spread = pick + (column == named + experts).astype(BF)
    gate_mat = w_gate.transpose(0, 2, 1).reshape(hid, model_width)
    up_mat = w_up.transpose(0, 2, 1).reshape(hid, model_width)
    down_mat = w_down.reshape(hid, model_width)
    part, gate_low, up_low, hidden_low = expert_blocks(
        second_all, cot_all, gate_mat, up_mat, down_mat, spread, pick.T
    )
    sums_own = reduce_all(part, 6)
    layer_piece, grad_residual, grad_norm2, back_cols, query_low, grad_kv, qgain_part = middle(
        sums_own, residual, gates, cot_own, row(norm2_gain), router_rows, w_out, query_rot, kv_all,
        logs, query_raw, row(query_gain), cos, sin, query_pos, key_pos, 7,
    )

    back_cols = back_cols.reshape(all_tok, -1)
    width_part = model_width // devices
    grad_out = dotf(attended_all, back_cols[:, :width_part], ((0,), (0,)))
    second_cols = lax.dynamic_slice_in_dim(second_all, me * width_part, width_part, axis=1)
    grad_router = dotf(second_cols, back_cols[:, width_part : width_part + experts], ((0,), (0,)))
    per = model_width // devices // 128
    vectors = jnp.concatenate(
        [
            jnp.zeros((devices, per, 128), F32),
            grad_norm2.reshape(devices, per, 128),
            jnp.broadcast_to(jnp.sum(qgain_part, axis=0), (devices, 1, 128)),
            jnp.zeros((devices, 7 - 2 * per, 128), F32),
        ],
        axis=1,
    )
    grad_input, layer_out, kv_low_all, query_low_all, total = tail(
        grad_kv, query_low, key_raw, row(key_gain), cos, sin, w_query, key_weight, value_weight,
        tokens_in, row(norm1_gain), grad_residual, layer_piece, vectors, 8,
    )
    grad_query = dotf(first_cols, query_low_all, ((0,), (0,)))
    kv_grads = dotf(first_cols, kv_low_all, ((0,), (0,)))
    grad_key = kv_grads[:, :head_size]
    grad_value = kv_grads[:, head_size:]
    grads = expert_grads(second_all, cot_all, gate_low, up_low, hidden_low)
    grad_gate, grad_up = (
        v.reshape(own_experts, units, model_width).transpose(0, 2, 1) for v in grads[:2]
    )
    grad_down = grads[2].reshape(own_experts, units, model_width)
    share = head_size // devices

    def gain_of(n):
        return lax.dynamic_slice_in_dim(total[n], me * share, share, axis=0)

    return (
        layer_out,
        grad_input,
        total[:per].reshape(-1),
        grad_query,
        grad_key,
        grad_value,
        gain_of(2 * per),
        gain_of(7),
        grad_out,
        total[per : 2 * per].reshape(-1),
        grad_router,
        grad_gate,
        grad_up,
        grad_down,
    )


def solution(mesh):
    in_specs = (
        P("ctx", None),
        P(),
        P("ctx", None),
        P(),
        P(None, "tp"),
        P(None, "tp"),
        P(None, "tp"),
        P(),
        P(),
        P("tp", None),
        P(),
        P(),
        P("ctx", None, "tp"),
        P("ctx", None, "tp"),
        P("ctx", "tp", None),
        P("ctx", None),
    )
    out_specs = (
        P("ctx", None),
        P("ctx", None),
        P("ctx"),
        P("ctx", "tp"),
        P("ctx", "tp"),
        P("ctx", "tp"),
        P("ctx"),
        P("ctx"),
        P("tp", "ctx"),
        P("ctx"),
        P("ctx", None),
        P("ctx", None, "tp"),
        P("ctx", None, "tp"),
        P("ctx", "tp", None),
    )
    own = mesh.shape["ctx"] == 8 and mesh.shape["tp"] == 4
    shards = fast_shards if own else plain_shards
    return jax.shard_map(shards, mesh=mesh, in_specs=in_specs, out_specs=out_specs, check_vma=False)
```

```python
import math
import jax
import jax.numpy as jnp
from jax import lax
from jax.sharding import PartitionSpec as P
from jax.experimental import pallas as pl
from jax.experimental.pallas import tpu as pltpu
MESH=pl.DeviceIdType.MESH

def coords():
    ctx=lax.axis_index("ctx"); tp=lax.axis_index("tp")
    return ctx//2, ctx%2, tp//2, tp%2
def dev(z,x,y,c): return (z*2+x, y*2+c)
def pid(z,x,y,c): return (z*2+x)*4+y*2+c

def neighbours():
    z,x,y,c=coords()
    ax=x+(1-c)*(1-2*x); ay=y+c*(1-2*y)
    bx=x+c*(1-2*x); by=y+(1-c)*(1-2*y)
    return z,x,y,c,ax,ay,bx,by

def barrier_all():
    z,x,y,c=coords()
    b=pltpu.get_barrier_semaphore()
    def sig(d): pl.semaphore_signal(b,inc=1,device_id=d,device_id_type=MESH)
    sig(dev(z,1-x,y,c)); sig(dev(z,x,1-y,c)); sig(dev(z,x,y,1-c))
    @pl.when(z<3)
    def _(): sig(dev(z+1,x,y,c))
    @pl.when(z>0)
    def _(): sig(dev(z-1,x,y,c))
    pl.semaphore_wait(b,5-(3-z)//3-z//3)

class Gather:
    def __init__(self, own_ref, out_ref, lsem, send, recv):
        self.own, self.out, self.lsem, self.send, self.recv = own_ref, out_ref, lsem, send, recv
        self.rows = own_ref.shape[0]
        z, x, y, c, ax, ay, bx, by = neighbours()
        self.at_me = (z, x, y, c, ax, ay, bx, by)
        self.up, self.down = dev(z + 1, x, y, c), dev(z - 1, x, y, c)
        self.A, self.B, self.C = dev(z, ax, ay, c), dev(z, bx, by, c), dev(z, x, y, 1 - c)

    def place(self, p):
        return self.out.at[pl.ds(pl.multiple_of(p * self.rows, self.rows), self.rows)]

    def copy(self, p, to, k, own=False):
        return pltpu.make_async_remote_copy(
            src_ref=self.own if own else self.place(p), dst_ref=self.place(p),
            send_sem=self.send.at[k, p], recv_sem=self.recv.at[p], device_id=to, device_id_type=MESH)

    def wait(self, p):
        self.copy(p, self.C, 4).wait_recv()

    def local(self):
        z, x, y, c = self.at_me[:4]
        return pltpu.make_async_copy(self.own, self.place(pid(z, x, y, c)), self.lsem)

    def start(self):
        z, x, y, c = self.at_me[:4]
        me = pid(z, x, y, c)
        self.local().start()

        @pl.when(z < 3)
        def _():
            self.copy(me, self.up, 0, True).start()

        @pl.when(z > 0)
        def _():
            self.copy(me, self.down, 1, True).start()

        for to, k in ((self.A, 2), (self.B, 3), (self.C, 4)):
            self.copy(me, to, k, True).start()

    def from_line(self, zz):
        z, x, y, c = self.at_me[:4]
        p = pid(zz, x, y, c)
        self.wait(p)

        @pl.when((zz < z) & (z < 3))
        def _():
            self.copy(p, self.up, 0).start()

        @pl.when((zz > z) & (z > 0))
        def _():
            self.copy(p, self.down, 1).start()

        for to, k in ((self.A, 2), (self.B, 3), (self.C, 4)):
            self.copy(p, to, k).start()

    def from_a(self, zz):
        z, x, y, c, ax, ay, bx, by = self.at_me

        p = pid(zz, ax, ay, c)
        self.wait(p)
        self.copy(p, self.B, 3).start()
        self.copy(p, self.C, 4).start()

    def from_b(self, zz, xx, yy):
        c = self.at_me[3]

        p = pid(zz, xx, yy, c)
        self.wait(p)
        self.copy(p, self.C, 4).start()

    def finish(self):
        z, x, y, c, ax, ay, bx, by = self.at_me

        def one(zz, carry):
            p = pid(zz, x, y, c)

            @pl.when((z < 3) & (zz <= z))
            def _():
                self.copy(p, self.up, 0).wait_send()

            @pl.when((z > 0) & (zz >= z))
            def _():
                self.copy(p, self.down, 1).wait_send()

            for to, k in ((self.A, 2), (self.B, 3), (self.C, 4)):
                self.copy(p, to, k).wait_send()
            p = pid(zz, ax, ay, c)
            self.copy(p, self.B, 3).wait_send()
            self.copy(p, self.C, 4).wait_send()
            self.copy(pid(zz, bx, by, c), self.C, 4).wait_send()
            self.copy(pid(zz, 1 - x, 1 - y, c), self.C, 4).wait_send()
            return carry

        lax.fori_loop(0, 4, one, 0)


def far_z(z, k):
    half = z // 2
    near = z + half * (3 - 2 * z)
    place = 3 - k + (k // 2) * (2 * (k % 2) - 1) * near
    return place + half * (3 - 2 * place)


def reduce_kernel(
    hs_ref, gl_ref, ul_ref, pair_ref, wd_ref, wg_ref, wu_ref, att_ref,
    out_ref, line_ref,
    acc, cbuf, bbuf, abuf, zbuf, blk, mats, low, pair,
    csend, crecv, bsend, brecv, asend, arecv, zsend, zrecv, msem, lsem, psem, nsem, nsend, nrecv,
):
    f32 = jnp.float32
    rows = out_ref.shape[0]
    width = wd_ref.shape[1]
    z, x, y, c, ax, ay, bx, by = neighbours()
    dx, dy = 1 - x, 1 - y
    A, B, C = dev(z, ax, ay, c), dev(z, bx, by, c), dev(z, x, y, 1 - c)
    up, down = dev(z + 1, x, y, c), dev(z - 1, x, y, c)
    tok = 4 * rows

    def q(zz, xx, yy):
        return zz * 4 + xx * 2 + yy

    def place_of(u):
        return far_z(z, u // 2), (u % 2) * (2 * x - 1) + 1 - x

    def loads(u):
        zz, xx = place_of(u)
        span = pl.ds(pl.multiple_of((zz * 2 + xx) * tok, tok), tok)
        slot = u % 2
        return [
            pltpu.make_async_copy(r.at[span], low.at[slot, n], lsem.at[slot, n])
            for n, r in enumerate((hs_ref, gl_ref, ul_ref))
        ] + [pltpu.make_async_copy(pair_ref.at[span], pair.at[slot], psem.at[slot])]

    def part_rows(slot, yy, cc):
        return blk.at[slot, pl.ds(pl.multiple_of((yy * 2 + cc) * rows, rows), rows)]

    def ccopy(zz, xx, yy, slot):
        i = q(zz, xx, yy)
        return pltpu.make_async_remote_copy(
            src_ref=part_rows(slot, yy, 1 - c), dst_ref=cbuf.at[i], send_sem=csend.at[slot, yy],
            recv_sem=crecv.at[i], device_id=C, device_id_type=MESH)

    def products(u):
        slot = u % 2
        zz, xx = place_of(u)
        for cp in loads(u):
            cp.wait()

        @pl.when(u < 7)
        def _():
            for cp in loads(u + 1):
                cp.start()

        @pl.when(u > 1)
        def _():
            for yy in range(2):
                ccopy(zz, xx, yy, slot).wait_send()

        blk[slot, :, :width] = nn(low[slot, 0], mats[0]).astype(blk.dtype)
        blk[slot, :, width : 2 * width] = (
            nn(low[slot, 1], mats[1]) + nn(low[slot, 2], mats[2])
        ).astype(blk.dtype)
        blk[slot, :, 2 * width :] = pair[slot]
        for yy in range(2):
            ccopy(zz, xx, yy, slot).start()
        for yy in range(2):
            acc[q(zz, xx, yy)] = part_rows(slot, yy, c)[...]

    def bcopy(zz, far):
        i = zz + 4 * far
        place = q(zz, dx, dy) if far else q(zz, bx, by)
        return pltpu.make_async_remote_copy(
            src_ref=acc.at[place], dst_ref=bbuf.at[i], send_sem=bsend.at[i],
            recv_sem=brecv.at[i], device_id=B, device_id_type=MESH)

    def acopy(zz):
        return pltpu.make_async_remote_copy(
            src_ref=acc.at[q(zz, ax, ay)], dst_ref=abuf.at[zz], send_sem=asend.at[zz],
            recv_sem=arecv.at[zz], device_id=A, device_id_type=MESH)

    def zcopy(zz, to, slot):
        return pltpu.make_async_remote_copy(
            src_ref=acc.at[q(zz, x, y)], dst_ref=zbuf.at[slot], send_sem=zsend.at[zz],
            recv_sem=zrecv.at[slot], device_id=to, device_id_type=MESH)

    def plus_c(zz, xx, yy):
        ccopy(zz, xx, yy, 0).wait_recv()
        i = q(zz, xx, yy)
        return acc[i].astype(f32) + cbuf[i].astype(f32)

    def stage_b(k, far):
        zz = far_z(z, k)
        xx, yy = (dx, dy) if far else (bx, by)
        acc[q(zz, xx, yy)] = plus_c(zz, xx, yy).astype(acc.dtype)
        bcopy(zz, far).start()

    def stage_a(k):
        zz = far_z(z, k)
        value = plus_c(zz, ax, ay)
        bcopy(zz, 1).wait_recv()
        acc[q(zz, ax, ay)] = (value + bbuf[zz + 4].astype(f32)).astype(acc.dtype)
        acopy(zz).start()

    def stage_z(k):
        zz = far_z(z, k)
        place = q(zz, x, y)
        value = plus_c(zz, x, y)
        bcopy(zz, 0).wait_recv()
        acopy(zz).wait_recv()
        value = value + bbuf[zz].astype(f32) + abuf[zz].astype(f32)

        @pl.when(zz != z)
        def _():
            acc[place] = value.astype(acc.dtype)

            @pl.when((zz > z) & (z > 0))
            def _():
                zcopy(zz, up, zz).wait_recv()
                acc[place] = (acc[place].astype(f32) + zbuf[zz].astype(f32)).astype(acc.dtype)

            @pl.when((zz < z) & (z < 3))
            def _():
                zcopy(zz, down, zz).wait_recv()
                acc[place] = (acc[place].astype(f32) + zbuf[zz].astype(f32)).astype(acc.dtype)

            @pl.when(zz > z)
            def _():
                zcopy(zz, up, zz).start()

            @pl.when((zz < z) & (zz != z - 1))
            def _():
                zcopy(zz, down, zz).start()

            @pl.when(zz == z - 1)
            def _():
                zcopy(zz, down, 4).start()

        @pl.when(zz == z)
        def _():
            out_ref[...] = value

            @pl.when(z > 0)
            def _():
                zcopy(z, up, z).wait_recv()
                out_ref[...] += zbuf[z].astype(f32)

            @pl.when(z < 3)
            def _():
                zcopy(z, down, 4).wait_recv()
                out_ref[...] += zbuf[4].astype(f32)

    weights = [pltpu.make_async_copy(r, mats.at[n], msem.at[n]) for n, r in enumerate((wd_ref, wg_ref, wu_ref))]
    for cp in weights:
        cp.start()
    for cp in loads(0):
        cp.start()
    line = Line(lambda zz: line_ref.at[zz], nsend, nrecv, att_ref)
    mine = pltpu.make_async_copy(att_ref, line_ref.at[z], nsem)
    mine.start()
    barrier_all()
    line.start()
    for cp in weights:
        cp.wait()

    def step(u, carry):
        @pl.when(u < 8)
        def _():
            products(u)

        for d in (1, 2, 3):
            @pl.when(u == 2 * d + 1)
            def _():
                line.pass_on(d)

        k = (u - 1) // 2

        @pl.when((u > 0) & (u < 9) & (u % 2 == 1))
        def _():
            stage_b(k, 1)

        @pl.when((u > 0) & (u < 9) & (u % 2 == 0))
        def _():
            stage_b(k, 0)

        @pl.when((u >= 5) & (u < 13) & (u % 2 == 1))
        def _():
            stage_a((u - 5) // 2)

        @pl.when((u >= 8) & (u % 2 == 0))
        def _():
            stage_z((u - 8) // 2)

        return carry

    lax.fori_loop(0, 15, step, 0)
    mine.wait()
    line.finish()
    for slot in range(2):
        for yy in range(2):
            ccopy(z, x, yy, slot).wait_send()

    def last(zz, carry):
        bcopy(zz, 1).wait_send()
        bcopy(zz, 0).wait_send()
        acopy(zz).wait_send()

        @pl.when(zz != z)
        def _():
            zcopy(zz, up, zz).wait_send()

        return carry

    lax.fori_loop(0, 4, last, 0)


def reduce_experts(hs, gl, ul, pair, wd, wg, wu, att, cid):
    n, hid = hs.shape
    width = wd.shape[1]
    rows = n // 32
    w = 2 * width + pair.shape[1]
    dma = pltpu.SemaphoreType.DMA
    bf = jnp.bfloat16

    def pieces(k):
        return pltpu.VMEM((k, rows, w), bf)

    anywhere = pl.BlockSpec(memory_space=pl.ANY)
    return pl.pallas_call(
        reduce_kernel,
        in_specs=[anywhere] * 8,
        out_specs=[pl.BlockSpec(memory_space=pltpu.VMEM), anywhere],
        out_shape=[
            jax.ShapeDtypeStruct((rows, w), jnp.float32), jax.ShapeDtypeStruct((4, *att.shape), bf),
        ],
        scratch_shapes=[
            pieces(16), pieces(16), pieces(8), pieces(4), pieces(5),
            pltpu.VMEM((2, 4 * rows, w), bf),
            pltpu.VMEM((3, hid, width), bf),
            pltpu.VMEM((2, 3, 4 * rows, hid), bf),
            pltpu.VMEM((2, 4 * rows, pair.shape[1]), bf),
            dma((2, 2)), dma((16,)), dma((8,)), dma((8,)), dma((4,)), dma((4,)),
            dma((4,)), dma((5,)), dma((3,)), dma((2, 3)), dma((2,)), dma, dma((2, 4)), dma((4,)),
        ],
        compiler_params=pltpu.CompilerParams(
            collective_id=cid, has_side_effects=True, vmem_limit_bytes=56 * 2**20
        ),
        cost_estimate=pl.CostEstimate(
            flops=6 * n * width * hid, bytes_accessed=10 * n * width, transcendentals=0
        ),
        name="reduce_experts",
    )(hs, gl, ul, pair, wd, wg, wu, att)


def barrier_wide():
    z, x, y, c = coords()
    ctx, tp = lax.axis_index("ctx"), lax.axis_index("tp")
    bar = pltpu.get_barrier_semaphore()
    for i in range(1, 8):
        pl.semaphore_signal(bar, inc=1, device_id=((ctx + i) % 8, tp), device_id_type=MESH)
    for to in (dev(z, x, 1 - y, c), dev(z, x, y, 1 - c), dev(z, x, 1 - y, 1 - c)):
        pl.semaphore_signal(bar, inc=1, device_id=to, device_id_type=MESH)
    pl.semaphore_wait(bar, 10)


class Columns:
    def __init__(self, src, buf, send, recv, tsend, trecv):
        self.src, self.buf, self.send, self.recv = src, buf, send, recv
        self.tsend, self.trecv = tsend, trecv
        self.tp = lax.axis_index("tp")
        z, x, y, c = coords()
        self.z, self.x, self.y, self.c = z, x, y, c
        self.Y, self.C = dev(z, x, 1 - y, c), dev(z, x, y, 1 - c)
        self.mine, self.by_y, self.by_c, self.by_d = y * 2 + c, (1 - y) * 2 + c, y * 2 + 1 - c, (1 - y) * 2 + 1 - c

    def push(self, i):
        to = (self.z + i) % 4
        return pltpu.make_async_remote_copy(
            src_ref=self.src.at[to], dst_ref=self.buf.at[self.z, self.tp],
            send_sem=self.send.at[i], recv_sem=self.recv.at[i],
            device_id=dev(to, self.x, self.y, self.c), device_id_type=MESH)

    def over(self, part, to, k):
        return pltpu.make_async_remote_copy(
            src_ref=self.buf.at[:, part], dst_ref=self.buf.at[:, part], send_sem=self.tsend.at[k],
            recv_sem=self.trecv.at[part], device_id=to, device_id_type=MESH)

    def start(self):
        for i in range(1, 4):
            self.push(i).start()
        self.buf[self.z, self.tp] = self.src[self.z]

    def exchange(self):
        for i in range(1, 4):
            self.push(i).wait_recv()
        self.over(self.mine, self.Y, 0).start()
        self.over(self.mine, self.C, 1).start()

    def forward(self):
        self.over(self.by_y, self.Y, 0).wait_recv()
        self.over(self.by_y, self.C, 2).start()

    def finish(self):
        self.over(self.by_c, self.C, 1).wait_recv()
        self.over(self.by_d, self.C, 2).wait_recv()
        for i in range(1, 4):
            self.push(i).wait_send()
        self.over(self.mine, self.Y, 0).wait_send()
        self.over(self.mine, self.C, 1).wait_send()
        self.over(self.by_y, self.C, 2).wait_send()


class Line:
    def __init__(self, place, send, recv, first=None):
        self.place, self.send, self.recv, self.first = place, send, recv, first
        z, x, y, c = coords()
        self.z = z
        self.up, self.down = dev(z + 1, x, y, c), dev(z - 1, x, y, c)

    def copy(self, zz, to, k, own=False):
        src = self.first if own and self.first is not None else self.place(zz)
        return pltpu.make_async_remote_copy(
            src_ref=src, dst_ref=self.place(zz), send_sem=self.send.at[k, zz],
            recv_sem=self.recv.at[zz], device_id=to, device_id_type=MESH)

    def start(self):
        @pl.when(self.z < 3)
        def _():
            self.copy(self.z, self.up, 0, True).start()

        @pl.when(self.z > 0)
        def _():
            self.copy(self.z, self.down, 1, True).start()

    def pass_on(self, d):
        z = self.z

        @pl.when(z - d >= 0)
        def _():
            self.copy(z - d, self.up, 0).wait_recv()

            @pl.when(z < 3)
            def _():
                self.copy(z - d, self.up, 0).start()

        @pl.when(z + d <= 3)
        def _():
            self.copy(z + d, self.down, 1).wait_recv()

            @pl.when(z > 0)
            def _():
                self.copy(z + d, self.down, 1).start()

    def finish(self):
        z = self.z
        for zz in range(4):
            @pl.when((z < 3) & (zz <= z))
            def _():
                self.copy(zz, self.up, 0).wait_send()

            @pl.when((z > 0) & (zz >= z))
            def _():
                self.copy(zz, self.down, 1).wait_send()


class Spread:
    def __init__(self, place, send, recv, first=None):
        self.place, self.send, self.recv, self.first = place, send, recv, first
        z, x, y, c = coords()
        self.z, self.x = z, x
        self.X = dev(z, 1 - x, y, c)
        self.up, self.down = dev(z + 1, x, y, c), dev(z - 1, x, y, c)
        self.me = z * 2 + x

    def copy(self, p, to, k, own=False):
        src = self.first if own and self.first is not None else self.place(p)
        return pltpu.make_async_remote_copy(
            src_ref=src, dst_ref=self.place(p), send_sem=self.send.at[k, p],
            recv_sem=self.recv.at[p], device_id=to, device_id_type=MESH)

    def start_x(self):
        self.copy(self.me, self.X, 2, True).start()

    def start_z(self):
        @pl.when(self.z < 3)
        def _():
            self.copy(self.me, self.up, 0, True).start()

        @pl.when(self.z > 0)
        def _():
            self.copy(self.me, self.down, 1, True).start()

    def pass_on(self, d):
        z, x = self.z, self.x

        @pl.when(z - d >= 0)
        def _():
            p = (z - d) * 2 + x
            self.copy(p, self.X, 2).wait_recv()

            @pl.when(z < 3)
            def _():
                self.copy(p, self.up, 0).start()

            self.copy(p, self.X, 2).start()

        @pl.when(z + d <= 3)
        def _():
            p = (z + d) * 2 + x
            self.copy(p, self.X, 2).wait_recv()

            @pl.when(z > 0)
            def _():
                self.copy(p, self.down, 1).start()

            self.copy(p, self.X, 2).start()

    def arrive(self):
        for zz in range(4):
            self.copy(zz * 2 + 1 - self.x, self.X, 2).wait_recv()

    def finish(self):
        z, x = self.z, self.x
        for zz in range(4):
            p = zz * 2 + x

            @pl.when((z < 3) & (zz <= z))
            def _():
                self.copy(p, self.up, 0).wait_send()

            @pl.when((z > 0) & (zz >= z))
            def _():
                self.copy(p, self.down, 1).wait_send()

            self.copy(p, self.X, 2).wait_send()


def row_norm(v):
    return lax.rsqrt(jnp.mean(v * v, axis=1, keepdims=True) + 1e-06)


def turn(v, cos, sin):
    return v * cos + pltpu.roll(v, v.shape[1] // 2, 1) * sin


def turn_back(v, cos, sin):
    return v * cos - pltpu.roll(v, v.shape[1] // 2, 1) * sin


def front_kernel(
    x_ref, g1_ref, wq_ref, wk_ref, wv_ref, qg_ref, kg_ref, cos_ref, sin_ref, qpos_ref, kpos_ref,
    wo_ref, g2_ref, wr_ref, routes_ref, cot_ref,
    first_ref, qraw_ref, kraw_ref, qrot_ref, kv_ref, att_ref, log_ref, res_ref, gates_ref, piece_ref, cols_ref,
    xs, wk, wv, turned, wq, wo, part, cbuf, ybuf, stage, csrc,
    wsem, ksend, krecv, csend, crecv, ysend, yrecv, psend, precv, tsend, trecv,
):
    f32, bf = jnp.float32, jnp.bfloat16
    z, x, y, c = coords()
    rows = res_ref.shape[0]
    experts = wr_ref.shape[0]
    head = qg_ref.shape[1]
    heads = wq_ref.shape[1] // head
    half = x_ref.shape[0] // 2
    xc, wkc, wvc, wqc, woc = (
        pltpu.make_async_copy(src, dst, wsem.at[n])
        for n, (src, dst) in enumerate(((x_ref, xs), (wk_ref, wk), (wv_ref, wv), (wq_ref, wq), (wo_ref, wo)))
    )
    for cp in (xc, wkc, wvc, wqc, woc):
        cp.start()
    own = pl.ds(pl.multiple_of((y * 2 + c) * rows, rows), rows)
    Y, C = dev(z, x, 1 - y, c), dev(z, x, y, 1 - c)
    barrier_wide()
    cotc = pltpu.make_async_copy(cot_ref.at[own], piece_ref.at[:, x_ref.shape[1] : 2 * x_ref.shape[1]], wsem.at[5])
    cotc.start()
    turned[...] = routes_ref[...].T
    xc.wait()
    value = xs[...].astype(f32)
    first = (value * row_norm(value) * g1_ref[...]).astype(bf)
    first_ref[...] = first
    cos, sin = cos_ref[...], sin_ref[...]
    wkc.wait()
    wvc.wait()
    kraw = nn(first, wk[...])
    kraw_ref[...] = kraw
    krot = turn(kraw * row_norm(kraw) * kg_ref[...], cos, sin).astype(bf)
    vrow = nn(first, wv[...]).astype(bf)
    me = z * 2 + x
    for s in range(2):
        kv_ref[s, me] = krot[s * half : (s + 1) * half]
        kv_ref[2 + s, me] = vrow[s * half : (s + 1) * half]

    keys_out = Spread(lambda p: kv_ref.at[:, p], ksend, krecv)
    keys_out.start_z()
    keys_out.start_x()

    wqc.wait()
    qraw_ref[...] = nn(first, wq[...])
    keys_out.pass_on(1)

    def rope_head(h, carry):
        lanes = pl.ds(pl.multiple_of(h * head, head), head)
        raw = qraw_ref[:, lanes]
        rot = turn(raw * row_norm(raw) * qg_ref[...], cos_ref[...], sin_ref[...]).astype(bf)
        qrot_ref[h] = rot[:half]
        qrot_ref[heads + h] = rot[half:]
        return carry

    lax.fori_loop(0, heads // 2, rope_head, 0)
    keys_out.pass_on(2)
    lax.fori_loop(heads // 2, heads, rope_head, 0)
    keys_out.pass_on(3)
    keys_out.arrive()
    width = first.shape[1]
    per = width // 4
    for i in range(4):
        csrc[i] = first_ref[own, i * per : (i + 1) * per]
    blocks = Columns(csrc, cols_ref, psend, precv, tsend, trecv)
    blocks.start()

    scale = 1.0 / math.sqrt(head)

    group = 4

    def attend(i, carry):
        s = i // (heads // group)
        h = i % (heads // group) * group
        span = pl.ds(pl.multiple_of(s * half, half), half)
        keys = kv_ref[s].reshape(8 * half, head)
        vals = kv_ref[2 + s].reshape(8 * half, head)
        query = qrot_ref[pl.ds(i * group, group)].reshape(group * half, head)
        scores = (nt(query, keys) * scale).reshape(group, half, 8 * half)
        allowed = qpos_ref[span, :1] >= kpos_ref[pl.ds(s, 1), :]
        scores = jnp.where(allowed[None], scores, -1e9).reshape(group * half, 8 * half)
        top = jnp.max(scores, axis=1, keepdims=True)
        weights = jnp.exp(scores - top)
        total = jnp.sum(weights, axis=1, keepdims=True)
        probs = (weights * (1.0 / total)).astype(bf)
        mixed = nn(probs, vals).astype(bf)
        logs = jnp.broadcast_to(top + jnp.log(total), (group * half, head))
        log_ref[pl.ds(i * group, group)] = logs.reshape(group, half, head)
        for g in range(group):
            lanes = pl.ds(pl.multiple_of((h + g) * head, head), head)
            att_ref[span, lanes] = mixed[g * half : (g + 1) * half]
        @pl.when(i == steps // 2 - 1)
        def _():
            blocks.exchange()
        return carry

    steps = 2 * heads // group
    lax.fori_loop(0, steps, attend, 0)
    blocks.forward()
    woc.wait()

    def at(yy, cc):
        return part.at[pl.ds(pl.multiple_of((yy * 2 + cc) * rows, rows), rows)]

    def project(yy):
        span = pl.ds(pl.multiple_of(yy * 2 * rows, 2 * rows), 2 * rows)
        part[span] = nn(att_ref[span], wo[...]).astype(bf)

    def ccopy(yy):
        return pltpu.make_async_remote_copy(
            src_ref=at(yy, 1 - c), dst_ref=cbuf.at[yy], send_sem=csend.at[yy],
            recv_sem=crecv.at[yy], device_id=C, device_id_type=MESH)

    project(1 - y)
    ccopy(1 - y).start()
    project(y)
    ccopy(y).start()
    ccopy(1 - y).wait_recv()
    stage[...] = (at(1 - y, c)[...].astype(f32) + cbuf[1 - y].astype(f32)).astype(bf)
    yc = pltpu.make_async_remote_copy(
        src_ref=stage, dst_ref=ybuf, send_sem=ysend, recv_sem=yrecv, device_id=Y, device_id_type=MESH)
    yc.start()
    ccopy(y).wait_recv()
    res = xs[own].astype(f32) + (at(y, c)[...].astype(f32) + cbuf[y].astype(f32))
    lane = lax.broadcasted_iota(jnp.int32, (rows, 4 * experts), 1)
    named = jnp.zeros((rows, 4 * experts), jnp.bool_)
    routes = turned[own]
    for k in range(routes.shape[1]):
        named = named | (lane % experts == routes[:, k : k + 1])
    yc.wait_recv()
    res = res + ybuf[...].astype(f32)
    res_ref[...] = res
    second = (res * row_norm(res) * g2_ref[...]).astype(bf)
    piece_ref[:, :width] = second
    logits = nt(second, wr_ref[...])
    logits = jnp.concatenate([logits, logits, jnp.zeros((rows, 2 * experts), f32)], axis=1)
    masked = jnp.where(named & (lane < 2 * experts), logits, -1e30)
    top = jnp.max(masked, axis=1, keepdims=True)
    weights = jnp.where(named & (lane < 2 * experts), jnp.exp(masked - top), 0.0)
    total = jnp.sum(jnp.where(lane < experts, weights, 0.0), axis=1, keepdims=True)
    gates = weights / total
    high = gates.astype(bf)
    low = (gates - high.astype(f32)).astype(bf)
    gates_ref[...] = jnp.where(lane < experts, gates, 0.0)
    piece_ref[:, 2 * width :] = jnp.where(lane < experts, high, low)

    yc.wait_send()
    ccopy(0).wait_send()
    ccopy(1).wait_send()
    blocks.finish()
    keys_out.finish()
    cotc.wait()


def front(x, g1, wq, wk, wv, qg, kg, cos, sin, qpos, kpos, wo, g2, wr, routes, cot, cid):
    tok, width = x.shape
    head = qg.shape[1]
    cols = wq.shape[1]
    heads = cols // head
    rows, half = tok // 4, tok // 2
    f32, bf = jnp.float32, jnp.bfloat16
    dma = pltpu.SemaphoreType.DMA
    vm, anywhere = pl.BlockSpec(memory_space=pltpu.VMEM), pl.BlockSpec(memory_space=pl.ANY)

    def out(shape, kind):
        return jax.ShapeDtypeStruct(shape, kind)

    return pl.pallas_call(
        front_kernel,
        in_specs=[anywhere, vm] + [anywhere] * 3 + [vm] * 6 + [anywhere] + [vm] * 3 + [anywhere],
        out_specs=[vm] * 11,
        out_shape=[
            out((tok, width), bf), out((tok, cols), f32), out((tok, head), f32),
            out((2 * heads, half, head), bf), out((4, 8, half, head), bf), out((tok, cols), bf),
            out((2 * heads, half, head), f32), out((rows, width), f32), out((rows, 128), f32),
            out((rows, 2 * width + 128), bf), out((4, 4, rows, width // 4), bf),
        ],
        scratch_shapes=[
            pltpu.VMEM((tok, width), bf), pltpu.VMEM((width, head), bf), pltpu.VMEM((width, head), bf),
            pltpu.VMEM(routes.shape[::-1], jnp.int32),
            pltpu.VMEM((width, cols), bf), pltpu.VMEM((cols, width), bf), pltpu.VMEM((tok, width), bf),
            pltpu.VMEM((2, rows, width), bf), pltpu.VMEM((rows, width), bf), pltpu.VMEM((rows, width), bf),
            pltpu.VMEM((4, rows, width // 4), bf),
            dma((6,)), dma((3, 8)), dma((8,)), dma((2,)), dma((2,)), dma, dma,
            dma((4,)), dma((4,)), dma((3,)), dma((4,)),
        ],
        compiler_params=pltpu.CompilerParams(
            collective_id=cid, has_side_effects=True, vmem_limit_bytes=52 * 2**20
        ),
        name="front",
    )(x, g1, wq, wk, wv, qg, kg, cos, sin, qpos, kpos, wo, g2, wr, routes, cot)


def middle_kernel(
    sums_ref, res_ref, gates_ref, cot_ref, g2_ref, wr_ref, wo_ref, qrot_ref, kv_ref, log_ref,
    qraw_ref, qg_ref, cos_ref, sin_ref, qpos_ref, kpos_ref,
    layer_ref, gres_ref, gn2_ref, cols_ref, qlow_ref, dkv_ref, qgain_ref,
    wo, back, mixed, dk, dv, csrc, wsem, send, recv, psend, precv, tsend, trecv,
):
    f32, bf = jnp.float32, jnp.bfloat16
    z, x, y, c = coords()
    rows, width = res_ref.shape
    experts = wr_ref.shape[0]
    head = qg_ref.shape[1]
    heads = qraw_ref.shape[1] // head
    half = qraw_ref.shape[0] // 2
    woc = pltpu.make_async_copy(wo_ref, wo, wsem)
    woc.start()
    barrier_wide()
    Y, C = dev(z, x, 1 - y, c), dev(z, x, y, 1 - c)

    def at(yy, cc):
        return back.at[pl.ds(pl.multiple_of((yy * 2 + cc) * rows, rows), rows)]

    res = res_ref[...]
    layer_ref[...] = (res + sums_ref[:, :width]).astype(bf)
    gates = gates_ref[...]
    pair = sums_ref[:, 2 * width :]
    glog = (gates * (pair - jnp.sum(gates * pair, axis=1, keepdims=True))).astype(bf)
    gsec = sums_ref[:, width : 2 * width] + nn(glog[:, :experts], wr_ref[...])
    rs = row_norm(res)
    unit = res * rs
    gn2_ref[...] = jnp.sum(gsec * unit, axis=0, keepdims=True)
    cg = gsec * g2_ref[...]
    gres = cot_ref[...].astype(f32) + rs * (cg - unit * jnp.mean(cg * unit, axis=1, keepdims=True))
    gres_ref[...] = gres
    mine = pl.ds(pl.multiple_of((y * 2 + c) * rows, rows), rows)
    glow = gres.astype(bf)
    back[mine] = glow

    def cp(yy, cc, to, k):
        return pltpu.make_async_remote_copy(
            src_ref=at(yy, cc), dst_ref=at(yy, cc), send_sem=send.at[k],
            recv_sem=recv.at[yy * 2 + cc], device_id=to, device_id_type=MESH)

    cp(y, c, Y, 0).start()
    cp(y, c, C, 1).start()
    per = width // 4
    for i in range(4):
        csrc[i, :, :per] = glow[:, i * per : (i + 1) * per]
        csrc[i, :, per:] = glog
    blocks = Columns(csrc, cols_ref, psend, precv, tsend, trecv)
    blocks.start()
    dk[...] = jnp.zeros_like(dk)
    dv[...] = jnp.zeros_like(dv)
    qgain_ref[...] = jnp.zeros_like(qgain_ref)
    woc.wait()

    def mix(yy):
        span = pl.ds(pl.multiple_of(yy * 2 * rows, 2 * rows), 2 * rows)
        both = nt(back[span], wo[...]).astype(bf)
        for h in range(heads):
            mixed[yy * heads + h] = both[:, h * head : (h + 1) * head]

    cp(y, 1 - c, C, 1).wait_recv()
    mix(y)
    cp(1 - y, c, Y, 0).wait_recv()
    cp(1 - y, c, C, 2).start()
    cp(1 - y, 1 - c, C, 2).wait_recv()
    mix(1 - y)
    scale = 1.0 / math.sqrt(head)

    group = 4

    def attend(i, carry):
        s = i // (heads // group)
        h = i % (heads // group) * group
        span = pl.ds(pl.multiple_of(s * half, half), half)
        mine = pl.ds(i * group, group)
        keys = kv_ref[s].reshape(8 * half, head)
        vals = kv_ref[2 + s].reshape(8 * half, head)
        query = qrot_ref[mine].reshape(group * half, head)
        grad = mixed[mine].reshape(group * half, head)
        scores = (nt(query, keys) * scale).reshape(group, half, 8 * half)
        allowed = qpos_ref[span, :1] >= kpos_ref[pl.ds(s, 1), :]
        logs = log_ref[mine][:, :, :1]
        probs = jnp.where(allowed[None], jnp.exp(scores - logs), 0.0).reshape(group * half, 8 * half)
        gprobs = nt(grad, vals)
        inner = jnp.sum(probs * gprobs, axis=1, keepdims=True)
        dots = (probs * (gprobs - inner) * scale).astype(bf)
        dk[s] += tn(dots, query)
        dv[s] += tn(probs.astype(bf), grad)
        drot = nn(dots, keys)
        for g in range(group):
            lanes = pl.ds(pl.multiple_of((h + g) * head, head), head)
            raw = qraw_ref[span, lanes]
            dn = turn_back(drot[g * half : (g + 1) * half], cos_ref[span], sin_ref[span])
            rs = row_norm(raw)
            unit = raw * rs
            qgain_ref[...] += jnp.sum((dn * unit).reshape(half // 8, 8, head), axis=0)
            cg = dn * qg_ref[...]
            low = rs * (cg - unit * jnp.mean(cg * unit, axis=1, keepdims=True))
            qlow_ref[span, lanes] = low.astype(bf)
        return carry

    steps = 2 * heads // group
    lax.fori_loop(0, steps // 2, attend, 0)
    blocks.exchange()
    lax.fori_loop(steps // 2, steps, attend, 0)
    blocks.forward()
    for s in range(2):
        dkv_ref[s] = dk[s].astype(bf).reshape(8, half, head)
        dkv_ref[2 + s] = dv[s].astype(bf).reshape(8, half, head)
    cp(y, c, Y, 0).wait_send()
    cp(y, c, C, 1).wait_send()
    cp(1 - y, c, C, 2).wait_send()
    blocks.finish()


def middle(sums, res, gates, cot, g2, wr, wo, qrot, kv, logs, qraw, qg, cos, sin, qpos, kpos, cid):
    rows, width = res.shape
    tok, cols = qraw.shape
    head = qg.shape[1]
    half = tok // 2
    f32, bf = jnp.float32, jnp.bfloat16
    dma = pltpu.SemaphoreType.DMA
    vm, anywhere = pl.BlockSpec(memory_space=pltpu.VMEM), pl.BlockSpec(memory_space=pl.ANY)

    def out(shape, kind):
        return jax.ShapeDtypeStruct(shape, kind)

    return pl.pallas_call(
        middle_kernel,
        in_specs=[vm] * 6 + [anywhere] + [vm] * 9,
        out_specs=[vm] * 7,
        out_shape=[
            out((rows, width), bf), out((rows, width), f32), out((1, width), f32),
            out((4, 4, rows, width // 4 + 128), bf), out((tok, cols), bf), out((4, 8, half, head), bf),
            out((8, head), f32),
        ],
        scratch_shapes=[
            pltpu.VMEM((cols, width), bf), pltpu.VMEM((tok, width), bf), pltpu.VMEM((2 * cols // head, half, head), bf),
            pltpu.VMEM((2, 8 * half, head), f32), pltpu.VMEM((2, 8 * half, head), f32),
            pltpu.VMEM((4, rows, width // 4 + 128), bf),
            dma, dma((3,)), dma((4,)), dma((4,)), dma((4,)), dma((3,)), dma((4,)),
        ],
        compiler_params=pltpu.CompilerParams(
            collective_id=cid, has_side_effects=True, vmem_limit_bytes=52 * 2**20
        ),
        name="middle",
    )(sums, res, gates, cot, g2, wr, wo, qrot, kv, logs, qraw, qg, cos, sin, qpos, kpos)


def tail_kernel(
    dkv_ref, qlow_ref, kraw_ref, kg_ref, cos_ref, sin_ref, wq_ref, wk_ref, wv_ref, x_ref, g1_ref,
    gres_ref, layer_ref, vec_ref, first_ref, out_part, router_part,
    gin_ref, lout_ref, gq_ref, gkv_ref, gout_ref, grouter_ref, vo_ref,
    wq, xbuf, zbuf, zst, part, cbuf, ybuf, stage, vbuf, vpart, tbuf, gin, qbuf, kvbuf, turned, osrc, obuf, rsrc, rbuf, qsrc, qgot, ksrc, kgot,
    wsem, xsend, xrecv, zsend, zrecv, csend, crecv, ysend, yrecv, send, recv, vsend, vrecv, tsend, trecv,
    qsend, qrecv, ksend, krecv, esend, erecv,
):
    f32, bf = jnp.float32, jnp.bfloat16
    z, x, y, c = coords()
    ctx, tp = lax.axis_index("ctx"), lax.axis_index("tp")
    rows, width = gres_ref.shape
    half, head = dkv_ref.shape[2:]
    wqc = pltpu.make_async_copy(wq_ref, wq, wsem.at[0])
    wqc.start()
    X, Y, C, D = dev(z, 1 - x, y, c), dev(z, x, 1 - y, c), dev(z, x, y, 1 - c), dev(z, x, 1 - y, 1 - c)
    up, down = dev(z + 1, x, y, c), dev(z - 1, x, y, c)
    barrier_wide()

    def xcopy(zz):
        return pltpu.make_async_remote_copy(
            src_ref=dkv_ref.at[:, zz * 2 + 1 - x], dst_ref=xbuf.at[zz], send_sem=xsend.at[zz],
            recv_sem=xrecv.at[zz], device_id=X, device_id_type=MESH)

    def zcopy(zz, to, slot):
        return pltpu.make_async_remote_copy(
            src_ref=zst.at[zz], dst_ref=zbuf.at[slot], send_sem=zsend.at[zz],
            recv_sem=zrecv.at[slot], device_id=to, device_id_type=MESH)

    span = qlow_ref.shape[1] // 2
    queries = [
        Line(lambda zz, n=n: qbuf.at[n, zz], qsend.at[n], qrecv.at[n]) for n in range(2)
    ]
    keys = Line(lambda zz: kvbuf.at[zz], ksend, krecv)
    for n in range(2):
        qbuf[n, z] = qlow_ref[:, n * span : (n + 1) * span]
    for k in range(4):
        xcopy(far_z(z, k)).start()
    queries[0].start()

    per = gq_ref.shape[0]
    own_cols = pl.ds(pl.multiple_of(x * per, per), per)
    far_cols = pl.ds(pl.multiple_of((1 - x) * per, per), per)

    def swap(n, src, dst):
        return pltpu.make_async_remote_copy(
            src_ref=src, dst_ref=dst, send_sem=esend.at[n], recv_sem=erecv.at[n], device_id=X,
            device_id_type=MESH)

    swaps = [
        swap(0, osrc, obuf), swap(1, rsrc, rbuf), swap(2, qsrc.at[0], qgot.at[0]),
        swap(3, qsrc.at[1], qgot.at[1]), swap(4, ksrc, kgot),
    ]
    osrc[...] = out_part[:, far_cols].astype(bf)
    rsrc[...] = router_part[far_cols].astype(bf)
    swaps[0].start()
    swaps[1].start()
    turned[...] = first_ref[...].T

    def query_part(n):
        right = qbuf[n].reshape(turned.shape[1], span)
        cols = slice(n * span, (n + 1) * span)
        qsrc[n] = nn(turned[far_cols], right).astype(bf)
        swaps[2 + n].start()
        gq_ref[:, cols] = nn(turned[own_cols], right)

    def sum_z(k):
        zz = far_z(z, k)
        xcopy(zz).wait_recv()
        total = dkv_ref[:, zz * 2 + x].astype(f32) + xbuf[zz].astype(f32)
        zst[zz] = total.astype(bf)

        @pl.when((zz > z) & (z > 0))
        def _():
            zcopy(zz, up, zz).wait_recv()
            zst[zz] = (zst[zz].astype(f32) + zbuf[zz].astype(f32)).astype(bf)

        @pl.when((zz < z) & (z < 3))
        def _():
            zcopy(zz, down, zz).wait_recv()
            zst[zz] = (zst[zz].astype(f32) + zbuf[zz].astype(f32)).astype(bf)

        @pl.when(zz > z)
        def _():
            zcopy(zz, up, zz).start()

        @pl.when((zz < z) & (zz != z - 1))
        def _():
            zcopy(zz, down, zz).start()

        @pl.when(zz == z - 1)
        def _():
            zcopy(zz, down, 4).start()

    def at(yy, cc):
        return part.at[pl.ds(pl.multiple_of((yy * 2 + cc) * rows, rows), rows)]

    def two(yy):
        return pl.ds(pl.multiple_of(yy * 2 * rows, 2 * rows), 2 * rows)

    sum_z(0)
    wqc.wait()
    first_a = nt(qlow_ref[two(1 - y)], wq[...])
    sum_z(1)
    first_b = nt(qlow_ref[two(y)], wq[...])
    queries[0].pass_on(1)
    sum_z(2)
    queries[1].start()
    xcopy(z).wait_recv()
    dkv = dkv_ref[:, ctx].astype(f32) + xbuf[z].astype(f32)

    @pl.when(z > 0)
    def _():
        zcopy(z, up, z).wait_recv()

    @pl.when(z == 0)
    def _():
        zbuf[0] = jnp.zeros_like(zbuf[0])

    @pl.when(z < 3)
    def _():
        zcopy(z, down, 4).wait_recv()

    @pl.when(z == 3)
    def _():
        zbuf[4] = jnp.zeros_like(zbuf[4])

    dkv = dkv + zbuf[z].astype(f32) + zbuf[4].astype(f32)
    dkey = jnp.concatenate([dkv[0], dkv[1]], axis=0)
    vlow = jnp.concatenate([dkv[2], dkv[3]], axis=0).astype(bf)
    raw = kraw_ref[...]
    dn = turn_back(dkey, cos_ref[...], sin_ref[...])
    rs = row_norm(raw)
    unit = raw * rs
    kgain = jnp.sum(dn * unit, axis=0, keepdims=True)
    cg = dn * kg_ref[...]
    klow = (rs * (cg - unit * jnp.mean(cg * unit, axis=1, keepdims=True))).astype(bf)
    kvbuf[z, :, :head] = klow
    kvbuf[z, :, head:] = vlow
    keys.start()
    queries[0].pass_on(2)

    def ccopy(yy):
        return pltpu.make_async_remote_copy(
            src_ref=at(yy, 1 - c), dst_ref=cbuf.at[yy], send_sem=csend.at[yy],
            recv_sem=crecv.at[yy], device_id=C, device_id_type=MESH)

    def project(yy, first):
        keys, vals = kvbuf[z, two(yy), :head], kvbuf[z, two(yy), head:]
        part[two(yy)] = (first + nt(keys, wk_ref[...]) + nt(vals, wv_ref[...])).astype(bf)
        ccopy(yy).start()

    project(1 - y, first_a)
    project(y, first_b)
    ccopy(1 - y).wait_recv()
    stage[...] = (at(1 - y, c)[...].astype(f32) + cbuf[1 - y].astype(f32)).astype(bf)
    yc = pltpu.make_async_remote_copy(
        src_ref=stage, dst_ref=ybuf, send_sem=ysend, recv_sem=yrecv, device_id=Y, device_id_type=MESH)
    yc.start()
    queries[1].pass_on(1)
    ccopy(y).wait_recv()
    gfirst = at(y, c)[...].astype(f32) + cbuf[y].astype(f32)
    own = pl.ds(pl.multiple_of((y * 2 + c) * rows, rows), rows)
    value = x_ref[own].astype(f32)
    rs = row_norm(value)
    unit = value * rs
    yc.wait_recv()
    gfirst = gfirst + ybuf[...].astype(f32)
    gn1 = jnp.sum(gfirst * unit, axis=0, keepdims=True)
    cg = gfirst * g1_ref[...]
    gin[...] = (gres_ref[...] + rs * (cg - unit * jnp.mean(cg * unit, axis=1, keepdims=True))).astype(bf)

    queries[0].pass_on(3)
    query_part(0)
    keys.pass_on(1)
    pairs = [(gin, gin_ref), (layer_ref, lout_ref)]

    def place(ref, yy, cc):
        return ref.at[pl.ds(pl.multiple_of((yy * 2 + cc) * rows, rows), rows)]

    def cp(n, src, yy, cc, to, k):
        return pltpu.make_async_remote_copy(
            src_ref=src, dst_ref=place(pairs[n][1], yy, cc), send_sem=send.at[n, k],
            recv_sem=recv.at[n, yy * 2 + cc], device_id=to, device_id_type=MESH)

    for n, (src, dst) in enumerate(pairs):
        cp(n, src, y, c, Y, 0).start()
        cp(n, src, y, c, C, 1).start()
        dst[own] = src[...]
    part_width = width // 8
    for i in range(8):
        for j in range(part_width // 128):
            lo = i * part_width + j * 128
            vpart[i, j : j + 1] = gn1[:, lo : lo + 128]
        vpart[i, part_width // 128 : 8] = vec_ref[i, part_width // 128 : 8]
        vpart[i, 7:8] = jnp.broadcast_to(kgain, (1, head))

    def vcopy(i):
        to = (ctx + i) % 8
        return pltpu.make_async_remote_copy(
            src_ref=vpart.at[to], dst_ref=vbuf.at[i], send_sem=vsend.at[i], recv_sem=vrecv.at[i],
            device_id=(to, tp), device_id_type=MESH)

    for i in range(1, 8):
        vcopy(i).start()
    queries[1].pass_on(2)
    keys.pass_on(2)
    total = vpart[ctx]
    for i in range(1, 8):
        vcopy(i).wait_recv()
        total = total + vbuf[i]
    tbuf[3] = total

    def tcopy(k, to):
        return pltpu.make_async_remote_copy(
            src_ref=tbuf.at[3], dst_ref=tbuf.at[k], send_sem=tsend.at[k], recv_sem=trecv.at[k],
            device_id=to, device_id_type=MESH)

    sums = [tcopy(k, to) for k, to in enumerate((Y, C, D))]
    for t in sums:
        t.start()
    for n, (src, dst) in enumerate(pairs):
        cp(n, src, 1 - y, c, Y, 0).wait_recv()
        cp(n, place(dst, 1 - y, c), 1 - y, c, C, 2).start()
    swaps[0].wait_recv()
    gout_ref[...] = out_part[:, own_cols] + obuf[...].astype(f32)
    swaps[1].wait_recv()
    grouter_ref[...] = router_part[own_cols] + rbuf[...].astype(f32)
    queries[1].pass_on(3)
    query_part(1)
    keys.pass_on(3)
    right = kvbuf[...].reshape(turned.shape[1], 2 * head)
    ksrc[...] = nn(turned[far_cols], right).astype(bf)
    swaps[4].start()
    gkv_ref[...] = nn(turned[own_cols], right)
    for t in sums:
        t.wait_recv()
    vo_ref[...] = (tbuf[3] + tbuf[0]) + (tbuf[1] + tbuf[2])
    for n, (src, dst) in enumerate(pairs):
        cp(n, src, y, 1 - c, C, 1).wait_recv()
        cp(n, src, 1 - y, 1 - c, C, 2).wait_recv()
        cp(n, src, y, c, Y, 0).wait_send()
        cp(n, src, y, c, C, 1).wait_send()
        cp(n, place(dst, 1 - y, c), 1 - y, c, C, 2).wait_send()
    for t in sums:
        t.wait_send()
    for i in range(1, 8):
        vcopy(i).wait_send()
    for line in (*queries, keys):
        line.finish()
    for n in range(2):
        swaps[2 + n].wait_recv()
        gq_ref[:, n * span : (n + 1) * span] += qgot[n].astype(f32)
    swaps[4].wait_recv()
    gkv_ref[...] += kgot[...].astype(f32)
    for s in swaps:
        s.wait_send()
    yc.wait_send()
    ccopy(0).wait_send()
    ccopy(1).wait_send()
    for zz in range(4):
        xcopy(zz).wait_send()

        @pl.when(zz != z)
        def _():
            zcopy(zz, up, zz).wait_send()


def tail(dkv, qlow, kraw, kg, cos, sin, wq, wk, wv, x, g1, gres, layer, vec, first, out_part, router_part, cid):
    tok, width = x.shape
    rows = gres.shape[0]
    half, head = dkv.shape[2:]
    per = first.shape[1] // 2
    f32, bf = jnp.float32, jnp.bfloat16
    dma = pltpu.SemaphoreType.DMA
    vm, anywhere = pl.BlockSpec(memory_space=pltpu.VMEM), pl.BlockSpec(memory_space=pl.ANY)

    def out(shape, kind):
        return jax.ShapeDtypeStruct(shape, kind)

    def mem(*shape, kind=bf):
        return pltpu.VMEM(shape, kind)

    return pl.pallas_call(
        tail_kernel,
        in_specs=[vm] * 6 + [anywhere] + [vm] * 10,
        out_specs=[vm] * 7,
        out_shape=[
            out((tok, width), bf), out((tok, width), bf), out((per, qlow.shape[1]), f32),
            out((per, 2 * head), f32), out((out_part.shape[0], per), f32),
            out((per, router_part.shape[1]), f32), out((8, 128), f32),
        ],
        scratch_shapes=[
            mem(*wq.shape), mem(4, 4, half, head), mem(5, 4, half, head), mem(4, 4, half, head),
            mem(tok, width), mem(2, rows, width), mem(rows, width), mem(rows, width),
            mem(8, 8, 128, kind=f32), mem(8, 8, 128, kind=f32), mem(4, 8, 128, kind=f32), mem(rows, width),
            mem(2, 4, tok, qlow.shape[1] // 2), mem(4, tok, 2 * head), mem(2 * per, first.shape[0]),
            mem(out_part.shape[0], per), mem(out_part.shape[0], per),
            mem(per, router_part.shape[1]), mem(per, router_part.shape[1]),
            mem(2, per, qlow.shape[1] // 2), mem(2, per, qlow.shape[1] // 2),
            mem(per, 2 * head), mem(per, 2 * head),
            dma((1,)), dma((4,)), dma((4,)), dma((4,)), dma((5,)), dma((2,)), dma((2,)), dma, dma,
            dma((2, 3)), dma((2, 4)), dma((8,)), dma((8,)), dma((3,)), dma((3,)),
            dma((2, 2, 4)), dma((2, 4)), dma((2, 4)), dma((4,)), dma((5,)), dma((5,)),
        ],
        compiler_params=pltpu.CompilerParams(
            collective_id=cid, has_side_effects=True, vmem_limit_bytes=52 * 2**20
        ),
        name="tail",
    )(dkv, qlow, kraw, kg, cos, sin, wq, wk, wv, x, g1, gres, layer, vec, first, out_part, router_part)


def experts_kernel(
    piece_ref, wg_ref, wu_ref, wd_ref, s_ref, t_ref,
    all_ref, pair_ref, hs_ref, gl_ref, ul_ref, hst_ref, glt_ref, ult_ref,
    land, mats, pairs, lows, turns,
    gsem, gsend, grecv, msem, asem, psem, lsem, tsem,
):
    bf, f32 = jnp.bfloat16, jnp.float32
    width = wg_ref.shape[1]
    extra = t_ref.shape[1]
    tok = 4 * piece_ref.shape[0]
    weights = [pltpu.make_async_copy(r, mats.at[n], msem.at[n]) for n, r in enumerate((wg_ref, wu_ref, wd_ref))]
    for cp in weights:
        cp.start()
    barrier_all()
    gather = Gather(piece_ref, land, gsem, gsend, grecv)
    gather.start()
    z, x, y, c, ax, ay, bx, by = gather.at_me

    def place_of(u):
        return far_z(z, 3 - u // 2), x + (u % 2) * (1 - 2 * x)

    def block_rows(u):
        zz, xx = place_of(u)
        return pl.ds(pl.multiple_of((zz * 2 + xx) * tok, tok), tok)

    def results(u):
        slot = u % 2
        span = block_rows(u)
        copies = [pltpu.make_async_copy(pairs.at[slot], pair_ref.at[span], psem.at[slot])]
        for n, (ref, turned) in enumerate(((hs_ref, hst_ref), (gl_ref, glt_ref), (ul_ref, ult_ref))):
            copies.append(pltpu.make_async_copy(lows.at[slot, n], ref.at[span], lsem.at[slot, n]))
            copies.append(pltpu.make_async_copy(turns.at[slot, n], turned.at[:, span], tsem.at[slot, n]))
        return copies

    def whole(u):
        span = block_rows(u)
        return pltpu.make_async_copy(land.at[span], all_ref.at[span], asem.at[u])

    gather.local().wait()

    def step(u, carry):
        zz, xx = place_of(u)
        slot = u % 2

        @pl.when(u % 2 == 0)
        def _():
            gather.from_a(zz)

            @pl.when(u < 6)
            def _():
                gather.from_line(far_z(z, 2 - u // 2))

            gather.from_b(zz, bx, by)

        @pl.when(u % 2 == 1)
        def _():
            gather.from_b(zz, 1 - x, 1 - y)

        for yy in range(2):
            gather.wait(pid(zz, xx, yy, 1 - c))

        whole(u).start()

        @pl.when(u == 0)
        def _():
            for cp in weights:
                cp.wait()

        @pl.when(u > 1)
        def _():
            for cp in results(u - 2):
                cp.wait()

        rows = block_rows(u)
        value = land[rows, :width]
        spread = nn(land[rows, 2 * width :], s_ref[...])
        gate = nt(value, mats[0])
        up = nt(value, mats[1])
        back = nt(land[rows, width : 2 * width], mats[2])
        sig = 1.0 / (1.0 + jnp.exp(-gate))
        silu = gate * sig
        hidden = silu * up
        hs = (hidden * spread).astype(bf)
        prod = hidden * back
        high = prod.astype(bf)
        low = (prod - high.astype(f32)).astype(bf)
        pairs[slot] = (nn(high, t_ref[...]) + nn(low, t_ref[...])).astype(bf)
        grad = back * spread
        gl = (grad * up * sig * (1.0 + gate * (1.0 - sig))).astype(bf)
        ul = (grad * silu).astype(bf)
        for n, v in enumerate((hs, gl, ul)):
            lows[slot, n] = v
            turns[slot, n] = v.T
        for cp in results(u):
            cp.start()
        return carry

    lax.fori_loop(0, 8, step, 0)
    for u in (6, 7):
        for cp in results(u):
            cp.wait()
    for u in range(8):
        whole(u).wait()
    gather.finish()


def experts_forward(piece, wg, wu, wd, spread, pick, cid):
    rows, wide = piece.shape
    hid, width = wg.shape
    n = 32 * rows
    tok = 4 * rows
    extra = pick.shape[1]
    bf = jnp.bfloat16
    dma = pltpu.SemaphoreType.DMA
    vm, anywhere = pl.BlockSpec(memory_space=pltpu.VMEM), pl.BlockSpec(memory_space=pl.ANY)

    def out(*shape):
        return jax.ShapeDtypeStruct(shape, bf)

    return pl.pallas_call(
        experts_kernel,
        in_specs=[anywhere] * 4 + [vm] * 2,
        out_specs=[anywhere] * 8,
        out_shape=[out(n, wide), out(n, extra)] + [out(n, hid)] * 3 + [out(hid, n)] * 3,
        scratch_shapes=[
            pltpu.VMEM((n, wide), bf), pltpu.VMEM((3, hid, width), bf), pltpu.VMEM((2, tok, extra), bf),
            pltpu.VMEM((2, 3, tok, hid), bf), pltpu.VMEM((2, 3, hid, tok), bf),
            dma, dma((5, 32)), dma((32,)), dma((3,)), dma((8,)), dma((2,)), dma((2, 3)), dma((2, 3)),
        ],
        compiler_params=pltpu.CompilerParams(
            collective_id=cid, has_side_effects=True, vmem_limit_bytes=56 * 2**20
        ),
        cost_estimate=pl.CostEstimate(
            flops=6 * n * width * hid, bytes_accessed=10 * n * width, transcendentals=n * hid
        ),
        name="experts_forward",
    )(piece, wg, wu, wd, spread, pick)


EPSILON = 1e-06
ROPE_BASE = 1000000.0
MASKED_SCORE = -1000000000.0
BF = jnp.bfloat16
F32 = jnp.float32


def dotf(a, b, dims):
    return lax.dot_general(a, b, (dims, ((), ())), preferred_element_type=F32)


def nt(a, b):
    return lax.dot_general(a, b, (((1,), (1,)), ((), ())), preferred_element_type=jnp.float32)


def nn(a, b):
    return lax.dot_general(a, b, (((1,), (0,)), ((), ())), preferred_element_type=jnp.float32)


def tn(a, b):
    return lax.dot_general(a, b, (((0,), (0,)), ((), ())), preferred_element_type=jnp.float32)


def plain_expert_kernel(x_ref, cot_ref, wg_ref, wu_ref, wd_ref, s_ref, t_ref, part_ref, gl_ref, ul_ref, hs_ref):
    bf = jnp.bfloat16
    width = cot_ref.shape[1]
    x = x_ref[:, :width]
    spread = nn(x_ref[:, width:], s_ref[...])
    gate = nt(x, wg_ref[...])
    up = nt(x, wu_ref[...])
    back = nt(cot_ref[...], wd_ref[...])
    sig = 1.0 / (1.0 + jnp.exp(-gate))
    silu = gate * sig
    hidden = silu * up
    hs = (hidden * spread).astype(bf)
    hs_ref[...] = hs.T
    part_ref[:, :width] = nn(hs, wd_ref[...]).astype(bf)
    prod = hidden * back
    high = prod.astype(bf)
    low = (prod - high.astype(jnp.float32)).astype(bf)
    part_ref[:, 2 * width :] = (nn(high, t_ref[...]) + nn(low, t_ref[...])).astype(bf)
    grad = back * spread
    gl = (grad * up * sig * (1.0 + gate * (1.0 - sig))).astype(bf)
    ul = (grad * silu).astype(bf)
    gl_ref[...] = gl.T
    ul_ref[...] = ul.T
    part_ref[:, width : 2 * width] = (nn(gl, wg_ref[...]) + nn(ul, wu_ref[...])).astype(bf)


def expert_blocks(x_all, cot_all, gate_mat, up_mat, down_mat, spread_mat, pick_mat, block=256):
    n, width = cot_all.shape
    wide = x_all.shape[1]
    hid = gate_mat.shape[0]
    bf = jnp.bfloat16

    def rows(w):
        return pl.BlockSpec((block, w), lambda i: (i, 0))

    def whole(v):
        return pl.BlockSpec(v.shape, lambda i: (0, 0), pipeline_mode=pl.Buffered(1))

    return pl.pallas_call(
        plain_expert_kernel,
        grid=(n // block,),
        in_specs=[rows(wide), rows(width)]
        + [whole(v) for v in (gate_mat, up_mat, down_mat, spread_mat, pick_mat)],
        out_specs=[rows(width + wide)] + [pl.BlockSpec((hid, block), lambda i: (0, i))] * 3,
        out_shape=[jax.ShapeDtypeStruct((n, width + wide), bf)]
        + [jax.ShapeDtypeStruct((hid, n), bf)] * 3,
        compiler_params=pltpu.CompilerParams(
            dimension_semantics=("arbitrary",), vmem_limit_bytes=56 * 2**20
        ),
        cost_estimate=pl.CostEstimate(
            flops=12 * n * width * hid, bytes_accessed=10 * n * width, transcendentals=n * hid
        ),
        name="plain_experts",
    )(x_all, cot_all, gate_mat, up_mat, down_mat, spread_mat, pick_mat)


def expert_grad_kernel(x_ref, cot_ref, gl_ref, ul_ref, hs_ref, gg_ref, gu_ref, gd_ref):
    first = pl.program_id(1) == 0

    def put(ref, low, full):
        value = nn(low[...], full[...])

        @pl.when(first)
        def _():
            ref[...] = value

        @pl.when(jnp.logical_not(first))
        def _():
            ref[...] += value

    put(gg_ref, gl_ref, x_ref)
    put(gu_ref, ul_ref, x_ref)
    put(gd_ref, hs_ref, cot_ref)


def expert_grads(x_all, cot_all, gl, ul, hs, width, first=0, block=256):
    n = x_all.shape[0]
    hid = gl.shape[0]
    span = min(n, 2048)
    cols = pl.BlockSpec((span, block), lambda i, j: (j, i))
    cots = pl.BlockSpec((span, block), lambda i, j: (j, i + first // block))
    rows = pl.BlockSpec((hid, span), lambda i, j: (0, j))
    out = pl.BlockSpec((hid, block), lambda i, j: (0, i))
    return pl.pallas_call(
        expert_grad_kernel,
        grid=(width // block, n // span),
        in_specs=[cols, cots, rows, rows, rows],
        out_specs=[out] * 3,
        out_shape=[jax.ShapeDtypeStruct((hid, width), jnp.float32)] * 3,
        compiler_params=pltpu.CompilerParams(
            dimension_semantics=("arbitrary", "arbitrary"), vmem_limit_bytes=56 * 2**20
        ),
        cost_estimate=pl.CostEstimate(
            flops=6 * n * width * hid, bytes_accessed=10 * n * width, transcendentals=0
        ),
        name="expert_grads",
    )(x_all, cot_all, gl, ul, hs)


class Links:
    def ag_all(self, piece):
        return lax.all_gather(piece, ("ctx", "tp"), axis=0, tiled=True)

    def rs_all(self, part):
        return lax.psum_scatter(part, ("ctx", "tp"), scatter_dimension=0, tiled=True).astype(F32)

    def ag_ctx(self, piece):
        return lax.all_gather(piece, "ctx", axis=0, tiled=True)

    def rs_ctx(self, part):
        return lax.psum_scatter(part, "ctx", scatter_dimension=0, tiled=True).astype(F32)

    def rs_tp(self, part):
        return lax.psum_scatter(part, "tp", scatter_dimension=0, tiled=True).astype(F32)

    def ag_tp(self, piece):
        return lax.all_gather(piece, "tp", axis=0, tiled=True)

    def finish(self, a, b, vectors):
        total = lax.psum_scatter(vectors, "ctx", scatter_dimension=0, tiled=True)
        gathered = (lax.all_gather(v, "tp", axis=0, tiled=True) for v in (a, b))
        return (*gathered, lax.psum(total, "tp"))


def rms_norm(values, gain_vec):
    factor = lax.rsqrt(jnp.mean(values * values, axis=-1, keepdims=True) + EPSILON)
    return values * factor * gain_vec


def rotate(values, rotary_angles):
    half_size = values.shape[-1] // 2
    first_half = values[..., :half_size]
    second_half = values[..., half_size:]
    cosine = jnp.cos(rotary_angles)
    sine_part = jnp.sin(rotary_angles)
    return jnp.concatenate(
        [
            first_half * cosine - second_half * sine_part,
            second_half * cosine + first_half * sine_part,
        ],
        axis=-1,
    )


def angles_of(token_positions, head_width):
    freq_steps = jnp.arange(head_width // 2).astype(F32) * (2.0 / head_width)
    frequency = jnp.exp(-math.log(ROPE_BASE) * freq_steps)
    return token_positions.astype(F32)[..., None] * frequency


def positions_of(block_order, dev_count, block_len):
    first_block = jnp.transpose(block_order)
    block_pair = jnp.stack([first_block, 2 * dev_count - 1 - first_block], axis=-1)
    spread = block_pair[..., None] * block_len + jnp.arange(block_len, dtype=jnp.int32)
    return spread.reshape(dev_count, block_order.shape[0], 2 * block_len)


def head_route_path(raw_heads, gain_vec, rotary_angles, head_count):
    shaped = raw_heads.reshape(raw_heads.shape[0], head_count, -1)
    return rotate(rms_norm(shaped, gain_vec), rotary_angles[:, None, :])


def attend_forward(seq_item):
    query_matrix, every_key_row, every_value_row, query_pos, key_pos = seq_item
    score_scale = 1.0 / math.sqrt(query_matrix.shape[-1])
    unscaled_scores = jnp.einsum(
        "upnj,apj->upna", query_matrix, every_key_row, preferred_element_type=F32
    )
    allowed = query_pos[:, None, None, None] >= key_pos[None, None, None, :]
    scores = jnp.where(allowed, unscaled_scores * score_scale, MASKED_SCORE)
    row_top = jnp.max(scores, axis=-1, keepdims=True)
    exp_scores = jnp.exp(scores - row_top)
    totals = jnp.sum(exp_scores, axis=-1, keepdims=True)
    lower_attention_probs = (exp_scores / totals).astype(BF)
    attended_mix = jnp.einsum(
        "jzfq,qzx->jzfx", lower_attention_probs, every_value_row, preferred_element_type=F32
    )
    return (attended_mix, (row_top + jnp.log(totals))[..., 0])


def attend_backward(seq_item):
    (
        query_matrix,
        every_key_row,
        every_value_row,
        query_pos,
        key_pos,
        grad_attended_mix,
        log_total,
    ) = seq_item
    score_scale = 1.0 / math.sqrt(query_matrix.shape[-1])
    unscaled_scores = jnp.einsum(
        "upnj,apj->upna", query_matrix, every_key_row, preferred_element_type=F32
    )
    allowed = query_pos[:, None, None, None] >= key_pos[None, None, None, :]
    scores = jnp.where(allowed, unscaled_scores * score_scale, MASKED_SCORE)
    attention_probs = jnp.exp(scores - log_total[..., None])
    grad_probs = jnp.einsum(
        "upnj,apj->upna", grad_attended_mix, every_value_row, preferred_element_type=F32
    )
    row_inner = jnp.sum(attention_probs * grad_probs, axis=-1, keepdims=True)
    grad_score_dots = (attention_probs * (grad_probs - row_inner) * score_scale).astype(BF)
    grad_queries = jnp.einsum(
        "jzfq,qzx->jzfx", grad_score_dots, every_key_row, preferred_element_type=F32
    )
    grad_key_rows = jnp.einsum(
        "axfv,axfz->vxz", grad_score_dots, query_matrix, preferred_element_type=F32
    )
    grad_values = jnp.einsum(
        "axfv,axfz->vxz", attention_probs.astype(BF), grad_attended_mix, preferred_element_type=F32
    )
    return (grad_queries, grad_key_rows, grad_values)


def gates_of(logits, routes):
    experts = logits.shape[1]
    named = jnp.any(routes[:, :, None] == jnp.arange(experts, dtype=jnp.int32), axis=1)
    masked = jnp.where(named, logits, -jnp.inf)
    top = jnp.max(masked, axis=1, keepdims=True)
    weights = jnp.where(named, jnp.exp(masked - top), 0.0)
    return weights / jnp.sum(weights, axis=1, keepdims=True)


def plain_shards(
    tokens_in,
    block_order,
    routes,
    norm1_gain,
    w_query,
    key_weight,
    value_weight,
    query_gain,
    key_gain,
    w_out,
    norm2_gain,
    w_router,
    w_gate,
    w_up,
    w_down,
    cotangent,
):
    tok_count, model_width = tokens_in.shape
    head_size = query_gain.shape[0]
    local_heads = w_query.shape[1] // head_size
    local_kv = key_weight.shape[1] // head_size
    query_group_width = local_heads // local_kv
    seq_count = block_order.shape[0]
    devices, tp_size = lax.axis_size("ctx"), lax.axis_size("tp")
    links = Links()
    me, tp_me = lax.axis_index("ctx"), lax.axis_index("tp")
    rows = tok_count // tp_size
    block_len = tok_count // (2 * seq_count)
    experts = w_router.shape[1]
    own_experts, _, units = w_gate.shape
    hid = own_experts * units
    all_tok = devices * tok_count

    def own_rows(v):
        return lax.dynamic_slice_in_dim(v, tp_me * rows, rows, axis=0)

    cot_own = own_rows(cotangent)
    cot_all = lax.all_gather(cot_own, ("ctx", "tp"), axis=0, tiled=True)

    token_positions = positions_of(block_order, devices, block_len)
    query_pos = lax.dynamic_index_in_dim(token_positions, me, 0, keepdims=False)
    key_pos = jnp.transpose(token_positions, (1, 0, 2)).reshape(seq_count, devices * 2 * block_len)
    rotary_angles = angles_of(query_pos.reshape(-1), head_size)
    inputs = tokens_in.astype(F32)
    first_in = rms_norm(inputs, norm1_gain).astype(BF)
    query_raw = jnp.dot(first_in, w_query, preferred_element_type=F32)
    unrotated_key = jnp.dot(first_in, key_weight, preferred_element_type=F32)
    value_rows = jnp.dot(first_in, value_weight, preferred_element_type=F32).astype(BF)

    def rope_heads(raw_query, raw_key, gain_query, key_norm_gain):
        return (
            head_route_path(raw_query, gain_query, rotary_angles, local_heads),
            head_route_path(raw_key, key_norm_gain, rotary_angles, local_kv),
        )

    (query_rot, key_rot), rope_back = jax.vjp(
        rope_heads, query_raw, unrotated_key, query_gain, key_gain
    )
    query_rows = query_rot.astype(BF).reshape(
        seq_count, 2 * block_len, local_kv, query_group_width, head_size
    )
    kv_width = local_kv * head_size
    kv_own = jnp.concatenate([key_rot.astype(BF).reshape(tok_count, kv_width), value_rows], axis=1)
    kv_all = links.ag_ctx(kv_own)
    kv_seq = kv_all.reshape(devices, seq_count, 2 * block_len, 2, local_kv, head_size)
    kv_seq = kv_seq.transpose(3, 1, 0, 2, 4, 5).reshape(
        2, seq_count, devices * 2 * block_len, local_kv, head_size
    )
    key_full, value_full = kv_seq[0], kv_seq[1]
    attended_mix, log_total = lax.map(
        attend_forward, (query_rows, key_full, value_full, query_pos, key_pos)
    )
    attended = attended_mix.reshape(tok_count, local_heads * head_size).astype(BF)
    attn_part = jnp.dot(attended, w_out, preferred_element_type=F32).astype(BF)
    residual = own_rows(inputs) + links.rs_tp(attn_part)
    second_normed, second_back = jax.vjp(rms_norm, residual, norm2_gain)
    second_in = second_normed.astype(BF)
    extra = -(-2 * experts // 128) * 128
    gates = gates_of(jnp.dot(second_in, w_router, preferred_element_type=F32), own_rows(routes))
    gates_high = gates.astype(BF)
    gates_low = (gates - gates_high.astype(F32)).astype(BF)
    pad = jnp.zeros((rows, extra - 2 * experts), BF)
    second_all = links.ag_all(
        jnp.concatenate([second_in, gates_high, gates_low, pad], axis=1)
    )
    column = jnp.arange(extra, dtype=jnp.int32)[:, None]
    named = me * own_experts + jnp.arange(hid, dtype=jnp.int32)[None, :] // units
    pick = (column == named).astype(BF)
    spread = pick + (column == named + experts).astype(BF)
    gate_mat = w_gate.transpose(0, 2, 1).reshape(hid, model_width)
    up_mat = w_up.transpose(0, 2, 1).reshape(hid, model_width)
    down_mat = w_down.reshape(hid, model_width)
    part, gate_low, up_low, hidden_low = expert_blocks(
        second_all, cot_all, gate_mat, up_mat, down_mat, spread, pick.T
    )
    sums_own = links.rs_all(part)
    out_own = sums_own[:, :model_width]
    entry_own = sums_own[:, model_width:]
    gate_total = entry_own[:, model_width : model_width + experts]
    grad_logits = (
        gates * (gate_total - jnp.sum(gates * gate_total, axis=1, keepdims=True))
    ).astype(BF)
    grad_second = entry_own[:, :model_width] + dotf(grad_logits, w_router, ((1,), (1,)))
    grad_resid_norm, grad_norm2 = second_back(grad_second)
    grad_residual = cot_own.astype(F32) + grad_resid_norm
    pad = jnp.zeros((rows, -experts % 128), BF)
    back_all = links.ag_tp(
        jnp.concatenate([grad_residual.astype(BF), grad_logits, pad], axis=1)
    )
    grad_attn_low = back_all[:, :model_width]
    second_own = lax.dynamic_slice(second_all, (me * tok_count, 0), (tok_count, model_width))
    router_part = dotf(second_own, back_all[:, model_width:], ((0,), (0,)))
    grad_out = dotf(attended, grad_attn_low, ((0,), (0,)))
    grad_mixed = dotf(grad_attn_low, w_out, ((1,), (1,))).astype(BF)
    grad_mixed = grad_mixed.reshape(
        seq_count, 2 * block_len, local_kv, query_group_width, head_size
    )
    grad_query_seq, grad_key_seq, grad_value_seq = lax.map(
        attend_backward,
        (query_rows, key_full, value_full, query_pos, key_pos, grad_mixed, log_total),
    )
    grad_kv = jnp.stack([grad_key_seq, grad_value_seq]).astype(BF)
    grad_kv = grad_kv.reshape(2, seq_count, devices, 2 * block_len, kv_width)
    grad_kv = grad_kv.transpose(2, 1, 3, 0, 4).reshape(all_tok, 2 * kv_width)
    grad_kv_own = links.rs_ctx(grad_kv)
    grad_query_rot = grad_query_seq.reshape(tok_count, local_heads, head_size)
    grad_key_rot = grad_kv_own[:, :kv_width].reshape(tok_count, local_kv, head_size)
    grad_query_raw, grad_key_raw, grad_qgain, grad_kgain = rope_back(
        (grad_query_rot, grad_key_rot)
    )
    query_low = grad_query_raw.astype(BF)
    key_low = grad_key_raw.astype(BF)
    value_low = grad_kv_own[:, kv_width:].astype(BF)
    first_part = dotf(query_low, w_query, ((1,), (1,)))
    first_part = first_part + dotf(key_low, key_weight, ((1,), (1,)))
    first_part = first_part + dotf(value_low, value_weight, ((1,), (1,)))
    grad_first = links.rs_tp(first_part.astype(BF))
    grad_first, gate_low = lax.optimization_barrier((grad_first, gate_low))
    grads = expert_grads(second_all, cot_all, gate_low, up_low, hidden_low, model_width)
    grad_gate, grad_up = (
        v.reshape(own_experts, units, model_width).transpose(0, 2, 1) for v in grads[:2]
    )
    grad_down = grads[2].reshape(own_experts, units, model_width)
    _, first_back = jax.vjp(rms_norm, own_rows(inputs), norm1_gain)
    grad_input_norm, grad_norm1 = first_back(grad_first)
    def over_ctx(v, dim):
        return lax.psum_scatter(v.astype(BF), "ctx", scatter_dimension=dim, tiled=True).astype(F32)

    grad_query = over_ctx(dotf(first_in, query_low, ((0,), (0,))), 0)
    kv_part = dotf(first_in, jnp.concatenate([key_low, value_low], axis=1), ((0,), (0,)))
    small = links.rs_ctx(jnp.concatenate([kv_part, router_part], axis=1).astype(BF))
    grad_key = small[:, :kv_width]
    grad_value = small[:, kv_width : 2 * kv_width]
    grad_router = small[:, 2 * kv_width : 2 * kv_width + experts]
    grad_out = over_ctx(grad_out, 1)
    vectors = [
        v.reshape(devices, -1) for v in (grad_norm1, grad_norm2, grad_qgain, grad_kgain)
    ]
    sizes = [v.shape[1] for v in vectors]
    pad = jnp.zeros((devices, -sum(sizes) % 1024), F32)
    packed = jnp.concatenate([*vectors, pad], axis=1).reshape(-1, 128)
    grad_input, layer_out, total = links.finish(
        (grad_residual + grad_input_norm).astype(BF), (residual + out_own).astype(BF), packed
    )
    total = total.reshape(-1)

    def piece_of(n):
        start = sum(sizes[:n])
        return total[start : start + sizes[n]]

    return (
        layer_out,
        grad_input,
        piece_of(0),
        grad_query,
        grad_key,
        grad_value,
        piece_of(2),
        piece_of(3),
        grad_out,
        piece_of(1),
        grad_router,
        grad_gate,
        grad_up,
        grad_down,
    )


def fast_shards(
    tokens_in,
    block_order,
    routes,
    norm1_gain,
    w_query,
    key_weight,
    value_weight,
    query_gain,
    key_gain,
    w_out,
    norm2_gain,
    w_router,
    w_gate,
    w_up,
    w_down,
    cotangent,
):
    tok_count, model_width = tokens_in.shape
    head_size = query_gain.shape[0]
    seq_count = block_order.shape[0]
    devices, tp_size = lax.axis_size("ctx"), lax.axis_size("tp")
    me, tp_me = lax.axis_index("ctx"), lax.axis_index("tp")
    rows = tok_count // tp_size
    block_len = tok_count // (2 * seq_count)
    experts = w_router.shape[1]
    own_experts, _, units = w_gate.shape
    hid = own_experts * units

    def own_rows(v):
        return lax.dynamic_slice_in_dim(v, tp_me * rows, rows, axis=0)

    def row(v):
        return v.reshape(1, -1)

    cot_own = own_rows(cotangent)

    token_positions = positions_of(block_order, devices, block_len)
    query_pos = lax.dynamic_index_in_dim(token_positions, me, 0, keepdims=False).reshape(-1)
    key_pos = jnp.transpose(token_positions, (1, 0, 2)).reshape(seq_count, -1).astype(F32)
    angles = angles_of(query_pos, head_size)
    cos = jnp.concatenate([jnp.cos(angles)] * 2, axis=1)
    sin = jnp.concatenate([-jnp.sin(angles), jnp.sin(angles)], axis=1)
    query_pos = jnp.broadcast_to(query_pos.astype(F32)[:, None], (tok_count, head_size))
    router_rows = w_router.T
    _, query_raw, key_raw, query_rot, kv_all, attended, logs, residual, gates, piece, first_cols = front(
        tokens_in, row(norm1_gain), w_query, key_weight, value_weight, row(query_gain),
        row(key_gain), cos, sin, query_pos, key_pos, w_out, row(norm2_gain), router_rows,
        routes.T, cotangent, 1,
    )

    extra = 4 * experts
    column = jnp.arange(extra, dtype=jnp.int32)[:, None]
    named = me * own_experts + jnp.arange(hid, dtype=jnp.int32)[None, :] // units
    pick = (column == named).astype(BF)
    spread = pick + (column == named + experts).astype(BF)
    gate_mat = w_gate.transpose(0, 2, 1).reshape(hid, model_width)
    up_mat = w_up.transpose(0, 2, 1).reshape(hid, model_width)
    down_mat = w_down.reshape(hid, model_width)
    all_rows, pair, hidden, gate_low, up_low, hidden_turned, gate_turned, up_turned = experts_forward(
        piece, gate_mat, up_mat, down_mat, spread, pick.T, 3
    )
    sums_own, attended_line = reduce_experts(
        hidden, gate_low, up_low, pair, down_mat, gate_mat, up_mat, attended, 6
    )
    layer_piece, grad_residual, grad_norm2, back_cols, query_low, grad_kv, qgain_part = middle(
        sums_own, residual, gates, cot_own, row(norm2_gain), router_rows, w_out, query_rot, kv_all,
        logs, query_raw, row(query_gain), cos, sin, query_pos, key_pos, 7,
    )

    line_tok = 4 * tok_count
    back_cols = back_cols.reshape(line_tok, -1)
    line_cols = model_width // 4
    out_part = dotf(
        attended_line.reshape(line_tok, -1), back_cols[:, :line_cols], ((0,), (0,))
    )
    second_line = all_rows.reshape(4, 2, tok_count, -1)
    second_line = lax.dynamic_slice(
        second_line, (0, me % 2, 0, me // 2 * line_cols), (4, 1, tok_count, line_cols)
    ).reshape(line_tok, line_cols)
    router_part = dotf(second_line, back_cols[:, line_cols:], ((0,), (0,)))
    per = model_width // devices // 128
    vectors = jnp.concatenate(
        [
            jnp.zeros((devices, per, 128), F32),
            grad_norm2.reshape(devices, per, 128),
            jnp.broadcast_to(jnp.sum(qgain_part, axis=0), (devices, 1, 128)),
            jnp.zeros((devices, 7 - 2 * per, 128), F32),
        ],
        axis=1,
    )
    grad_input, layer_out, grad_query, kv_grads, grad_out, grad_router, total = tail(
        grad_kv, query_low, key_raw, row(key_gain), cos, sin, w_query, key_weight, value_weight,
        tokens_in, row(norm1_gain), grad_residual, layer_piece, vectors,
        first_cols.reshape(line_tok, -1), out_part, router_part, 8,
    )
    grad_key = kv_grads[:, :head_size]
    grad_value = kv_grads[:, head_size:]
    total, gate_turned = lax.optimization_barrier((total, gate_turned))
    grads = expert_grads(all_rows, all_rows, gate_turned, up_turned, hidden_turned, model_width, model_width)
    grad_gate, grad_up = (
        v.reshape(own_experts, units, model_width).transpose(0, 2, 1) for v in grads[:2]
    )
    grad_down = grads[2].reshape(own_experts, units, model_width)
    share = head_size // devices

    def gain_of(n):
        return lax.dynamic_slice_in_dim(total[n], me * share, share, axis=0)

    return (
        layer_out,
        grad_input,
        total[:per].reshape(-1),
        grad_query,
        grad_key,
        grad_value,
        gain_of(2 * per),
        gain_of(7),
        grad_out,
        total[per : 2 * per].reshape(-1),
        grad_router[:, :experts],
        grad_gate,
        grad_up,
        grad_down,
    )


def solution(mesh):
    in_specs = (
        P("ctx", None),
        P(),
        P("ctx", None),
        P(),
        P(None, "tp"),
        P(None, "tp"),
        P(None, "tp"),
        P(),
        P(),
        P("tp", None),
        P(),
        P(),
        P("ctx", None, "tp"),
        P("ctx", None, "tp"),
        P("ctx", "tp", None),
        P("ctx", None),
    )
    out_specs = (
        P("ctx", None),
        P("ctx", None),
        P("ctx"),
        P("ctx", "tp"),
        P("ctx", "tp"),
        P("ctx", "tp"),
        P("ctx"),
        P("ctx"),
        P("tp", "ctx"),
        P("ctx"),
        P("ctx", None),
        P("ctx", None, "tp"),
        P("ctx", None, "tp"),
        P("ctx", "tp", None),
    )
    own = mesh.shape["ctx"] == 8 and mesh.shape["tp"] == 4
    shards = fast_shards if own else plain_shards
    return jax.shard_map(shards, mesh=mesh, in_specs=in_specs, out_specs=out_specs, check_vma=False)
```

```python
import math
import functools
import jax
import jax.numpy as jnp
from jax import lax
from jax.sharding import PartitionSpec as P
from jax.experimental import pallas as pl
from jax.experimental.pallas import tpu as pltpu
MESH=pl.DeviceIdType.MESH

def coords():
    ctx=lax.axis_index("ctx"); tp=lax.axis_index("tp")
    return ctx//2, ctx%2, tp//2, tp%2
def dev(z,x,y,c): return (z*2+x, y*2+c)
def pid(z,x,y,c): return (z*2+x)*4+y*2+c

def neighbours():
    z,x,y,c=coords()
    ax=x+(1-c)*(1-2*x); ay=y+c*(1-2*y)
    bx=x+c*(1-2*x); by=y+(1-c)*(1-2*y)
    return z,x,y,c,ax,ay,bx,by

def barrier_all():
    z,x,y,c=coords()
    b=pltpu.get_barrier_semaphore()
    def sig(d): pl.semaphore_signal(b,inc=1,device_id=d,device_id_type=MESH)
    sig(dev(z,1-x,y,c)); sig(dev(z,x,1-y,c)); sig(dev(z,x,y,1-c))
    @pl.when(z<3)
    def _(): sig(dev(z+1,x,y,c))
    @pl.when(z>0)
    def _(): sig(dev(z-1,x,y,c))
    pl.semaphore_wait(b,5-(3-z)//3-z//3)

class Gather:
    def __init__(self, own_ref, out_ref, cols, send, recv):
        self.own, self.out, self.cols, self.send, self.recv = own_ref, out_ref, cols, send, recv
        self.rows = own_ref.shape[0]
        z, x, y, c, ax, ay, bx, by = neighbours()
        self.at_me = (z, x, y, c, ax, ay, bx, by)
        self.up, self.down = dev(z + 1, x, y, c), dev(z - 1, x, y, c)
        self.A, self.B, self.C = dev(z, ax, ay, c), dev(z, bx, by, c), dev(z, x, y, 1 - c)

    def place(self, p):
        return self.out.at[pl.ds(pl.multiple_of(p * self.rows, self.rows), self.rows), self.cols]

    def copy(self, p, to, k, own=False):
        return pltpu.make_async_remote_copy(
            src_ref=self.own.at[:, self.cols] if own else self.place(p), dst_ref=self.place(p),
            send_sem=self.send.at[k, p], recv_sem=self.recv.at[p], device_id=to, device_id_type=MESH)

    def wait(self, p):
        self.copy(p, self.C, 4).wait_recv()

    def start(self):
        z, x, y, c = self.at_me[:4]
        me = pid(z, x, y, c)
        @pl.when(z < 3)
        def _():
            self.copy(me, self.up, 0, True).start()

        @pl.when(z > 0)
        def _():
            self.copy(me, self.down, 1, True).start()

        for to, k in ((self.A, 2), (self.B, 3), (self.C, 4)):
            self.copy(me, to, k, True).start()

    def from_line(self, zz):
        z, x, y, c = self.at_me[:4]
        p = pid(zz, x, y, c)
        self.wait(p)

        @pl.when((zz < z) & (z < 3))
        def _():
            self.copy(p, self.up, 0).start()

        @pl.when((zz > z) & (z > 0))
        def _():
            self.copy(p, self.down, 1).start()

        for to, k in ((self.A, 2), (self.B, 3), (self.C, 4)):
            self.copy(p, to, k).start()

    def from_a(self, zz):
        z, x, y, c, ax, ay, bx, by = self.at_me

        p = pid(zz, ax, ay, c)
        self.wait(p)
        self.copy(p, self.B, 3).start()
        self.copy(p, self.C, 4).start()

    def from_b(self, zz, xx, yy):
        c = self.at_me[3]

        p = pid(zz, xx, yy, c)
        self.wait(p)
        self.copy(p, self.C, 4).start()

    def finish(self):
        z, x, y, c, ax, ay, bx, by = self.at_me

        def one(zz, carry):
            p = pid(zz, x, y, c)

            @pl.when((z < 3) & (zz <= z))
            def _():
                self.copy(p, self.up, 0).wait_send()

            @pl.when((z > 0) & (zz >= z))
            def _():
                self.copy(p, self.down, 1).wait_send()

            for to, k in ((self.A, 2), (self.B, 3), (self.C, 4)):
                self.copy(p, to, k).wait_send()
            p = pid(zz, ax, ay, c)
            self.copy(p, self.B, 3).wait_send()
            self.copy(p, self.C, 4).wait_send()
            self.copy(pid(zz, bx, by, c), self.C, 4).wait_send()
            self.copy(pid(zz, 1 - x, 1 - y, c), self.C, 4).wait_send()
            return carry

        lax.fori_loop(0, 4, one, 0)


def far_z(z, k):
    half = z // 2
    near = z + half * (3 - 2 * z)
    place = 3 - k + (k // 2) * (2 * (k % 2) - 1) * near
    return place + half * (3 - 2 * place)


def reduce_kernel(
    hs_ref, gl_ref, ul_ref, pair_ref, wd_ref, wg_ref, wu_ref, att_ref,
    out_ref, line_ref,
    acc, cbuf, bbuf, abuf, zbuf, blk, mats, low, pair,
    csend, crecv, bsend, brecv, asend, arecv, zsend, zrecv, msem, lsem, psem, nsem, nsend, nrecv,
):
    f32 = jnp.float32
    rows = out_ref.shape[0]
    width = wd_ref.shape[1]
    z, x, y, c, ax, ay, bx, by = neighbours()
    dx, dy = 1 - x, 1 - y
    A, B, C = dev(z, ax, ay, c), dev(z, bx, by, c), dev(z, x, y, 1 - c)
    up, down = dev(z + 1, x, y, c), dev(z - 1, x, y, c)
    tok = 4 * rows

    def q(zz, xx, yy):
        return zz * 4 + xx * 2 + yy

    def place_of(u):
        return far_z(z, u // 2), (u % 2) * (2 * x - 1) + 1 - x

    def loads(u):
        zz, xx = place_of(u)
        span = pl.ds(pl.multiple_of((zz * 2 + xx) * tok, tok), tok)
        slot = u % 2
        return [
            pltpu.make_async_copy(r.at[span], low.at[slot, n], lsem.at[slot, n])
            for n, r in enumerate((hs_ref, gl_ref, ul_ref))
        ] + [pltpu.make_async_copy(pair_ref.at[span], pair.at[slot], psem.at[slot])]

    def part_rows(slot, yy, cc):
        return blk.at[slot, pl.ds(pl.multiple_of((yy * 2 + cc) * rows, rows), rows)]

    def ccopy(zz, xx, yy, slot):
        i = q(zz, xx, yy)
        return pltpu.make_async_remote_copy(
            src_ref=part_rows(slot, yy, 1 - c), dst_ref=cbuf.at[i], send_sem=csend.at[slot, yy],
            recv_sem=crecv.at[i], device_id=C, device_id_type=MESH)

    weights = [pltpu.make_async_copy(r, mats.at[n], msem.at[n]) for n, r in enumerate((wd_ref, wg_ref, wu_ref))]
    for cp in weights:
        cp.start()
    for cp in loads(0):
        cp.start()

    def products(u):
        slot = u % 2
        zz, xx = place_of(u)
        for cp in loads(u):
            cp.wait()

        @pl.when(u < 7)
        def _():
            for cp in loads(u + 1):
                cp.start()

        @pl.when(u > 1)
        def _():
            for yy in range(2):
                ccopy(zz, xx, yy, slot).wait_send()

        blk[slot, :, :width] = nn(low[slot, 0], mats[0]).astype(blk.dtype)
        @pl.when(u == 0)
        def _():
            weights[1].wait()
            weights[2].wait()

        blk[slot, :, width : 2 * width] = (
            nn(low[slot, 1], mats[1]) + nn(low[slot, 2], mats[2])
        ).astype(blk.dtype)
        blk[slot, :, 2 * width :] = pair[slot]
        for yy in range(2):
            ccopy(zz, xx, yy, slot).start()
        for yy in range(2):
            acc[q(zz, xx, yy)] = part_rows(slot, yy, c)[...]

    def bcopy(zz, far):
        i = zz + 4 * far
        place = q(zz, dx, dy) if far else q(zz, bx, by)
        return pltpu.make_async_remote_copy(
            src_ref=acc.at[place], dst_ref=bbuf.at[i], send_sem=bsend.at[i],
            recv_sem=brecv.at[i], device_id=B, device_id_type=MESH)

    def acopy(zz):
        return pltpu.make_async_remote_copy(
            src_ref=acc.at[q(zz, ax, ay)], dst_ref=abuf.at[zz], send_sem=asend.at[zz],
            recv_sem=arecv.at[zz], device_id=A, device_id_type=MESH)

    def zcopy(zz, to, slot):
        return pltpu.make_async_remote_copy(
            src_ref=acc.at[q(zz, x, y)], dst_ref=zbuf.at[slot], send_sem=zsend.at[zz],
            recv_sem=zrecv.at[slot], device_id=to, device_id_type=MESH)

    def plus_c(zz, xx, yy):
        ccopy(zz, xx, yy, 0).wait_recv()
        i = q(zz, xx, yy)
        return acc[i].astype(f32) + cbuf[i].astype(f32)

    def stage_b(k, far):
        zz = far_z(z, k)
        xx, yy = (dx, dy) if far else (bx, by)
        acc[q(zz, xx, yy)] = plus_c(zz, xx, yy).astype(acc.dtype)
        bcopy(zz, far).start()

    def stage_a(k):
        zz = far_z(z, k)
        value = plus_c(zz, ax, ay)
        bcopy(zz, 1).wait_recv()
        acc[q(zz, ax, ay)] = (value + bbuf[zz + 4].astype(f32)).astype(acc.dtype)
        acopy(zz).start()

    def stage_z(k):
        zz = far_z(z, k)
        place = q(zz, x, y)
        value = plus_c(zz, x, y)
        bcopy(zz, 0).wait_recv()
        acopy(zz).wait_recv()
        value = value + bbuf[zz].astype(f32) + abuf[zz].astype(f32)

        @pl.when(zz != z)
        def _():
            acc[place] = value.astype(acc.dtype)

            @pl.when((zz > z) & (z > 0))
            def _():
                zcopy(zz, up, zz).wait_recv()
                acc[place] = (acc[place].astype(f32) + zbuf[zz].astype(f32)).astype(acc.dtype)

            @pl.when((zz < z) & (z < 3))
            def _():
                zcopy(zz, down, zz).wait_recv()
                acc[place] = (acc[place].astype(f32) + zbuf[zz].astype(f32)).astype(acc.dtype)

            @pl.when(zz > z)
            def _():
                zcopy(zz, up, zz).start()

            @pl.when((zz < z) & (zz != z - 1))
            def _():
                zcopy(zz, down, zz).start()

            @pl.when(zz == z - 1)
            def _():
                zcopy(zz, down, 4).start()

        @pl.when(zz == z)
        def _():
            out_ref[...] = value

            @pl.when(z > 0)
            def _():
                zcopy(z, up, z).wait_recv()
                out_ref[...] += zbuf[z].astype(f32)

            @pl.when(z < 3)
            def _():
                zcopy(z, down, 4).wait_recv()
                out_ref[...] += zbuf[4].astype(f32)

    line = Line(lambda zz: line_ref.at[zz], nsend, nrecv, att_ref)
    mine = pltpu.make_async_copy(att_ref, line_ref.at[z], nsem)
    mine.start()
    barrier_all()
    line.start()
    weights[0].wait()

    def step(u, carry):
        @pl.when(u == 1)
        def _():
            stage_b(0, 1)

        @pl.when(u < 8)
        def _():
            products(u)

        for d in (1, 2, 3):
            @pl.when(u == 2 * d + 1)
            def _():
                line.pass_on(d)

        k = (u - 1) // 2

        @pl.when((u > 1) & (u < 9) & (u % 2 == 1))
        def _():
            stage_b(k, 1)

        @pl.when((u > 0) & (u < 9) & (u % 2 == 0))
        def _():
            stage_b(k, 0)

        @pl.when((u >= 5) & (u < 13) & (u % 2 == 1))
        def _():
            stage_a((u - 5) // 2)

        @pl.when((u >= 8) & (u % 2 == 0))
        def _():
            stage_z((u - 8) // 2)

        return carry

    lax.fori_loop(0, 15, step, 0)
    mine.wait()
    line.finish()
    for slot in range(2):
        for yy in range(2):
            ccopy(z, x, yy, slot).wait_send()

    def last(zz, carry):
        bcopy(zz, 1).wait_send()
        bcopy(zz, 0).wait_send()
        acopy(zz).wait_send()

        @pl.when(zz != z)
        def _():
            zcopy(zz, up, zz).wait_send()

        return carry

    lax.fori_loop(0, 4, last, 0)


def reduce_experts(hs, gl, ul, pair, wd, wg, wu, att, cid):
    n, hid = hs.shape
    width = wd.shape[1]
    rows = n // 32
    w = 2 * width + pair.shape[1]
    dma = pltpu.SemaphoreType.DMA
    bf = jnp.bfloat16

    def pieces(k):
        return pltpu.VMEM((k, rows, w), bf)

    anywhere = pl.BlockSpec(memory_space=pl.ANY)
    return pl.pallas_call(
        reduce_kernel,
        in_specs=[anywhere] * 8,
        out_specs=[pl.BlockSpec(memory_space=pltpu.VMEM), anywhere],
        out_shape=[
            jax.ShapeDtypeStruct((rows, w), jnp.float32), jax.ShapeDtypeStruct((4, *att.shape), bf),
        ],
        scratch_shapes=[
            pieces(16), pieces(16), pieces(8), pieces(4), pieces(5),
            pltpu.VMEM((2, 4 * rows, w), bf),
            pltpu.VMEM((3, hid, width), bf),
            pltpu.VMEM((2, 3, 4 * rows, hid), bf),
            pltpu.VMEM((2, 4 * rows, pair.shape[1]), bf),
            dma((2, 2)), dma((16,)), dma((8,)), dma((8,)), dma((4,)), dma((4,)),
            dma((4,)), dma((5,)), dma((3,)), dma((2, 3)), dma((2,)), dma, dma((2, 4)), dma((4,)),
        ],
        compiler_params=pltpu.CompilerParams(
            collective_id=cid, has_side_effects=True, vmem_limit_bytes=56 * 2**20
        ),
        cost_estimate=pl.CostEstimate(
            flops=6 * n * width * hid, bytes_accessed=10 * n * width, transcendentals=0
        ),
        name="reduce_experts",
    )(hs, gl, ul, pair, wd, wg, wu, att)


def barrier_wide():
    z, x, y, c = coords()
    ctx, tp = lax.axis_index("ctx"), lax.axis_index("tp")
    bar = pltpu.get_barrier_semaphore()
    for i in range(1, 8):
        pl.semaphore_signal(bar, inc=1, device_id=((ctx + i) % 8, tp), device_id_type=MESH)
    for to in (dev(z, x, 1 - y, c), dev(z, x, y, 1 - c), dev(z, x, 1 - y, 1 - c)):
        pl.semaphore_signal(bar, inc=1, device_id=to, device_id_type=MESH)
    pl.semaphore_wait(bar, 10)


class Columns:
    def __init__(self, src, buf, send, recv, tsend, trecv):
        self.src, self.buf, self.send, self.recv = src, buf, send, recv
        self.tsend, self.trecv = tsend, trecv
        self.tp = lax.axis_index("tp")
        z, x, y, c = coords()
        self.z, self.x, self.y, self.c = z, x, y, c
        self.Y, self.C = dev(z, x, 1 - y, c), dev(z, x, y, 1 - c)
        self.mine, self.by_y, self.by_c, self.by_d = y * 2 + c, (1 - y) * 2 + c, y * 2 + 1 - c, (1 - y) * 2 + 1 - c

    def push(self, i):
        to = (self.z + i) % 4
        return pltpu.make_async_remote_copy(
            src_ref=self.src.at[to], dst_ref=self.buf.at[self.z, self.tp],
            send_sem=self.send.at[i], recv_sem=self.recv.at[i],
            device_id=dev(to, self.x, self.y, self.c), device_id_type=MESH)

    def over(self, part, to, k):
        return pltpu.make_async_remote_copy(
            src_ref=self.buf.at[:, part], dst_ref=self.buf.at[:, part], send_sem=self.tsend.at[k],
            recv_sem=self.trecv.at[part], device_id=to, device_id_type=MESH)

    def start(self):
        for i in range(1, 4):
            self.push(i).start()
        self.buf[self.z, self.tp] = self.src[self.z]

    def exchange(self):
        for i in range(1, 4):
            self.push(i).wait_recv()
        self.over(self.mine, self.Y, 0).start()
        self.over(self.mine, self.C, 1).start()

    def forward(self):
        self.over(self.by_y, self.Y, 0).wait_recv()
        self.over(self.by_y, self.C, 2).start()

    def finish(self):
        self.over(self.by_c, self.C, 1).wait_recv()
        self.over(self.by_d, self.C, 2).wait_recv()
        for i in range(1, 4):
            self.push(i).wait_send()
        self.over(self.mine, self.Y, 0).wait_send()
        self.over(self.mine, self.C, 1).wait_send()
        self.over(self.by_y, self.C, 2).wait_send()


class Line:
    def __init__(self, place, send, recv, first=None):
        self.place, self.send, self.recv, self.first = place, send, recv, first
        z, x, y, c = coords()
        self.z = z
        self.up, self.down = dev(z + 1, x, y, c), dev(z - 1, x, y, c)

    def copy(self, zz, to, k, own=False):
        src = self.first if own and self.first is not None else self.place(zz)
        return pltpu.make_async_remote_copy(
            src_ref=src, dst_ref=self.place(zz), send_sem=self.send.at[k, zz],
            recv_sem=self.recv.at[zz], device_id=to, device_id_type=MESH)

    def start(self):
        @pl.when(self.z < 3)
        def _():
            self.copy(self.z, self.up, 0, True).start()

        @pl.when(self.z > 0)
        def _():
            self.copy(self.z, self.down, 1, True).start()

    def pass_on(self, d):
        z = self.z

        @pl.when(z - d >= 0)
        def _():
            self.copy(z - d, self.up, 0).wait_recv()

            @pl.when(z < 3)
            def _():
                self.copy(z - d, self.up, 0).start()

        @pl.when(z + d <= 3)
        def _():
            self.copy(z + d, self.down, 1).wait_recv()

            @pl.when(z > 0)
            def _():
                self.copy(z + d, self.down, 1).start()

    def finish(self):
        z = self.z
        for zz in range(4):
            @pl.when((z < 3) & (zz <= z))
            def _():
                self.copy(zz, self.up, 0).wait_send()

            @pl.when((z > 0) & (zz >= z))
            def _():
                self.copy(zz, self.down, 1).wait_send()


class Spread:
    def __init__(self, place, send, recv, first=None):
        self.place, self.send, self.recv, self.first = place, send, recv, first
        z, x, y, c = coords()
        self.z, self.x = z, x
        self.X = dev(z, 1 - x, y, c)
        self.up, self.down = dev(z + 1, x, y, c), dev(z - 1, x, y, c)
        self.me = z * 2 + x

    def copy(self, p, to, k, own=False):
        src = self.first if own and self.first is not None else self.place(p)
        return pltpu.make_async_remote_copy(
            src_ref=src, dst_ref=self.place(p), send_sem=self.send.at[k, p],
            recv_sem=self.recv.at[p], device_id=to, device_id_type=MESH)

    def start_x(self):
        self.copy(self.me, self.X, 2, True).start()

    def start_z(self):
        @pl.when(self.z < 3)
        def _():
            self.copy(self.me, self.up, 0, True).start()

        @pl.when(self.z > 0)
        def _():
            self.copy(self.me, self.down, 1, True).start()

    def pass_on(self, d):
        z, x = self.z, self.x

        @pl.when(z - d >= 0)
        def _():
            p = (z - d) * 2 + x
            self.copy(p, self.X, 2).wait_recv()

            @pl.when(z < 3)
            def _():
                self.copy(p, self.up, 0).start()

            self.copy(p, self.X, 2).start()

        @pl.when(z + d <= 3)
        def _():
            p = (z + d) * 2 + x
            self.copy(p, self.X, 2).wait_recv()

            @pl.when(z > 0)
            def _():
                self.copy(p, self.down, 1).start()

            self.copy(p, self.X, 2).start()

    def arrive(self):
        for zz in range(4):
            self.copy(zz * 2 + 1 - self.x, self.X, 2).wait_recv()

    def finish(self):
        z, x = self.z, self.x
        for zz in range(4):
            p = zz * 2 + x

            @pl.when((z < 3) & (zz <= z))
            def _():
                self.copy(p, self.up, 0).wait_send()

            @pl.when((z > 0) & (zz >= z))
            def _():
                self.copy(p, self.down, 1).wait_send()

            self.copy(p, self.X, 2).wait_send()


def row_norm(v):
    return lax.rsqrt(jnp.mean(v * v, axis=1, keepdims=True) + 1e-06)


def turn(v, cos, sin):
    return v * cos + pltpu.roll(v, v.shape[1] // 2, 1) * sin


def turn_back(v, cos, sin):
    return v * cos - pltpu.roll(v, v.shape[1] // 2, 1) * sin


def front_kernel(
    x_ref, g1_in, wq_ref, wk_ref, wv_ref, qg_in, kg_in, cos_ref, sin_ref, qpos_ref, kpos_ref,
    wo_ref, g2_in, wr_in, routes_in, cot_ref,
    first_ref, qraw_ref, kraw_ref, qrot_ref, kv_ref, att_ref, log_ref, res_ref, gates_ref, piece_ref, cols_ref,
    xs, g1_ref, qg_ref, kg_ref, g2_ref, wr_ref, routes_ref, wk, wv, turned, wq, wo, part, cbuf, ybuf, stage, csrc,
    wsem, ksend, krecv, csend, crecv, ysend, yrecv, psend, precv, tsend, trecv,
):
    f32, bf = jnp.float32, jnp.bfloat16
    z, x, y, c = coords()
    rows = res_ref.shape[0]
    experts = wr_ref.shape[0]
    head = qg_ref.shape[1]
    heads = wq_ref.shape[1] // head
    half = x_ref.shape[0] // 2
    fetched = [
        pltpu.make_async_copy(src, dst, wsem.at[n])
        for n, (src, dst) in enumerate((
            (x_ref, xs), (g1_in, g1_ref), (qg_in, qg_ref), (kg_in, kg_ref), (g2_in, g2_ref),
            (wr_in, wr_ref), (routes_in, routes_ref), (wk_ref, wk), (wv_ref, wv), (wq_ref, wq), (wo_ref, wo),
        ))
    ]
    for cp in fetched:
        cp.start()
    wqc, woc = fetched[9:]
    own = pl.ds(pl.multiple_of((y * 2 + c) * rows, rows), rows)
    Y, C = dev(z, x, 1 - y, c), dev(z, x, y, 1 - c)
    barrier_wide()
    cotc = pltpu.make_async_copy(cot_ref.at[own], piece_ref.at[:, x_ref.shape[1] : 2 * x_ref.shape[1]], wsem.at[11])
    cotc.start()
    for cp in fetched[:9]:
        cp.wait()
    turned[...] = routes_ref[...].T
    value = xs[...].astype(f32)
    first = (value * row_norm(value) * g1_ref[...]).astype(bf)
    first_ref[...] = first
    cos, sin = cos_ref[...], sin_ref[...]
    kraw = nn(first, wk[...])
    kraw_ref[...] = kraw
    krot = turn(kraw * row_norm(kraw) * kg_ref[...], cos, sin).astype(bf)
    vrow = nn(first, wv[...]).astype(bf)
    me = z * 2 + x
    for s in range(2):
        kv_ref[s, me] = krot[s * half : (s + 1) * half]
        kv_ref[2 + s, me] = vrow[s * half : (s + 1) * half]

    keys_out = Spread(lambda p: kv_ref.at[:, p], ksend, krecv)
    keys_out.start_z()
    keys_out.start_x()

    wqc.wait()
    qraw_ref[...] = nn(first, wq[...])
    keys_out.pass_on(1)

    def rope_head(h, carry):
        lanes = pl.ds(pl.multiple_of(h * head, head), head)
        raw = qraw_ref[:, lanes]
        rot = turn(raw * row_norm(raw) * qg_ref[...], cos_ref[...], sin_ref[...]).astype(bf)
        qrot_ref[h] = rot[:half]
        qrot_ref[heads + h] = rot[half:]
        return carry

    lax.fori_loop(0, heads // 2, rope_head, 0)
    keys_out.pass_on(2)
    lax.fori_loop(heads // 2, heads, rope_head, 0)
    keys_out.pass_on(3)
    keys_out.arrive()
    width = first.shape[1]
    per = width // 4
    for i in range(4):
        csrc[i] = first_ref[own, i * per : (i + 1) * per]
    blocks = Columns(csrc, cols_ref, psend, precv, tsend, trecv)
    blocks.start()

    scale = 1.0 / math.sqrt(head)

    group = 4

    def attend(i, carry):
        s = i // (heads // group)
        h = i % (heads // group) * group
        span = pl.ds(pl.multiple_of(s * half, half), half)
        keys = kv_ref[s].reshape(8 * half, head)
        vals = kv_ref[2 + s].reshape(8 * half, head)
        query = qrot_ref[pl.ds(i * group, group)].reshape(group * half, head)
        scores = (nt(query, keys) * scale).reshape(group, half, 8 * half)
        allowed = qpos_ref[span, :1] >= kpos_ref[pl.ds(s, 1), :]
        scores = jnp.where(allowed[None], scores, -1e9).reshape(group * half, 8 * half)
        top = jnp.max(scores, axis=1, keepdims=True)
        weights = jnp.exp(scores - top)
        total = jnp.sum(weights, axis=1, keepdims=True)
        probs = (weights * (1.0 / total)).astype(bf)
        mixed = nn(probs, vals).astype(bf)
        logs = jnp.broadcast_to(top + jnp.log(total), (group * half, head))
        log_ref[pl.ds(i * group, group)] = logs.reshape(group, half, head)
        for g in range(group):
            lanes = pl.ds(pl.multiple_of((h + g) * head, head), head)
            att_ref[span, lanes] = mixed[g * half : (g + 1) * half]
        @pl.when(i == steps // 2 - 1)
        def _():
            blocks.exchange()
        return carry

    steps = 2 * heads // group
    lax.fori_loop(0, steps, attend, 0)
    blocks.forward()
    woc.wait()

    def at(yy, cc):
        return part.at[pl.ds(pl.multiple_of((yy * 2 + cc) * rows, rows), rows)]

    def project(yy):
        span = pl.ds(pl.multiple_of(yy * 2 * rows, 2 * rows), 2 * rows)
        part[span] = nn(att_ref[span], wo[...]).astype(bf)

    def ccopy(yy):
        return pltpu.make_async_remote_copy(
            src_ref=at(yy, 1 - c), dst_ref=cbuf.at[yy], send_sem=csend.at[yy],
            recv_sem=crecv.at[yy], device_id=C, device_id_type=MESH)

    project(1 - y)
    ccopy(1 - y).start()
    project(y)
    ccopy(y).start()
    ccopy(1 - y).wait_recv()
    stage[...] = (at(1 - y, c)[...].astype(f32) + cbuf[1 - y].astype(f32)).astype(bf)
    yc = pltpu.make_async_remote_copy(
        src_ref=stage, dst_ref=ybuf, send_sem=ysend, recv_sem=yrecv, device_id=Y, device_id_type=MESH)
    yc.start()
    ccopy(y).wait_recv()
    res = xs[own].astype(f32) + (at(y, c)[...].astype(f32) + cbuf[y].astype(f32))
    lane = lax.broadcasted_iota(jnp.int32, (rows, 4 * experts), 1)
    named = jnp.zeros((rows, 4 * experts), jnp.bool_)
    routes = turned[own]
    for k in range(routes.shape[1]):
        named = named | (lane % experts == routes[:, k : k + 1])
    yc.wait_recv()
    res = res + ybuf[...].astype(f32)
    res_ref[...] = res
    second = (res * row_norm(res) * g2_ref[...]).astype(bf)
    piece_ref[:, :width] = second
    logits = nt(second, wr_ref[...])
    logits = jnp.concatenate([logits, logits, jnp.zeros((rows, 2 * experts), f32)], axis=1)
    masked = jnp.where(named & (lane < 2 * experts), logits, -1e30)
    top = jnp.max(masked, axis=1, keepdims=True)
    weights = jnp.where(named & (lane < 2 * experts), jnp.exp(masked - top), 0.0)
    total = jnp.sum(jnp.where(lane < experts, weights, 0.0), axis=1, keepdims=True)
    gates = weights / total
    high = gates.astype(bf)
    low = (gates - high.astype(f32)).astype(bf)
    gates_ref[...] = jnp.where(lane < experts, gates, 0.0)
    piece_ref[:, 2 * width :] = jnp.where(lane < experts, high, low)

    yc.wait_send()
    ccopy(0).wait_send()
    ccopy(1).wait_send()
    blocks.finish()
    keys_out.finish()
    cotc.wait()


def front(x, g1, wq, wk, wv, qg, kg, cos, sin, qpos, kpos, wo, g2, wr, routes, cot, cid):
    tok, width = x.shape
    head = qg.shape[1]
    cols = wq.shape[1]
    heads = cols // head
    rows, half = tok // 4, tok // 2
    f32, bf = jnp.float32, jnp.bfloat16
    dma = pltpu.SemaphoreType.DMA
    vm, anywhere = pl.BlockSpec(memory_space=pltpu.VMEM), pl.BlockSpec(memory_space=pl.ANY)

    def out(shape, kind):
        return jax.ShapeDtypeStruct(shape, kind)

    return pl.pallas_call(
        front_kernel,
        in_specs=[anywhere] * 7 + [vm] * 4 + [anywhere] * 5,
        out_specs=[vm] * 11,
        out_shape=[
            out((tok, width), bf), out((tok, cols), f32), out((tok, head), f32),
            out((2 * heads, half, head), bf), out((4, 8, half, head), bf), out((tok, cols), bf),
            out((2 * heads, half, head), f32), out((rows, width), f32), out((rows, 128), f32),
            out((rows, 2 * width + 128), bf), out((4, 4, rows, width // 4), bf),
        ],
        scratch_shapes=[
            pltpu.VMEM((tok, width), bf), pltpu.VMEM(g1.shape, f32), pltpu.VMEM(qg.shape, f32),
            pltpu.VMEM(kg.shape, f32), pltpu.VMEM(g2.shape, f32), pltpu.VMEM(wr.shape, bf),
            pltpu.VMEM(routes.shape, jnp.int32), pltpu.VMEM((width, head), bf), pltpu.VMEM((width, head), bf),
            pltpu.VMEM(routes.shape[::-1], jnp.int32),
            pltpu.VMEM((width, cols), bf), pltpu.VMEM((cols, width), bf), pltpu.VMEM((tok, width), bf),
            pltpu.VMEM((2, rows, width), bf), pltpu.VMEM((rows, width), bf), pltpu.VMEM((rows, width), bf),
            pltpu.VMEM((4, rows, width // 4), bf),
            dma((12,)), dma((3, 8)), dma((8,)), dma((2,)), dma((2,)), dma, dma,
            dma((4,)), dma((4,)), dma((3,)), dma((4,)),
        ],
        compiler_params=pltpu.CompilerParams(
            collective_id=cid, has_side_effects=True, vmem_limit_bytes=52 * 2**20
        ),
        name="front",
    )(x, g1, wq, wk, wv, qg, kg, cos, sin, qpos, kpos, wo, g2, wr, routes, cot)


def middle_kernel(
    sums_ref, res_ref, gates_ref, cot_in, g2_in, wr_in, wo_ref, qrot_ref, kv_ref, log_ref,
    qraw_ref, qg_in, cos_ref, sin_ref, qpos_ref, kpos_ref,
    layer_ref, gres_ref, gn2_ref, cols_ref, qlow_ref, dkv_ref, qgain_ref,
    cot_ref, g2_ref, wr_ref, qg_ref, wo, back, mixed, dk, dv, csrc, wsem, send, recv, psend, precv, tsend, trecv,
):
    f32, bf = jnp.float32, jnp.bfloat16
    z, x, y, c = coords()
    rows, width = res_ref.shape
    experts = wr_in.shape[0]
    head = qg_in.shape[1]
    heads = qraw_ref.shape[1] // head
    half = qraw_ref.shape[0] // 2
    mine = pl.ds(pl.multiple_of((y * 2 + c) * rows, rows), rows)
    fetched = [
        pltpu.make_async_copy(src, dst, wsem.at[n])
        for n, (src, dst) in enumerate((
            (cot_in.at[mine], cot_ref), (g2_in, g2_ref), (wr_in, wr_ref), (qg_in, qg_ref), (wo_ref, wo)))
    ]
    for item in fetched:
        item.start()
    woc = fetched[4]
    barrier_wide()
    Y, C = dev(z, x, 1 - y, c), dev(z, x, y, 1 - c)

    def at(yy, cc):
        return back.at[pl.ds(pl.multiple_of((yy * 2 + cc) * rows, rows), rows)]

    for item in fetched[:4]:
        item.wait()
    res = res_ref[...]
    layer_ref[...] = (res + sums_ref[:, :width]).astype(bf)
    gates = gates_ref[...]
    pair = sums_ref[:, 2 * width :]
    glog = (gates * (pair - jnp.sum(gates * pair, axis=1, keepdims=True))).astype(bf)
    gsec = sums_ref[:, width : 2 * width] + nn(glog[:, :experts], wr_ref[...])
    rs = row_norm(res)
    unit = res * rs
    gn2_ref[...] = jnp.sum(gsec * unit, axis=0, keepdims=True)
    cg = gsec * g2_ref[...]
    gres = cot_ref[...].astype(f32) + rs * (cg - unit * jnp.mean(cg * unit, axis=1, keepdims=True))
    gres_ref[...] = gres
    glow = gres.astype(bf)
    back[mine] = glow

    def cp(yy, cc, to, k):
        return pltpu.make_async_remote_copy(
            src_ref=at(yy, cc), dst_ref=at(yy, cc), send_sem=send.at[k],
            recv_sem=recv.at[yy * 2 + cc], device_id=to, device_id_type=MESH)

    cp(y, c, Y, 0).start()
    cp(y, c, C, 1).start()
    per = width // 4
    for i in range(4):
        csrc[i, :, :per] = glow[:, i * per : (i + 1) * per]
        csrc[i, :, per:] = glog
    blocks = Columns(csrc, cols_ref, psend, precv, tsend, trecv)
    blocks.start()
    dk[...] = jnp.zeros_like(dk)
    dv[...] = jnp.zeros_like(dv)
    qgain_ref[...] = jnp.zeros_like(qgain_ref)
    woc.wait()

    def mix(yy):
        span = pl.ds(pl.multiple_of(yy * 2 * rows, 2 * rows), 2 * rows)
        both = nt(back[span], wo[...]).astype(bf)
        for h in range(heads):
            mixed[yy * heads + h] = both[:, h * head : (h + 1) * head]

    cp(y, 1 - c, C, 1).wait_recv()
    mix(y)
    cp(1 - y, c, Y, 0).wait_recv()
    cp(1 - y, c, C, 2).start()
    cp(1 - y, 1 - c, C, 2).wait_recv()
    mix(1 - y)
    scale = 1.0 / math.sqrt(head)

    group = 4

    def attend(i, carry):
        s = i // (heads // group)
        h = i % (heads // group) * group
        span = pl.ds(pl.multiple_of(s * half, half), half)
        mine = pl.ds(i * group, group)
        keys = kv_ref[s].reshape(8 * half, head)
        vals = kv_ref[2 + s].reshape(8 * half, head)
        query = qrot_ref[mine].reshape(group * half, head)
        grad = mixed[mine].reshape(group * half, head)
        scores = (nt(query, keys) * scale).reshape(group, half, 8 * half)
        allowed = qpos_ref[span, :1] >= kpos_ref[pl.ds(s, 1), :]
        logs = log_ref[mine][:, :, :1]
        probs = jnp.where(allowed[None], jnp.exp(scores - logs), 0.0).reshape(group * half, 8 * half)
        gprobs = nt(grad, vals)
        inner = jnp.sum(probs * gprobs, axis=1, keepdims=True)
        dots = (probs * (gprobs - inner) * scale).astype(bf)
        dk[s] += tn(dots, query)
        dv[s] += tn(probs.astype(bf), grad)
        drot = nn(dots, keys)
        for g in range(group):
            lanes = pl.ds(pl.multiple_of((h + g) * head, head), head)
            raw = qraw_ref[span, lanes]
            dn = turn_back(drot[g * half : (g + 1) * half], cos_ref[span], sin_ref[span])
            rs = row_norm(raw)
            unit = raw * rs
            qgain_ref[...] += jnp.sum((dn * unit).reshape(half // 8, 8, head), axis=0)
            cg = dn * qg_ref[...]
            low = rs * (cg - unit * jnp.mean(cg * unit, axis=1, keepdims=True))
            qlow_ref[span, lanes] = low.astype(bf)
        return carry

    steps = 2 * heads // group
    lax.fori_loop(0, steps // 2, attend, 0)
    blocks.exchange()
    lax.fori_loop(steps // 2, steps, attend, 0)
    blocks.forward()
    for s in range(2):
        dkv_ref[s] = dk[s].astype(bf).reshape(8, half, head)
        dkv_ref[2 + s] = dv[s].astype(bf).reshape(8, half, head)
    cp(y, c, Y, 0).wait_send()
    cp(y, c, C, 1).wait_send()
    cp(1 - y, c, C, 2).wait_send()
    blocks.finish()


def middle(sums, res, gates, cot, g2, wr, wo, qrot, kv, logs, qraw, qg, cos, sin, qpos, kpos, cid):
    rows, width = res.shape
    tok, cols = qraw.shape
    head = qg.shape[1]
    half = tok // 2
    f32, bf = jnp.float32, jnp.bfloat16
    dma = pltpu.SemaphoreType.DMA
    vm, anywhere = pl.BlockSpec(memory_space=pltpu.VMEM), pl.BlockSpec(memory_space=pl.ANY)

    def out(shape, kind):
        return jax.ShapeDtypeStruct(shape, kind)

    return pl.pallas_call(
        middle_kernel,
        in_specs=[vm] * 3 + [anywhere] * 4 + [vm] * 4 + [anywhere] + [vm] * 4,
        out_specs=[vm] * 7,
        out_shape=[
            out((rows, width), bf), out((rows, width), f32), out((1, width), f32),
            out((4, 4, rows, width // 4 + 128), bf), out((tok, cols), bf), out((4, 8, half, head), bf),
            out((8, head), f32),
        ],
        scratch_shapes=[
            pltpu.VMEM((rows, width), bf), pltpu.VMEM(g2.shape, f32), pltpu.VMEM(wr.shape, bf),
            pltpu.VMEM(qg.shape, f32),
            pltpu.VMEM((cols, width), bf), pltpu.VMEM((tok, width), bf), pltpu.VMEM((2 * cols // head, half, head), bf),
            pltpu.VMEM((2, 8 * half, head), f32), pltpu.VMEM((2, 8 * half, head), f32),
            pltpu.VMEM((4, rows, width // 4 + 128), bf),
            dma((5,)), dma((3,)), dma((4,)), dma((4,)), dma((4,)), dma((3,)), dma((4,)),
        ],
        compiler_params=pltpu.CompilerParams(
            collective_id=cid, has_side_effects=True, vmem_limit_bytes=52 * 2**20
        ),
        name="middle",
    )(sums, res, gates, cot, g2, wr, wo, qrot, kv, logs, qraw, qg, cos, sin, qpos, kpos)


def tail_kernel(
    dkv_ref, qlow_ref, kraw_ref, kg_in, cos_ref, sin_ref, wq_ref, wk_in, wv_in, x_in, g1_in,
    gres_ref, layer_ref, gn2_ref, qgain_ref, first_in, att_in, back_ref, rows_in,
    gin_ref, lout_ref, gq_ref, gkv_ref, gout_ref, grouter_ref, vo_ref,
    wq, kg_ref, wk_ref, wv_ref, x_ref, g1_ref, first_ref, att, second, att_t, xbuf, zbuf, zst, part, cbuf, ybuf, stage, vbuf, vpart, tbuf, gin, qbuf, kvbuf, turned, osrc, obuf, rsrc, rbuf, qsrc, qgot, ksrc, kgot, grouter_both,
    wsem, xsend, xrecv, zsend, zrecv, csend, crecv, ysend, yrecv, send, recv, vsend, vrecv, tsend, trecv,
    qsend, qrecv, ksend, krecv, esend, erecv,
):
    f32, bf = jnp.float32, jnp.bfloat16
    z, x, y, c = coords()
    ctx, tp = lax.axis_index("ctx"), lax.axis_index("tp")
    rows, width = gres_ref.shape
    half, head = dkv_ref.shape[2:]
    line_cols = first_in.shape[1]
    tok = x_in.shape[0]
    fetched = [
        pltpu.make_async_copy(src, dst, wsem.at[n])
        for n, (src, dst) in enumerate((
            (first_in, first_ref), (att_in, att), (wq_ref, wq), (kg_in, kg_ref), (wk_in, wk_ref),
            (wv_in, wv_ref), (x_in, x_ref), (g1_in, g1_ref),
            *(
                (rows_in.at[pl.ds(pl.multiple_of((zz * 2 + x) * tok, tok), tok),
                            pl.ds(pl.multiple_of(z * line_cols, line_cols), line_cols)],
                 second.at[pl.ds(zz * tok, tok)])
                for zz in range(4)
            ),
        ))
    ]
    for item in fetched:
        item.start()
    X, Y, C, D = dev(z, 1 - x, y, c), dev(z, x, 1 - y, c), dev(z, x, y, 1 - c), dev(z, x, 1 - y, 1 - c)
    up, down = dev(z + 1, x, y, c), dev(z - 1, x, y, c)
    barrier_wide()

    def xcopy(zz):
        return pltpu.make_async_remote_copy(
            src_ref=dkv_ref.at[:, zz * 2 + 1 - x], dst_ref=xbuf.at[zz], send_sem=xsend.at[zz],
            recv_sem=xrecv.at[zz], device_id=X, device_id_type=MESH)

    def zcopy(zz, to, slot):
        return pltpu.make_async_remote_copy(
            src_ref=zst.at[zz], dst_ref=zbuf.at[slot], send_sem=zsend.at[zz],
            recv_sem=zrecv.at[slot], device_id=to, device_id_type=MESH)

    span = qlow_ref.shape[1] // 2
    queries = [
        Line(lambda zz, n=n: qbuf.at[n, zz], qsend.at[n], qrecv.at[n]) for n in range(2)
    ]
    keys = Line(lambda zz: kvbuf.at[zz], ksend, krecv)
    for n in range(2):
        qbuf[n, z] = qlow_ref[:, n * span : (n + 1) * span]
    for k in range(4):
        xcopy(far_z(z, k)).start()
    queries[0].start()

    pairs = [(gin, gin_ref), (layer_ref, lout_ref)]

    def place(ref, yy, cc):
        return ref.at[pl.ds(pl.multiple_of((yy * 2 + cc) * rows, rows), rows)]

    def cp(n, src, yy, cc, to, k):
        return pltpu.make_async_remote_copy(
            src_ref=src, dst_ref=place(pairs[n][1], yy, cc), send_sem=send.at[n, k],
            recv_sem=recv.at[n, yy * 2 + cc], device_id=to, device_id_type=MESH)

    own = pl.ds(pl.multiple_of((y * 2 + c) * rows, rows), rows)
    cp(1, layer_ref, y, c, Y, 0).start()
    cp(1, layer_ref, y, c, C, 1).start()
    lout_ref[own] = layer_ref[...]

    per = gq_ref.shape[0]
    own_cols = pl.ds(pl.multiple_of(x * per, per), per)
    far_cols = pl.ds(pl.multiple_of((1 - x) * per, per), per)

    def swap(n, src, dst):
        return pltpu.make_async_remote_copy(
            src_ref=src, dst_ref=dst, send_sem=esend.at[n], recv_sem=erecv.at[n], device_id=X,
            device_id_type=MESH)

    swaps = [
        swap(0, osrc, obuf), swap(1, rsrc, rbuf), swap(2, qsrc.at[0], qgot.at[0]),
        swap(3, qsrc.at[1], qgot.at[1]), swap(4, ksrc, kgot),
    ]
    own_lanes = pl.ds(pl.multiple_of(x * per, 128), per)
    far_lanes = pl.ds(pl.multiple_of((1 - x) * per, 128), per)
    for item in fetched[:2]:
        item.wait()
    att_t[...] = att[...].T
    osrc[...] = nn(att_t[...], back_ref[:, far_lanes]).astype(bf)
    swaps[0].start()
    turned[...] = first_ref[...].T

    def query_part(n):
        right = qbuf[n].reshape(turned.shape[1], span)
        cols = slice(n * span, (n + 1) * span)
        qsrc[n] = nn(turned[far_cols], right).astype(bf)
        swaps[2 + n].start()
        gq_ref[:, cols] = nn(turned[own_cols], right)

    def sum_z(k):
        zz = far_z(z, k)
        xcopy(zz).wait_recv()
        total = dkv_ref[:, zz * 2 + x].astype(f32) + xbuf[zz].astype(f32)
        zst[zz] = total.astype(bf)

        @pl.when((zz > z) & (z > 0))
        def _():
            zcopy(zz, up, zz).wait_recv()
            zst[zz] = (zst[zz].astype(f32) + zbuf[zz].astype(f32)).astype(bf)

        @pl.when((zz < z) & (z < 3))
        def _():
            zcopy(zz, down, zz).wait_recv()
            zst[zz] = (zst[zz].astype(f32) + zbuf[zz].astype(f32)).astype(bf)

        @pl.when(zz > z)
        def _():
            zcopy(zz, up, zz).start()

        @pl.when((zz < z) & (zz != z - 1))
        def _():
            zcopy(zz, down, zz).start()

        @pl.when(zz == z - 1)
        def _():
            zcopy(zz, down, 4).start()

    def at(yy, cc):
        return part.at[pl.ds(pl.multiple_of((yy * 2 + cc) * rows, rows), rows)]

    def two(yy):
        return pl.ds(pl.multiple_of(yy * 2 * rows, 2 * rows), 2 * rows)

    sum_z(0)
    for item in fetched[2:]:
        item.wait()
    first_a = nt(qlow_ref[two(1 - y)], wq[...])
    sum_z(1)
    first_b = nt(qlow_ref[two(y)], wq[...])
    queries[0].pass_on(1)
    sum_z(2)
    queries[1].start()
    router_part = tn(second[...], back_ref[:, line_cols:])
    part_of = jnp.stack([router_part[:per], router_part[per:]])
    grouter_both[...] = part_of
    rsrc[...] = grouter_both[1 - x].astype(bf)
    swaps[1].start()
    xcopy(z).wait_recv()
    dkv = dkv_ref[:, ctx].astype(f32) + xbuf[z].astype(f32)

    @pl.when(z > 0)
    def _():
        zcopy(z, up, z).wait_recv()

    @pl.when(z == 0)
    def _():
        zbuf[0] = jnp.zeros_like(zbuf[0])

    @pl.when(z < 3)
    def _():
        zcopy(z, down, 4).wait_recv()

    @pl.when(z == 3)
    def _():
        zbuf[4] = jnp.zeros_like(zbuf[4])

    dkv = dkv + zbuf[z].astype(f32) + zbuf[4].astype(f32)
    dkey = jnp.concatenate([dkv[0], dkv[1]], axis=0)
    vlow = jnp.concatenate([dkv[2], dkv[3]], axis=0).astype(bf)
    raw = kraw_ref[...]
    dn = turn_back(dkey, cos_ref[...], sin_ref[...])
    rs = row_norm(raw)
    unit = raw * rs
    kgain = jnp.sum(dn * unit, axis=0, keepdims=True)
    cg = dn * kg_ref[...]
    klow = (rs * (cg - unit * jnp.mean(cg * unit, axis=1, keepdims=True))).astype(bf)
    kvbuf[z, :, :head] = klow
    kvbuf[z, :, head:] = vlow
    keys.start()
    queries[0].pass_on(2)

    def ccopy(yy):
        return pltpu.make_async_remote_copy(
            src_ref=at(yy, 1 - c), dst_ref=cbuf.at[yy], send_sem=csend.at[yy],
            recv_sem=crecv.at[yy], device_id=C, device_id_type=MESH)

    def project(yy, first):
        keys, vals = kvbuf[z, two(yy), :head], kvbuf[z, two(yy), head:]
        part[two(yy)] = (first + nt(keys, wk_ref[...]) + nt(vals, wv_ref[...])).astype(bf)
        ccopy(yy).start()

    project(1 - y, first_a)
    project(y, first_b)
    ccopy(1 - y).wait_recv()
    stage[...] = (at(1 - y, c)[...].astype(f32) + cbuf[1 - y].astype(f32)).astype(bf)
    yc = pltpu.make_async_remote_copy(
        src_ref=stage, dst_ref=ybuf, send_sem=ysend, recv_sem=yrecv, device_id=Y, device_id_type=MESH)
    yc.start()
    queries[1].pass_on(1)
    ccopy(y).wait_recv()
    gfirst = at(y, c)[...].astype(f32) + cbuf[y].astype(f32)
    value = x_ref[own].astype(f32)
    rs = row_norm(value)
    unit = value * rs
    yc.wait_recv()
    gfirst = gfirst + ybuf[...].astype(f32)
    gn1 = jnp.sum(gfirst * unit, axis=0, keepdims=True)
    cg = gfirst * g1_ref[...]
    gin[...] = (gres_ref[...] + rs * (cg - unit * jnp.mean(cg * unit, axis=1, keepdims=True))).astype(bf)

    queries[0].pass_on(3)
    query_part(0)
    keys.pass_on(1)
    cp(0, gin, y, c, Y, 0).start()
    cp(0, gin, y, c, C, 1).start()
    gin_ref[own] = gin[...]
    part_width = width // 8
    qgain = jnp.sum(qgain_ref[...], axis=0, keepdims=True)
    for i in range(8):
        for j in range(part_width // 128):
            lo = i * part_width + j * 128
            vpart[i, j : j + 1] = gn1[:, lo : lo + 128]
            vpart[i, part_width // 128 + j : part_width // 128 + j + 1] = gn2_ref[:, lo : lo + 128]
        vpart[i, 2 * part_width // 128 : 7] = jnp.broadcast_to(qgain, (7 - 2 * part_width // 128, head))
        vpart[i, 7:8] = kgain

    def vcopy(i):
        to = (ctx + i) % 8
        return pltpu.make_async_remote_copy(
            src_ref=vpart.at[to], dst_ref=vbuf.at[i], send_sem=vsend.at[i], recv_sem=vrecv.at[i],
            device_id=(to, tp), device_id_type=MESH)

    for i in range(1, 8):
        vcopy(i).start()
    queries[1].pass_on(2)
    keys.pass_on(2)
    total = vpart[ctx]
    for i in range(1, 8):
        vcopy(i).wait_recv()
        total = total + vbuf[i]
    tbuf[3] = total

    def tcopy(k, to):
        return pltpu.make_async_remote_copy(
            src_ref=tbuf.at[3], dst_ref=tbuf.at[k], send_sem=tsend.at[k], recv_sem=trecv.at[k],
            device_id=to, device_id_type=MESH)

    sums = [tcopy(k, to) for k, to in enumerate((Y, C, D))]
    for t in sums:
        t.start()
    for n, (src, dst) in enumerate(pairs):
        cp(n, src, 1 - y, c, Y, 0).wait_recv()
        cp(n, place(dst, 1 - y, c), 1 - y, c, C, 2).start()
    swaps[0].wait_recv()
    gout_ref[...] = nn(att_t[...], back_ref[:, own_lanes]) + obuf[...].astype(f32)
    swaps[1].wait_recv()
    grouter_ref[...] = grouter_both[x] + rbuf[...].astype(f32)
    queries[1].pass_on(3)
    query_part(1)
    keys.pass_on(3)
    right = kvbuf[...].reshape(turned.shape[1], 2 * head)
    ksrc[...] = nn(turned[far_cols], right).astype(bf)
    swaps[4].start()
    gkv_ref[...] = nn(turned[own_cols], right)
    for t in sums:
        t.wait_recv()
    vo_ref[...] = (tbuf[3] + tbuf[0]) + (tbuf[1] + tbuf[2])
    for n, (src, dst) in enumerate(pairs):
        cp(n, src, y, 1 - c, C, 1).wait_recv()
        cp(n, src, 1 - y, 1 - c, C, 2).wait_recv()
        cp(n, src, y, c, Y, 0).wait_send()
        cp(n, src, y, c, C, 1).wait_send()
        cp(n, place(dst, 1 - y, c), 1 - y, c, C, 2).wait_send()
    for t in sums:
        t.wait_send()
    for i in range(1, 8):
        vcopy(i).wait_send()
    for line in (*queries, keys):
        line.finish()
    for n in range(2):
        swaps[2 + n].wait_recv()
        gq_ref[:, n * span : (n + 1) * span] += qgot[n].astype(f32)
    swaps[4].wait_recv()
    gkv_ref[...] += kgot[...].astype(f32)
    for s in swaps:
        s.wait_send()
    yc.wait_send()
    ccopy(0).wait_send()
    ccopy(1).wait_send()
    for zz in range(4):
        xcopy(zz).wait_send()

        @pl.when(zz != z)
        def _():
            zcopy(zz, up, zz).wait_send()


def tail(dkv, qlow, kraw, kg, cos, sin, wq, wk, wv, x, g1, gres, layer, gn2, qgain, first, att, back, rows_all, cid):
    tok, width = x.shape
    rows = gres.shape[0]
    half, head = dkv.shape[2:]
    per = first.shape[1] // 2
    f32, bf = jnp.float32, jnp.bfloat16
    dma = pltpu.SemaphoreType.DMA
    vm, anywhere = pl.BlockSpec(memory_space=pltpu.VMEM), pl.BlockSpec(memory_space=pl.ANY)

    def out(shape, kind):
        return jax.ShapeDtypeStruct(shape, kind)

    def mem(*shape, kind=bf):
        return pltpu.VMEM(shape, kind)

    return pl.pallas_call(
        tail_kernel,
        in_specs=[vm] * 3 + [anywhere] + [vm] * 2 + [anywhere] * 5 + [vm] * 4 + [anywhere] * 2 + [vm] + [anywhere],
        out_specs=[vm] * 7,
        out_shape=[
            out((tok, width), bf), out((tok, width), bf), out((per, qlow.shape[1]), f32),
            out((per, 2 * head), f32), out((att.shape[1], per), f32),
            out((per, 128), f32), out((8, 128), f32),
        ],
        scratch_shapes=[
            mem(*wq.shape), mem(*kg.shape, kind=f32), mem(*wk.shape), mem(*wv.shape), mem(*x.shape),
            mem(*g1.shape, kind=f32), mem(*first.shape), mem(*att.shape), mem(*first.shape),
            mem(att.shape[1], att.shape[0]), mem(4, 4, half, head), mem(5, 4, half, head), mem(4, 4, half, head),
            mem(tok, width), mem(2, rows, width), mem(rows, width), mem(rows, width),
            mem(8, 8, 128, kind=f32), mem(8, 8, 128, kind=f32), mem(4, 8, 128, kind=f32), mem(rows, width),
            mem(2, 4, tok, qlow.shape[1] // 2), mem(4, tok, 2 * head), mem(2 * per, first.shape[0]),
            mem(att.shape[1], per), mem(att.shape[1], per),
            mem(per, 128), mem(per, 128),
            mem(2, per, qlow.shape[1] // 2), mem(2, per, qlow.shape[1] // 2),
            mem(per, 2 * head), mem(per, 2 * head), mem(2, per, 128, kind=f32),
            dma((12,)), dma((4,)), dma((4,)), dma((4,)), dma((5,)), dma((2,)), dma((2,)), dma, dma,
            dma((2, 3)), dma((2, 4)), dma((8,)), dma((8,)), dma((3,)), dma((3,)),
            dma((2, 2, 4)), dma((2, 4)), dma((2, 4)), dma((4,)), dma((5,)), dma((5,)),
        ],
        compiler_params=pltpu.CompilerParams(
            collective_id=cid, has_side_effects=True, vmem_limit_bytes=52 * 2**20
        ),
        name="tail",
    )(dkv, qlow, kraw, kg, cos, sin, wq, wk, wv, x, g1, gres, layer, gn2, qgain, first, att, back, rows_all)


def experts_kernel(
    own,
    piece_ref, wg_ref, wu_ref, wd_ref,
    all_ref, pair_ref, hs_ref, gl_ref, ul_ref, hst_ref, glt_ref, ult_ref,
    land, mats, s_ref, t_ref, pairs, lows, turns,
    gsem, gsend, grecv, msem, asem, psem, lsem, tsem,
):
    bf, f32 = jnp.bfloat16, jnp.float32
    width = wg_ref.shape[1]
    extra = t_ref.shape[1]
    hid = wg_ref.shape[0]
    tok = 4 * piece_ref.shape[0]
    weights = [pltpu.make_async_copy(r, mats.at[n], msem.at[n]) for n, r in enumerate((wg_ref, wu_ref, wd_ref))]
    for cp in weights:
        cp.start()
    named = lax.axis_index("ctx") * own

    def expert_of(index):
        return named + sum((index >= e * hid // own).astype(jnp.int32) for e in range(1, own))

    shape = s_ref.shape
    expert = expert_of(lax.broadcasted_iota(jnp.int32, shape, 1))
    place = lax.broadcasted_iota(jnp.int32, shape, 0)
    s_ref[...] = ((place == expert) | (place == expert + extra // 4)).astype(f32).astype(bf)
    expert = expert_of(lax.broadcasted_iota(jnp.int32, shape[::-1], 0))
    place = lax.broadcasted_iota(jnp.int32, shape[::-1], 1)
    t_ref[...] = (place == expert).astype(f32).astype(bf)
    barrier_all()
    wide = piece_ref.shape[1]
    cut = wide // 256 * 128
    gathers = [
        Gather(piece_ref, land, pl.ds(0, cut), gsend.at[0], grecv.at[0]),
        Gather(piece_ref, land, pl.ds(cut, wide - cut), gsend.at[1], grecv.at[1]),
    ]
    for gather in gathers:
        gather.start()
    z, x, y, c, ax, ay, bx, by = gathers[0].at_me
    rows = piece_ref.shape[0]
    me = pid(z, x, y, c)
    local = pltpu.make_async_copy(
        piece_ref, land.at[pl.ds(pl.multiple_of(me * rows, rows), rows)], gsem)
    local.start()

    def place_of(u):
        return far_z(z, 3 - u // 2), x + (u % 2) * (1 - 2 * x)

    def block_rows(u):
        zz, xx = place_of(u)
        return pl.ds(pl.multiple_of((zz * 2 + xx) * tok, tok), tok)

    def results(u):
        slot = u % 2
        span = block_rows(u)
        copies = [pltpu.make_async_copy(pairs.at[slot], pair_ref.at[span], psem.at[slot])]
        for n, (ref, turned) in enumerate(((hs_ref, hst_ref), (gl_ref, glt_ref), (ul_ref, ult_ref))):
            copies.append(pltpu.make_async_copy(lows.at[slot, n], ref.at[span], lsem.at[slot, n]))
            copies.append(pltpu.make_async_copy(turns.at[slot, n], turned.at[:, span], tsem.at[slot, n]))
        return copies

    def whole(u):
        span = block_rows(u)
        return pltpu.make_async_copy(land.at[span], all_ref.at[span], asem.at[u])

    local.wait()

    def step(u, carry):
        zz, xx = place_of(u)
        slot = u % 2

        @pl.when(u % 2 == 0)
        def _():
            for gather in gathers:
                gather.from_a(zz)

            @pl.when(u < 6)
            def _():
                for gather in gathers:
                    gather.from_line(far_z(z, 2 - u // 2))

            for gather in gathers:
                gather.from_b(zz, bx, by)

        @pl.when(u % 2 == 1)
        def _():
            for gather in gathers:
                gather.from_b(zz, 1 - x, 1 - y)

        for yy in range(2):
            for gather in gathers:
                gather.wait(pid(zz, xx, yy, 1 - c))

        whole(u).start()

        @pl.when(u == 0)
        def _():
            for cp in weights:
                cp.wait()

        @pl.when(u > 1)
        def _():
            for cp in results(u - 2):
                cp.wait()

        rows = block_rows(u)
        value = land[rows, :width]
        spread = nn(land[rows, 2 * width :], s_ref[...])
        gate = nt(value, mats[0])
        up = nt(value, mats[1])
        back = nt(land[rows, width : 2 * width], mats[2])
        sig = 1.0 / (1.0 + jnp.exp(-gate))
        silu = gate * sig
        hidden = silu * up
        hs = (hidden * spread).astype(bf)
        prod = hidden * back
        high = prod.astype(bf)
        low = (prod - high.astype(f32)).astype(bf)
        pairs[slot] = (nn(high, t_ref[...]) + nn(low, t_ref[...])).astype(bf)
        grad = back * spread
        gl = (grad * up * sig * (1.0 + gate * (1.0 - sig))).astype(bf)
        ul = (grad * silu).astype(bf)
        for n, v in enumerate((hs, gl, ul)):
            lows[slot, n] = v
            turns[slot, n] = v.T
        for cp in results(u):
            cp.start()
        return carry

    lax.fori_loop(0, 8, step, 0)
    for u in (6, 7):
        for cp in results(u):
            cp.wait()
    for u in range(8):
        whole(u).wait()
    for gather in gathers:
        gather.finish()


def experts_forward(piece, wg, wu, wd, own, cid):
    rows, wide = piece.shape
    hid, width = wg.shape
    n = 32 * rows
    tok = 4 * rows
    extra = wide - 2 * width
    bf = jnp.bfloat16
    dma = pltpu.SemaphoreType.DMA
    anywhere = pl.BlockSpec(memory_space=pl.ANY)

    def out(*shape):
        return jax.ShapeDtypeStruct(shape, bf)

    return pl.pallas_call(
        functools.partial(experts_kernel, own),
        in_specs=[anywhere] * 4,
        out_specs=[anywhere] * 8,
        out_shape=[out(n, wide), out(n, extra)] + [out(n, hid)] * 3 + [out(hid, n)] * 3,
        scratch_shapes=[
            pltpu.VMEM((n, wide), bf), pltpu.VMEM((3, hid, width), bf), pltpu.VMEM((extra, hid), bf),
            pltpu.VMEM((hid, extra), bf), pltpu.VMEM((2, tok, extra), bf),
            pltpu.VMEM((2, 3, tok, hid), bf), pltpu.VMEM((2, 3, hid, tok), bf),
            dma, dma((2, 5, 32)), dma((2, 32)), dma((3,)), dma((8,)), dma((2,)), dma((2, 3)), dma((2, 3)),
        ],
        compiler_params=pltpu.CompilerParams(
            collective_id=cid, has_side_effects=True, vmem_limit_bytes=56 * 2**20
        ),
        cost_estimate=pl.CostEstimate(
            flops=6 * n * width * hid, bytes_accessed=10 * n * width, transcendentals=n * hid
        ),
        name="experts_forward",
    )(piece, wg, wu, wd)


EPSILON = 1e-06
ROPE_BASE = 1000000.0
MASKED_SCORE = -1000000000.0
BF = jnp.bfloat16
F32 = jnp.float32


def dotf(a, b, dims):
    return lax.dot_general(a, b, (dims, ((), ())), preferred_element_type=F32)


def nt(a, b):
    return lax.dot_general(a, b, (((1,), (1,)), ((), ())), preferred_element_type=jnp.float32)


def nn(a, b):
    return lax.dot_general(a, b, (((1,), (0,)), ((), ())), preferred_element_type=jnp.float32)


def tn(a, b):
    return lax.dot_general(a, b, (((0,), (0,)), ((), ())), preferred_element_type=jnp.float32)


def plain_expert_kernel(x_ref, cot_ref, wg_ref, wu_ref, wd_ref, s_ref, t_ref, part_ref, gl_ref, ul_ref, hs_ref):
    bf = jnp.bfloat16
    width = cot_ref.shape[1]
    x = x_ref[:, :width]
    spread = nn(x_ref[:, width:], s_ref[...])
    gate = nt(x, wg_ref[...])
    up = nt(x, wu_ref[...])
    back = nt(cot_ref[...], wd_ref[...])
    sig = 1.0 / (1.0 + jnp.exp(-gate))
    silu = gate * sig
    hidden = silu * up
    hs = (hidden * spread).astype(bf)
    hs_ref[...] = hs.T
    part_ref[:, :width] = nn(hs, wd_ref[...]).astype(bf)
    prod = hidden * back
    high = prod.astype(bf)
    low = (prod - high.astype(jnp.float32)).astype(bf)
    part_ref[:, 2 * width :] = (nn(high, t_ref[...]) + nn(low, t_ref[...])).astype(bf)
    grad = back * spread
    gl = (grad * up * sig * (1.0 + gate * (1.0 - sig))).astype(bf)
    ul = (grad * silu).astype(bf)
    gl_ref[...] = gl.T
    ul_ref[...] = ul.T
    part_ref[:, width : 2 * width] = (nn(gl, wg_ref[...]) + nn(ul, wu_ref[...])).astype(bf)


def expert_blocks(x_all, cot_all, gate_mat, up_mat, down_mat, spread_mat, pick_mat, block=256):
    n, width = cot_all.shape
    wide = x_all.shape[1]
    hid = gate_mat.shape[0]
    bf = jnp.bfloat16

    def rows(w):
        return pl.BlockSpec((block, w), lambda i: (i, 0))

    def whole(v):
        return pl.BlockSpec(v.shape, lambda i: (0, 0), pipeline_mode=pl.Buffered(1))

    return pl.pallas_call(
        plain_expert_kernel,
        grid=(n // block,),
        in_specs=[rows(wide), rows(width)]
        + [whole(v) for v in (gate_mat, up_mat, down_mat, spread_mat, pick_mat)],
        out_specs=[rows(width + wide)] + [pl.BlockSpec((hid, block), lambda i: (0, i))] * 3,
        out_shape=[jax.ShapeDtypeStruct((n, width + wide), bf)]
        + [jax.ShapeDtypeStruct((hid, n), bf)] * 3,
        compiler_params=pltpu.CompilerParams(
            dimension_semantics=("arbitrary",), vmem_limit_bytes=56 * 2**20
        ),
        cost_estimate=pl.CostEstimate(
            flops=12 * n * width * hid, bytes_accessed=10 * n * width, transcendentals=n * hid
        ),
        name="plain_experts",
    )(x_all, cot_all, gate_mat, up_mat, down_mat, spread_mat, pick_mat)


def expert_grad_kernel(x_ref, cot_ref, gl_ref, ul_ref, hs_ref, gg_ref, gu_ref, gd_ref):
    first = pl.program_id(1) == 0

    def put(ref, low, full):
        value = nn(low[...], full[...])

        @pl.when(first)
        def _():
            ref[...] = value

        @pl.when(jnp.logical_not(first))
        def _():
            ref[...] += value

    put(gg_ref, gl_ref, x_ref)
    put(gu_ref, ul_ref, x_ref)
    put(gd_ref, hs_ref, cot_ref)


def expert_grads(x_all, cot_all, gl, ul, hs, width, first=0, block=256):
    n = x_all.shape[0]
    hid = gl.shape[0]
    span = min(n, 2048)
    cols = pl.BlockSpec((span, block), lambda i, j: (j, i))
    cots = pl.BlockSpec((span, block), lambda i, j: (j, i + first // block))
    rows = pl.BlockSpec((hid, span), lambda i, j: (0, j))
    out = pl.BlockSpec((hid, block), lambda i, j: (0, i))
    return pl.pallas_call(
        expert_grad_kernel,
        grid=(width // block, n // span),
        in_specs=[cols, cots, rows, rows, rows],
        out_specs=[out] * 3,
        out_shape=[jax.ShapeDtypeStruct((hid, width), jnp.float32)] * 3,
        compiler_params=pltpu.CompilerParams(
            dimension_semantics=("arbitrary", "arbitrary"), vmem_limit_bytes=56 * 2**20
        ),
        cost_estimate=pl.CostEstimate(
            flops=6 * n * width * hid, bytes_accessed=10 * n * width, transcendentals=0
        ),
        name="expert_grads",
    )(x_all, cot_all, gl, ul, hs)


class Links:
    def ag_all(self, piece):
        return lax.all_gather(piece, ("ctx", "tp"), axis=0, tiled=True)

    def rs_all(self, part):
        return lax.psum_scatter(part, ("ctx", "tp"), scatter_dimension=0, tiled=True).astype(F32)

    def ag_ctx(self, piece):
        return lax.all_gather(piece, "ctx", axis=0, tiled=True)

    def rs_ctx(self, part):
        return lax.psum_scatter(part, "ctx", scatter_dimension=0, tiled=True).astype(F32)

    def rs_tp(self, part):
        return lax.psum_scatter(part, "tp", scatter_dimension=0, tiled=True).astype(F32)

    def ag_tp(self, piece):
        return lax.all_gather(piece, "tp", axis=0, tiled=True)

    def finish(self, a, b, vectors):
        total = lax.psum_scatter(vectors, "ctx", scatter_dimension=0, tiled=True)
        gathered = (lax.all_gather(v, "tp", axis=0, tiled=True) for v in (a, b))
        return (*gathered, lax.psum(total, "tp"))


def rms_norm(values, gain_vec):
    factor = lax.rsqrt(jnp.mean(values * values, axis=-1, keepdims=True) + EPSILON)
    return values * factor * gain_vec


def rotate(values, rotary_angles):
    half_size = values.shape[-1] // 2
    first_half = values[..., :half_size]
    second_half = values[..., half_size:]
    cosine = jnp.cos(rotary_angles)
    sine_part = jnp.sin(rotary_angles)
    return jnp.concatenate(
        [
            first_half * cosine - second_half * sine_part,
            second_half * cosine + first_half * sine_part,
        ],
        axis=-1,
    )


def angles_of(token_positions, head_width):
    freq_steps = jnp.arange(head_width // 2).astype(F32) * (2.0 / head_width)
    frequency = jnp.exp(-math.log(ROPE_BASE) * freq_steps)
    return token_positions.astype(F32)[..., None] * frequency


def positions_of(block_order, dev_count, block_len):
    first_block = jnp.transpose(block_order)
    block_pair = jnp.stack([first_block, 2 * dev_count - 1 - first_block], axis=-1)
    spread = block_pair[..., None] * block_len + jnp.arange(block_len, dtype=jnp.int32)
    return spread.reshape(dev_count, block_order.shape[0], 2 * block_len)


def head_route_path(raw_heads, gain_vec, rotary_angles, head_count):
    shaped = raw_heads.reshape(raw_heads.shape[0], head_count, -1)
    return rotate(rms_norm(shaped, gain_vec), rotary_angles[:, None, :])


def attend_forward(seq_item):
    query_matrix, every_key_row, every_value_row, query_pos, key_pos = seq_item
    score_scale = 1.0 / math.sqrt(query_matrix.shape[-1])
    unscaled_scores = jnp.einsum(
        "upnj,apj->upna", query_matrix, every_key_row, preferred_element_type=F32
    )
    allowed = query_pos[:, None, None, None] >= key_pos[None, None, None, :]
    scores = jnp.where(allowed, unscaled_scores * score_scale, MASKED_SCORE)
    row_top = jnp.max(scores, axis=-1, keepdims=True)
    exp_scores = jnp.exp(scores - row_top)
    totals = jnp.sum(exp_scores, axis=-1, keepdims=True)
    lower_attention_probs = (exp_scores / totals).astype(BF)
    attended_mix = jnp.einsum(
        "jzfq,qzx->jzfx", lower_attention_probs, every_value_row, preferred_element_type=F32
    )
    return (attended_mix, (row_top + jnp.log(totals))[..., 0])


def attend_backward(seq_item):
    (
        query_matrix,
        every_key_row,
        every_value_row,
        query_pos,
        key_pos,
        grad_attended_mix,
        log_total,
    ) = seq_item
    score_scale = 1.0 / math.sqrt(query_matrix.shape[-1])
    unscaled_scores = jnp.einsum(
        "upnj,apj->upna", query_matrix, every_key_row, preferred_element_type=F32
    )
    allowed = query_pos[:, None, None, None] >= key_pos[None, None, None, :]
    scores = jnp.where(allowed, unscaled_scores * score_scale, MASKED_SCORE)
    attention_probs = jnp.exp(scores - log_total[..., None])
    grad_probs = jnp.einsum(
        "upnj,apj->upna", grad_attended_mix, every_value_row, preferred_element_type=F32
    )
    row_inner = jnp.sum(attention_probs * grad_probs, axis=-1, keepdims=True)
    grad_score_dots = (attention_probs * (grad_probs - row_inner) * score_scale).astype(BF)
    grad_queries = jnp.einsum(
        "jzfq,qzx->jzfx", grad_score_dots, every_key_row, preferred_element_type=F32
    )
    grad_key_rows = jnp.einsum(
        "axfv,axfz->vxz", grad_score_dots, query_matrix, preferred_element_type=F32
    )
    grad_values = jnp.einsum(
        "axfv,axfz->vxz", attention_probs.astype(BF), grad_attended_mix, preferred_element_type=F32
    )
    return (grad_queries, grad_key_rows, grad_values)


def gates_of(logits, routes):
    experts = logits.shape[1]
    named = jnp.any(routes[:, :, None] == jnp.arange(experts, dtype=jnp.int32), axis=1)
    masked = jnp.where(named, logits, -jnp.inf)
    top = jnp.max(masked, axis=1, keepdims=True)
    weights = jnp.where(named, jnp.exp(masked - top), 0.0)
    return weights / jnp.sum(weights, axis=1, keepdims=True)


def plain_shards(
    tokens_in,
    block_order,
    routes,
    norm1_gain,
    w_query,
    key_weight,
    value_weight,
    query_gain,
    key_gain,
    w_out,
    norm2_gain,
    w_router,
    w_gate,
    w_up,
    w_down,
    cotangent,
):
    tok_count, model_width = tokens_in.shape
    head_size = query_gain.shape[0]
    local_heads = w_query.shape[1] // head_size
    local_kv = key_weight.shape[1] // head_size
    query_group_width = local_heads // local_kv
    seq_count = block_order.shape[0]
    devices, tp_size = lax.axis_size("ctx"), lax.axis_size("tp")
    links = Links()
    me, tp_me = lax.axis_index("ctx"), lax.axis_index("tp")
    rows = tok_count // tp_size
    block_len = tok_count // (2 * seq_count)
    experts = w_router.shape[1]
    own_experts, _, units = w_gate.shape
    hid = own_experts * units
    all_tok = devices * tok_count

    def own_rows(v):
        return lax.dynamic_slice_in_dim(v, tp_me * rows, rows, axis=0)

    cot_own = own_rows(cotangent)
    cot_all = lax.all_gather(cot_own, ("ctx", "tp"), axis=0, tiled=True)

    token_positions = positions_of(block_order, devices, block_len)
    query_pos = lax.dynamic_index_in_dim(token_positions, me, 0, keepdims=False)
    key_pos = jnp.transpose(token_positions, (1, 0, 2)).reshape(seq_count, devices * 2 * block_len)
    rotary_angles = angles_of(query_pos.reshape(-1), head_size)
    inputs = tokens_in.astype(F32)
    first_in = rms_norm(inputs, norm1_gain).astype(BF)
    query_raw = jnp.dot(first_in, w_query, preferred_element_type=F32)
    unrotated_key = jnp.dot(first_in, key_weight, preferred_element_type=F32)
    value_rows = jnp.dot(first_in, value_weight, preferred_element_type=F32).astype(BF)

    def rope_heads(raw_query, raw_key, gain_query, key_norm_gain):
        return (
            head_route_path(raw_query, gain_query, rotary_angles, local_heads),
            head_route_path(raw_key, key_norm_gain, rotary_angles, local_kv),
        )

    (query_rot, key_rot), rope_back = jax.vjp(
        rope_heads, query_raw, unrotated_key, query_gain, key_gain
    )
    query_rows = query_rot.astype(BF).reshape(
        seq_count, 2 * block_len, local_kv, query_group_width, head_size
    )
    kv_width = local_kv * head_size
    kv_own = jnp.concatenate([key_rot.astype(BF).reshape(tok_count, kv_width), value_rows], axis=1)
    kv_all = links.ag_ctx(kv_own)
    kv_seq = kv_all.reshape(devices, seq_count, 2 * block_len, 2, local_kv, head_size)
    kv_seq = kv_seq.transpose(3, 1, 0, 2, 4, 5).reshape(
        2, seq_count, devices * 2 * block_len, local_kv, head_size
    )
    key_full, value_full = kv_seq[0], kv_seq[1]
    attended_mix, log_total = lax.map(
        attend_forward, (query_rows, key_full, value_full, query_pos, key_pos)
    )
    attended = attended_mix.reshape(tok_count, local_heads * head_size).astype(BF)
    attn_part = jnp.dot(attended, w_out, preferred_element_type=F32).astype(BF)
    residual = own_rows(inputs) + links.rs_tp(attn_part)
    second_normed, second_back = jax.vjp(rms_norm, residual, norm2_gain)
    second_in = second_normed.astype(BF)
    extra = -(-2 * experts // 128) * 128
    gates = gates_of(jnp.dot(second_in, w_router, preferred_element_type=F32), own_rows(routes))
    gates_high = gates.astype(BF)
    gates_low = (gates - gates_high.astype(F32)).astype(BF)
    pad = jnp.zeros((rows, extra - 2 * experts), BF)
    second_all = links.ag_all(
        jnp.concatenate([second_in, gates_high, gates_low, pad], axis=1)
    )
    column = jnp.arange(extra, dtype=jnp.int32)[:, None]
    named = me * own_experts + jnp.arange(hid, dtype=jnp.int32)[None, :] // units
    pick = (column == named).astype(BF)
    spread = pick + (column == named + experts).astype(BF)
    gate_mat = w_gate.transpose(0, 2, 1).reshape(hid, model_width)
    up_mat = w_up.transpose(0, 2, 1).reshape(hid, model_width)
    down_mat = w_down.reshape(hid, model_width)
    part, gate_low, up_low, hidden_low = expert_blocks(
        second_all, cot_all, gate_mat, up_mat, down_mat, spread, pick.T
    )
    sums_own = links.rs_all(part)
    out_own = sums_own[:, :model_width]
    entry_own = sums_own[:, model_width:]
    gate_total = entry_own[:, model_width : model_width + experts]
    grad_logits = (
        gates * (gate_total - jnp.sum(gates * gate_total, axis=1, keepdims=True))
    ).astype(BF)
    grad_second = entry_own[:, :model_width] + dotf(grad_logits, w_router, ((1,), (1,)))
    grad_resid_norm, grad_norm2 = second_back(grad_second)
    grad_residual = cot_own.astype(F32) + grad_resid_norm
    pad = jnp.zeros((rows, -experts % 128), BF)
    back_all = links.ag_tp(
        jnp.concatenate([grad_residual.astype(BF), grad_logits, pad], axis=1)
    )
    grad_attn_low = back_all[:, :model_width]
    second_own = lax.dynamic_slice(second_all, (me * tok_count, 0), (tok_count, model_width))
    router_part = dotf(second_own, back_all[:, model_width:], ((0,), (0,)))
    grad_out = dotf(attended, grad_attn_low, ((0,), (0,)))
    grad_mixed = dotf(grad_attn_low, w_out, ((1,), (1,))).astype(BF)
    grad_mixed = grad_mixed.reshape(
        seq_count, 2 * block_len, local_kv, query_group_width, head_size
    )
    grad_query_seq, grad_key_seq, grad_value_seq = lax.map(
        attend_backward,
        (query_rows, key_full, value_full, query_pos, key_pos, grad_mixed, log_total),
    )
    grad_kv = jnp.stack([grad_key_seq, grad_value_seq]).astype(BF)
    grad_kv = grad_kv.reshape(2, seq_count, devices, 2 * block_len, kv_width)
    grad_kv = grad_kv.transpose(2, 1, 3, 0, 4).reshape(all_tok, 2 * kv_width)
    grad_kv_own = links.rs_ctx(grad_kv)
    grad_query_rot = grad_query_seq.reshape(tok_count, local_heads, head_size)
    grad_key_rot = grad_kv_own[:, :kv_width].reshape(tok_count, local_kv, head_size)
    grad_query_raw, grad_key_raw, grad_qgain, grad_kgain = rope_back(
        (grad_query_rot, grad_key_rot)
    )
    query_low = grad_query_raw.astype(BF)
    key_low = grad_key_raw.astype(BF)
    value_low = grad_kv_own[:, kv_width:].astype(BF)
    first_part = dotf(query_low, w_query, ((1,), (1,)))
    first_part = first_part + dotf(key_low, key_weight, ((1,), (1,)))
    first_part = first_part + dotf(value_low, value_weight, ((1,), (1,)))
    grad_first = links.rs_tp(first_part.astype(BF))
    grad_first, gate_low = lax.optimization_barrier((grad_first, gate_low))
    grads = expert_grads(second_all, cot_all, gate_low, up_low, hidden_low, model_width)
    grad_gate, grad_up = (
        v.reshape(own_experts, units, model_width).transpose(0, 2, 1) for v in grads[:2]
    )
    grad_down = grads[2].reshape(own_experts, units, model_width)
    _, first_back = jax.vjp(rms_norm, own_rows(inputs), norm1_gain)
    grad_input_norm, grad_norm1 = first_back(grad_first)
    def over_ctx(v, dim):
        return lax.psum_scatter(v.astype(BF), "ctx", scatter_dimension=dim, tiled=True).astype(F32)

    grad_query = over_ctx(dotf(first_in, query_low, ((0,), (0,))), 0)
    kv_part = dotf(first_in, jnp.concatenate([key_low, value_low], axis=1), ((0,), (0,)))
    small = links.rs_ctx(jnp.concatenate([kv_part, router_part], axis=1).astype(BF))
    grad_key = small[:, :kv_width]
    grad_value = small[:, kv_width : 2 * kv_width]
    grad_router = small[:, 2 * kv_width : 2 * kv_width + experts]
    grad_out = over_ctx(grad_out, 1)
    vectors = [
        v.reshape(devices, -1) for v in (grad_norm1, grad_norm2, grad_qgain, grad_kgain)
    ]
    sizes = [v.shape[1] for v in vectors]
    pad = jnp.zeros((devices, -sum(sizes) % 1024), F32)
    packed = jnp.concatenate([*vectors, pad], axis=1).reshape(-1, 128)
    grad_input, layer_out, total = links.finish(
        (grad_residual + grad_input_norm).astype(BF), (residual + out_own).astype(BF), packed
    )
    total = total.reshape(-1)

    def piece_of(n):
        start = sum(sizes[:n])
        return total[start : start + sizes[n]]

    return (
        layer_out,
        grad_input,
        piece_of(0),
        grad_query,
        grad_key,
        grad_value,
        piece_of(2),
        piece_of(3),
        grad_out,
        piece_of(1),
        grad_router,
        grad_gate,
        grad_up,
        grad_down,
    )


def fast_shards(
    tokens_in,
    block_order,
    routes,
    norm1_gain,
    w_query,
    key_weight,
    value_weight,
    query_gain,
    key_gain,
    w_out,
    norm2_gain,
    w_router,
    w_gate,
    w_up,
    w_down,
    cotangent,
):
    tok_count, model_width = tokens_in.shape
    head_size = query_gain.shape[0]
    seq_count = block_order.shape[0]
    devices, tp_size = lax.axis_size("ctx"), lax.axis_size("tp")
    me, tp_me = lax.axis_index("ctx"), lax.axis_index("tp")
    rows = tok_count // tp_size
    block_len = tok_count // (2 * seq_count)
    experts = w_router.shape[1]
    own_experts, _, units = w_gate.shape
    hid = own_experts * units

    def row(v):
        return v.reshape(1, -1)


    token_positions = positions_of(block_order, devices, block_len)
    query_pos = lax.dynamic_index_in_dim(token_positions, me, 0, keepdims=False).reshape(-1)
    key_pos = jnp.transpose(token_positions, (1, 0, 2)).reshape(seq_count, -1).astype(F32)
    angles = angles_of(query_pos, head_size)
    cos = jnp.concatenate([jnp.cos(angles)] * 2, axis=1)
    sin = jnp.concatenate([-jnp.sin(angles), jnp.sin(angles)], axis=1)
    query_pos = jnp.broadcast_to(query_pos.astype(F32)[:, None], (tok_count, head_size))
    router_rows = w_router.T
    _, query_raw, key_raw, query_rot, kv_all, attended, logs, residual, gates, piece, first_cols = front(
        tokens_in, row(norm1_gain), w_query, key_weight, value_weight, row(query_gain),
        row(key_gain), cos, sin, query_pos, key_pos, w_out, row(norm2_gain), router_rows,
        routes.T, cotangent, 1,
    )

    gate_mat = w_gate.transpose(0, 2, 1).reshape(hid, model_width)
    up_mat = w_up.transpose(0, 2, 1).reshape(hid, model_width)
    down_mat = w_down.reshape(hid, model_width)
    all_rows, pair, hidden, gate_low, up_low, hidden_turned, gate_turned, up_turned = experts_forward(
        piece, gate_mat, up_mat, down_mat, own_experts, 3
    )
    sums_own, attended_line = reduce_experts(
        hidden, gate_low, up_low, pair, down_mat, gate_mat, up_mat, attended, 6
    )
    layer_piece, grad_residual, grad_norm2, back_cols, query_low, grad_kv, qgain_part = middle(
        sums_own, residual, gates, cotangent, row(norm2_gain), router_rows, w_out, query_rot, kv_all,
        logs, query_raw, row(query_gain), cos, sin, query_pos, key_pos, 7,
    )

    line_tok = 4 * tok_count
    back_cols = back_cols.reshape(line_tok, -1)
    grad_input, layer_out, grad_query, kv_grads, grad_out, grad_router, total = tail(
        grad_kv, query_low, key_raw, row(key_gain), cos, sin, w_query, key_weight, value_weight,
        tokens_in, row(norm1_gain), grad_residual, layer_piece, grad_norm2, qgain_part,
        first_cols.reshape(line_tok, -1), attended_line.reshape(line_tok, -1), back_cols, all_rows, 8,
    )
    per = model_width // devices // 128
    grad_key = kv_grads[:, :head_size]
    grad_value = kv_grads[:, head_size:]
    total, gate_turned = lax.optimization_barrier((total, gate_turned))
    grads = expert_grads(all_rows, all_rows, gate_turned, up_turned, hidden_turned, model_width, model_width)
    grad_gate, grad_up = (
        v.reshape(own_experts, units, model_width).transpose(0, 2, 1) for v in grads[:2]
    )
    grad_down = grads[2].reshape(own_experts, units, model_width)
    share = head_size // devices

    def gain_of(n):
        return lax.dynamic_slice_in_dim(total[n], me * share, share, axis=0)

    return (
        layer_out,
        grad_input,
        total[:per].reshape(-1),
        grad_query,
        grad_key,
        grad_value,
        gain_of(2 * per),
        gain_of(7),
        grad_out,
        total[per : 2 * per].reshape(-1),
        grad_router[:, :experts],
        grad_gate,
        grad_up,
        grad_down,
    )


def solution(mesh):
    in_specs = (
        P("ctx", None),
        P(),
        P("ctx", None),
        P(),
        P(None, "tp"),
        P(None, "tp"),
        P(None, "tp"),
        P(),
        P(),
        P("tp", None),
        P(),
        P(),
        P("ctx", None, "tp"),
        P("ctx", None, "tp"),
        P("ctx", "tp", None),
        P("ctx", None),
    )
    out_specs = (
        P("ctx", None),
        P("ctx", None),
        P("ctx"),
        P("ctx", "tp"),
        P("ctx", "tp"),
        P("ctx", "tp"),
        P("ctx"),
        P("ctx"),
        P("tp", "ctx"),
        P("ctx"),
        P("ctx", None),
        P("ctx", None, "tp"),
        P("ctx", None, "tp"),
        P("ctx", "tp", None),
    )
    own = mesh.shape["ctx"] == 8 and mesh.shape["tp"] == 4
    shards = fast_shards if own else plain_shards
    return jax.shard_map(shards, mesh=mesh, in_specs=in_specs, out_specs=out_specs, check_vma=False)
```

```python
import math
import functools
import jax
import jax.numpy as jnp
from jax import lax
from jax.sharding import PartitionSpec as P
from jax.experimental import pallas as pl
from jax.experimental.pallas import tpu as pltpu
MESH=pl.DeviceIdType.MESH

def coords():
    ctx=lax.axis_index("ctx"); tp=lax.axis_index("tp")
    return ctx//2, ctx%2, tp//2, tp%2
def dev(z,x,y,c): return (z*2+x, y*2+c)
def pid(z,x,y,c): return (z*2+x)*4+y*2+c

def neighbours():
    z,x,y,c=coords()
    ax=x+(1-c)*(1-2*x); ay=y+c*(1-2*y)
    bx=x+c*(1-2*x); by=y+(1-c)*(1-2*y)
    return z,x,y,c,ax,ay,bx,by

def barrier_all():
    z,x,y,c=coords()
    b=pltpu.get_barrier_semaphore()
    def sig(d): pl.semaphore_signal(b,inc=1,device_id=d,device_id_type=MESH)
    sig(dev(z,1-x,y,c)); sig(dev(z,x,1-y,c)); sig(dev(z,x,y,1-c))
    @pl.when(z<3)
    def _(): sig(dev(z+1,x,y,c))
    @pl.when(z>0)
    def _(): sig(dev(z-1,x,y,c))
    pl.semaphore_wait(b,5-(3-z)//3-z//3)

class Gather:
    def __init__(self, own_ref, out_ref, cols, send, recv):
        self.own, self.out, self.cols, self.send, self.recv = own_ref, out_ref, cols, send, recv
        self.rows = own_ref.shape[0]
        z, x, y, c, ax, ay, bx, by = neighbours()
        self.at_me = (z, x, y, c, ax, ay, bx, by)
        self.up, self.down = dev(z + 1 - z // 3, x, y, c), dev(z - 1 + (3 - z) // 3, x, y, c)
        self.A, self.B, self.C = dev(z, ax, ay, c), dev(z, bx, by, c), dev(z, x, y, 1 - c)

    def place(self, p):
        return self.out.at[pl.ds(pl.multiple_of(p * self.rows, self.rows), self.rows), self.cols]

    def copy(self, p, to, k, own=False):
        return pltpu.make_async_remote_copy(
            src_ref=self.own.at[:, self.cols] if own else self.place(p), dst_ref=self.place(p),
            send_sem=self.send.at[k, p], recv_sem=self.recv.at[p], device_id=to, device_id_type=MESH)

    def wait(self, p):
        self.copy(p, self.C, 4).wait_recv()

    def start(self):
        z, x, y, c = self.at_me[:4]
        me = pid(z, x, y, c)
        @pl.when(z < 3)
        def _():
            self.copy(me, self.up, 0, True).start()

        @pl.when(z > 0)
        def _():
            self.copy(me, self.down, 1, True).start()

        for to, k in ((self.A, 2), (self.B, 3), (self.C, 4)):
            self.copy(me, to, k, True).start()

    def from_line(self, zz):
        z, x, y, c = self.at_me[:4]
        p = pid(zz, x, y, c)
        self.wait(p)

        @pl.when((zz < z) & (z < 3))
        def _():
            self.copy(p, self.up, 0).start()

        @pl.when((zz > z) & (z > 0))
        def _():
            self.copy(p, self.down, 1).start()

        for to, k in ((self.A, 2), (self.B, 3), (self.C, 4)):
            self.copy(p, to, k).start()

    def from_a(self, zz):
        z, x, y, c, ax, ay, bx, by = self.at_me

        p = pid(zz, ax, ay, c)
        self.wait(p)
        self.copy(p, self.B, 3).start()
        self.copy(p, self.C, 4).start()

    def from_b(self, zz, xx, yy):
        c = self.at_me[3]

        p = pid(zz, xx, yy, c)
        self.wait(p)
        self.copy(p, self.C, 4).start()

    def finish(self):
        z, x, y, c, ax, ay, bx, by = self.at_me

        def one(zz, carry):
            p = pid(zz, x, y, c)

            @pl.when((z < 3) & (zz <= z))
            def _():
                self.copy(p, self.up, 0).wait_send()

            @pl.when((z > 0) & (zz >= z))
            def _():
                self.copy(p, self.down, 1).wait_send()

            for to, k in ((self.A, 2), (self.B, 3), (self.C, 4)):
                self.copy(p, to, k).wait_send()
            p = pid(zz, ax, ay, c)
            self.copy(p, self.B, 3).wait_send()
            self.copy(p, self.C, 4).wait_send()
            self.copy(pid(zz, bx, by, c), self.C, 4).wait_send()
            self.copy(pid(zz, 1 - x, 1 - y, c), self.C, 4).wait_send()
            return carry

        lax.fori_loop(0, 4, one, 0)


def far_z(z, k):
    half = z // 2
    near = z + half * (3 - 2 * z)
    place = 3 - k + (k // 2) * (2 * (k % 2) - 1) * near
    return place + half * (3 - 2 * place)


def reduce_kernel(
    hs_ref, gl_ref, ul_ref, pair_ref, wd_ref, wg_ref, wu_ref, att_ref,
    out_ref, line_ref,
    acc, cbuf, bbuf, abuf, zbuf, blk, mats, low, pair,
    csend, crecv, bsend, brecv, asend, arecv, zsend, zrecv, msem, lsem, psem, nsem, nsend, nrecv,
):
    f32 = jnp.float32
    rows = out_ref.shape[0]
    width = wd_ref.shape[1]
    z, x, y, c, ax, ay, bx, by = neighbours()
    dx, dy = 1 - x, 1 - y
    A, B, C = dev(z, ax, ay, c), dev(z, bx, by, c), dev(z, x, y, 1 - c)
    up, down = dev(z + 1 - z // 3, x, y, c), dev(z - 1 + (3 - z) // 3, x, y, c)
    tok = 4 * rows

    def q(zz, xx, yy):
        return zz * 4 + xx * 2 + yy

    def place_of(u):
        return far_z(z, u // 2), (u % 2) * (2 * x - 1) + 1 - x

    def loads(u):
        zz, xx = place_of(u)
        span = pl.ds(pl.multiple_of((zz * 2 + xx) * tok, tok), tok)
        slot = u % 2
        return [
            pltpu.make_async_copy(r.at[span], low.at[slot, n], lsem.at[slot, n])
            for n, r in enumerate((hs_ref, gl_ref, ul_ref))
        ] + [pltpu.make_async_copy(pair_ref.at[span], pair.at[slot], psem.at[slot])]

    def part_rows(slot, yy, cc):
        return blk.at[slot, pl.ds(pl.multiple_of((yy * 2 + cc) * rows, rows), rows)]

    def ccopy(zz, xx, yy, slot):
        i = q(zz, xx, yy)
        return pltpu.make_async_remote_copy(
            src_ref=part_rows(slot, yy, 1 - c), dst_ref=cbuf.at[i], send_sem=csend.at[slot, yy],
            recv_sem=crecv.at[i], device_id=C, device_id_type=MESH)

    weights = [pltpu.make_async_copy(r, mats.at[n], msem.at[n]) for n, r in enumerate((wd_ref, wg_ref, wu_ref))]
    for cp in weights:
        cp.start()
    for cp in loads(0):
        cp.start()

    def products(u):
        slot = u % 2
        zz, xx = place_of(u)
        for cp in loads(u):
            cp.wait()

        @pl.when(u < 7)
        def _():
            for cp in loads(u + 1):
                cp.start()

        @pl.when(u > 1)
        def _():
            for yy in range(2):
                ccopy(zz, xx, yy, slot).wait_send()

        blk[slot, :, :width] = nn(low[slot, 0], mats[0]).astype(blk.dtype)
        @pl.when(u == 0)
        def _():
            weights[1].wait()
            weights[2].wait()

        blk[slot, :, width : 2 * width] = (
            nn(low[slot, 1], mats[1]) + nn(low[slot, 2], mats[2])
        ).astype(blk.dtype)
        blk[slot, :, 2 * width :] = pair[slot]
        for yy in range(2):
            ccopy(zz, xx, yy, slot).start()
        for yy in range(2):
            acc[q(zz, xx, yy)] = part_rows(slot, yy, c)[...]

    def bcopy(zz, far):
        i = zz + 4 * far
        place = q(zz, dx, dy) if far else q(zz, bx, by)
        return pltpu.make_async_remote_copy(
            src_ref=acc.at[place], dst_ref=bbuf.at[i], send_sem=bsend.at[i],
            recv_sem=brecv.at[i], device_id=B, device_id_type=MESH)

    def acopy(zz):
        return pltpu.make_async_remote_copy(
            src_ref=acc.at[q(zz, ax, ay)], dst_ref=abuf.at[zz], send_sem=asend.at[zz],
            recv_sem=arecv.at[zz], device_id=A, device_id_type=MESH)

    def zcopy(zz, to, slot):
        return pltpu.make_async_remote_copy(
            src_ref=acc.at[q(zz, x, y)], dst_ref=zbuf.at[slot], send_sem=zsend.at[zz],
            recv_sem=zrecv.at[slot], device_id=to, device_id_type=MESH)

    def plus_c(zz, xx, yy):
        ccopy(zz, xx, yy, 0).wait_recv()
        i = q(zz, xx, yy)
        return acc[i].astype(f32) + cbuf[i].astype(f32)

    def stage_b(k, far):
        zz = far_z(z, k)
        xx, yy = (dx, dy) if far else (bx, by)
        acc[q(zz, xx, yy)] = plus_c(zz, xx, yy).astype(acc.dtype)
        bcopy(zz, far).start()

    def stage_a(k):
        zz = far_z(z, k)
        value = plus_c(zz, ax, ay)
        bcopy(zz, 1).wait_recv()
        acc[q(zz, ax, ay)] = (value + bbuf[zz + 4].astype(f32)).astype(acc.dtype)
        acopy(zz).start()

    def stage_z(k):
        zz = far_z(z, k)
        place = q(zz, x, y)
        value = plus_c(zz, x, y)
        bcopy(zz, 0).wait_recv()
        acopy(zz).wait_recv()
        value = value + bbuf[zz].astype(f32) + abuf[zz].astype(f32)

        @pl.when(zz != z)
        def _():
            acc[place] = value.astype(acc.dtype)

            @pl.when((zz > z) & (z > 0))
            def _():
                zcopy(zz, up, zz).wait_recv()
                acc[place] = (acc[place].astype(f32) + zbuf[zz].astype(f32)).astype(acc.dtype)

            @pl.when((zz < z) & (z < 3))
            def _():
                zcopy(zz, down, zz).wait_recv()
                acc[place] = (acc[place].astype(f32) + zbuf[zz].astype(f32)).astype(acc.dtype)

            @pl.when(zz > z)
            def _():
                zcopy(zz, up, zz).start()

            @pl.when((zz < z) & (zz != z - 1))
            def _():
                zcopy(zz, down, zz).start()

            @pl.when(zz == z - 1)
            def _():
                zcopy(zz, down, 4).start()

        @pl.when(zz == z)
        def _():
            out_ref[...] = value

            @pl.when(z > 0)
            def _():
                zcopy(z, up, z).wait_recv()
                out_ref[...] += zbuf[z].astype(f32)

            @pl.when(z < 3)
            def _():
                zcopy(z, down, 4).wait_recv()
                out_ref[...] += zbuf[4].astype(f32)

    line = Line(lambda zz: line_ref.at[zz], nsend, nrecv, att_ref)
    mine = pltpu.make_async_copy(att_ref, line_ref.at[z], nsem)
    mine.start()
    barrier_all()
    line.start()
    weights[0].wait()

    def step(u, carry):
        @pl.when(u == 1)
        def _():
            stage_b(0, 1)

        @pl.when(u < 8)
        def _():
            products(u)

        for d in (1, 2, 3):
            @pl.when(u == 2 * d + 1)
            def _():
                line.pass_on(d)

        k = (u - 1) // 2

        @pl.when((u > 1) & (u < 9) & (u % 2 == 1))
        def _():
            stage_b(k, 1)

        @pl.when((u > 0) & (u < 9) & (u % 2 == 0))
        def _():
            stage_b(k, 0)

        @pl.when((u >= 5) & (u < 13) & (u % 2 == 1))
        def _():
            stage_a((u - 5) // 2)

        @pl.when((u >= 8) & (u % 2 == 0))
        def _():
            stage_z((u - 8) // 2)

        return carry

    lax.fori_loop(0, 15, step, 0)
    mine.wait()
    line.finish()
    for slot in range(2):
        for yy in range(2):
            ccopy(z, x, yy, slot).wait_send()

    def last(zz, carry):
        bcopy(zz, 1).wait_send()
        bcopy(zz, 0).wait_send()
        acopy(zz).wait_send()

        @pl.when(zz != z)
        def _():
            zcopy(zz, up, zz).wait_send()

        return carry

    lax.fori_loop(0, 4, last, 0)


def reduce_experts(hs, gl, ul, pair, wd, wg, wu, att, cid):
    n, hid = hs.shape
    width = wd.shape[1]
    rows = n // 32
    w = 2 * width + pair.shape[1]
    dma = pltpu.SemaphoreType.DMA
    bf = jnp.bfloat16

    def pieces(k):
        return pltpu.VMEM((k, rows, w), bf)

    anywhere = pl.BlockSpec(memory_space=pl.ANY)
    return pl.pallas_call(
        reduce_kernel,
        in_specs=[anywhere] * 8,
        out_specs=[pl.BlockSpec(memory_space=pltpu.VMEM), anywhere],
        out_shape=[
            jax.ShapeDtypeStruct((rows, w), jnp.float32), jax.ShapeDtypeStruct((4, *att.shape), bf),
        ],
        scratch_shapes=[
            pieces(16), pieces(16), pieces(8), pieces(4), pieces(5),
            pltpu.VMEM((2, 4 * rows, w), bf),
            pltpu.VMEM((3, hid, width), bf),
            pltpu.VMEM((2, 3, 4 * rows, hid), bf),
            pltpu.VMEM((2, 4 * rows, pair.shape[1]), bf),
            dma((2, 2)), dma((16,)), dma((8,)), dma((8,)), dma((4,)), dma((4,)),
            dma((4,)), dma((5,)), dma((3,)), dma((2, 3)), dma((2,)), dma, dma((2, 4)), dma((4,)),
        ],
        compiler_params=pltpu.CompilerParams(
            collective_id=cid, has_side_effects=True, vmem_limit_bytes=56 * 2**20
        ),
        cost_estimate=pl.CostEstimate(
            flops=6 * n * width * hid, bytes_accessed=10 * n * width, transcendentals=0
        ),
        name="reduce_experts",
    )(hs, gl, ul, pair, wd, wg, wu, att)


def barrier_wide():
    z, x, y, c = coords()
    ctx, tp = lax.axis_index("ctx"), lax.axis_index("tp")
    bar = pltpu.get_barrier_semaphore()
    for i in range(1, 8):
        pl.semaphore_signal(bar, inc=1, device_id=((ctx + i) % 8, tp), device_id_type=MESH)
    for to in (dev(z, x, 1 - y, c), dev(z, x, y, 1 - c), dev(z, x, 1 - y, 1 - c)):
        pl.semaphore_signal(bar, inc=1, device_id=to, device_id_type=MESH)
    pl.semaphore_wait(bar, 10)


class Columns:
    def __init__(self, src, buf, send, recv, tsend, trecv):
        self.src, self.buf, self.send, self.recv = src, buf, send, recv
        self.tsend, self.trecv = tsend, trecv
        self.tp = lax.axis_index("tp")
        z, x, y, c = coords()
        self.z, self.x, self.y, self.c = z, x, y, c
        self.Y, self.C = dev(z, x, 1 - y, c), dev(z, x, y, 1 - c)
        self.mine, self.by_y, self.by_c, self.by_d = y * 2 + c, (1 - y) * 2 + c, y * 2 + 1 - c, (1 - y) * 2 + 1 - c

    def push(self, i):
        to = (self.z + i) % 4
        return pltpu.make_async_remote_copy(
            src_ref=self.src.at[to], dst_ref=self.buf.at[self.z, self.tp],
            send_sem=self.send.at[i], recv_sem=self.recv.at[i],
            device_id=dev(to, self.x, self.y, self.c), device_id_type=MESH)

    def over(self, part, to, k):
        return pltpu.make_async_remote_copy(
            src_ref=self.buf.at[:, part], dst_ref=self.buf.at[:, part], send_sem=self.tsend.at[k],
            recv_sem=self.trecv.at[part], device_id=to, device_id_type=MESH)

    def start(self):
        for i in range(1, 4):
            self.push(i).start()
        self.buf[self.z, self.tp] = self.src[self.z]

    def exchange(self):
        for i in range(1, 4):
            self.push(i).wait_recv()
        self.over(self.mine, self.Y, 0).start()
        self.over(self.mine, self.C, 1).start()

    def forward(self):
        self.over(self.by_y, self.Y, 0).wait_recv()
        self.over(self.by_y, self.C, 2).start()

    def finish(self):
        self.over(self.by_c, self.C, 1).wait_recv()
        self.over(self.by_d, self.C, 2).wait_recv()
        for i in range(1, 4):
            self.push(i).wait_send()
        self.over(self.mine, self.Y, 0).wait_send()
        self.over(self.mine, self.C, 1).wait_send()
        self.over(self.by_y, self.C, 2).wait_send()


class Line:
    def __init__(self, place, send, recv, first=None):
        self.place, self.send, self.recv, self.first = place, send, recv, first
        z, x, y, c = coords()
        self.z = z
        self.up, self.down = dev(z + 1 - z // 3, x, y, c), dev(z - 1 + (3 - z) // 3, x, y, c)

    def copy(self, zz, to, k, own=False):
        src = self.first if own and self.first is not None else self.place(zz)
        return pltpu.make_async_remote_copy(
            src_ref=src, dst_ref=self.place(zz), send_sem=self.send.at[k, zz],
            recv_sem=self.recv.at[zz], device_id=to, device_id_type=MESH)

    def start(self):
        @pl.when(self.z < 3)
        def _():
            self.copy(self.z, self.up, 0, True).start()

        @pl.when(self.z > 0)
        def _():
            self.copy(self.z, self.down, 1, True).start()

    def pass_on(self, d):
        z = self.z

        @pl.when(z - d >= 0)
        def _():
            self.copy(z - d, self.up, 0).wait_recv()

            @pl.when(z < 3)
            def _():
                self.copy(z - d, self.up, 0).start()

        @pl.when(z + d <= 3)
        def _():
            self.copy(z + d, self.down, 1).wait_recv()

            @pl.when(z > 0)
            def _():
                self.copy(z + d, self.down, 1).start()

    def finish(self):
        z = self.z
        for zz in range(4):
            @pl.when((z < 3) & (zz <= z))
            def _():
                self.copy(zz, self.up, 0).wait_send()

            @pl.when((z > 0) & (zz >= z))
            def _():
                self.copy(zz, self.down, 1).wait_send()


class Spread:
    def __init__(self, place, send, recv, first=None):
        self.place, self.send, self.recv, self.first = place, send, recv, first
        z, x, y, c = coords()
        self.z, self.x = z, x
        self.X = dev(z, 1 - x, y, c)
        self.up, self.down = dev(z + 1 - z // 3, x, y, c), dev(z - 1 + (3 - z) // 3, x, y, c)
        self.me = z * 2 + x

    def copy(self, p, to, k, own=False):
        src = self.first if own and self.first is not None else self.place(p)
        return pltpu.make_async_remote_copy(
            src_ref=src, dst_ref=self.place(p), send_sem=self.send.at[k, p],
            recv_sem=self.recv.at[p], device_id=to, device_id_type=MESH)

    def start_x(self):
        self.copy(self.me, self.X, 2, True).start()

    def start_z(self):
        @pl.when(self.z < 3)
        def _():
            self.copy(self.me, self.up, 0, True).start()

        @pl.when(self.z > 0)
        def _():
            self.copy(self.me, self.down, 1, True).start()

    def pass_on(self, d):
        z, x = self.z, self.x

        @pl.when(z - d >= 0)
        def _():
            p = (z - d) * 2 + x
            self.copy(p, self.X, 2).wait_recv()

            @pl.when(z < 3)
            def _():
                self.copy(p, self.up, 0).start()

            self.copy(p, self.X, 2).start()

        @pl.when(z + d <= 3)
        def _():
            p = (z + d) * 2 + x
            self.copy(p, self.X, 2).wait_recv()

            @pl.when(z > 0)
            def _():
                self.copy(p, self.down, 1).start()

            self.copy(p, self.X, 2).start()

    def arrive(self):
        for zz in range(4):
            self.copy(zz * 2 + 1 - self.x, self.X, 2).wait_recv()

    def finish(self):
        z, x = self.z, self.x
        for zz in range(4):
            p = zz * 2 + x

            @pl.when((z < 3) & (zz <= z))
            def _():
                self.copy(p, self.up, 0).wait_send()

            @pl.when((z > 0) & (zz >= z))
            def _():
                self.copy(p, self.down, 1).wait_send()

            self.copy(p, self.X, 2).wait_send()


def row_norm(v):
    return lax.rsqrt(jnp.mean(v * v, axis=1, keepdims=True) + 1e-06)


def turn(v, cos, sin):
    return v * cos + pltpu.roll(v, v.shape[1] // 2, 1) * sin


def turn_back(v, cos, sin):
    return v * cos - pltpu.roll(v, v.shape[1] // 2, 1) * sin


def front_kernel(
    x_ref, g1_in, wq_ref, wk_ref, wv_ref, qg_in, kg_in, cos_ref, sin_ref, qpos_ref, kpos_ref,
    wo_ref, g2_in, wr_in, routes_in, cot_ref,
    first_ref, qraw_ref, kraw_ref, qrot_ref, kv_ref, att_ref, log_ref, res_ref, gates_ref, piece_ref, cols_ref,
    xs, g1_ref, qg_ref, kg_ref, g2_ref, wr_ref, routes_ref, wk, wv, turned, wq, wo, part, cbuf, ybuf, stage, csrc,
    wsem, ksend, krecv, csend, crecv, ysend, yrecv, psend, precv, tsend, trecv,
):
    f32, bf = jnp.float32, jnp.bfloat16
    z, x, y, c = coords()
    rows = res_ref.shape[0]
    experts = wr_ref.shape[0]
    head = qg_ref.shape[1]
    heads = wq_ref.shape[1] // head
    half = x_ref.shape[0] // 2
    fetched = [
        pltpu.make_async_copy(src, dst, wsem.at[n])
        for n, (src, dst) in enumerate((
            (x_ref, xs), (g1_in, g1_ref), (qg_in, qg_ref), (kg_in, kg_ref), (g2_in, g2_ref),
            (wr_in, wr_ref), (routes_in, routes_ref), (wk_ref, wk), (wv_ref, wv), (wq_ref, wq), (wo_ref, wo),
        ))
    ]
    for cp in fetched:
        cp.start()
    wqc, woc = fetched[9:]
    own = pl.ds(pl.multiple_of((y * 2 + c) * rows, rows), rows)
    Y, C = dev(z, x, 1 - y, c), dev(z, x, y, 1 - c)
    barrier_wide()
    cotc = pltpu.make_async_copy(cot_ref.at[own], piece_ref.at[:, x_ref.shape[1] : 2 * x_ref.shape[1]], wsem.at[11])
    cotc.start()
    for cp in fetched[:9]:
        cp.wait()
    turned[...] = routes_ref[...].T
    value = xs[...].astype(f32)
    first = (value * row_norm(value) * g1_ref[...]).astype(bf)
    first_ref[...] = first
    cos, sin = cos_ref[...], sin_ref[...]
    kraw = nn(first, wk[...])
    kraw_ref[...] = kraw
    krot = turn(kraw * row_norm(kraw) * kg_ref[...], cos, sin).astype(bf)
    vrow = nn(first, wv[...]).astype(bf)
    me = z * 2 + x
    for s in range(2):
        kv_ref[s, me] = krot[s * half : (s + 1) * half]
        kv_ref[2 + s, me] = vrow[s * half : (s + 1) * half]

    keys_out = Spread(lambda p: kv_ref.at[:, p], ksend, krecv)
    keys_out.start_z()
    keys_out.start_x()

    wqc.wait()
    qraw_ref[...] = nn(first, wq[...])
    keys_out.pass_on(1)

    def rope_head(h, carry):
        lanes = pl.ds(pl.multiple_of(h * head, head), head)
        raw = qraw_ref[:, lanes]
        rot = turn(raw * row_norm(raw) * qg_ref[...], cos_ref[...], sin_ref[...]).astype(bf)
        qrot_ref[h] = rot[:half]
        qrot_ref[heads + h] = rot[half:]
        return carry

    lax.fori_loop(0, heads // 2, rope_head, 0)
    keys_out.pass_on(2)
    lax.fori_loop(heads // 2, heads, rope_head, 0)
    keys_out.pass_on(3)
    keys_out.arrive()
    width = first.shape[1]
    per = width // 4
    for i in range(4):
        csrc[i] = first_ref[own, i * per : (i + 1) * per]
    blocks = Columns(csrc, cols_ref, psend, precv, tsend, trecv)
    blocks.start()

    scale = 1.0 / math.sqrt(head)

    group = 4

    def attend(i, carry):
        s = i // (heads // group)
        h = i % (heads // group) * group
        span = pl.ds(pl.multiple_of(s * half, half), half)
        keys = kv_ref[s].reshape(8 * half, head)
        vals = kv_ref[2 + s].reshape(8 * half, head)
        query = qrot_ref[pl.ds(i * group, group)].reshape(group * half, head)
        scores = (nt(query, keys) * scale).reshape(group, half, 8 * half)
        allowed = qpos_ref[span, :1] >= kpos_ref[pl.ds(s, 1), :]
        scores = jnp.where(allowed[None], scores, -1e9).reshape(group * half, 8 * half)
        top = jnp.max(scores, axis=1, keepdims=True)
        weights = jnp.exp(scores - top)
        total = jnp.sum(weights, axis=1, keepdims=True)
        probs = (weights * (1.0 / total)).astype(bf)
        mixed = nn(probs, vals).astype(bf)
        logs = jnp.broadcast_to(top + jnp.log(total), (group * half, head))
        log_ref[pl.ds(i * group, group)] = logs.reshape(group, half, head)
        for g in range(group):
            lanes = pl.ds(pl.multiple_of((h + g) * head, head), head)
            att_ref[span, lanes] = mixed[g * half : (g + 1) * half]
        @pl.when(i == steps // 2 - 1)
        def _():
            blocks.exchange()
        return carry

    steps = 2 * heads // group
    lax.fori_loop(0, steps, attend, 0)
    blocks.forward()
    woc.wait()

    def at(yy, cc):
        return part.at[pl.ds(pl.multiple_of((yy * 2 + cc) * rows, rows), rows)]

    def project(yy):
        span = pl.ds(pl.multiple_of(yy * 2 * rows, 2 * rows), 2 * rows)
        part[span] = nn(att_ref[span], wo[...]).astype(bf)

    def ccopy(yy):
        return pltpu.make_async_remote_copy(
            src_ref=at(yy, 1 - c), dst_ref=cbuf.at[yy], send_sem=csend.at[yy],
            recv_sem=crecv.at[yy], device_id=C, device_id_type=MESH)

    project(1 - y)
    ccopy(1 - y).start()
    project(y)
    ccopy(y).start()
    ccopy(1 - y).wait_recv()
    stage[...] = (at(1 - y, c)[...].astype(f32) + cbuf[1 - y].astype(f32)).astype(bf)
    yc = pltpu.make_async_remote_copy(
        src_ref=stage, dst_ref=ybuf, send_sem=ysend, recv_sem=yrecv, device_id=Y, device_id_type=MESH)
    yc.start()
    ccopy(y).wait_recv()
    res = xs[own].astype(f32) + (at(y, c)[...].astype(f32) + cbuf[y].astype(f32))
    lane = lax.broadcasted_iota(jnp.int32, (rows, 4 * experts), 1)
    named = jnp.zeros((rows, 4 * experts), jnp.bool_)
    routes = turned[own]
    for k in range(routes.shape[1]):
        named = named | (lane % experts == routes[:, k : k + 1])
    yc.wait_recv()
    res = res + ybuf[...].astype(f32)
    res_ref[...] = res
    second = (res * row_norm(res) * g2_ref[...]).astype(bf)
    piece_ref[:, :width] = second
    logits = nt(second, wr_ref[...])
    logits = jnp.concatenate([logits, logits, jnp.zeros((rows, 2 * experts), f32)], axis=1)
    masked = jnp.where(named & (lane < 2 * experts), logits, -1e30)
    top = jnp.max(masked, axis=1, keepdims=True)
    weights = jnp.where(named & (lane < 2 * experts), jnp.exp(masked - top), 0.0)
    total = jnp.sum(jnp.where(lane < experts, weights, 0.0), axis=1, keepdims=True)
    gates = weights / total
    high = gates.astype(bf)
    low = (gates - high.astype(f32)).astype(bf)
    gates_ref[...] = jnp.where(lane < experts, gates, 0.0)
    piece_ref[:, 2 * width :] = jnp.where(lane < experts, high, low)

    yc.wait_send()
    ccopy(0).wait_send()
    ccopy(1).wait_send()
    blocks.finish()
    keys_out.finish()
    cotc.wait()


def front(x, g1, wq, wk, wv, qg, kg, cos, sin, qpos, kpos, wo, g2, wr, routes, cot, cid):
    tok, width = x.shape
    head = qg.shape[1]
    cols = wq.shape[1]
    heads = cols // head
    rows, half = tok // 4, tok // 2
    f32, bf = jnp.float32, jnp.bfloat16
    dma = pltpu.SemaphoreType.DMA
    vm, anywhere = pl.BlockSpec(memory_space=pltpu.VMEM), pl.BlockSpec(memory_space=pl.ANY)

    def out(shape, kind):
        return jax.ShapeDtypeStruct(shape, kind)

    return pl.pallas_call(
        front_kernel,
        in_specs=[anywhere] * 7 + [vm] * 4 + [anywhere] * 5,
        out_specs=[vm] * 11,
        out_shape=[
            out((tok, width), bf), out((tok, cols), f32), out((tok, head), f32),
            out((2 * heads, half, head), bf), out((4, 8, half, head), bf), out((tok, cols), bf),
            out((2 * heads, half, head), f32), out((rows, width), f32), out((rows, 128), f32),
            out((rows, 2 * width + 128), bf), out((4, 4, rows, width // 4), bf),
        ],
        scratch_shapes=[
            pltpu.VMEM((tok, width), bf), pltpu.VMEM(g1.shape, f32), pltpu.VMEM(qg.shape, f32),
            pltpu.VMEM(kg.shape, f32), pltpu.VMEM(g2.shape, f32), pltpu.VMEM(wr.shape, bf),
            pltpu.VMEM(routes.shape, jnp.int32), pltpu.VMEM((width, head), bf), pltpu.VMEM((width, head), bf),
            pltpu.VMEM(routes.shape[::-1], jnp.int32),
            pltpu.VMEM((width, cols), bf), pltpu.VMEM((cols, width), bf), pltpu.VMEM((tok, width), bf),
            pltpu.VMEM((2, rows, width), bf), pltpu.VMEM((rows, width), bf), pltpu.VMEM((rows, width), bf),
            pltpu.VMEM((4, rows, width // 4), bf),
            dma((12,)), dma((3, 8)), dma((8,)), dma((2,)), dma((2,)), dma, dma,
            dma((4,)), dma((4,)), dma((3,)), dma((4,)),
        ],
        compiler_params=pltpu.CompilerParams(
            collective_id=cid, has_side_effects=True, vmem_limit_bytes=60 * 2**20
        ),
        name="front",
    )(x, g1, wq, wk, wv, qg, kg, cos, sin, qpos, kpos, wo, g2, wr, routes, cot)


def middle_kernel(
    sums_ref, res_ref, gates_ref, cot_in, g2_in, wr_in, wo_ref, qrot_ref, kv_ref, log_ref,
    qraw_ref, qg_in, cos_ref, sin_ref, qpos_ref, kpos_ref,
    layer_ref, gres_ref, gn2_ref, cols_ref, qlow_ref, dkv_ref, qgain_ref,
    cot_ref, g2_ref, wr_ref, qg_ref, wo, back, mixed, dk, dv, csrc, wsem, send, recv, psend, precv, tsend, trecv,
):
    f32, bf = jnp.float32, jnp.bfloat16
    z, x, y, c = coords()
    rows, width = res_ref.shape
    experts = wr_in.shape[0]
    head = qg_in.shape[1]
    heads = qraw_ref.shape[1] // head
    half = qraw_ref.shape[0] // 2
    mine = pl.ds(pl.multiple_of((y * 2 + c) * rows, rows), rows)
    fetched = [
        pltpu.make_async_copy(src, dst, wsem.at[n])
        for n, (src, dst) in enumerate((
            (cot_in.at[mine], cot_ref), (g2_in, g2_ref), (wr_in, wr_ref), (qg_in, qg_ref), (wo_ref, wo)))
    ]
    for item in fetched:
        item.start()
    woc = fetched[4]
    barrier_wide()
    Y, C = dev(z, x, 1 - y, c), dev(z, x, y, 1 - c)

    def at(yy, cc):
        return back.at[pl.ds(pl.multiple_of((yy * 2 + cc) * rows, rows), rows)]

    for item in fetched[:4]:
        item.wait()
    res = res_ref[...]
    layer_ref[...] = (res + sums_ref[:, :width]).astype(bf)
    gates = gates_ref[...]
    pair = sums_ref[:, 2 * width :]
    glog = (gates * (pair - jnp.sum(gates * pair, axis=1, keepdims=True))).astype(bf)
    gsec = sums_ref[:, width : 2 * width] + nn(glog[:, :experts], wr_ref[...])
    rs = row_norm(res)
    unit = res * rs
    gn2_ref[...] = jnp.sum(gsec * unit, axis=0, keepdims=True)
    cg = gsec * g2_ref[...]
    gres = cot_ref[...].astype(f32) + rs * (cg - unit * jnp.mean(cg * unit, axis=1, keepdims=True))
    gres_ref[...] = gres
    glow = gres.astype(bf)
    back[mine] = glow

    def cp(yy, cc, to, k):
        return pltpu.make_async_remote_copy(
            src_ref=at(yy, cc), dst_ref=at(yy, cc), send_sem=send.at[k],
            recv_sem=recv.at[yy * 2 + cc], device_id=to, device_id_type=MESH)

    cp(y, c, Y, 0).start()
    cp(y, c, C, 1).start()
    per = width // 4
    for i in range(4):
        csrc[i, :, :per] = glow[:, i * per : (i + 1) * per]
        csrc[i, :, per:] = glog
    blocks = Columns(csrc, cols_ref, psend, precv, tsend, trecv)
    blocks.start()
    dk[...] = jnp.zeros_like(dk)
    dv[...] = jnp.zeros_like(dv)
    qgain_ref[...] = jnp.zeros_like(qgain_ref)
    woc.wait()

    def mix(yy):
        span = pl.ds(pl.multiple_of(yy * 2 * rows, 2 * rows), 2 * rows)
        both = nt(back[span], wo[...]).astype(bf)
        for h in range(heads):
            mixed[yy * heads + h] = both[:, h * head : (h + 1) * head]

    cp(y, 1 - c, C, 1).wait_recv()
    mix(y)
    cp(1 - y, c, Y, 0).wait_recv()
    cp(1 - y, c, C, 2).start()
    cp(1 - y, 1 - c, C, 2).wait_recv()
    mix(1 - y)
    scale = 1.0 / math.sqrt(head)

    group = 4

    def attend(i, carry):
        s = i // (heads // group)
        h = i % (heads // group) * group
        span = pl.ds(pl.multiple_of(s * half, half), half)
        mine = pl.ds(i * group, group)
        keys = kv_ref[s].reshape(8 * half, head)
        vals = kv_ref[2 + s].reshape(8 * half, head)
        query = qrot_ref[mine].reshape(group * half, head)
        grad = mixed[mine].reshape(group * half, head)
        scores = (nt(query, keys) * scale).reshape(group, half, 8 * half)
        allowed = qpos_ref[span, :1] >= kpos_ref[pl.ds(s, 1), :]
        logs = log_ref[mine][:, :, :1]
        probs = jnp.where(allowed[None], jnp.exp(scores - logs), 0.0).reshape(group * half, 8 * half)
        gprobs = nt(grad, vals)
        inner = jnp.sum(probs * gprobs, axis=1, keepdims=True)
        dots = (probs * (gprobs - inner) * scale).astype(bf)
        dk[s] += tn(dots, query)
        dv[s] += tn(probs.astype(bf), grad)
        drot = nn(dots, keys)
        for g in range(group):
            lanes = pl.ds(pl.multiple_of((h + g) * head, head), head)
            raw = qraw_ref[span, lanes]
            dn = turn_back(drot[g * half : (g + 1) * half], cos_ref[span], sin_ref[span])
            rs = row_norm(raw)
            unit = raw * rs
            qgain_ref[...] += jnp.sum((dn * unit).reshape(half // 8, 8, head), axis=0)
            cg = dn * qg_ref[...]
            low = rs * (cg - unit * jnp.mean(cg * unit, axis=1, keepdims=True))
            qlow_ref[span, lanes] = low.astype(bf)
        return carry

    steps = 2 * heads // group
    lax.fori_loop(0, steps // 2, attend, 0)
    blocks.exchange()
    lax.fori_loop(steps // 2, steps, attend, 0)
    blocks.forward()
    for s in range(2):
        dkv_ref[s] = dk[s].astype(bf).reshape(8, half, head)
        dkv_ref[2 + s] = dv[s].astype(bf).reshape(8, half, head)
    cp(y, c, Y, 0).wait_send()
    cp(y, c, C, 1).wait_send()
    cp(1 - y, c, C, 2).wait_send()
    blocks.finish()


def middle(sums, res, gates, cot, g2, wr, wo, qrot, kv, logs, qraw, qg, cos, sin, qpos, kpos, cid):
    rows, width = res.shape
    tok, cols = qraw.shape
    head = qg.shape[1]
    half = tok // 2
    f32, bf = jnp.float32, jnp.bfloat16
    dma = pltpu.SemaphoreType.DMA
    vm, anywhere = pl.BlockSpec(memory_space=pltpu.VMEM), pl.BlockSpec(memory_space=pl.ANY)

    def out(shape, kind):
        return jax.ShapeDtypeStruct(shape, kind)

    return pl.pallas_call(
        middle_kernel,
        in_specs=[vm] * 3 + [anywhere] * 4 + [vm] * 4 + [anywhere] + [vm] * 4,
        out_specs=[vm] * 7,
        out_shape=[
            out((rows, width), bf), out((rows, width), f32), out((1, width), f32),
            out((4, 4, rows, width // 4 + 128), bf), out((tok, cols), bf), out((4, 8, half, head), bf),
            out((8, head), f32),
        ],
        scratch_shapes=[
            pltpu.VMEM((rows, width), bf), pltpu.VMEM(g2.shape, f32), pltpu.VMEM(wr.shape, bf),
            pltpu.VMEM(qg.shape, f32),
            pltpu.VMEM((cols, width), bf), pltpu.VMEM((tok, width), bf), pltpu.VMEM((2 * cols // head, half, head), bf),
            pltpu.VMEM((2, 8 * half, head), f32), pltpu.VMEM((2, 8 * half, head), f32),
            pltpu.VMEM((4, rows, width // 4 + 128), bf),
            dma((5,)), dma((3,)), dma((4,)), dma((4,)), dma((4,)), dma((3,)), dma((4,)),
        ],
        compiler_params=pltpu.CompilerParams(
            collective_id=cid, has_side_effects=True, vmem_limit_bytes=52 * 2**20
        ),
        name="middle",
    )(sums, res, gates, cot, g2, wr, wo, qrot, kv, logs, qraw, qg, cos, sin, qpos, kpos)


def tail_kernel(
    dkv_ref, qlow_ref, kraw_ref, kg_in, cos_ref, sin_ref, wq_ref, wk_in, wv_in, x_in, g1_in,
    gres_ref, layer_ref, gn2_ref, qgain_ref, first_in, att_in, back_ref, rows_in,
    gin_ref, lout_ref, gq_ref, gkv_ref, gout_ref, grouter_ref, vo_ref,
    wq, kg_ref, wk_ref, wv_ref, x_ref, g1_ref, first_ref, att, second, att_t, xbuf, zbuf, zst, part, cbuf, ybuf, stage, vbuf, vpart, tbuf, gin, qbuf, kvbuf, turned, osrc, obuf, rsrc, rbuf, qsrc, qgot, ksrc, kgot, grouter_both,
    wsem, xsend, xrecv, zsend, zrecv, csend, crecv, ysend, yrecv, send, recv, vsend, vrecv, tsend, trecv,
    qsend, qrecv, ksend, krecv, esend, erecv,
):
    f32, bf = jnp.float32, jnp.bfloat16
    z, x, y, c = coords()
    ctx, tp = lax.axis_index("ctx"), lax.axis_index("tp")
    rows, width = gres_ref.shape
    half, head = dkv_ref.shape[2:]
    line_cols = first_in.shape[1]
    tok = x_in.shape[0]
    fetched = [
        pltpu.make_async_copy(src, dst, wsem.at[n])
        for n, (src, dst) in enumerate((
            (first_in, first_ref), (att_in, att), (wq_ref, wq), (kg_in, kg_ref), (wk_in, wk_ref),
            (wv_in, wv_ref), (x_in, x_ref), (g1_in, g1_ref),
            *(
                (rows_in.at[pl.ds(pl.multiple_of((zz * 2 + x) * tok, tok), tok),
                            pl.ds(pl.multiple_of(z * line_cols, line_cols), line_cols)],
                 second.at[pl.ds(zz * tok, tok)])
                for zz in range(4)
            ),
        ))
    ]
    for item in fetched:
        item.start()
    X, Y, C, D = dev(z, 1 - x, y, c), dev(z, x, 1 - y, c), dev(z, x, y, 1 - c), dev(z, x, 1 - y, 1 - c)
    up, down = dev(z + 1 - z // 3, x, y, c), dev(z - 1 + (3 - z) // 3, x, y, c)
    barrier_wide()

    def xcopy(zz):
        return pltpu.make_async_remote_copy(
            src_ref=dkv_ref.at[:, zz * 2 + 1 - x], dst_ref=xbuf.at[zz], send_sem=xsend.at[zz],
            recv_sem=xrecv.at[zz], device_id=X, device_id_type=MESH)

    def zcopy(zz, to, slot):
        return pltpu.make_async_remote_copy(
            src_ref=zst.at[zz], dst_ref=zbuf.at[slot], send_sem=zsend.at[zz],
            recv_sem=zrecv.at[slot], device_id=to, device_id_type=MESH)

    span = qlow_ref.shape[1] // 2
    queries = [
        Line(lambda zz, n=n: qbuf.at[n, zz], qsend.at[n], qrecv.at[n]) for n in range(2)
    ]
    keys = Line(lambda zz: kvbuf.at[zz], ksend, krecv)
    for n in range(2):
        qbuf[n, z] = qlow_ref[:, n * span : (n + 1) * span]
    for k in range(4):
        xcopy(far_z(z, k)).start()
    queries[0].start()

    pairs = [(gin, gin_ref), (layer_ref, lout_ref)]

    def place(ref, yy, cc):
        return ref.at[pl.ds(pl.multiple_of((yy * 2 + cc) * rows, rows), rows)]

    def cp(n, src, yy, cc, to, k):
        return pltpu.make_async_remote_copy(
            src_ref=src, dst_ref=place(pairs[n][1], yy, cc), send_sem=send.at[n, k],
            recv_sem=recv.at[n, yy * 2 + cc], device_id=to, device_id_type=MESH)

    own = pl.ds(pl.multiple_of((y * 2 + c) * rows, rows), rows)
    cp(1, layer_ref, y, c, Y, 0).start()
    cp(1, layer_ref, y, c, C, 1).start()
    lout_ref[own] = layer_ref[...]

    per = gq_ref.shape[0]
    own_cols = pl.ds(pl.multiple_of(x * per, per), per)
    far_cols = pl.ds(pl.multiple_of((1 - x) * per, per), per)

    def swap(n, src, dst):
        return pltpu.make_async_remote_copy(
            src_ref=src, dst_ref=dst, send_sem=esend.at[n], recv_sem=erecv.at[n], device_id=X,
            device_id_type=MESH)

    swaps = [
        swap(0, osrc, obuf), swap(1, rsrc, rbuf), swap(2, qsrc.at[0], qgot.at[0]),
        swap(3, qsrc.at[1], qgot.at[1]), swap(4, ksrc, kgot),
    ]
    own_lanes = pl.ds(pl.multiple_of(x * per, 128), per)
    far_lanes = pl.ds(pl.multiple_of((1 - x) * per, 128), per)
    for item in fetched[:2]:
        item.wait()
    att_t[...] = att[...].T
    osrc[...] = nn(att_t[...], back_ref[:, far_lanes]).astype(bf)
    swaps[0].start()
    turned[...] = first_ref[...].T

    def query_part(n):
        right = qbuf[n].reshape(turned.shape[1], span)
        cols = slice(n * span, (n + 1) * span)
        qsrc[n] = nn(turned[far_cols], right).astype(bf)
        swaps[2 + n].start()
        gq_ref[:, cols] = nn(turned[own_cols], right)

    def sum_z(k):
        zz = far_z(z, k)
        xcopy(zz).wait_recv()
        total = dkv_ref[:, zz * 2 + x].astype(f32) + xbuf[zz].astype(f32)
        zst[zz] = total.astype(bf)

        @pl.when((zz > z) & (z > 0))
        def _():
            zcopy(zz, up, zz).wait_recv()
            zst[zz] = (zst[zz].astype(f32) + zbuf[zz].astype(f32)).astype(bf)

        @pl.when((zz < z) & (z < 3))
        def _():
            zcopy(zz, down, zz).wait_recv()
            zst[zz] = (zst[zz].astype(f32) + zbuf[zz].astype(f32)).astype(bf)

        @pl.when(zz > z)
        def _():
            zcopy(zz, up, zz).start()

        @pl.when((zz < z) & (zz != z - 1))
        def _():
            zcopy(zz, down, zz).start()

        @pl.when(zz == z - 1)
        def _():
            zcopy(zz, down, 4).start()

    def at(yy, cc):
        return part.at[pl.ds(pl.multiple_of((yy * 2 + cc) * rows, rows), rows)]

    def two(yy):
        return pl.ds(pl.multiple_of(yy * 2 * rows, 2 * rows), 2 * rows)

    sum_z(0)
    for item in fetched[2:]:
        item.wait()
    first_a = nt(qlow_ref[two(1 - y)], wq[...])
    sum_z(1)
    first_b = nt(qlow_ref[two(y)], wq[...])
    queries[0].pass_on(1)
    sum_z(2)
    queries[1].start()
    router_part = tn(second[...], back_ref[:, line_cols:])
    part_of = jnp.stack([router_part[:per], router_part[per:]])
    grouter_both[...] = part_of
    rsrc[...] = grouter_both[1 - x].astype(bf)
    swaps[1].start()
    xcopy(z).wait_recv()
    dkv = dkv_ref[:, ctx].astype(f32) + xbuf[z].astype(f32)

    @pl.when(z > 0)
    def _():
        zcopy(z, up, z).wait_recv()

    @pl.when(z == 0)
    def _():
        zbuf[0] = jnp.zeros_like(zbuf[0])

    @pl.when(z < 3)
    def _():
        zcopy(z, down, 4).wait_recv()

    @pl.when(z == 3)
    def _():
        zbuf[4] = jnp.zeros_like(zbuf[4])

    dkv = dkv + zbuf[z].astype(f32) + zbuf[4].astype(f32)
    dkey = jnp.concatenate([dkv[0], dkv[1]], axis=0)
    vlow = jnp.concatenate([dkv[2], dkv[3]], axis=0).astype(bf)
    raw = kraw_ref[...]
    dn = turn_back(dkey, cos_ref[...], sin_ref[...])
    rs = row_norm(raw)
    unit = raw * rs
    kgain = jnp.sum(dn * unit, axis=0, keepdims=True)
    cg = dn * kg_ref[...]
    klow = (rs * (cg - unit * jnp.mean(cg * unit, axis=1, keepdims=True))).astype(bf)
    kvbuf[z, :, :head] = klow
    kvbuf[z, :, head:] = vlow
    keys.start()
    queries[0].pass_on(2)

    def ccopy(yy):
        return pltpu.make_async_remote_copy(
            src_ref=at(yy, 1 - c), dst_ref=cbuf.at[yy], send_sem=csend.at[yy],
            recv_sem=crecv.at[yy], device_id=C, device_id_type=MESH)

    def project(yy, first):
        keys, vals = kvbuf[z, two(yy), :head], kvbuf[z, two(yy), head:]
        part[two(yy)] = (first + nt(keys, wk_ref[...]) + nt(vals, wv_ref[...])).astype(bf)
        ccopy(yy).start()

    project(1 - y, first_a)
    project(y, first_b)
    ccopy(1 - y).wait_recv()
    stage[...] = (at(1 - y, c)[...].astype(f32) + cbuf[1 - y].astype(f32)).astype(bf)
    yc = pltpu.make_async_remote_copy(
        src_ref=stage, dst_ref=ybuf, send_sem=ysend, recv_sem=yrecv, device_id=Y, device_id_type=MESH)
    yc.start()
    queries[1].pass_on(1)
    ccopy(y).wait_recv()
    gfirst = at(y, c)[...].astype(f32) + cbuf[y].astype(f32)
    value = x_ref[own].astype(f32)
    rs = row_norm(value)
    unit = value * rs
    yc.wait_recv()
    gfirst = gfirst + ybuf[...].astype(f32)
    gn1 = jnp.sum(gfirst * unit, axis=0, keepdims=True)
    cg = gfirst * g1_ref[...]
    gin[...] = (gres_ref[...] + rs * (cg - unit * jnp.mean(cg * unit, axis=1, keepdims=True))).astype(bf)

    queries[0].pass_on(3)
    query_part(0)
    keys.pass_on(1)
    cp(0, gin, y, c, Y, 0).start()
    cp(0, gin, y, c, C, 1).start()
    gin_ref[own] = gin[...]
    part_width = width // 8
    qgain = jnp.sum(qgain_ref[...], axis=0, keepdims=True)
    for i in range(8):
        for j in range(part_width // 128):
            lo = i * part_width + j * 128
            vpart[i, j : j + 1] = gn1[:, lo : lo + 128]
            vpart[i, part_width // 128 + j : part_width // 128 + j + 1] = gn2_ref[:, lo : lo + 128]
        vpart[i, 2 * part_width // 128 : 7] = jnp.broadcast_to(qgain, (7 - 2 * part_width // 128, head))
        vpart[i, 7:8] = kgain

    def vcopy(i):
        to = (ctx + i) % 8
        return pltpu.make_async_remote_copy(
            src_ref=vpart.at[to], dst_ref=vbuf.at[i], send_sem=vsend.at[i], recv_sem=vrecv.at[i],
            device_id=(to, tp), device_id_type=MESH)

    for i in range(1, 8):
        vcopy(i).start()
    queries[1].pass_on(2)
    keys.pass_on(2)
    total = vpart[ctx]
    for i in range(1, 8):
        vcopy(i).wait_recv()
        total = total + vbuf[i]
    tbuf[3] = total

    def tcopy(k, to):
        return pltpu.make_async_remote_copy(
            src_ref=tbuf.at[3], dst_ref=tbuf.at[k], send_sem=tsend.at[k], recv_sem=trecv.at[k],
            device_id=to, device_id_type=MESH)

    sums = [tcopy(k, to) for k, to in enumerate((Y, C, D))]
    for t in sums:
        t.start()
    for n, (src, dst) in enumerate(pairs):
        cp(n, src, 1 - y, c, Y, 0).wait_recv()
        cp(n, place(dst, 1 - y, c), 1 - y, c, C, 2).start()
    swaps[0].wait_recv()
    gout_ref[...] = nn(att_t[...], back_ref[:, own_lanes]) + obuf[...].astype(f32)
    swaps[1].wait_recv()
    grouter_ref[...] = grouter_both[x] + rbuf[...].astype(f32)
    queries[1].pass_on(3)
    query_part(1)
    keys.pass_on(3)
    right = kvbuf[...].reshape(turned.shape[1], 2 * head)
    ksrc[...] = nn(turned[far_cols], right).astype(bf)
    swaps[4].start()
    gkv_ref[...] = nn(turned[own_cols], right)
    for t in sums:
        t.wait_recv()
    vo_ref[...] = (tbuf[3] + tbuf[0]) + (tbuf[1] + tbuf[2])
    for n, (src, dst) in enumerate(pairs):
        cp(n, src, y, 1 - c, C, 1).wait_recv()
        cp(n, src, 1 - y, 1 - c, C, 2).wait_recv()
        cp(n, src, y, c, Y, 0).wait_send()
        cp(n, src, y, c, C, 1).wait_send()
        cp(n, place(dst, 1 - y, c), 1 - y, c, C, 2).wait_send()
    for t in sums:
        t.wait_send()
    for i in range(1, 8):
        vcopy(i).wait_send()
    for line in (*queries, keys):
        line.finish()
    for n in range(2):
        swaps[2 + n].wait_recv()
        gq_ref[:, n * span : (n + 1) * span] += qgot[n].astype(f32)
    swaps[4].wait_recv()
    gkv_ref[...] += kgot[...].astype(f32)
    for s in swaps:
        s.wait_send()
    yc.wait_send()
    ccopy(0).wait_send()
    ccopy(1).wait_send()
    for zz in range(4):
        xcopy(zz).wait_send()

        @pl.when(zz != z)
        def _():
            zcopy(zz, up, zz).wait_send()


def tail(dkv, qlow, kraw, kg, cos, sin, wq, wk, wv, x, g1, gres, layer, gn2, qgain, first, att, back, rows_all, cid):
    tok, width = x.shape
    rows = gres.shape[0]
    half, head = dkv.shape[2:]
    per = first.shape[1] // 2
    f32, bf = jnp.float32, jnp.bfloat16
    dma = pltpu.SemaphoreType.DMA
    vm, anywhere = pl.BlockSpec(memory_space=pltpu.VMEM), pl.BlockSpec(memory_space=pl.ANY)

    def out(shape, kind):
        return jax.ShapeDtypeStruct(shape, kind)

    def mem(*shape, kind=bf):
        return pltpu.VMEM(shape, kind)

    return pl.pallas_call(
        tail_kernel,
        in_specs=[vm] * 3 + [anywhere] + [vm] * 2 + [anywhere] * 5 + [vm] * 4 + [anywhere] * 2 + [vm] + [anywhere],
        out_specs=[vm] * 7,
        out_shape=[
            out((tok, width), bf), out((tok, width), bf), out((per, qlow.shape[1]), f32),
            out((per, 2 * head), f32), out((att.shape[1], per), f32),
            out((per, 128), f32), out((8, 128), f32),
        ],
        scratch_shapes=[
            mem(*wq.shape), mem(*kg.shape, kind=f32), mem(*wk.shape), mem(*wv.shape), mem(*x.shape),
            mem(*g1.shape, kind=f32), mem(*first.shape), mem(*att.shape), mem(*first.shape),
            mem(att.shape[1], att.shape[0]), mem(4, 4, half, head), mem(5, 4, half, head), mem(4, 4, half, head),
            mem(tok, width), mem(2, rows, width), mem(rows, width), mem(rows, width),
            mem(8, 8, 128, kind=f32), mem(8, 8, 128, kind=f32), mem(4, 8, 128, kind=f32), mem(rows, width),
            mem(2, 4, tok, qlow.shape[1] // 2), mem(4, tok, 2 * head), mem(2 * per, first.shape[0]),
            mem(att.shape[1], per), mem(att.shape[1], per),
            mem(per, 128), mem(per, 128),
            mem(2, per, qlow.shape[1] // 2), mem(2, per, qlow.shape[1] // 2),
            mem(per, 2 * head), mem(per, 2 * head), mem(2, per, 128, kind=f32),
            dma((12,)), dma((4,)), dma((4,)), dma((4,)), dma((5,)), dma((2,)), dma((2,)), dma, dma,
            dma((2, 3)), dma((2, 4)), dma((8,)), dma((8,)), dma((3,)), dma((3,)),
            dma((2, 2, 4)), dma((2, 4)), dma((2, 4)), dma((4,)), dma((5,)), dma((5,)),
        ],
        compiler_params=pltpu.CompilerParams(
            collective_id=cid, has_side_effects=True, vmem_limit_bytes=52 * 2**20
        ),
        name="tail",
    )(dkv, qlow, kraw, kg, cos, sin, wq, wk, wv, x, g1, gres, layer, gn2, qgain, first, att, back, rows_all)


def experts_kernel(
    own,
    piece_ref, wg_ref, wu_ref, wd_ref,
    all_ref, pair_ref, hs_ref, gl_ref, ul_ref, hst_ref, glt_ref, ult_ref,
    land, mats, s_ref, t_ref, pairs, lows, turns,
    gsem, gsend, grecv, msem, asem, psem, lsem, tsem,
):
    bf, f32 = jnp.bfloat16, jnp.float32
    width = wg_ref.shape[1]
    extra = t_ref.shape[1]
    hid = wg_ref.shape[0]
    tok = 4 * piece_ref.shape[0]
    weights = [pltpu.make_async_copy(r, mats.at[n], msem.at[n]) for n, r in enumerate((wg_ref, wu_ref, wd_ref))]
    for cp in weights:
        cp.start()
    named = lax.axis_index("ctx") * own

    def expert_of(index):
        return named + sum((index >= e * hid // own).astype(jnp.int32) for e in range(1, own))

    shape = s_ref.shape
    expert = expert_of(lax.broadcasted_iota(jnp.int32, shape, 1))
    place = lax.broadcasted_iota(jnp.int32, shape, 0)
    s_ref[...] = ((place == expert) | (place == expert + extra // 4)).astype(f32).astype(bf)
    expert = expert_of(lax.broadcasted_iota(jnp.int32, shape[::-1], 0))
    place = lax.broadcasted_iota(jnp.int32, shape[::-1], 1)
    t_ref[...] = (place == expert).astype(f32).astype(bf)
    barrier_all()
    wide = piece_ref.shape[1]
    cut = wide // 256 * 128
    gathers = [
        Gather(piece_ref, land, pl.ds(0, cut), gsend.at[0], grecv.at[0]),
        Gather(piece_ref, land, pl.ds(cut, wide - cut), gsend.at[1], grecv.at[1]),
    ]
    for gather in gathers:
        gather.start()
    z, x, y, c, ax, ay, bx, by = gathers[0].at_me
    rows = piece_ref.shape[0]
    me = pid(z, x, y, c)
    local = pltpu.make_async_copy(
        piece_ref, land.at[pl.ds(pl.multiple_of(me * rows, rows), rows)], gsem)
    local.start()

    def place_of(u):
        return far_z(z, 3 - u // 2), x + (u % 2) * (1 - 2 * x)

    def block_rows(u):
        zz, xx = place_of(u)
        return pl.ds(pl.multiple_of((zz * 2 + xx) * tok, tok), tok)

    def results(u):
        slot = u % 2
        span = block_rows(u)
        copies = [pltpu.make_async_copy(pairs.at[slot], pair_ref.at[span], psem.at[slot])]
        for n, (ref, turned) in enumerate(((hs_ref, hst_ref), (gl_ref, glt_ref), (ul_ref, ult_ref))):
            copies.append(pltpu.make_async_copy(lows.at[slot, n], ref.at[span], lsem.at[slot, n]))
            copies.append(pltpu.make_async_copy(turns.at[slot, n], turned.at[:, span], tsem.at[slot, n]))
        return copies

    def whole(u):
        span = block_rows(u)
        return pltpu.make_async_copy(land.at[span], all_ref.at[span], asem.at[u])

    local.wait()

    def step(u, carry):
        zz, xx = place_of(u)
        slot = u % 2

        @pl.when(u % 2 == 0)
        def _():
            for gather in gathers:
                gather.from_a(zz)
                gather.from_b(zz, bx, by)

            @pl.when(u < 6)
            def _():
                for gather in gathers:
                    gather.from_line(far_z(z, 2 - u // 2))

        @pl.when(u % 2 == 1)
        def _():
            for gather in gathers:
                gather.from_b(zz, 1 - x, 1 - y)

        for yy in range(2):
            for gather in gathers:
                gather.wait(pid(zz, xx, yy, 1 - c))

        whole(u).start()

        @pl.when(u == 0)
        def _():
            for cp in weights:
                cp.wait()

        @pl.when(u > 1)
        def _():
            for cp in results(u - 2):
                cp.wait()

        rows = block_rows(u)
        value = land[rows, :width]
        spread = nn(land[rows, 2 * width :], s_ref[...])
        gate = nt(value, mats[0])
        up = nt(value, mats[1])
        back = nt(land[rows, width : 2 * width], mats[2])
        sig = 1.0 / (1.0 + jnp.exp(-gate))
        silu = gate * sig
        hidden = silu * up
        hs = (hidden * spread).astype(bf)
        prod = hidden * back
        high = prod.astype(bf)
        low = (prod - high.astype(f32)).astype(bf)
        pairs[slot] = (nn(high, t_ref[...]) + nn(low, t_ref[...])).astype(bf)
        grad = back * spread
        gl = (grad * up * sig * (1.0 + gate * (1.0 - sig))).astype(bf)
        ul = (grad * silu).astype(bf)
        for n, v in enumerate((hs, gl, ul)):
            lows[slot, n] = v
            turns[slot, n] = v.T
        for cp in results(u):
            cp.start()
        return carry

    lax.fori_loop(0, 8, step, 0)
    for u in (6, 7):
        for cp in results(u):
            cp.wait()
    for u in range(8):
        whole(u).wait()
    for gather in gathers:
        gather.finish()


def experts_forward(piece, wg, wu, wd, own, cid):
    rows, wide = piece.shape
    hid, width = wg.shape
    n = 32 * rows
    tok = 4 * rows
    extra = wide - 2 * width
    bf = jnp.bfloat16
    dma = pltpu.SemaphoreType.DMA
    anywhere = pl.BlockSpec(memory_space=pl.ANY)

    def out(*shape):
        return jax.ShapeDtypeStruct(shape, bf)

    return pl.pallas_call(
        functools.partial(experts_kernel, own),
        in_specs=[anywhere] * 4,
        out_specs=[anywhere] * 8,
        out_shape=[out(n, wide), out(n, extra)] + [out(n, hid)] * 3 + [out(hid, n)] * 3,
        scratch_shapes=[
            pltpu.VMEM((n, wide), bf), pltpu.VMEM((3, hid, width), bf), pltpu.VMEM((extra, hid), bf),
            pltpu.VMEM((hid, extra), bf), pltpu.VMEM((2, tok, extra), bf),
            pltpu.VMEM((2, 3, tok, hid), bf), pltpu.VMEM((2, 3, hid, tok), bf),
            dma, dma((2, 5, 32)), dma((2, 32)), dma((3,)), dma((8,)), dma((2,)), dma((2, 3)), dma((2, 3)),
        ],
        compiler_params=pltpu.CompilerParams(
            collective_id=cid, has_side_effects=True, vmem_limit_bytes=60 * 2**20
        ),
        cost_estimate=pl.CostEstimate(
            flops=6 * n * width * hid, bytes_accessed=10 * n * width, transcendentals=n * hid
        ),
        name="experts_forward",
    )(piece, wg, wu, wd)


EPSILON = 1e-06
ROPE_BASE = 1000000.0
MASKED_SCORE = -1000000000.0
BF = jnp.bfloat16
F32 = jnp.float32


def dotf(a, b, dims):
    return lax.dot_general(a, b, (dims, ((), ())), preferred_element_type=F32)


def nt(a, b):
    return lax.dot_general(a, b, (((1,), (1,)), ((), ())), preferred_element_type=jnp.float32)


def nn(a, b):
    return lax.dot_general(a, b, (((1,), (0,)), ((), ())), preferred_element_type=jnp.float32)


def tn(a, b):
    return lax.dot_general(a, b, (((0,), (0,)), ((), ())), preferred_element_type=jnp.float32)


def plain_expert_kernel(x_ref, cot_ref, wg_ref, wu_ref, wd_ref, s_ref, t_ref, part_ref, gl_ref, ul_ref, hs_ref):
    bf = jnp.bfloat16
    width = cot_ref.shape[1]
    x = x_ref[:, :width]
    spread = nn(x_ref[:, width:], s_ref[...])
    gate = nt(x, wg_ref[...])
    up = nt(x, wu_ref[...])
    back = nt(cot_ref[...], wd_ref[...])
    sig = 1.0 / (1.0 + jnp.exp(-gate))
    silu = gate * sig
    hidden = silu * up
    hs = (hidden * spread).astype(bf)
    hs_ref[...] = hs.T
    part_ref[:, :width] = nn(hs, wd_ref[...]).astype(bf)
    prod = hidden * back
    high = prod.astype(bf)
    low = (prod - high.astype(jnp.float32)).astype(bf)
    part_ref[:, 2 * width :] = (nn(high, t_ref[...]) + nn(low, t_ref[...])).astype(bf)
    grad = back * spread
    gl = (grad * up * sig * (1.0 + gate * (1.0 - sig))).astype(bf)
    ul = (grad * silu).astype(bf)
    gl_ref[...] = gl.T
    ul_ref[...] = ul.T
    part_ref[:, width : 2 * width] = (nn(gl, wg_ref[...]) + nn(ul, wu_ref[...])).astype(bf)


def expert_blocks(x_all, cot_all, gate_mat, up_mat, down_mat, spread_mat, pick_mat, block=256):
    n, width = cot_all.shape
    wide = x_all.shape[1]
    hid = gate_mat.shape[0]
    bf = jnp.bfloat16

    def rows(w):
        return pl.BlockSpec((block, w), lambda i: (i, 0))

    def whole(v):
        return pl.BlockSpec(v.shape, lambda i: (0, 0), pipeline_mode=pl.Buffered(1))

    return pl.pallas_call(
        plain_expert_kernel,
        grid=(n // block,),
        in_specs=[rows(wide), rows(width)]
        + [whole(v) for v in (gate_mat, up_mat, down_mat, spread_mat, pick_mat)],
        out_specs=[rows(width + wide)] + [pl.BlockSpec((hid, block), lambda i: (0, i))] * 3,
        out_shape=[jax.ShapeDtypeStruct((n, width + wide), bf)]
        + [jax.ShapeDtypeStruct((hid, n), bf)] * 3,
        compiler_params=pltpu.CompilerParams(
            dimension_semantics=("arbitrary",), vmem_limit_bytes=56 * 2**20
        ),
        cost_estimate=pl.CostEstimate(
            flops=12 * n * width * hid, bytes_accessed=10 * n * width, transcendentals=n * hid
        ),
        name="plain_experts",
    )(x_all, cot_all, gate_mat, up_mat, down_mat, spread_mat, pick_mat)


def expert_grad_kernel(x_ref, cot_ref, gl_ref, ul_ref, hs_ref, gg_ref, gu_ref, gd_ref):
    first = pl.program_id(1) == 0

    def put(ref, low, full):
        value = nn(low[...], full[...])

        @pl.when(first)
        def _():
            ref[...] = value

        @pl.when(jnp.logical_not(first))
        def _():
            ref[...] += value

    put(gg_ref, gl_ref, x_ref)
    put(gu_ref, ul_ref, x_ref)
    put(gd_ref, hs_ref, cot_ref)


def expert_grads(x_all, cot_all, gl, ul, hs, width, first=0, block=256):
    n = x_all.shape[0]
    hid = gl.shape[0]
    span = min(n, 2048)
    cols = pl.BlockSpec((span, block), lambda i, j: (j, i))
    cots = pl.BlockSpec((span, block), lambda i, j: (j, i + first // block))
    rows = pl.BlockSpec((hid, span), lambda i, j: (0, j))
    out = pl.BlockSpec((hid, block), lambda i, j: (0, i))
    return pl.pallas_call(
        expert_grad_kernel,
        grid=(width // block, n // span),
        in_specs=[cols, cots, rows, rows, rows],
        out_specs=[out] * 3,
        out_shape=[jax.ShapeDtypeStruct((hid, width), jnp.float32)] * 3,
        compiler_params=pltpu.CompilerParams(
            dimension_semantics=("arbitrary", "arbitrary"), vmem_limit_bytes=56 * 2**20
        ),
        cost_estimate=pl.CostEstimate(
            flops=6 * n * width * hid, bytes_accessed=10 * n * width, transcendentals=0
        ),
        name="expert_grads",
    )(x_all, cot_all, gl, ul, hs)


class Links:
    def ag_all(self, piece):
        return lax.all_gather(piece, ("ctx", "tp"), axis=0, tiled=True)

    def rs_all(self, part):
        return lax.psum_scatter(part, ("ctx", "tp"), scatter_dimension=0, tiled=True).astype(F32)

    def ag_ctx(self, piece):
        return lax.all_gather(piece, "ctx", axis=0, tiled=True)

    def rs_ctx(self, part):
        return lax.psum_scatter(part, "ctx", scatter_dimension=0, tiled=True).astype(F32)

    def rs_tp(self, part):
        return lax.psum_scatter(part, "tp", scatter_dimension=0, tiled=True).astype(F32)

    def ag_tp(self, piece):
        return lax.all_gather(piece, "tp", axis=0, tiled=True)

    def finish(self, a, b, vectors):
        total = lax.psum_scatter(vectors, "ctx", scatter_dimension=0, tiled=True)
        gathered = (lax.all_gather(v, "tp", axis=0, tiled=True) for v in (a, b))
        return (*gathered, lax.psum(total, "tp"))


def rms_norm(values, gain_vec):
    factor = lax.rsqrt(jnp.mean(values * values, axis=-1, keepdims=True) + EPSILON)
    return values * factor * gain_vec


def rotate(values, rotary_angles):
    half_size = values.shape[-1] // 2
    first_half = values[..., :half_size]
    second_half = values[..., half_size:]
    cosine = jnp.cos(rotary_angles)
    sine_part = jnp.sin(rotary_angles)
    return jnp.concatenate(
        [
            first_half * cosine - second_half * sine_part,
            second_half * cosine + first_half * sine_part,
        ],
        axis=-1,
    )


def angles_of(token_positions, head_width):
    freq_steps = jnp.arange(head_width // 2).astype(F32) * (2.0 / head_width)
    frequency = jnp.exp(-math.log(ROPE_BASE) * freq_steps)
    return token_positions.astype(F32)[..., None] * frequency


def positions_of(block_order, dev_count, block_len):
    first_block = jnp.transpose(block_order)
    block_pair = jnp.stack([first_block, 2 * dev_count - 1 - first_block], axis=-1)
    spread = block_pair[..., None] * block_len + jnp.arange(block_len, dtype=jnp.int32)
    return spread.reshape(dev_count, block_order.shape[0], 2 * block_len)


def head_route_path(raw_heads, gain_vec, rotary_angles, head_count):
    shaped = raw_heads.reshape(raw_heads.shape[0], head_count, -1)
    return rotate(rms_norm(shaped, gain_vec), rotary_angles[:, None, :])


def attend_forward(seq_item):
    query_matrix, every_key_row, every_value_row, query_pos, key_pos = seq_item
    score_scale = 1.0 / math.sqrt(query_matrix.shape[-1])
    unscaled_scores = jnp.einsum(
        "upnj,apj->upna", query_matrix, every_key_row, preferred_element_type=F32
    )
    allowed = query_pos[:, None, None, None] >= key_pos[None, None, None, :]
    scores = jnp.where(allowed, unscaled_scores * score_scale, MASKED_SCORE)
    row_top = jnp.max(scores, axis=-1, keepdims=True)
    exp_scores = jnp.exp(scores - row_top)
    totals = jnp.sum(exp_scores, axis=-1, keepdims=True)
    lower_attention_probs = (exp_scores / totals).astype(BF)
    attended_mix = jnp.einsum(
        "jzfq,qzx->jzfx", lower_attention_probs, every_value_row, preferred_element_type=F32
    )
    return (attended_mix, (row_top + jnp.log(totals))[..., 0])


def attend_backward(seq_item):
    (
        query_matrix,
        every_key_row,
        every_value_row,
        query_pos,
        key_pos,
        grad_attended_mix,
        log_total,
    ) = seq_item
    score_scale = 1.0 / math.sqrt(query_matrix.shape[-1])
    unscaled_scores = jnp.einsum(
        "upnj,apj->upna", query_matrix, every_key_row, preferred_element_type=F32
    )
    allowed = query_pos[:, None, None, None] >= key_pos[None, None, None, :]
    scores = jnp.where(allowed, unscaled_scores * score_scale, MASKED_SCORE)
    attention_probs = jnp.exp(scores - log_total[..., None])
    grad_probs = jnp.einsum(
        "upnj,apj->upna", grad_attended_mix, every_value_row, preferred_element_type=F32
    )
    row_inner = jnp.sum(attention_probs * grad_probs, axis=-1, keepdims=True)
    grad_score_dots = (attention_probs * (grad_probs - row_inner) * score_scale).astype(BF)
    grad_queries = jnp.einsum(
        "jzfq,qzx->jzfx", grad_score_dots, every_key_row, preferred_element_type=F32
    )
    grad_key_rows = jnp.einsum(
        "axfv,axfz->vxz", grad_score_dots, query_matrix, preferred_element_type=F32
    )
    grad_values = jnp.einsum(
        "axfv,axfz->vxz", attention_probs.astype(BF), grad_attended_mix, preferred_element_type=F32
    )
    return (grad_queries, grad_key_rows, grad_values)


def gates_of(logits, routes):
    experts = logits.shape[1]
    named = jnp.any(routes[:, :, None] == jnp.arange(experts, dtype=jnp.int32), axis=1)
    masked = jnp.where(named, logits, -jnp.inf)
    top = jnp.max(masked, axis=1, keepdims=True)
    weights = jnp.where(named, jnp.exp(masked - top), 0.0)
    return weights / jnp.sum(weights, axis=1, keepdims=True)


def plain_shards(
    tokens_in,
    block_order,
    routes,
    norm1_gain,
    w_query,
    key_weight,
    value_weight,
    query_gain,
    key_gain,
    w_out,
    norm2_gain,
    w_router,
    w_gate,
    w_up,
    w_down,
    cotangent,
):
    tok_count, model_width = tokens_in.shape
    head_size = query_gain.shape[0]
    local_heads = w_query.shape[1] // head_size
    local_kv = key_weight.shape[1] // head_size
    query_group_width = local_heads // local_kv
    seq_count = block_order.shape[0]
    devices, tp_size = lax.axis_size("ctx"), lax.axis_size("tp")
    links = Links()
    me, tp_me = lax.axis_index("ctx"), lax.axis_index("tp")
    rows = tok_count // tp_size
    block_len = tok_count // (2 * seq_count)
    experts = w_router.shape[1]
    own_experts, _, units = w_gate.shape
    hid = own_experts * units
    all_tok = devices * tok_count

    def own_rows(v):
        return lax.dynamic_slice_in_dim(v, tp_me * rows, rows, axis=0)

    cot_own = own_rows(cotangent)
    cot_all = lax.all_gather(cot_own, ("ctx", "tp"), axis=0, tiled=True)

    token_positions = positions_of(block_order, devices, block_len)
    query_pos = lax.dynamic_index_in_dim(token_positions, me, 0, keepdims=False)
    key_pos = jnp.transpose(token_positions, (1, 0, 2)).reshape(seq_count, devices * 2 * block_len)
    rotary_angles = angles_of(query_pos.reshape(-1), head_size)
    inputs = tokens_in.astype(F32)
    first_in = rms_norm(inputs, norm1_gain).astype(BF)
    query_raw = jnp.dot(first_in, w_query, preferred_element_type=F32)
    unrotated_key = jnp.dot(first_in, key_weight, preferred_element_type=F32)
    value_rows = jnp.dot(first_in, value_weight, preferred_element_type=F32).astype(BF)

    def rope_heads(raw_query, raw_key, gain_query, key_norm_gain):
        return (
            head_route_path(raw_query, gain_query, rotary_angles, local_heads),
            head_route_path(raw_key, key_norm_gain, rotary_angles, local_kv),
        )

    (query_rot, key_rot), rope_back = jax.vjp(
        rope_heads, query_raw, unrotated_key, query_gain, key_gain
    )
    query_rows = query_rot.astype(BF).reshape(
        seq_count, 2 * block_len, local_kv, query_group_width, head_size
    )
    kv_width = local_kv * head_size
    kv_own = jnp.concatenate([key_rot.astype(BF).reshape(tok_count, kv_width), value_rows], axis=1)
    kv_all = links.ag_ctx(kv_own)
    kv_seq = kv_all.reshape(devices, seq_count, 2 * block_len, 2, local_kv, head_size)
    kv_seq = kv_seq.transpose(3, 1, 0, 2, 4, 5).reshape(
        2, seq_count, devices * 2 * block_len, local_kv, head_size
    )
    key_full, value_full = kv_seq[0], kv_seq[1]
    attended_mix, log_total = lax.map(
        attend_forward, (query_rows, key_full, value_full, query_pos, key_pos)
    )
    attended = attended_mix.reshape(tok_count, local_heads * head_size).astype(BF)
    attn_part = jnp.dot(attended, w_out, preferred_element_type=F32).astype(BF)
    residual = own_rows(inputs) + links.rs_tp(attn_part)
    second_normed, second_back = jax.vjp(rms_norm, residual, norm2_gain)
    second_in = second_normed.astype(BF)
    extra = -(-2 * experts // 128) * 128
    gates = gates_of(jnp.dot(second_in, w_router, preferred_element_type=F32), own_rows(routes))
    gates_high = gates.astype(BF)
    gates_low = (gates - gates_high.astype(F32)).astype(BF)
    pad = jnp.zeros((rows, extra - 2 * experts), BF)
    second_all = links.ag_all(
        jnp.concatenate([second_in, gates_high, gates_low, pad], axis=1)
    )
    column = jnp.arange(extra, dtype=jnp.int32)[:, None]
    named = me * own_experts + jnp.arange(hid, dtype=jnp.int32)[None, :] // units
    pick = (column == named).astype(BF)
    spread = pick + (column == named + experts).astype(BF)
    gate_mat = w_gate.transpose(0, 2, 1).reshape(hid, model_width)
    up_mat = w_up.transpose(0, 2, 1).reshape(hid, model_width)
    down_mat = w_down.reshape(hid, model_width)
    part, gate_low, up_low, hidden_low = expert_blocks(
        second_all, cot_all, gate_mat, up_mat, down_mat, spread, pick.T
    )
    sums_own = links.rs_all(part)
    out_own = sums_own[:, :model_width]
    entry_own = sums_own[:, model_width:]
    gate_total = entry_own[:, model_width : model_width + experts]
    grad_logits = (
        gates * (gate_total - jnp.sum(gates * gate_total, axis=1, keepdims=True))
    ).astype(BF)
    grad_second = entry_own[:, :model_width] + dotf(grad_logits, w_router, ((1,), (1,)))
    grad_resid_norm, grad_norm2 = second_back(grad_second)
    grad_residual = cot_own.astype(F32) + grad_resid_norm
    pad = jnp.zeros((rows, -experts % 128), BF)
    back_all = links.ag_tp(
        jnp.concatenate([grad_residual.astype(BF), grad_logits, pad], axis=1)
    )
    grad_attn_low = back_all[:, :model_width]
    second_own = lax.dynamic_slice(second_all, (me * tok_count, 0), (tok_count, model_width))
    router_part = dotf(second_own, back_all[:, model_width:], ((0,), (0,)))
    grad_out = dotf(attended, grad_attn_low, ((0,), (0,)))
    grad_mixed = dotf(grad_attn_low, w_out, ((1,), (1,))).astype(BF)
    grad_mixed = grad_mixed.reshape(
        seq_count, 2 * block_len, local_kv, query_group_width, head_size
    )
    grad_query_seq, grad_key_seq, grad_value_seq = lax.map(
        attend_backward,
        (query_rows, key_full, value_full, query_pos, key_pos, grad_mixed, log_total),
    )
    grad_kv = jnp.stack([grad_key_seq, grad_value_seq]).astype(BF)
    grad_kv = grad_kv.reshape(2, seq_count, devices, 2 * block_len, kv_width)
    grad_kv = grad_kv.transpose(2, 1, 3, 0, 4).reshape(all_tok, 2 * kv_width)
    grad_kv_own = links.rs_ctx(grad_kv)
    grad_query_rot = grad_query_seq.reshape(tok_count, local_heads, head_size)
    grad_key_rot = grad_kv_own[:, :kv_width].reshape(tok_count, local_kv, head_size)
    grad_query_raw, grad_key_raw, grad_qgain, grad_kgain = rope_back(
        (grad_query_rot, grad_key_rot)
    )
    query_low = grad_query_raw.astype(BF)
    key_low = grad_key_raw.astype(BF)
    value_low = grad_kv_own[:, kv_width:].astype(BF)
    first_part = dotf(query_low, w_query, ((1,), (1,)))
    first_part = first_part + dotf(key_low, key_weight, ((1,), (1,)))
    first_part = first_part + dotf(value_low, value_weight, ((1,), (1,)))
    grad_first = links.rs_tp(first_part.astype(BF))
    grad_first, gate_low = lax.optimization_barrier((grad_first, gate_low))
    grads = expert_grads(second_all, cot_all, gate_low, up_low, hidden_low, model_width)
    grad_gate, grad_up = (
        v.reshape(own_experts, units, model_width).transpose(0, 2, 1) for v in grads[:2]
    )
    grad_down = grads[2].reshape(own_experts, units, model_width)
    _, first_back = jax.vjp(rms_norm, own_rows(inputs), norm1_gain)
    grad_input_norm, grad_norm1 = first_back(grad_first)
    def over_ctx(v, dim):
        return lax.psum_scatter(v.astype(BF), "ctx", scatter_dimension=dim, tiled=True).astype(F32)

    grad_query = over_ctx(dotf(first_in, query_low, ((0,), (0,))), 0)
    kv_part = dotf(first_in, jnp.concatenate([key_low, value_low], axis=1), ((0,), (0,)))
    small = links.rs_ctx(jnp.concatenate([kv_part, router_part], axis=1).astype(BF))
    grad_key = small[:, :kv_width]
    grad_value = small[:, kv_width : 2 * kv_width]
    grad_router = small[:, 2 * kv_width : 2 * kv_width + experts]
    grad_out = over_ctx(grad_out, 1)
    vectors = [
        v.reshape(devices, -1) for v in (grad_norm1, grad_norm2, grad_qgain, grad_kgain)
    ]
    sizes = [v.shape[1] for v in vectors]
    pad = jnp.zeros((devices, -sum(sizes) % 1024), F32)
    packed = jnp.concatenate([*vectors, pad], axis=1).reshape(-1, 128)
    grad_input, layer_out, total = links.finish(
        (grad_residual + grad_input_norm).astype(BF), (residual + out_own).astype(BF), packed
    )
    total = total.reshape(-1)

    def piece_of(n):
        start = sum(sizes[:n])
        return total[start : start + sizes[n]]

    return (
        layer_out,
        grad_input,
        piece_of(0),
        grad_query,
        grad_key,
        grad_value,
        piece_of(2),
        piece_of(3),
        grad_out,
        piece_of(1),
        grad_router,
        grad_gate,
        grad_up,
        grad_down,
    )


def fast_shards(
    tokens_in,
    block_order,
    routes,
    norm1_gain,
    w_query,
    key_weight,
    value_weight,
    query_gain,
    key_gain,
    w_out,
    norm2_gain,
    w_router,
    w_gate,
    w_up,
    w_down,
    cotangent,
):
    tok_count, model_width = tokens_in.shape
    head_size = query_gain.shape[0]
    seq_count = block_order.shape[0]
    devices, tp_size = lax.axis_size("ctx"), lax.axis_size("tp")
    me, tp_me = lax.axis_index("ctx"), lax.axis_index("tp")
    rows = tok_count // tp_size
    block_len = tok_count // (2 * seq_count)
    experts = w_router.shape[1]
    own_experts, _, units = w_gate.shape
    hid = own_experts * units

    def row(v):
        return v.reshape(1, -1)


    token_positions = positions_of(block_order, devices, block_len)
    query_pos = lax.dynamic_index_in_dim(token_positions, me, 0, keepdims=False).reshape(-1)
    key_pos = jnp.transpose(token_positions, (1, 0, 2)).reshape(seq_count, -1).astype(F32)
    angles = angles_of(query_pos, head_size)
    cos = jnp.concatenate([jnp.cos(angles)] * 2, axis=1)
    sin = jnp.concatenate([-jnp.sin(angles), jnp.sin(angles)], axis=1)
    query_pos = jnp.broadcast_to(query_pos.astype(F32)[:, None], (tok_count, head_size))
    router_rows = w_router.T
    _, query_raw, key_raw, query_rot, kv_all, attended, logs, residual, gates, piece, first_cols = front(
        tokens_in, row(norm1_gain), w_query, key_weight, value_weight, row(query_gain),
        row(key_gain), cos, sin, query_pos, key_pos, w_out, row(norm2_gain), router_rows,
        routes.T, cotangent, 1,
    )

    gate_mat = w_gate.transpose(0, 2, 1).reshape(hid, model_width)
    up_mat = w_up.transpose(0, 2, 1).reshape(hid, model_width)
    down_mat = w_down.reshape(hid, model_width)
    all_rows, pair, hidden, gate_low, up_low, hidden_turned, gate_turned, up_turned = experts_forward(
        piece, gate_mat, up_mat, down_mat, own_experts, 3
    )
    sums_own, attended_line = reduce_experts(
        hidden, gate_low, up_low, pair, down_mat, gate_mat, up_mat, attended, 6
    )
    layer_piece, grad_residual, grad_norm2, back_cols, query_low, grad_kv, qgain_part = middle(
        sums_own, residual, gates, cotangent, row(norm2_gain), router_rows, w_out, query_rot, kv_all,
        logs, query_raw, row(query_gain), cos, sin, query_pos, key_pos, 7,
    )

    line_tok = 4 * tok_count
    back_cols = back_cols.reshape(line_tok, -1)
    grad_input, layer_out, grad_query, kv_grads, grad_out, grad_router, total = tail(
        grad_kv, query_low, key_raw, row(key_gain), cos, sin, w_query, key_weight, value_weight,
        tokens_in, row(norm1_gain), grad_residual, layer_piece, grad_norm2, qgain_part,
        first_cols.reshape(line_tok, -1), attended_line.reshape(line_tok, -1), back_cols, all_rows, 8,
    )
    per = model_width // devices // 128
    grad_key = kv_grads[:, :head_size]
    grad_value = kv_grads[:, head_size:]
    total, gate_turned = lax.optimization_barrier((total, gate_turned))
    grads = expert_grads(all_rows, all_rows, gate_turned, up_turned, hidden_turned, model_width, model_width)
    grad_gate, grad_up = (
        v.reshape(own_experts, units, model_width).transpose(0, 2, 1) for v in grads[:2]
    )
    grad_down = grads[2].reshape(own_experts, units, model_width)
    share = head_size // devices

    def gain_of(n):
        return lax.dynamic_slice_in_dim(total[n], me * share, share, axis=0)

    return (
        layer_out,
        grad_input,
        total[:per].reshape(-1),
        grad_query,
        grad_key,
        grad_value,
        gain_of(2 * per),
        gain_of(7),
        grad_out,
        total[per : 2 * per].reshape(-1),
        grad_router[:, :experts],
        grad_gate,
        grad_up,
        grad_down,
    )


def solution(mesh):
    in_specs = (
        P("ctx", None),
        P(),
        P("ctx", None),
        P(),
        P(None, "tp"),
        P(None, "tp"),
        P(None, "tp"),
        P(),
        P(),
        P("tp", None),
        P(),
        P(),
        P("ctx", None, "tp"),
        P("ctx", None, "tp"),
        P("ctx", "tp", None),
        P("ctx", None),
    )
    out_specs = (
        P("ctx", None),
        P("ctx", None),
        P("ctx"),
        P("ctx", "tp"),
        P("ctx", "tp"),
        P("ctx", "tp"),
        P("ctx"),
        P("ctx"),
        P("tp", "ctx"),
        P("ctx"),
        P("ctx", None),
        P("ctx", None, "tp"),
        P("ctx", None, "tp"),
        P("ctx", "tp", None),
    )
    own = mesh.shape["ctx"] == 8 and mesh.shape["tp"] == 4
    shards = fast_shards if own else plain_shards
    return jax.shard_map(shards, mesh=mesh, in_specs=in_specs, out_specs=out_specs, check_vma=False)
```

```python
import math
import functools
import jax
import jax.numpy as jnp
from jax import lax
from jax.sharding import PartitionSpec as P
from jax.experimental import pallas as pl
from jax.experimental.pallas import tpu as pltpu
MESH=pl.DeviceIdType.MESH

def coords():
    ctx=lax.axis_index("ctx"); tp=lax.axis_index("tp")
    return ctx//2, ctx%2, tp//2, tp%2
def dev(z,x,y,c): return (z*2+x, y*2+c)
def pid(z,x,y,c): return (z*2+x)*4+y*2+c

def neighbours():
    z,x,y,c=coords()
    ax=x+(1-c)*(1-2*x); ay=y+c*(1-2*y)
    bx=x+c*(1-2*x); by=y+(1-c)*(1-2*y)
    return z,x,y,c,ax,ay,bx,by

def barrier_all():
    z,x,y,c=coords()
    b=pltpu.get_barrier_semaphore()
    def sig(d): pl.semaphore_signal(b,inc=1,device_id=d,device_id_type=MESH)
    sig(dev(z,1-x,y,c)); sig(dev(z,x,1-y,c)); sig(dev(z,x,y,1-c))
    @pl.when(z<3)
    def _(): sig(dev(z+1,x,y,c))
    @pl.when(z>0)
    def _(): sig(dev(z-1,x,y,c))
    pl.semaphore_wait(b,5-(3-z)//3-z//3)

class Gather:
    def __init__(self, own_ref, out_ref, cols, send, recv):
        self.own, self.out, self.cols, self.send, self.recv = own_ref, out_ref, cols, send, recv
        self.rows = own_ref.shape[0]
        z, x, y, c, ax, ay, bx, by = neighbours()
        self.at_me = (z, x, y, c, ax, ay, bx, by)
        self.up, self.down = dev(z + 1 - z // 3, x, y, c), dev(z - 1 + (3 - z) // 3, x, y, c)
        self.A, self.B, self.C = dev(z, ax, ay, c), dev(z, bx, by, c), dev(z, x, y, 1 - c)

    def place(self, p):
        return self.out.at[pl.ds(pl.multiple_of(p * self.rows, self.rows), self.rows), self.cols]

    def copy(self, p, to, k, own=False):
        return pltpu.make_async_remote_copy(
            src_ref=self.own.at[:, self.cols] if own else self.place(p), dst_ref=self.place(p),
            send_sem=self.send.at[k, p], recv_sem=self.recv.at[p], device_id=to, device_id_type=MESH)

    def wait(self, p):
        self.copy(p, self.C, 4).wait_recv()

    def start(self):
        z, x, y, c = self.at_me[:4]
        me = pid(z, x, y, c)
        @pl.when(z < 3)
        def _():
            self.copy(me, self.up, 0, True).start()

        @pl.when(z > 0)
        def _():
            self.copy(me, self.down, 1, True).start()

        for to, k in ((self.A, 2), (self.B, 3), (self.C, 4)):
            self.copy(me, to, k, True).start()

    def from_line(self, zz):
        z, x, y, c = self.at_me[:4]
        p = pid(zz, x, y, c)
        self.wait(p)

        @pl.when((zz < z) & (z < 3))
        def _():
            self.copy(p, self.up, 0).start()

        @pl.when((zz > z) & (z > 0))
        def _():
            self.copy(p, self.down, 1).start()

        for to, k in ((self.A, 2), (self.B, 3), (self.C, 4)):
            self.copy(p, to, k).start()

    def from_a(self, zz):
        z, x, y, c, ax, ay, bx, by = self.at_me

        p = pid(zz, ax, ay, c)
        self.wait(p)
        self.copy(p, self.B, 3).start()
        self.copy(p, self.C, 4).start()

    def from_b(self, zz, xx, yy):
        c = self.at_me[3]

        p = pid(zz, xx, yy, c)
        self.wait(p)
        self.copy(p, self.C, 4).start()

    def finish(self):
        z, x, y, c, ax, ay, bx, by = self.at_me

        def one(zz, carry):
            p = pid(zz, x, y, c)

            @pl.when((z < 3) & (zz <= z))
            def _():
                self.copy(p, self.up, 0).wait_send()

            @pl.when((z > 0) & (zz >= z))
            def _():
                self.copy(p, self.down, 1).wait_send()

            for to, k in ((self.A, 2), (self.B, 3), (self.C, 4)):
                self.copy(p, to, k).wait_send()
            p = pid(zz, ax, ay, c)
            self.copy(p, self.B, 3).wait_send()
            self.copy(p, self.C, 4).wait_send()
            self.copy(pid(zz, bx, by, c), self.C, 4).wait_send()
            self.copy(pid(zz, 1 - x, 1 - y, c), self.C, 4).wait_send()
            return carry

        lax.fori_loop(0, 4, one, 0)


def far_z(z, k):
    half = z // 2
    near = z + half * (3 - 2 * z)
    place = 3 - k + (k // 2) * (2 * (k % 2) - 1) * near
    return place + half * (3 - 2 * place)


def reduce_kernel(
    hs_ref, gl_ref, ul_ref, pair_ref, wd_ref, wg_ref, wu_ref, att_ref,
    out_ref, line_ref,
    acc, cbuf, bbuf, abuf, zbuf, blk, mats, low, pair,
    csend, crecv, bsend, brecv, asend, arecv, zsend, zrecv, msem, lsem, psem, nsem, nsend, nrecv,
):
    f32 = jnp.float32
    rows = out_ref.shape[0]
    width = wd_ref.shape[1]
    z, x, y, c, ax, ay, bx, by = neighbours()
    dx, dy = 1 - x, 1 - y
    A, B, C = dev(z, ax, ay, c), dev(z, bx, by, c), dev(z, x, y, 1 - c)
    up, down = dev(z + 1 - z // 3, x, y, c), dev(z - 1 + (3 - z) // 3, x, y, c)
    tok = 4 * rows

    def q(zz, xx, yy):
        return zz * 4 + xx * 2 + yy

    def place_of(u):
        return far_z(z, u // 2), (u % 2) * (2 * x - 1) + 1 - x

    def loads(u):
        zz, xx = place_of(u)
        span = pl.ds(pl.multiple_of((zz * 2 + xx) * tok, tok), tok)
        slot = u % 2
        return [
            pltpu.make_async_copy(r.at[span], low.at[slot, n], lsem.at[slot, n])
            for n, r in enumerate((hs_ref, gl_ref, ul_ref))
        ] + [pltpu.make_async_copy(pair_ref.at[span], pair.at[slot], psem.at[slot])]

    def part_rows(slot, yy, cc):
        return blk.at[slot, pl.ds(pl.multiple_of((yy * 2 + cc) * rows, rows), rows)]

    def ccopy(zz, xx, yy, slot):
        i = q(zz, xx, yy)
        return pltpu.make_async_remote_copy(
            src_ref=part_rows(slot, yy, 1 - c), dst_ref=cbuf.at[i], send_sem=csend.at[slot, yy],
            recv_sem=crecv.at[i], device_id=C, device_id_type=MESH)

    weights = [pltpu.make_async_copy(r, mats.at[n], msem.at[n]) for n, r in enumerate((wd_ref, wg_ref, wu_ref))]
    for cp in weights:
        cp.start()
    for cp in loads(0):
        cp.start()

    def products(u):
        slot = u % 2
        zz, xx = place_of(u)
        for cp in loads(u):
            cp.wait()

        @pl.when(u < 7)
        def _():
            for cp in loads(u + 1):
                cp.start()

        @pl.when(u > 1)
        def _():
            for yy in range(2):
                ccopy(zz, xx, yy, slot).wait_send()

        blk[slot, :, :width] = nn(low[slot, 0], mats[0]).astype(blk.dtype)
        @pl.when(u == 0)
        def _():
            weights[1].wait()
            weights[2].wait()

        blk[slot, :, width : 2 * width] = (
            nn(low[slot, 1], mats[1]) + nn(low[slot, 2], mats[2])
        ).astype(blk.dtype)
        blk[slot, :, 2 * width :] = pair[slot]
        for yy in range(2):
            ccopy(zz, xx, yy, slot).start()
        for yy in range(2):
            acc[q(zz, xx, yy)] = part_rows(slot, yy, c)[...]

    def bcopy(zz, far):
        i = zz + 4 * far
        place = q(zz, dx, dy) if far else q(zz, bx, by)
        return pltpu.make_async_remote_copy(
            src_ref=acc.at[place], dst_ref=bbuf.at[i], send_sem=bsend.at[i],
            recv_sem=brecv.at[i], device_id=B, device_id_type=MESH)

    def acopy(zz):
        return pltpu.make_async_remote_copy(
            src_ref=acc.at[q(zz, ax, ay)], dst_ref=abuf.at[zz], send_sem=asend.at[zz],
            recv_sem=arecv.at[zz], device_id=A, device_id_type=MESH)

    def zcopy(zz, to, slot):
        return pltpu.make_async_remote_copy(
            src_ref=acc.at[q(zz, x, y)], dst_ref=zbuf.at[slot], send_sem=zsend.at[zz],
            recv_sem=zrecv.at[slot], device_id=to, device_id_type=MESH)

    def plus_c(zz, xx, yy):
        ccopy(zz, xx, yy, 0).wait_recv()
        i = q(zz, xx, yy)
        return acc[i].astype(f32) + cbuf[i].astype(f32)

    def stage_b(k, far):
        zz = far_z(z, k)
        xx, yy = (dx, dy) if far else (bx, by)
        acc[q(zz, xx, yy)] = plus_c(zz, xx, yy).astype(acc.dtype)
        bcopy(zz, far).start()

    def stage_a(k):
        zz = far_z(z, k)
        value = plus_c(zz, ax, ay)
        bcopy(zz, 1).wait_recv()
        acc[q(zz, ax, ay)] = (value + bbuf[zz + 4].astype(f32)).astype(acc.dtype)
        acopy(zz).start()

    def stage_z(k):
        zz = far_z(z, k)
        place = q(zz, x, y)
        value = plus_c(zz, x, y)
        bcopy(zz, 0).wait_recv()
        acopy(zz).wait_recv()
        value = value + bbuf[zz].astype(f32) + abuf[zz].astype(f32)

        @pl.when(zz != z)
        def _():
            acc[place] = value.astype(acc.dtype)

            @pl.when((zz > z) & (z > 0))
            def _():
                zcopy(zz, up, zz).wait_recv()
                acc[place] = (acc[place].astype(f32) + zbuf[zz].astype(f32)).astype(acc.dtype)

            @pl.when((zz < z) & (z < 3))
            def _():
                zcopy(zz, down, zz).wait_recv()
                acc[place] = (acc[place].astype(f32) + zbuf[zz].astype(f32)).astype(acc.dtype)

            @pl.when(zz > z)
            def _():
                zcopy(zz, up, zz).start()

            @pl.when((zz < z) & (zz != z - 1))
            def _():
                zcopy(zz, down, zz).start()

            @pl.when(zz == z - 1)
            def _():
                zcopy(zz, down, 4).start()

        @pl.when(zz == z)
        def _():
            out_ref[...] = value

            @pl.when(z > 0)
            def _():
                zcopy(z, up, z).wait_recv()
                out_ref[...] += zbuf[z].astype(f32)

            @pl.when(z < 3)
            def _():
                zcopy(z, down, 4).wait_recv()
                out_ref[...] += zbuf[4].astype(f32)

    line = Line(lambda zz: line_ref.at[zz], nsend, nrecv, att_ref)
    mine = pltpu.make_async_copy(att_ref, line_ref.at[z], nsem)
    mine.start()
    barrier_all()
    line.start()
    weights[0].wait()

    def step(u, carry):
        @pl.when(u == 1)
        def _():
            stage_b(0, 1)

        @pl.when(u < 8)
        def _():
            products(u)

        for d in (1, 2, 3):
            @pl.when(u == 2 * d + 1)
            def _():
                line.pass_on(d)

        k = (u - 1) // 2

        @pl.when((u > 1) & (u < 9) & (u % 2 == 1))
        def _():
            stage_b(k, 1)

        @pl.when((u > 0) & (u < 9) & (u % 2 == 0))
        def _():
            stage_b(k, 0)

        @pl.when((u >= 5) & (u < 13) & (u % 2 == 1))
        def _():
            stage_a((u - 5) // 2)

        @pl.when((u >= 8) & (u % 2 == 0))
        def _():
            stage_z((u - 8) // 2)

        return carry

    lax.fori_loop(0, 15, step, 0)
    mine.wait()
    line.finish()
    for slot in range(2):
        for yy in range(2):
            ccopy(z, x, yy, slot).wait_send()

    def last(zz, carry):
        bcopy(zz, 1).wait_send()
        bcopy(zz, 0).wait_send()
        acopy(zz).wait_send()

        @pl.when(zz != z)
        def _():
            zcopy(zz, up, zz).wait_send()

        return carry

    lax.fori_loop(0, 4, last, 0)


def reduce_experts(hs, gl, ul, pair, wd, wg, wu, att, cid):
    n, hid = hs.shape
    width = wd.shape[1]
    rows = n // 32
    w = 2 * width + pair.shape[1]
    dma = pltpu.SemaphoreType.DMA
    bf = jnp.bfloat16

    def pieces(k):
        return pltpu.VMEM((k, rows, w), bf)

    anywhere = pl.BlockSpec(memory_space=pl.ANY)
    return pl.pallas_call(
        reduce_kernel,
        in_specs=[anywhere] * 8,
        out_specs=[pl.BlockSpec(memory_space=pltpu.VMEM), anywhere],
        out_shape=[
            jax.ShapeDtypeStruct((rows, w), jnp.float32), jax.ShapeDtypeStruct((4, *att.shape), bf),
        ],
        scratch_shapes=[
            pieces(16), pieces(16), pieces(8), pieces(4), pieces(5),
            pltpu.VMEM((2, 4 * rows, w), bf),
            pltpu.VMEM((3, hid, width), bf),
            pltpu.VMEM((2, 3, 4 * rows, hid), bf),
            pltpu.VMEM((2, 4 * rows, pair.shape[1]), bf),
            dma((2, 2)), dma((16,)), dma((8,)), dma((8,)), dma((4,)), dma((4,)),
            dma((4,)), dma((5,)), dma((3,)), dma((2, 3)), dma((2,)), dma, dma((2, 4)), dma((4,)),
        ],
        compiler_params=pltpu.CompilerParams(
            collective_id=cid, has_side_effects=True, vmem_limit_bytes=56 * 2**20
        ),
        cost_estimate=pl.CostEstimate(
            flops=6 * n * width * hid, bytes_accessed=10 * n * width, transcendentals=0
        ),
        name="reduce_experts",
    )(hs, gl, ul, pair, wd, wg, wu, att)


def barrier_wide():
    z, x, y, c = coords()
    ctx, tp = lax.axis_index("ctx"), lax.axis_index("tp")
    bar = pltpu.get_barrier_semaphore()
    for i in range(1, 8):
        pl.semaphore_signal(bar, inc=1, device_id=((ctx + i) % 8, tp), device_id_type=MESH)
    for to in (dev(z, x, 1 - y, c), dev(z, x, y, 1 - c), dev(z, x, 1 - y, 1 - c)):
        pl.semaphore_signal(bar, inc=1, device_id=to, device_id_type=MESH)
    pl.semaphore_wait(bar, 10)


class Columns:
    def __init__(self, src, buf, send, recv, tsend, trecv):
        self.src, self.buf, self.send, self.recv = src, buf, send, recv
        self.tsend, self.trecv = tsend, trecv
        self.tp = lax.axis_index("tp")
        z, x, y, c = coords()
        self.z, self.x, self.y, self.c = z, x, y, c
        self.Y, self.C = dev(z, x, 1 - y, c), dev(z, x, y, 1 - c)
        self.mine, self.by_y, self.by_c, self.by_d = y * 2 + c, (1 - y) * 2 + c, y * 2 + 1 - c, (1 - y) * 2 + 1 - c

    def push(self, i):
        to = (self.z + i) % 4
        return pltpu.make_async_remote_copy(
            src_ref=self.src.at[to], dst_ref=self.buf.at[self.z, self.tp],
            send_sem=self.send.at[i], recv_sem=self.recv.at[i],
            device_id=dev(to, self.x, self.y, self.c), device_id_type=MESH)

    def over(self, part, to, k):
        return pltpu.make_async_remote_copy(
            src_ref=self.buf.at[:, part], dst_ref=self.buf.at[:, part], send_sem=self.tsend.at[k],
            recv_sem=self.trecv.at[part], device_id=to, device_id_type=MESH)

    def start(self):
        for i in range(1, 4):
            self.push(i).start()
        self.buf[self.z, self.tp] = self.src[self.z]

    def exchange(self):
        for i in range(1, 4):
            self.push(i).wait_recv()
        self.over(self.mine, self.Y, 0).start()
        self.over(self.mine, self.C, 1).start()

    def forward(self):
        self.over(self.by_y, self.Y, 0).wait_recv()
        self.over(self.by_y, self.C, 2).start()

    def finish(self):
        self.over(self.by_c, self.C, 1).wait_recv()
        self.over(self.by_d, self.C, 2).wait_recv()
        for i in range(1, 4):
            self.push(i).wait_send()
        self.over(self.mine, self.Y, 0).wait_send()
        self.over(self.mine, self.C, 1).wait_send()
        self.over(self.by_y, self.C, 2).wait_send()


class Line:
    def __init__(self, place, send, recv, first=None):
        self.place, self.send, self.recv, self.first = place, send, recv, first
        z, x, y, c = coords()
        self.z = z
        self.up, self.down = dev(z + 1 - z // 3, x, y, c), dev(z - 1 + (3 - z) // 3, x, y, c)

    def copy(self, zz, to, k, own=False):
        src = self.first if own and self.first is not None else self.place(zz)
        return pltpu.make_async_remote_copy(
            src_ref=src, dst_ref=self.place(zz), send_sem=self.send.at[k, zz],
            recv_sem=self.recv.at[zz], device_id=to, device_id_type=MESH)

    def start(self):
        @pl.when(self.z < 3)
        def _():
            self.copy(self.z, self.up, 0, True).start()

        @pl.when(self.z > 0)
        def _():
            self.copy(self.z, self.down, 1, True).start()

    def pass_on(self, d):
        z = self.z

        @pl.when(z - d >= 0)
        def _():
            self.copy(z - d, self.up, 0).wait_recv()

            @pl.when(z < 3)
            def _():
                self.copy(z - d, self.up, 0).start()

        @pl.when(z + d <= 3)
        def _():
            self.copy(z + d, self.down, 1).wait_recv()

            @pl.when(z > 0)
            def _():
                self.copy(z + d, self.down, 1).start()

    def finish(self):
        z = self.z
        for zz in range(4):
            @pl.when((z < 3) & (zz <= z))
            def _():
                self.copy(zz, self.up, 0).wait_send()

            @pl.when((z > 0) & (zz >= z))
            def _():
                self.copy(zz, self.down, 1).wait_send()


class Spread:
    def __init__(self, place, send, recv, first=None):
        self.place, self.send, self.recv, self.first = place, send, recv, first
        z, x, y, c = coords()
        self.z, self.x = z, x
        self.X = dev(z, 1 - x, y, c)
        self.up, self.down = dev(z + 1 - z // 3, x, y, c), dev(z - 1 + (3 - z) // 3, x, y, c)
        self.me = z * 2 + x

    def copy(self, p, to, k, own=False):
        src = self.first if own and self.first is not None else self.place(p)
        return pltpu.make_async_remote_copy(
            src_ref=src, dst_ref=self.place(p), send_sem=self.send.at[k, p],
            recv_sem=self.recv.at[p], device_id=to, device_id_type=MESH)

    def start_x(self):
        self.copy(self.me, self.X, 2, True).start()

    def start_z(self):
        @pl.when(self.z < 3)
        def _():
            self.copy(self.me, self.up, 0, True).start()

        @pl.when(self.z > 0)
        def _():
            self.copy(self.me, self.down, 1, True).start()

    def pass_on(self, d):
        z, x = self.z, self.x

        @pl.when(z - d >= 0)
        def _():
            p = (z - d) * 2 + x
            self.copy(p, self.X, 2).wait_recv()

            @pl.when(z < 3)
            def _():
                self.copy(p, self.up, 0).start()

            self.copy(p, self.X, 2).start()

        @pl.when(z + d <= 3)
        def _():
            p = (z + d) * 2 + x
            self.copy(p, self.X, 2).wait_recv()

            @pl.when(z > 0)
            def _():
                self.copy(p, self.down, 1).start()

            self.copy(p, self.X, 2).start()

    def arrive(self):
        for zz in range(4):
            self.copy(zz * 2 + 1 - self.x, self.X, 2).wait_recv()

    def finish(self):
        z, x = self.z, self.x
        for zz in range(4):
            p = zz * 2 + x

            @pl.when((z < 3) & (zz <= z))
            def _():
                self.copy(p, self.up, 0).wait_send()

            @pl.when((z > 0) & (zz >= z))
            def _():
                self.copy(p, self.down, 1).wait_send()

            self.copy(p, self.X, 2).wait_send()


def row_norm(v):
    return lax.rsqrt(jnp.mean(v * v, axis=1, keepdims=True) + 1e-06)


def turn(v, cos, sin):
    return v * cos + pltpu.roll(v, v.shape[1] // 2, 1) * sin


def turn_back(v, cos, sin):
    return v * cos - pltpu.roll(v, v.shape[1] // 2, 1) * sin


def front_kernel(
    x_ref, g1_in, wq_ref, wk_ref, wv_ref, qg_in, kg_in, cos_ref, sin_ref, qpos_ref, kpos_ref,
    wo_ref, g2_in, wr_in, routes_in, cot_ref,
    first_ref, qraw_ref, kraw_ref, qrot_ref, kv_ref, att_ref, log_ref, res_ref, gates_ref, piece_ref, cols_ref,
    xs, g1_ref, qg_ref, kg_ref, g2_ref, wr_ref, routes_ref, wk, wv, turned, wq, wo, part, cbuf, ybuf, stage, csrc,
    wsem, ksend, krecv, csend, crecv, ysend, yrecv, psend, precv, tsend, trecv,
):
    f32, bf = jnp.float32, jnp.bfloat16
    z, x, y, c = coords()
    rows = res_ref.shape[0]
    experts = wr_ref.shape[0]
    head = qg_ref.shape[1]
    heads = wq_ref.shape[1] // head
    half = x_ref.shape[0] // 2
    fetched = [
        pltpu.make_async_copy(src, dst, wsem.at[n])
        for n, (src, dst) in enumerate((
            (x_ref, xs), (g1_in, g1_ref), (qg_in, qg_ref), (kg_in, kg_ref), (g2_in, g2_ref),
            (wr_in, wr_ref), (routes_in, routes_ref), (wk_ref, wk), (wv_ref, wv), (wq_ref, wq), (wo_ref, wo),
        ))
    ]
    for cp in fetched:
        cp.start()
    wqc, woc = fetched[9:]
    own = pl.ds(pl.multiple_of((y * 2 + c) * rows, rows), rows)
    Y, C = dev(z, x, 1 - y, c), dev(z, x, y, 1 - c)
    barrier_wide()
    cotc = pltpu.make_async_copy(cot_ref.at[own], piece_ref.at[:, x_ref.shape[1] : 2 * x_ref.shape[1]], wsem.at[11])
    cotc.start()
    for cp in fetched[:9]:
        cp.wait()
    turned[...] = routes_ref[...].T
    value = xs[...].astype(f32)
    first = (value * row_norm(value) * g1_ref[...]).astype(bf)
    first_ref[...] = first
    cos, sin = cos_ref[...], sin_ref[...]
    kraw = nn(first, wk[...])
    kraw_ref[...] = kraw
    krot = turn(kraw * row_norm(kraw) * kg_ref[...], cos, sin).astype(bf)
    vrow = nn(first, wv[...]).astype(bf)
    me = z * 2 + x
    for s in range(2):
        kv_ref[s, me] = krot[s * half : (s + 1) * half]
        kv_ref[2 + s, me] = vrow[s * half : (s + 1) * half]

    keys_out = Spread(lambda p: kv_ref.at[:, p], ksend, krecv)
    keys_out.start_z()
    keys_out.start_x()

    wqc.wait()
    qraw_ref[...] = nn(first, wq[...])
    keys_out.pass_on(1)

    def rope_head(h, carry):
        lanes = pl.ds(pl.multiple_of(h * head, head), head)
        raw = qraw_ref[:, lanes]
        rot = turn(raw * row_norm(raw) * qg_ref[...], cos_ref[...], sin_ref[...]).astype(bf)
        qrot_ref[h] = rot[:half]
        qrot_ref[heads + h] = rot[half:]
        return carry

    lax.fori_loop(0, heads // 2, rope_head, 0)
    keys_out.pass_on(2)
    lax.fori_loop(heads // 2, heads, rope_head, 0)
    keys_out.pass_on(3)
    keys_out.arrive()
    width = first.shape[1]
    per = width // 4
    for i in range(4):
        csrc[i] = first_ref[own, i * per : (i + 1) * per]
    blocks = Columns(csrc, cols_ref, psend, precv, tsend, trecv)
    blocks.start()

    scale = 1.0 / math.sqrt(head)

    group = 4

    def attend(i, carry):
        s = i // (heads // group)
        h = i % (heads // group) * group
        span = pl.ds(pl.multiple_of(s * half, half), half)
        keys = kv_ref[s].reshape(8 * half, head)
        vals = kv_ref[2 + s].reshape(8 * half, head)
        query = qrot_ref[pl.ds(i * group, group)].reshape(group * half, head)
        scores = (nt(query, keys) * scale).reshape(group, half, 8 * half)
        allowed = qpos_ref[span, :1] >= kpos_ref[pl.ds(s, 1), :]
        scores = jnp.where(allowed[None], scores, -1e9).reshape(group * half, 8 * half)
        top = jnp.max(scores, axis=1, keepdims=True)
        weights = jnp.exp(scores - top)
        total = jnp.sum(weights, axis=1, keepdims=True)
        probs = (weights * (1.0 / total)).astype(bf)
        mixed = nn(probs, vals).astype(bf)
        logs = jnp.broadcast_to(top + jnp.log(total), (group * half, head))
        log_ref[pl.ds(i * group, group)] = logs.reshape(group, half, head)
        for g in range(group):
            lanes = pl.ds(pl.multiple_of((h + g) * head, head), head)
            att_ref[span, lanes] = mixed[g * half : (g + 1) * half]
        @pl.when(i == steps // 2 - 1)
        def _():
            blocks.exchange()
        return carry

    steps = 2 * heads // group
    lax.fori_loop(0, steps, attend, 0)
    blocks.forward()
    woc.wait()

    def at(yy, cc):
        return part.at[pl.ds(pl.multiple_of((yy * 2 + cc) * rows, rows), rows)]

    def project(yy):
        span = pl.ds(pl.multiple_of(yy * 2 * rows, 2 * rows), 2 * rows)
        part[span] = nn(att_ref[span], wo[...]).astype(bf)

    def ccopy(yy):
        return pltpu.make_async_remote_copy(
            src_ref=at(yy, 1 - c), dst_ref=cbuf.at[yy], send_sem=csend.at[yy],
            recv_sem=crecv.at[yy], device_id=C, device_id_type=MESH)

    project(1 - y)
    ccopy(1 - y).start()
    project(y)
    ccopy(y).start()
    ccopy(1 - y).wait_recv()
    stage[...] = (at(1 - y, c)[...].astype(f32) + cbuf[1 - y].astype(f32)).astype(bf)
    yc = pltpu.make_async_remote_copy(
        src_ref=stage, dst_ref=ybuf, send_sem=ysend, recv_sem=yrecv, device_id=Y, device_id_type=MESH)
    yc.start()
    ccopy(y).wait_recv()
    res = xs[own].astype(f32) + (at(y, c)[...].astype(f32) + cbuf[y].astype(f32))
    lane = lax.broadcasted_iota(jnp.int32, (rows, 4 * experts), 1)
    named = jnp.zeros((rows, 4 * experts), jnp.bool_)
    routes = turned[own]
    for k in range(routes.shape[1]):
        named = named | (lane % experts == routes[:, k : k + 1])
    yc.wait_recv()
    res = res + ybuf[...].astype(f32)
    res_ref[...] = res
    second = (res * row_norm(res) * g2_ref[...]).astype(bf)
    piece_ref[:, :width] = second
    logits = nt(second, wr_ref[...])
    logits = jnp.concatenate([logits, logits, jnp.zeros((rows, 2 * experts), f32)], axis=1)
    masked = jnp.where(named & (lane < 2 * experts), logits, -1e30)
    top = jnp.max(masked, axis=1, keepdims=True)
    weights = jnp.where(named & (lane < 2 * experts), jnp.exp(masked - top), 0.0)
    total = jnp.sum(jnp.where(lane < experts, weights, 0.0), axis=1, keepdims=True)
    gates = weights / total
    high = gates.astype(bf)
    low = (gates - high.astype(f32)).astype(bf)
    gates_ref[...] = jnp.where(lane < experts, gates, 0.0)
    piece_ref[:, 2 * width :] = jnp.where(lane < experts, high, low)

    yc.wait_send()
    ccopy(0).wait_send()
    ccopy(1).wait_send()
    blocks.finish()
    keys_out.finish()
    cotc.wait()


def front(x, g1, wq, wk, wv, qg, kg, cos, sin, qpos, kpos, wo, g2, wr, routes, cot, cid):
    tok, width = x.shape
    head = qg.shape[1]
    cols = wq.shape[1]
    heads = cols // head
    rows, half = tok // 4, tok // 2
    f32, bf = jnp.float32, jnp.bfloat16
    dma = pltpu.SemaphoreType.DMA
    vm, anywhere = pl.BlockSpec(memory_space=pltpu.VMEM), pl.BlockSpec(memory_space=pl.ANY)

    def out(shape, kind):
        return jax.ShapeDtypeStruct(shape, kind)

    return pl.pallas_call(
        front_kernel,
        in_specs=[anywhere] * 7 + [vm] * 4 + [anywhere] * 5,
        out_specs=[vm] * 11,
        out_shape=[
            out((tok, width), bf), out((tok, cols), f32), out((tok, head), f32),
            out((2 * heads, half, head), bf), out((4, 8, half, head), bf), out((tok, cols), bf),
            out((2 * heads, half, head), f32), out((rows, width), f32), out((rows, 128), f32),
            out((rows, 2 * width + 128), bf), out((4, 4, rows, width // 4), bf),
        ],
        scratch_shapes=[
            pltpu.VMEM((tok, width), bf), pltpu.VMEM(g1.shape, f32), pltpu.VMEM(qg.shape, f32),
            pltpu.VMEM(kg.shape, f32), pltpu.VMEM(g2.shape, f32), pltpu.VMEM(wr.shape, bf),
            pltpu.VMEM(routes.shape, jnp.int32), pltpu.VMEM((width, head), bf), pltpu.VMEM((width, head), bf),
            pltpu.VMEM(routes.shape[::-1], jnp.int32),
            pltpu.VMEM((width, cols), bf), pltpu.VMEM((cols, width), bf), pltpu.VMEM((tok, width), bf),
            pltpu.VMEM((2, rows, width), bf), pltpu.VMEM((rows, width), bf), pltpu.VMEM((rows, width), bf),
            pltpu.VMEM((4, rows, width // 4), bf),
            dma((12,)), dma((3, 8)), dma((8,)), dma((2,)), dma((2,)), dma, dma,
            dma((4,)), dma((4,)), dma((3,)), dma((4,)),
        ],
        compiler_params=pltpu.CompilerParams(
            collective_id=cid, has_side_effects=True, vmem_limit_bytes=60 * 2**20
        ),
        name="front",
    )(x, g1, wq, wk, wv, qg, kg, cos, sin, qpos, kpos, wo, g2, wr, routes, cot)


def middle_kernel(
    sums_ref, res_ref, gates_ref, cot_in, g2_in, wr_in, wo_ref, qrot_ref, kv_ref, log_ref,
    qraw_ref, qg_in, cos_ref, sin_ref, qpos_ref, kpos_ref,
    layer_ref, gres_ref, gn2_ref, cols_ref, qlow_ref, dkv_ref, qgain_ref,
    cot_ref, g2_ref, wr_ref, qg_ref, wo, back, mixed, dk, dv, csrc, wsem, send, recv, psend, precv, tsend, trecv,
):
    f32, bf = jnp.float32, jnp.bfloat16
    z, x, y, c = coords()
    rows, width = res_ref.shape
    experts = wr_in.shape[0]
    head = qg_in.shape[1]
    heads = qraw_ref.shape[1] // head
    half = qraw_ref.shape[0] // 2
    mine = pl.ds(pl.multiple_of((y * 2 + c) * rows, rows), rows)
    fetched = [
        pltpu.make_async_copy(src, dst, wsem.at[n])
        for n, (src, dst) in enumerate((
            (cot_in.at[mine], cot_ref), (g2_in, g2_ref), (wr_in, wr_ref), (qg_in, qg_ref), (wo_ref, wo)))
    ]
    for item in fetched:
        item.start()
    woc = fetched[4]
    barrier_wide()
    Y, C = dev(z, x, 1 - y, c), dev(z, x, y, 1 - c)

    def at(yy, cc):
        return back.at[pl.ds(pl.multiple_of((yy * 2 + cc) * rows, rows), rows)]

    for item in fetched[:4]:
        item.wait()
    res = res_ref[...]
    layer_ref[...] = (res + sums_ref[:, :width]).astype(bf)
    gates = gates_ref[...]
    pair = sums_ref[:, 2 * width :]
    glog = (gates * (pair - jnp.sum(gates * pair, axis=1, keepdims=True))).astype(bf)
    gsec = sums_ref[:, width : 2 * width] + nn(glog[:, :experts], wr_ref[...])
    rs = row_norm(res)
    unit = res * rs
    gn2_ref[...] = jnp.sum(gsec * unit, axis=0, keepdims=True)
    cg = gsec * g2_ref[...]
    gres = cot_ref[...].astype(f32) + rs * (cg - unit * jnp.mean(cg * unit, axis=1, keepdims=True))
    gres_ref[...] = gres
    glow = gres.astype(bf)
    back[mine] = glow

    def cp(yy, cc, to, k):
        return pltpu.make_async_remote_copy(
            src_ref=at(yy, cc), dst_ref=at(yy, cc), send_sem=send.at[k],
            recv_sem=recv.at[yy * 2 + cc], device_id=to, device_id_type=MESH)

    cp(y, c, Y, 0).start()
    cp(y, c, C, 1).start()
    per = width // 4
    for i in range(4):
        csrc[i, :, :per] = glow[:, i * per : (i + 1) * per]
        csrc[i, :, per:] = glog
    blocks = Columns(csrc, cols_ref, psend, precv, tsend, trecv)
    blocks.start()
    dk[...] = jnp.zeros_like(dk)
    dv[...] = jnp.zeros_like(dv)
    qgain_ref[...] = jnp.zeros_like(qgain_ref)
    woc.wait()

    def mix(yy):
        span = pl.ds(pl.multiple_of(yy * 2 * rows, 2 * rows), 2 * rows)
        both = nt(back[span], wo[...]).astype(bf)
        for h in range(heads):
            mixed[yy * heads + h] = both[:, h * head : (h + 1) * head]

    cp(y, 1 - c, C, 1).wait_recv()
    mix(y)
    cp(1 - y, c, Y, 0).wait_recv()
    cp(1 - y, c, C, 2).start()
    cp(1 - y, 1 - c, C, 2).wait_recv()
    mix(1 - y)
    scale = 1.0 / math.sqrt(head)

    group = 4

    def attend(i, carry):
        s = i // (heads // group)
        h = i % (heads // group) * group
        span = pl.ds(pl.multiple_of(s * half, half), half)
        mine = pl.ds(i * group, group)
        keys = kv_ref[s].reshape(8 * half, head)
        vals = kv_ref[2 + s].reshape(8 * half, head)
        query = qrot_ref[mine].reshape(group * half, head)
        grad = mixed[mine].reshape(group * half, head)
        scores = (nt(query, keys) * scale).reshape(group, half, 8 * half)
        allowed = qpos_ref[span, :1] >= kpos_ref[pl.ds(s, 1), :]
        logs = log_ref[mine][:, :, :1]
        probs = jnp.where(allowed[None], jnp.exp(scores - logs), 0.0).reshape(group * half, 8 * half)
        gprobs = nt(grad, vals)
        inner = jnp.sum(probs * gprobs, axis=1, keepdims=True)
        dots = (probs * (gprobs - inner) * scale).astype(bf)
        dk[s] += tn(dots, query)
        dv[s] += tn(probs.astype(bf), grad)
        drot = nn(dots, keys)
        for g in range(group):
            lanes = pl.ds(pl.multiple_of((h + g) * head, head), head)
            raw = qraw_ref[span, lanes]
            dn = turn_back(drot[g * half : (g + 1) * half], cos_ref[span], sin_ref[span])
            rs = row_norm(raw)
            unit = raw * rs
            qgain_ref[...] += jnp.sum((dn * unit).reshape(half // 8, 8, head), axis=0)
            cg = dn * qg_ref[...]
            low = rs * (cg - unit * jnp.mean(cg * unit, axis=1, keepdims=True))
            qlow_ref[span, lanes] = low.astype(bf)
        return carry

    steps = 2 * heads // group
    lax.fori_loop(0, steps // 2, attend, 0)
    blocks.exchange()
    lax.fori_loop(steps // 2, steps, attend, 0)
    blocks.forward()
    for s in range(2):
        dkv_ref[s] = dk[s].astype(bf).reshape(8, half, head)
        dkv_ref[2 + s] = dv[s].astype(bf).reshape(8, half, head)
    cp(y, c, Y, 0).wait_send()
    cp(y, c, C, 1).wait_send()
    cp(1 - y, c, C, 2).wait_send()
    blocks.finish()


def middle(sums, res, gates, cot, g2, wr, wo, qrot, kv, logs, qraw, qg, cos, sin, qpos, kpos, cid):
    rows, width = res.shape
    tok, cols = qraw.shape
    head = qg.shape[1]
    half = tok // 2
    f32, bf = jnp.float32, jnp.bfloat16
    dma = pltpu.SemaphoreType.DMA
    vm, anywhere = pl.BlockSpec(memory_space=pltpu.VMEM), pl.BlockSpec(memory_space=pl.ANY)

    def out(shape, kind):
        return jax.ShapeDtypeStruct(shape, kind)

    return pl.pallas_call(
        middle_kernel,
        in_specs=[vm] * 3 + [anywhere] * 4 + [vm] * 4 + [anywhere] + [vm] * 4,
        out_specs=[vm] * 7,
        out_shape=[
            out((rows, width), bf), out((rows, width), f32), out((1, width), f32),
            out((4, 4, rows, width // 4 + 128), bf), out((tok, cols), bf), out((4, 8, half, head), bf),
            out((8, head), f32),
        ],
        scratch_shapes=[
            pltpu.VMEM((rows, width), bf), pltpu.VMEM(g2.shape, f32), pltpu.VMEM(wr.shape, bf),
            pltpu.VMEM(qg.shape, f32),
            pltpu.VMEM((cols, width), bf), pltpu.VMEM((tok, width), bf), pltpu.VMEM((2 * cols // head, half, head), bf),
            pltpu.VMEM((2, 8 * half, head), f32), pltpu.VMEM((2, 8 * half, head), f32),
            pltpu.VMEM((4, rows, width // 4 + 128), bf),
            dma((5,)), dma((3,)), dma((4,)), dma((4,)), dma((4,)), dma((3,)), dma((4,)),
        ],
        compiler_params=pltpu.CompilerParams(
            collective_id=cid, has_side_effects=True, vmem_limit_bytes=52 * 2**20
        ),
        name="middle",
    )(sums, res, gates, cot, g2, wr, wo, qrot, kv, logs, qraw, qg, cos, sin, qpos, kpos)


def tail_kernel(
    dkv_ref, qlow_ref, kraw_ref, kg_in, cos_ref, sin_ref, wq_ref, wk_in, wv_in, x_in, g1_in,
    gres_ref, layer_ref, gn2_ref, qgain_ref, first_in, att_in, back_ref, rows_in,
    gin_ref, lout_ref, gq_ref, gkv_ref, gout_ref, grouter_ref, vo_ref,
    wq, kg_ref, wk_ref, wv_ref, x_ref, g1_ref, first_ref, att, second, att_t, xbuf, zbuf, zst, part, cbuf, ybuf, stage, vbuf, vpart, tbuf, gin, qbuf, kvbuf, turned, osrc, obuf, rsrc, rbuf, qsrc, qgot, ksrc, kgot, grouter_both,
    wsem, xsend, xrecv, zsend, zrecv, csend, crecv, ysend, yrecv, send, recv, vsend, vrecv, tsend, trecv,
    qsend, qrecv, ksend, krecv, esend, erecv,
):
    f32, bf = jnp.float32, jnp.bfloat16
    z, x, y, c = coords()
    ctx, tp = lax.axis_index("ctx"), lax.axis_index("tp")
    rows, width = gres_ref.shape
    half, head = dkv_ref.shape[2:]
    line_cols = first_in.shape[1]
    tok = x_in.shape[0]
    fetched = [
        pltpu.make_async_copy(src, dst, wsem.at[n])
        for n, (src, dst) in enumerate((
            (first_in, first_ref), (att_in, att), (wq_ref, wq), (kg_in, kg_ref), (wk_in, wk_ref),
            (wv_in, wv_ref), (x_in, x_ref), (g1_in, g1_ref),
            *(
                (rows_in.at[pl.ds(pl.multiple_of((zz * 2 + x) * tok, tok), tok),
                            pl.ds(pl.multiple_of(z * line_cols, line_cols), line_cols)],
                 second.at[pl.ds(zz * tok, tok)])
                for zz in range(4)
            ),
        ))
    ]
    for item in fetched:
        item.start()
    X, Y, C, D = dev(z, 1 - x, y, c), dev(z, x, 1 - y, c), dev(z, x, y, 1 - c), dev(z, x, 1 - y, 1 - c)
    up, down = dev(z + 1 - z // 3, x, y, c), dev(z - 1 + (3 - z) // 3, x, y, c)
    barrier_wide()

    def xcopy(zz):
        return pltpu.make_async_remote_copy(
            src_ref=dkv_ref.at[:, zz * 2 + 1 - x], dst_ref=xbuf.at[zz], send_sem=xsend.at[zz],
            recv_sem=xrecv.at[zz], device_id=X, device_id_type=MESH)

    def zcopy(zz, to, slot):
        return pltpu.make_async_remote_copy(
            src_ref=zst.at[zz], dst_ref=zbuf.at[slot], send_sem=zsend.at[zz],
            recv_sem=zrecv.at[slot], device_id=to, device_id_type=MESH)

    span = qlow_ref.shape[1] // 2
    queries = [
        Line(lambda zz, n=n: qbuf.at[n, zz], qsend.at[n], qrecv.at[n]) for n in range(2)
    ]
    keys = Line(lambda zz: kvbuf.at[zz], ksend, krecv)
    for n in range(2):
        qbuf[n, z] = qlow_ref[:, n * span : (n + 1) * span]
    for k in range(4):
        xcopy(far_z(z, k)).start()
    queries[0].start()

    pairs = [(gin, gin_ref), (layer_ref, lout_ref)]

    def place(ref, yy, cc):
        return ref.at[pl.ds(pl.multiple_of((yy * 2 + cc) * rows, rows), rows)]

    def cp(n, src, yy, cc, to, k):
        return pltpu.make_async_remote_copy(
            src_ref=src, dst_ref=place(pairs[n][1], yy, cc), send_sem=send.at[n, k],
            recv_sem=recv.at[n, yy * 2 + cc], device_id=to, device_id_type=MESH)

    own = pl.ds(pl.multiple_of((y * 2 + c) * rows, rows), rows)
    cp(1, layer_ref, y, c, Y, 0).start()
    cp(1, layer_ref, y, c, C, 1).start()
    lout_ref[own] = layer_ref[...]

    per = gq_ref.shape[0]
    own_cols = pl.ds(pl.multiple_of(x * per, per), per)
    far_cols = pl.ds(pl.multiple_of((1 - x) * per, per), per)

    def swap(n, src, dst):
        return pltpu.make_async_remote_copy(
            src_ref=src, dst_ref=dst, send_sem=esend.at[n], recv_sem=erecv.at[n], device_id=X,
            device_id_type=MESH)

    swaps = [
        swap(0, osrc, obuf), swap(1, rsrc, rbuf), swap(2, qsrc.at[0], qgot.at[0]),
        swap(3, qsrc.at[1], qgot.at[1]), swap(4, ksrc, kgot),
    ]
    own_lanes = pl.ds(pl.multiple_of(x * per, 128), per)
    far_lanes = pl.ds(pl.multiple_of((1 - x) * per, 128), per)
    for item in fetched[:2]:
        item.wait()
    att_t[...] = att[...].T
    osrc[...] = nn(att_t[...], back_ref[:, far_lanes]).astype(bf)
    swaps[0].start()
    turned[...] = first_ref[...].T

    def query_part(n):
        right = qbuf[n].reshape(turned.shape[1], span)
        cols = slice(n * span, (n + 1) * span)
        qsrc[n] = nn(turned[far_cols], right).astype(bf)
        swaps[2 + n].start()
        gq_ref[:, cols] = nn(turned[own_cols], right)

    def sum_z(k):
        zz = far_z(z, k)
        xcopy(zz).wait_recv()
        total = dkv_ref[:, zz * 2 + x].astype(f32) + xbuf[zz].astype(f32)
        zst[zz] = total.astype(bf)

        @pl.when((zz > z) & (z > 0))
        def _():
            zcopy(zz, up, zz).wait_recv()
            zst[zz] = (zst[zz].astype(f32) + zbuf[zz].astype(f32)).astype(bf)

        @pl.when((zz < z) & (z < 3))
        def _():
            zcopy(zz, down, zz).wait_recv()
            zst[zz] = (zst[zz].astype(f32) + zbuf[zz].astype(f32)).astype(bf)

        @pl.when(zz > z)
        def _():
            zcopy(zz, up, zz).start()

        @pl.when((zz < z) & (zz != z - 1))
        def _():
            zcopy(zz, down, zz).start()

        @pl.when(zz == z - 1)
        def _():
            zcopy(zz, down, 4).start()

    def at(yy, cc):
        return part.at[pl.ds(pl.multiple_of((yy * 2 + cc) * rows, rows), rows)]

    def two(yy):
        return pl.ds(pl.multiple_of(yy * 2 * rows, 2 * rows), 2 * rows)

    sum_z(0)
    for item in fetched[2:]:
        item.wait()
    first_a = nt(qlow_ref[two(1 - y)], wq[...])
    sum_z(1)
    first_b = nt(qlow_ref[two(y)], wq[...])
    queries[0].pass_on(1)
    sum_z(2)
    queries[1].start()
    router_part = tn(second[...], back_ref[:, line_cols:])
    part_of = jnp.stack([router_part[:per], router_part[per:]])
    grouter_both[...] = part_of
    rsrc[...] = grouter_both[1 - x].astype(bf)
    swaps[1].start()
    xcopy(z).wait_recv()
    dkv = dkv_ref[:, ctx].astype(f32) + xbuf[z].astype(f32)

    @pl.when(z > 0)
    def _():
        zcopy(z, up, z).wait_recv()

    @pl.when(z == 0)
    def _():
        zbuf[0] = jnp.zeros_like(zbuf[0])

    @pl.when(z < 3)
    def _():
        zcopy(z, down, 4).wait_recv()

    @pl.when(z == 3)
    def _():
        zbuf[4] = jnp.zeros_like(zbuf[4])

    dkv = dkv + zbuf[z].astype(f32) + zbuf[4].astype(f32)
    dkey = jnp.concatenate([dkv[0], dkv[1]], axis=0)
    vlow = jnp.concatenate([dkv[2], dkv[3]], axis=0).astype(bf)
    raw = kraw_ref[...]
    dn = turn_back(dkey, cos_ref[...], sin_ref[...])
    rs = row_norm(raw)
    unit = raw * rs
    kgain = jnp.sum(dn * unit, axis=0, keepdims=True)
    cg = dn * kg_ref[...]
    klow = (rs * (cg - unit * jnp.mean(cg * unit, axis=1, keepdims=True))).astype(bf)
    kvbuf[z, :, :head] = klow
    kvbuf[z, :, head:] = vlow
    keys.start()
    queries[0].pass_on(2)

    def ccopy(yy):
        return pltpu.make_async_remote_copy(
            src_ref=at(yy, 1 - c), dst_ref=cbuf.at[yy], send_sem=csend.at[yy],
            recv_sem=crecv.at[yy], device_id=C, device_id_type=MESH)

    def project(yy, first):
        keys, vals = kvbuf[z, two(yy), :head], kvbuf[z, two(yy), head:]
        part[two(yy)] = (first + nt(keys, wk_ref[...]) + nt(vals, wv_ref[...])).astype(bf)
        ccopy(yy).start()

    project(1 - y, first_a)
    project(y, first_b)
    ccopy(1 - y).wait_recv()
    stage[...] = (at(1 - y, c)[...].astype(f32) + cbuf[1 - y].astype(f32)).astype(bf)
    yc = pltpu.make_async_remote_copy(
        src_ref=stage, dst_ref=ybuf, send_sem=ysend, recv_sem=yrecv, device_id=Y, device_id_type=MESH)
    yc.start()
    queries[1].pass_on(1)
    ccopy(y).wait_recv()
    gfirst = at(y, c)[...].astype(f32) + cbuf[y].astype(f32)
    value = x_ref[own].astype(f32)
    rs = row_norm(value)
    unit = value * rs
    yc.wait_recv()
    gfirst = gfirst + ybuf[...].astype(f32)
    gn1 = jnp.sum(gfirst * unit, axis=0, keepdims=True)
    cg = gfirst * g1_ref[...]
    gin[...] = (gres_ref[...] + rs * (cg - unit * jnp.mean(cg * unit, axis=1, keepdims=True))).astype(bf)

    queries[0].pass_on(3)
    query_part(0)
    keys.pass_on(1)
    cp(0, gin, y, c, Y, 0).start()
    cp(0, gin, y, c, C, 1).start()
    gin_ref[own] = gin[...]
    part_width = width // 8
    qgain = jnp.sum(qgain_ref[...], axis=0, keepdims=True)
    for i in range(8):
        for j in range(part_width // 128):
            lo = i * part_width + j * 128
            vpart[i, j : j + 1] = gn1[:, lo : lo + 128]
            vpart[i, part_width // 128 + j : part_width // 128 + j + 1] = gn2_ref[:, lo : lo + 128]
        vpart[i, 2 * part_width // 128 : 7] = jnp.broadcast_to(qgain, (7 - 2 * part_width // 128, head))
        vpart[i, 7:8] = kgain

    def vcopy(i):
        to = (ctx + i) % 8
        return pltpu.make_async_remote_copy(
            src_ref=vpart.at[to], dst_ref=vbuf.at[i], send_sem=vsend.at[i], recv_sem=vrecv.at[i],
            device_id=(to, tp), device_id_type=MESH)

    for i in range(1, 8):
        vcopy(i).start()
    queries[1].pass_on(2)
    keys.pass_on(2)
    total = vpart[ctx]
    for i in range(1, 8):
        vcopy(i).wait_recv()
        total = total + vbuf[i]
    tbuf[3] = total

    def tcopy(k, to):
        return pltpu.make_async_remote_copy(
            src_ref=tbuf.at[3], dst_ref=tbuf.at[k], send_sem=tsend.at[k], recv_sem=trecv.at[k],
            device_id=to, device_id_type=MESH)

    sums = [tcopy(k, to) for k, to in enumerate((Y, C, D))]
    for t in sums:
        t.start()
    for n, (src, dst) in enumerate(pairs):
        cp(n, src, 1 - y, c, Y, 0).wait_recv()
        cp(n, place(dst, 1 - y, c), 1 - y, c, C, 2).start()
    swaps[0].wait_recv()
    gout_ref[...] = nn(att_t[...], back_ref[:, own_lanes]) + obuf[...].astype(f32)
    swaps[1].wait_recv()
    grouter_ref[...] = (grouter_both[x] + rbuf[...].astype(f32)).T[: grouter_ref.shape[0]]
    queries[1].pass_on(3)
    query_part(1)
    keys.pass_on(3)
    right = kvbuf[...].reshape(turned.shape[1], 2 * head)
    ksrc[...] = nn(turned[far_cols], right).astype(bf)
    swaps[4].start()
    gkv_ref[...] = nn(turned[own_cols], right)
    for t in sums:
        t.wait_recv()
    vo_ref[...] = (tbuf[3] + tbuf[0]) + (tbuf[1] + tbuf[2])
    for n, (src, dst) in enumerate(pairs):
        cp(n, src, y, 1 - c, C, 1).wait_recv()
        cp(n, src, 1 - y, 1 - c, C, 2).wait_recv()
        cp(n, src, y, c, Y, 0).wait_send()
        cp(n, src, y, c, C, 1).wait_send()
        cp(n, place(dst, 1 - y, c), 1 - y, c, C, 2).wait_send()
    for t in sums:
        t.wait_send()
    for i in range(1, 8):
        vcopy(i).wait_send()
    for line in (*queries, keys):
        line.finish()
    for n in range(2):
        swaps[2 + n].wait_recv()
        gq_ref[:, n * span : (n + 1) * span] += qgot[n].astype(f32)
    swaps[4].wait_recv()
    gkv_ref[...] += kgot[...].astype(f32)
    for s in swaps:
        s.wait_send()
    yc.wait_send()
    ccopy(0).wait_send()
    ccopy(1).wait_send()
    for zz in range(4):
        xcopy(zz).wait_send()

        @pl.when(zz != z)
        def _():
            zcopy(zz, up, zz).wait_send()


def tail(dkv, qlow, kraw, kg, cos, sin, wq, wk, wv, x, g1, gres, layer, gn2, qgain, first, att, back, rows_all, experts, cid):
    tok, width = x.shape
    rows = gres.shape[0]
    half, head = dkv.shape[2:]
    per = first.shape[1] // 2
    f32, bf = jnp.float32, jnp.bfloat16
    dma = pltpu.SemaphoreType.DMA
    vm, anywhere = pl.BlockSpec(memory_space=pltpu.VMEM), pl.BlockSpec(memory_space=pl.ANY)

    def out(shape, kind):
        return jax.ShapeDtypeStruct(shape, kind)

    def mem(*shape, kind=bf):
        return pltpu.VMEM(shape, kind)

    return pl.pallas_call(
        tail_kernel,
        in_specs=[vm] * 3 + [anywhere] + [vm] * 2 + [anywhere] * 5 + [vm] * 4 + [anywhere] * 2 + [vm] + [anywhere],
        out_specs=[vm] * 7,
        out_shape=[
            out((tok, width), bf), out((tok, width), bf), out((per, qlow.shape[1]), f32),
            out((per, 2 * head), f32), out((att.shape[1], per), f32),
            out((experts, per), f32), out((8, 128), f32),
        ],
        scratch_shapes=[
            mem(*wq.shape), mem(*kg.shape, kind=f32), mem(*wk.shape), mem(*wv.shape), mem(*x.shape),
            mem(*g1.shape, kind=f32), mem(*first.shape), mem(*att.shape), mem(*first.shape),
            mem(att.shape[1], att.shape[0]), mem(4, 4, half, head), mem(5, 4, half, head), mem(4, 4, half, head),
            mem(tok, width), mem(2, rows, width), mem(rows, width), mem(rows, width),
            mem(8, 8, 128, kind=f32), mem(8, 8, 128, kind=f32), mem(4, 8, 128, kind=f32), mem(rows, width),
            mem(2, 4, tok, qlow.shape[1] // 2), mem(4, tok, 2 * head), mem(2 * per, first.shape[0]),
            mem(att.shape[1], per), mem(att.shape[1], per),
            mem(per, 128), mem(per, 128),
            mem(2, per, qlow.shape[1] // 2), mem(2, per, qlow.shape[1] // 2),
            mem(per, 2 * head), mem(per, 2 * head), mem(2, per, 128, kind=f32),
            dma((12,)), dma((4,)), dma((4,)), dma((4,)), dma((5,)), dma((2,)), dma((2,)), dma, dma,
            dma((2, 3)), dma((2, 4)), dma((8,)), dma((8,)), dma((3,)), dma((3,)),
            dma((2, 2, 4)), dma((2, 4)), dma((2, 4)), dma((4,)), dma((5,)), dma((5,)),
        ],
        compiler_params=pltpu.CompilerParams(
            collective_id=cid, has_side_effects=True, vmem_limit_bytes=52 * 2**20
        ),
        name="tail",
    )(dkv, qlow, kraw, kg, cos, sin, wq, wk, wv, x, g1, gres, layer, gn2, qgain, first, att, back, rows_all)


def experts_kernel(
    own,
    piece_ref, wg_ref, wu_ref, wd_ref,
    all_ref, pair_ref, hs_ref, gl_ref, ul_ref, hst_ref, glt_ref, ult_ref,
    land, mats, s_ref, t_ref, pairs, lows, turns,
    gsem, gsend, grecv, msem, asem, psem, lsem, tsem,
):
    bf, f32 = jnp.bfloat16, jnp.float32
    width = wg_ref.shape[1]
    extra = t_ref.shape[1]
    hid = wg_ref.shape[0]
    tok = 4 * piece_ref.shape[0]
    weights = [pltpu.make_async_copy(r, mats.at[n], msem.at[n]) for n, r in enumerate((wg_ref, wu_ref, wd_ref))]
    for cp in weights:
        cp.start()
    named = lax.axis_index("ctx") * own

    def expert_of(index):
        return named + sum((index >= e * hid // own).astype(jnp.int32) for e in range(1, own))

    shape = s_ref.shape
    expert = expert_of(lax.broadcasted_iota(jnp.int32, shape, 1))
    place = lax.broadcasted_iota(jnp.int32, shape, 0)
    s_ref[...] = ((place == expert) | (place == expert + extra // 4)).astype(f32).astype(bf)
    expert = expert_of(lax.broadcasted_iota(jnp.int32, shape[::-1], 0))
    place = lax.broadcasted_iota(jnp.int32, shape[::-1], 1)
    t_ref[...] = (place == expert).astype(f32).astype(bf)
    barrier_all()
    wide = piece_ref.shape[1]
    cut = wide // 256 * 128
    gathers = [
        Gather(piece_ref, land, pl.ds(0, cut), gsend.at[0], grecv.at[0]),
        Gather(piece_ref, land, pl.ds(cut, wide - cut), gsend.at[1], grecv.at[1]),
    ]
    for gather in gathers:
        gather.start()
    z, x, y, c, ax, ay, bx, by = gathers[0].at_me
    rows = piece_ref.shape[0]
    me = pid(z, x, y, c)
    local = pltpu.make_async_copy(
        piece_ref, land.at[pl.ds(pl.multiple_of(me * rows, rows), rows)], gsem)
    local.start()

    def place_of(u):
        return far_z(z, 3 - u // 2), x + (u % 2) * (1 - 2 * x)

    def block_rows(u):
        zz, xx = place_of(u)
        return pl.ds(pl.multiple_of((zz * 2 + xx) * tok, tok), tok)

    def results(u):
        slot = u % 2
        span = block_rows(u)
        copies = [pltpu.make_async_copy(pairs.at[slot], pair_ref.at[span], psem.at[slot])]
        for n, (ref, turned) in enumerate(((hs_ref, hst_ref), (gl_ref, glt_ref), (ul_ref, ult_ref))):
            copies.append(pltpu.make_async_copy(lows.at[slot, n], ref.at[span], lsem.at[slot, n]))
            copies.append(pltpu.make_async_copy(turns.at[slot, n], turned.at[:, span], tsem.at[slot, n]))
        return copies

    def whole(u):
        span = block_rows(u)
        return pltpu.make_async_copy(land.at[span], all_ref.at[span], asem.at[u])

    local.wait()

    def step(u, carry):
        zz, xx = place_of(u)
        slot = u % 2

        @pl.when(u % 2 == 0)
        def _():
            for gather in gathers:
                gather.from_a(zz)
                gather.from_b(zz, bx, by)

            @pl.when(u < 6)
            def _():
                for gather in gathers:
                    gather.from_line(far_z(z, 2 - u // 2))

        @pl.when(u % 2 == 1)
        def _():
            for gather in gathers:
                gather.from_b(zz, 1 - x, 1 - y)

        for yy in range(2):
            for gather in gathers:
                gather.wait(pid(zz, xx, yy, 1 - c))

        whole(u).start()

        @pl.when(u == 0)
        def _():
            for cp in weights:
                cp.wait()

        @pl.when(u > 1)
        def _():
            for cp in results(u - 2):
                cp.wait()

        rows = block_rows(u)
        value = land[rows, :width]
        spread = nn(land[rows, 2 * width :], s_ref[...])
        gate = nt(value, mats[0])
        up = nt(value, mats[1])
        back = nt(land[rows, width : 2 * width], mats[2])
        sig = 1.0 / (1.0 + jnp.exp(-gate))
        silu = gate * sig
        hidden = silu * up
        hs = (hidden * spread).astype(bf)
        prod = hidden * back
        high = prod.astype(bf)
        low = (prod - high.astype(f32)).astype(bf)
        pairs[slot] = (nn(high, t_ref[...]) + nn(low, t_ref[...])).astype(bf)
        grad = back * spread
        gl = (grad * up * sig * (1.0 + gate * (1.0 - sig))).astype(bf)
        ul = (grad * silu).astype(bf)
        for n, v in enumerate((hs, gl, ul)):
            lows[slot, n] = v
            turns[slot, n] = v.T
        for cp in results(u):
            cp.start()
        return carry

    lax.fori_loop(0, 8, step, 0)
    for u in (6, 7):
        for cp in results(u):
            cp.wait()
    for u in range(8):
        whole(u).wait()
    for gather in gathers:
        gather.finish()


def experts_forward(piece, wg, wu, wd, own, cid):
    rows, wide = piece.shape
    hid, width = wg.shape
    n = 32 * rows
    tok = 4 * rows
    extra = wide - 2 * width
    bf = jnp.bfloat16
    dma = pltpu.SemaphoreType.DMA
    anywhere = pl.BlockSpec(memory_space=pl.ANY)

    def out(*shape):
        return jax.ShapeDtypeStruct(shape, bf)

    return pl.pallas_call(
        functools.partial(experts_kernel, own),
        in_specs=[anywhere] * 4,
        out_specs=[anywhere] * 8,
        out_shape=[out(n, wide), out(n, extra)] + [out(n, hid)] * 3 + [out(hid, n)] * 3,
        scratch_shapes=[
            pltpu.VMEM((n, wide), bf), pltpu.VMEM((3, hid, width), bf), pltpu.VMEM((extra, hid), bf),
            pltpu.VMEM((hid, extra), bf), pltpu.VMEM((2, tok, extra), bf),
            pltpu.VMEM((2, 3, tok, hid), bf), pltpu.VMEM((2, 3, hid, tok), bf),
            dma, dma((2, 5, 32)), dma((2, 32)), dma((3,)), dma((8,)), dma((2,)), dma((2, 3)), dma((2, 3)),
        ],
        compiler_params=pltpu.CompilerParams(
            collective_id=cid, has_side_effects=True, vmem_limit_bytes=60 * 2**20
        ),
        cost_estimate=pl.CostEstimate(
            flops=6 * n * width * hid, bytes_accessed=10 * n * width, transcendentals=n * hid
        ),
        name="experts_forward",
    )(piece, wg, wu, wd)


EPSILON = 1e-06
ROPE_BASE = 1000000.0
MASKED_SCORE = -1000000000.0
BF = jnp.bfloat16
F32 = jnp.float32


def dotf(a, b, dims):
    return lax.dot_general(a, b, (dims, ((), ())), preferred_element_type=F32)


def nt(a, b):
    return lax.dot_general(a, b, (((1,), (1,)), ((), ())), preferred_element_type=jnp.float32)


def nn(a, b):
    return lax.dot_general(a, b, (((1,), (0,)), ((), ())), preferred_element_type=jnp.float32)


def tn(a, b):
    return lax.dot_general(a, b, (((0,), (0,)), ((), ())), preferred_element_type=jnp.float32)


def plain_expert_kernel(x_ref, cot_ref, wg_ref, wu_ref, wd_ref, s_ref, t_ref, part_ref, gl_ref, ul_ref, hs_ref):
    bf = jnp.bfloat16
    width = cot_ref.shape[1]
    x = x_ref[:, :width]
    spread = nn(x_ref[:, width:], s_ref[...])
    gate = nt(x, wg_ref[...])
    up = nt(x, wu_ref[...])
    back = nt(cot_ref[...], wd_ref[...])
    sig = 1.0 / (1.0 + jnp.exp(-gate))
    silu = gate * sig
    hidden = silu * up
    hs = (hidden * spread).astype(bf)
    hs_ref[...] = hs.T
    part_ref[:, :width] = nn(hs, wd_ref[...]).astype(bf)
    prod = hidden * back
    high = prod.astype(bf)
    low = (prod - high.astype(jnp.float32)).astype(bf)
    part_ref[:, 2 * width :] = (nn(high, t_ref[...]) + nn(low, t_ref[...])).astype(bf)
    grad = back * spread
    gl = (grad * up * sig * (1.0 + gate * (1.0 - sig))).astype(bf)
    ul = (grad * silu).astype(bf)
    gl_ref[...] = gl.T
    ul_ref[...] = ul.T
    part_ref[:, width : 2 * width] = (nn(gl, wg_ref[...]) + nn(ul, wu_ref[...])).astype(bf)


def expert_blocks(x_all, cot_all, gate_mat, up_mat, down_mat, spread_mat, pick_mat, block=256):
    n, width = cot_all.shape
    wide = x_all.shape[1]
    hid = gate_mat.shape[0]
    bf = jnp.bfloat16

    def rows(w):
        return pl.BlockSpec((block, w), lambda i: (i, 0))

    def whole(v):
        return pl.BlockSpec(v.shape, lambda i: (0, 0), pipeline_mode=pl.Buffered(1))

    return pl.pallas_call(
        plain_expert_kernel,
        grid=(n // block,),
        in_specs=[rows(wide), rows(width)]
        + [whole(v) for v in (gate_mat, up_mat, down_mat, spread_mat, pick_mat)],
        out_specs=[rows(width + wide)] + [pl.BlockSpec((hid, block), lambda i: (0, i))] * 3,
        out_shape=[jax.ShapeDtypeStruct((n, width + wide), bf)]
        + [jax.ShapeDtypeStruct((hid, n), bf)] * 3,
        compiler_params=pltpu.CompilerParams(
            dimension_semantics=("arbitrary",), vmem_limit_bytes=56 * 2**20
        ),
        cost_estimate=pl.CostEstimate(
            flops=12 * n * width * hid, bytes_accessed=10 * n * width, transcendentals=n * hid
        ),
        name="plain_experts",
    )(x_all, cot_all, gate_mat, up_mat, down_mat, spread_mat, pick_mat)


def expert_grad_kernel(x_ref, cot_ref, gl_ref, ul_ref, hs_ref, gg_ref, gu_ref, gd_ref):
    first = pl.program_id(1) == 0

    def put(ref, low, full):
        value = nn(low[...], full[...])

        @pl.when(first)
        def _():
            ref[...] = value

        @pl.when(jnp.logical_not(first))
        def _():
            ref[...] += value

    put(gg_ref, gl_ref, x_ref)
    put(gu_ref, ul_ref, x_ref)
    put(gd_ref, hs_ref, cot_ref)


def expert_grads(x_all, cot_all, gl, ul, hs, width, first=0, block=256):
    n = x_all.shape[0]
    hid = gl.shape[0]
    span = min(n, 2048)
    cols = pl.BlockSpec((span, block), lambda i, j: (j, i))
    cots = pl.BlockSpec((span, block), lambda i, j: (j, i + first // block))
    rows = pl.BlockSpec((hid, span), lambda i, j: (0, j))
    out = pl.BlockSpec((hid, block), lambda i, j: (0, i))
    return pl.pallas_call(
        expert_grad_kernel,
        grid=(width // block, n // span),
        in_specs=[cols, cots, rows, rows, rows],
        out_specs=[out] * 3,
        out_shape=[jax.ShapeDtypeStruct((hid, width), jnp.float32)] * 3,
        compiler_params=pltpu.CompilerParams(
            dimension_semantics=("arbitrary", "arbitrary"), vmem_limit_bytes=56 * 2**20
        ),
        cost_estimate=pl.CostEstimate(
            flops=6 * n * width * hid, bytes_accessed=10 * n * width, transcendentals=0
        ),
        name="expert_grads",
    )(x_all, cot_all, gl, ul, hs)


class Links:
    def ag_all(self, piece):
        return lax.all_gather(piece, ("ctx", "tp"), axis=0, tiled=True)

    def rs_all(self, part):
        return lax.psum_scatter(part, ("ctx", "tp"), scatter_dimension=0, tiled=True).astype(F32)

    def ag_ctx(self, piece):
        return lax.all_gather(piece, "ctx", axis=0, tiled=True)

    def rs_ctx(self, part):
        return lax.psum_scatter(part, "ctx", scatter_dimension=0, tiled=True).astype(F32)

    def rs_tp(self, part):
        return lax.psum_scatter(part, "tp", scatter_dimension=0, tiled=True).astype(F32)

    def ag_tp(self, piece):
        return lax.all_gather(piece, "tp", axis=0, tiled=True)

    def finish(self, a, b, vectors):
        total = lax.psum_scatter(vectors, "ctx", scatter_dimension=0, tiled=True)
        gathered = (lax.all_gather(v, "tp", axis=0, tiled=True) for v in (a, b))
        return (*gathered, lax.psum(total, "tp"))


def rms_norm(values, gain_vec):
    factor = lax.rsqrt(jnp.mean(values * values, axis=-1, keepdims=True) + EPSILON)
    return values * factor * gain_vec


def rotate(values, rotary_angles):
    half_size = values.shape[-1] // 2
    first_half = values[..., :half_size]
    second_half = values[..., half_size:]
    cosine = jnp.cos(rotary_angles)
    sine_part = jnp.sin(rotary_angles)
    return jnp.concatenate(
        [
            first_half * cosine - second_half * sine_part,
            second_half * cosine + first_half * sine_part,
        ],
        axis=-1,
    )


def angles_of(token_positions, head_width):
    freq_steps = jnp.arange(head_width // 2).astype(F32) * (2.0 / head_width)
    frequency = jnp.exp(-math.log(ROPE_BASE) * freq_steps)
    return token_positions.astype(F32)[..., None] * frequency


def positions_of(block_order, dev_count, block_len):
    first_block = jnp.transpose(block_order)
    block_pair = jnp.stack([first_block, 2 * dev_count - 1 - first_block], axis=-1)
    spread = block_pair[..., None] * block_len + jnp.arange(block_len, dtype=jnp.int32)
    return spread.reshape(dev_count, block_order.shape[0], 2 * block_len)


def head_route_path(raw_heads, gain_vec, rotary_angles, head_count):
    shaped = raw_heads.reshape(raw_heads.shape[0], head_count, -1)
    return rotate(rms_norm(shaped, gain_vec), rotary_angles[:, None, :])


def attend_forward(seq_item):
    query_matrix, every_key_row, every_value_row, query_pos, key_pos = seq_item
    score_scale = 1.0 / math.sqrt(query_matrix.shape[-1])
    unscaled_scores = jnp.einsum(
        "upnj,apj->upna", query_matrix, every_key_row, preferred_element_type=F32
    )
    allowed = query_pos[:, None, None, None] >= key_pos[None, None, None, :]
    scores = jnp.where(allowed, unscaled_scores * score_scale, MASKED_SCORE)
    row_top = jnp.max(scores, axis=-1, keepdims=True)
    exp_scores = jnp.exp(scores - row_top)
    totals = jnp.sum(exp_scores, axis=-1, keepdims=True)
    lower_attention_probs = (exp_scores / totals).astype(BF)
    attended_mix = jnp.einsum(
        "jzfq,qzx->jzfx", lower_attention_probs, every_value_row, preferred_element_type=F32
    )
    return (attended_mix, (row_top + jnp.log(totals))[..., 0])


def attend_backward(seq_item):
    (
        query_matrix,
        every_key_row,
        every_value_row,
        query_pos,
        key_pos,
        grad_attended_mix,
        log_total,
    ) = seq_item
    score_scale = 1.0 / math.sqrt(query_matrix.shape[-1])
    unscaled_scores = jnp.einsum(
        "upnj,apj->upna", query_matrix, every_key_row, preferred_element_type=F32
    )
    allowed = query_pos[:, None, None, None] >= key_pos[None, None, None, :]
    scores = jnp.where(allowed, unscaled_scores * score_scale, MASKED_SCORE)
    attention_probs = jnp.exp(scores - log_total[..., None])
    grad_probs = jnp.einsum(
        "upnj,apj->upna", grad_attended_mix, every_value_row, preferred_element_type=F32
    )
    row_inner = jnp.sum(attention_probs * grad_probs, axis=-1, keepdims=True)
    grad_score_dots = (attention_probs * (grad_probs - row_inner) * score_scale).astype(BF)
    grad_queries = jnp.einsum(
        "jzfq,qzx->jzfx", grad_score_dots, every_key_row, preferred_element_type=F32
    )
    grad_key_rows = jnp.einsum(
        "axfv,axfz->vxz", grad_score_dots, query_matrix, preferred_element_type=F32
    )
    grad_values = jnp.einsum(
        "axfv,axfz->vxz", attention_probs.astype(BF), grad_attended_mix, preferred_element_type=F32
    )
    return (grad_queries, grad_key_rows, grad_values)


def gates_of(logits, routes):
    experts = logits.shape[1]
    named = jnp.any(routes[:, :, None] == jnp.arange(experts, dtype=jnp.int32), axis=1)
    masked = jnp.where(named, logits, -jnp.inf)
    top = jnp.max(masked, axis=1, keepdims=True)
    weights = jnp.where(named, jnp.exp(masked - top), 0.0)
    return weights / jnp.sum(weights, axis=1, keepdims=True)


def plain_shards(
    tokens_in,
    block_order,
    routes,
    norm1_gain,
    w_query,
    key_weight,
    value_weight,
    query_gain,
    key_gain,
    w_out,
    norm2_gain,
    w_router,
    w_gate,
    w_up,
    w_down,
    cotangent,
):
    tok_count, model_width = tokens_in.shape
    head_size = query_gain.shape[0]
    local_heads = w_query.shape[1] // head_size
    local_kv = key_weight.shape[1] // head_size
    query_group_width = local_heads // local_kv
    seq_count = block_order.shape[0]
    devices, tp_size = lax.axis_size("ctx"), lax.axis_size("tp")
    links = Links()
    me, tp_me = lax.axis_index("ctx"), lax.axis_index("tp")
    rows = tok_count // tp_size
    block_len = tok_count // (2 * seq_count)
    experts = w_router.shape[1]
    own_experts, _, units = w_gate.shape
    hid = own_experts * units
    all_tok = devices * tok_count

    def own_rows(v):
        return lax.dynamic_slice_in_dim(v, tp_me * rows, rows, axis=0)

    cot_own = own_rows(cotangent)
    cot_all = lax.all_gather(cot_own, ("ctx", "tp"), axis=0, tiled=True)

    token_positions = positions_of(block_order, devices, block_len)
    query_pos = lax.dynamic_index_in_dim(token_positions, me, 0, keepdims=False)
    key_pos = jnp.transpose(token_positions, (1, 0, 2)).reshape(seq_count, devices * 2 * block_len)
    rotary_angles = angles_of(query_pos.reshape(-1), head_size)
    inputs = tokens_in.astype(F32)
    first_in = rms_norm(inputs, norm1_gain).astype(BF)
    query_raw = jnp.dot(first_in, w_query, preferred_element_type=F32)
    unrotated_key = jnp.dot(first_in, key_weight, preferred_element_type=F32)
    value_rows = jnp.dot(first_in, value_weight, preferred_element_type=F32).astype(BF)

    def rope_heads(raw_query, raw_key, gain_query, key_norm_gain):
        return (
            head_route_path(raw_query, gain_query, rotary_angles, local_heads),
            head_route_path(raw_key, key_norm_gain, rotary_angles, local_kv),
        )

    (query_rot, key_rot), rope_back = jax.vjp(
        rope_heads, query_raw, unrotated_key, query_gain, key_gain
    )
    query_rows = query_rot.astype(BF).reshape(
        seq_count, 2 * block_len, local_kv, query_group_width, head_size
    )
    kv_width = local_kv * head_size
    kv_own = jnp.concatenate([key_rot.astype(BF).reshape(tok_count, kv_width), value_rows], axis=1)
    kv_all = links.ag_ctx(kv_own)
    kv_seq = kv_all.reshape(devices, seq_count, 2 * block_len, 2, local_kv, head_size)
    kv_seq = kv_seq.transpose(3, 1, 0, 2, 4, 5).reshape(
        2, seq_count, devices * 2 * block_len, local_kv, head_size
    )
    key_full, value_full = kv_seq[0], kv_seq[1]
    attended_mix, log_total = lax.map(
        attend_forward, (query_rows, key_full, value_full, query_pos, key_pos)
    )
    attended = attended_mix.reshape(tok_count, local_heads * head_size).astype(BF)
    attn_part = jnp.dot(attended, w_out, preferred_element_type=F32).astype(BF)
    residual = own_rows(inputs) + links.rs_tp(attn_part)
    second_normed, second_back = jax.vjp(rms_norm, residual, norm2_gain)
    second_in = second_normed.astype(BF)
    extra = -(-2 * experts // 128) * 128
    gates = gates_of(jnp.dot(second_in, w_router, preferred_element_type=F32), own_rows(routes))
    gates_high = gates.astype(BF)
    gates_low = (gates - gates_high.astype(F32)).astype(BF)
    pad = jnp.zeros((rows, extra - 2 * experts), BF)
    second_all = links.ag_all(
        jnp.concatenate([second_in, gates_high, gates_low, pad], axis=1)
    )
    column = jnp.arange(extra, dtype=jnp.int32)[:, None]
    named = me * own_experts + jnp.arange(hid, dtype=jnp.int32)[None, :] // units
    pick = (column == named).astype(BF)
    spread = pick + (column == named + experts).astype(BF)
    gate_mat = w_gate.transpose(0, 2, 1).reshape(hid, model_width)
    up_mat = w_up.transpose(0, 2, 1).reshape(hid, model_width)
    down_mat = w_down.reshape(hid, model_width)
    part, gate_low, up_low, hidden_low = expert_blocks(
        second_all, cot_all, gate_mat, up_mat, down_mat, spread, pick.T
    )
    sums_own = links.rs_all(part)
    out_own = sums_own[:, :model_width]
    entry_own = sums_own[:, model_width:]
    gate_total = entry_own[:, model_width : model_width + experts]
    grad_logits = (
        gates * (gate_total - jnp.sum(gates * gate_total, axis=1, keepdims=True))
    ).astype(BF)
    grad_second = entry_own[:, :model_width] + dotf(grad_logits, w_router, ((1,), (1,)))
    grad_resid_norm, grad_norm2 = second_back(grad_second)
    grad_residual = cot_own.astype(F32) + grad_resid_norm
    pad = jnp.zeros((rows, -experts % 128), BF)
    back_all = links.ag_tp(
        jnp.concatenate([grad_residual.astype(BF), grad_logits, pad], axis=1)
    )
    grad_attn_low = back_all[:, :model_width]
    second_own = lax.dynamic_slice(second_all, (me * tok_count, 0), (tok_count, model_width))
    router_part = dotf(second_own, back_all[:, model_width:], ((0,), (0,)))
    grad_out = dotf(attended, grad_attn_low, ((0,), (0,)))
    grad_mixed = dotf(grad_attn_low, w_out, ((1,), (1,))).astype(BF)
    grad_mixed = grad_mixed.reshape(
        seq_count, 2 * block_len, local_kv, query_group_width, head_size
    )
    grad_query_seq, grad_key_seq, grad_value_seq = lax.map(
        attend_backward,
        (query_rows, key_full, value_full, query_pos, key_pos, grad_mixed, log_total),
    )
    grad_kv = jnp.stack([grad_key_seq, grad_value_seq]).astype(BF)
    grad_kv = grad_kv.reshape(2, seq_count, devices, 2 * block_len, kv_width)
    grad_kv = grad_kv.transpose(2, 1, 3, 0, 4).reshape(all_tok, 2 * kv_width)
    grad_kv_own = links.rs_ctx(grad_kv)
    grad_query_rot = grad_query_seq.reshape(tok_count, local_heads, head_size)
    grad_key_rot = grad_kv_own[:, :kv_width].reshape(tok_count, local_kv, head_size)
    grad_query_raw, grad_key_raw, grad_qgain, grad_kgain = rope_back(
        (grad_query_rot, grad_key_rot)
    )
    query_low = grad_query_raw.astype(BF)
    key_low = grad_key_raw.astype(BF)
    value_low = grad_kv_own[:, kv_width:].astype(BF)
    first_part = dotf(query_low, w_query, ((1,), (1,)))
    first_part = first_part + dotf(key_low, key_weight, ((1,), (1,)))
    first_part = first_part + dotf(value_low, value_weight, ((1,), (1,)))
    grad_first = links.rs_tp(first_part.astype(BF))
    grad_first, gate_low = lax.optimization_barrier((grad_first, gate_low))
    grads = expert_grads(second_all, cot_all, gate_low, up_low, hidden_low, model_width)
    grad_gate, grad_up = (
        v.reshape(own_experts, units, model_width).transpose(0, 2, 1) for v in grads[:2]
    )
    grad_down = grads[2].reshape(own_experts, units, model_width)
    _, first_back = jax.vjp(rms_norm, own_rows(inputs), norm1_gain)
    grad_input_norm, grad_norm1 = first_back(grad_first)
    def over_ctx(v, dim):
        return lax.psum_scatter(v.astype(BF), "ctx", scatter_dimension=dim, tiled=True).astype(F32)

    grad_query = over_ctx(dotf(first_in, query_low, ((0,), (0,))), 0)
    kv_part = dotf(first_in, jnp.concatenate([key_low, value_low], axis=1), ((0,), (0,)))
    small = links.rs_ctx(jnp.concatenate([kv_part, router_part], axis=1).astype(BF))
    grad_key = small[:, :kv_width]
    grad_value = small[:, kv_width : 2 * kv_width]
    grad_router = small[:, 2 * kv_width : 2 * kv_width + experts]
    grad_out = over_ctx(grad_out, 1)
    vectors = [
        v.reshape(devices, -1) for v in (grad_norm1, grad_norm2, grad_qgain, grad_kgain)
    ]
    sizes = [v.shape[1] for v in vectors]
    pad = jnp.zeros((devices, -sum(sizes) % 1024), F32)
    packed = jnp.concatenate([*vectors, pad], axis=1).reshape(-1, 128)
    grad_input, layer_out, total = links.finish(
        (grad_residual + grad_input_norm).astype(BF), (residual + out_own).astype(BF), packed
    )
    total = total.reshape(-1)

    def piece_of(n):
        start = sum(sizes[:n])
        return total[start : start + sizes[n]]

    return (
        layer_out,
        grad_input,
        piece_of(0),
        grad_query,
        grad_key,
        grad_value,
        piece_of(2),
        piece_of(3),
        grad_out,
        piece_of(1),
        grad_router,
        grad_gate,
        grad_up,
        grad_down,
    )


def fast_shards(
    tokens_in,
    block_order,
    routes,
    norm1_gain,
    w_query,
    key_weight,
    value_weight,
    query_gain,
    key_gain,
    w_out,
    norm2_gain,
    w_router,
    w_gate,
    w_up,
    w_down,
    cotangent,
):
    tok_count, model_width = tokens_in.shape
    head_size = query_gain.shape[0]
    seq_count = block_order.shape[0]
    devices, tp_size = lax.axis_size("ctx"), lax.axis_size("tp")
    me, tp_me = lax.axis_index("ctx"), lax.axis_index("tp")
    rows = tok_count // tp_size
    block_len = tok_count // (2 * seq_count)
    experts = w_router.shape[1]
    own_experts, _, units = w_gate.shape
    hid = own_experts * units

    def row(v):
        return v.reshape(1, -1)


    token_positions = positions_of(block_order, devices, block_len)
    query_pos = lax.dynamic_index_in_dim(token_positions, me, 0, keepdims=False).reshape(-1)
    key_pos = jnp.transpose(token_positions, (1, 0, 2)).reshape(seq_count, -1).astype(F32)
    angles = angles_of(query_pos, head_size)
    cos = jnp.concatenate([jnp.cos(angles)] * 2, axis=1)
    sin = jnp.concatenate([-jnp.sin(angles), jnp.sin(angles)], axis=1)
    query_pos = jnp.broadcast_to(query_pos.astype(F32)[:, None], (tok_count, head_size))
    router_rows = w_router.T
    _, query_raw, key_raw, query_rot, kv_all, attended, logs, residual, gates, piece, first_cols = front(
        tokens_in, row(norm1_gain), w_query, key_weight, value_weight, row(query_gain),
        row(key_gain), cos, sin, query_pos, key_pos, w_out, row(norm2_gain), router_rows,
        routes.T, cotangent, 1,
    )

    gate_mat = w_gate.transpose(0, 2, 1).reshape(hid, model_width)
    up_mat = w_up.transpose(0, 2, 1).reshape(hid, model_width)
    down_mat = w_down.reshape(hid, model_width)
    all_rows, pair, hidden, gate_low, up_low, hidden_turned, gate_turned, up_turned = experts_forward(
        piece, gate_mat, up_mat, down_mat, own_experts, 3
    )
    sums_own, attended_line = reduce_experts(
        hidden, gate_low, up_low, pair, down_mat, gate_mat, up_mat, attended, 6
    )
    layer_piece, grad_residual, grad_norm2, back_cols, query_low, grad_kv, qgain_part = middle(
        sums_own, residual, gates, cotangent, row(norm2_gain), router_rows, w_out, query_rot, kv_all,
        logs, query_raw, row(query_gain), cos, sin, query_pos, key_pos, 7,
    )

    line_tok = 4 * tok_count
    back_cols = back_cols.reshape(line_tok, -1)
    grad_input, layer_out, grad_query, kv_grads, grad_out, grad_router, total = tail(
        grad_kv, query_low, key_raw, row(key_gain), cos, sin, w_query, key_weight, value_weight,
        tokens_in, row(norm1_gain), grad_residual, layer_piece, grad_norm2, qgain_part,
        first_cols.reshape(line_tok, -1), attended_line.reshape(line_tok, -1), back_cols, all_rows, experts, 8,
    )
    per = model_width // devices // 128
    grad_key = kv_grads[:, :head_size]
    grad_value = kv_grads[:, head_size:]
    total, gate_turned = lax.optimization_barrier((total, gate_turned))
    grads = expert_grads(all_rows, all_rows, gate_turned, up_turned, hidden_turned, model_width, model_width)
    grad_gate, grad_up = (
        v.reshape(own_experts, units, model_width).transpose(0, 2, 1) for v in grads[:2]
    )
    grad_down = grads[2].reshape(own_experts, units, model_width)
    share = head_size // devices

    def gain_of(n):
        return lax.dynamic_slice_in_dim(total[n], me * share, share, axis=0)

    return (
        layer_out,
        grad_input,
        total[:per].reshape(-1),
        grad_query,
        grad_key,
        grad_value,
        gain_of(2 * per),
        gain_of(7),
        grad_out,
        total[per : 2 * per].reshape(-1),
        grad_router.T,
        grad_gate,
        grad_up,
        grad_down,
    )


def solution(mesh):
    in_specs = (
        P("ctx", None),
        P(),
        P("ctx", None),
        P(),
        P(None, "tp"),
        P(None, "tp"),
        P(None, "tp"),
        P(),
        P(),
        P("tp", None),
        P(),
        P(),
        P("ctx", None, "tp"),
        P("ctx", None, "tp"),
        P("ctx", "tp", None),
        P("ctx", None),
    )
    out_specs = (
        P("ctx", None),
        P("ctx", None),
        P("ctx"),
        P("ctx", "tp"),
        P("ctx", "tp"),
        P("ctx", "tp"),
        P("ctx"),
        P("ctx"),
        P("tp", "ctx"),
        P("ctx"),
        P("ctx", None),
        P("ctx", None, "tp"),
        P("ctx", None, "tp"),
        P("ctx", "tp", None),
    )
    own = mesh.shape["ctx"] == 8 and mesh.shape["tp"] == 4
    shards = fast_shards if own else plain_shards
    return jax.shard_map(shards, mesh=mesh, in_specs=in_specs, out_specs=out_specs, check_vma=False)
```
